32 devices in a mesh: dp: 16 (over z, x, core), tensor: 2 (over y).
Axes of the slice: x: 2, y: 2, z: 4, core: 2. Of those that a mesh axis runs over, the one named last changes fastest.
Arguments:
- tokens: bfloat16 [24576, 768], P('dp'), may hold values from -6 to 6
- cotangent: bfloat16 [24576, 768], P('dp'), may hold values from -6 to 6
- segment_ids: int32 [16, 1536], P('dp'), may hold values from 0 to 1, never falling along the last dimension, each value on 1 to 1024 neighbouring positions
- timesteps: int32 [16, 2], P('dp'), may hold values from 0 to 1999
- qkv_weight: float32 [768, 3, 768], P('dp', None, 'tensor'), may hold values from -0.25 to 0.25
- out_weight: float32 [768, 768], P('tensor', 'dp'), may hold values from -0.625 to 0.625
- up_weight: float32 [768, 4, 768], P('dp', None, 'tensor'), may hold values from -0.21875 to 0.21875
- down_weight: float32 [4, 768, 768], P(None, 'tensor', 'dp'), may hold values from -0.109375 to 0.109375
- time_inner: float32 [128, 512], P('dp'), may hold values from -0.5 to 0.5
- time_outer: float32 [512, 768], P('dp'), may hold values from -0.25 to 0.25
- time_bias: float32 [512], P('dp'), may hold values from -3 to 3
- head_vectors: float32 [6, 2, 384], P(None, 'tensor', 'dp'), may hold values from -1 to 1
- layer_vectors: float32 [7, 768], P(None, 'dp'), may hold values from 0.5 to 6
- qkv_moment: float32 [768, 3, 768], P('dp', None, 'tensor'), may hold values from -0.001953125 to 0.001953125
- out_moment: float32 [768, 768], P('tensor', 'dp'), may hold values from -0.001953125 to 0.001953125
- up_moment: float32 [768, 4, 768], P('dp', None, 'tensor'), may hold values from -0.001953125 to 0.001953125
- down_moment: float32 [4, 768, 768], P(None, 'tensor', 'dp'), may hold values from -0.001953125 to 0.001953125
- inner_moment: float32 [128, 512], P('dp'), may hold values from -0.001953125 to 0.001953125
- outer_moment: float32 [512, 768], P('dp'), may hold values from -0.001953125 to 0.001953125
- bias_moment: float32 [512], P('dp'), may hold values from -0.001953125 to 0.001953125
- head_moment: float32 [6, 2, 384], P(None, 'tensor', 'dp'), may hold values from -0.001953125 to 0.001953125
- layer_moment: float32 [7, 768], P(None, 'dp'), may hold values from -0.001953125 to 0.001953125
- qkv_average: float32 [768, 3, 768], P('dp', None, 'tensor'), may hold values from -0.25 to 0.25
- out_average: float32 [768, 768], P('tensor', 'dp'), may hold values from -0.625 to 0.625
- up_average: float32 [768, 4, 768], P('dp', None, 'tensor'), may hold values from -0.21875 to 0.21875
- down_average: float32 [4, 768, 768], P(None, 'tensor', 'dp'), may hold values from -0.109375 to 0.109375
- inner_average: float32 [128, 512], P('dp'), may hold values from -0.5 to 0.5
- outer_average: float32 [512, 768], P('dp'), may hold values from -0.25 to 0.25
- bias_average: float32 [512], P('dp'), may hold values from -3 to 3
- head_average: float32 [6, 2, 384], P(None, 'tensor', 'dp'), may hold values from -1 to 1
- layer_average: float32 [7, 768], P(None, 'dp'), may hold values from 0.5 to 1.5
Outputs:
- output: bfloat16 [24576, 768], P('dp')
- input_grad: bfloat16 [24576, 768], P('dp')
- norm: float32 [], replicated
- qkv_master: float32 [768, 3, 768], P('dp', None, 'tensor')
- out_master: float32 [768, 768], P('tensor', 'dp')
- up_master: float32 [768, 4, 768], P('dp', None, 'tensor')
- down_master: float32 [4, 768, 768], P(None, 'tensor', 'dp')
- inner_master: float32 [128, 512], P('dp')
- outer_master: float32 [512, 768], P('dp')
- bias_master: float32 [512], P('dp')
- head_master: float32 [6, 2, 384], P(None, 'tensor', 'dp')
- layer_master: float32 [7, 768], P(None, 'dp')
- qkv_velocity: float32 [768, 3, 768], P('dp', None, 'tensor')
- out_velocity: float32 [768, 768], P('tensor', 'dp')
- up_velocity: float32 [768, 4, 768], P('dp', None, 'tensor')
- down_velocity: float32 [4, 768, 768], P(None, 'tensor', 'dp')
- inner_velocity: float32 [128, 512], P('dp')
- outer_velocity: float32 [512, 768], P('dp')
- bias_velocity: float32 [512], P('dp')
- head_velocity: float32 [6, 2, 384], P(None, 'tensor', 'dp')
- layer_velocity: float32 [7, 768], P(None, 'dp')
- qkv_smoothed: float32 [768, 3, 768], P('dp', None, 'tensor')
- out_smoothed: float32 [768, 768], P('tensor', 'dp')
- up_smoothed: float32 [768, 4, 768], P('dp', None, 'tensor')
- down_smoothed: float32 [4, 768, 768], P(None, 'tensor', 'dp')
- inner_smoothed: float32 [128, 512], P('dp')
- outer_smoothed: float32 [512, 768], P('dp')
- bias_smoothed: float32 [512], P('dp')
- head_smoothed: float32 [6, 2, 384], P(None, 'tensor', 'dp')
- layer_smoothed: float32 [7, 768], P(None, 'dp')
The draws below stay inside these ranges and needn't reach their ends.
Inputs may be any that keep to these rules, and one draw needn't show every extreme that they name: `segment_ids`: within each pack the sequence number never falls, and each of the 2 sequences holds 512 to 1024 tokens.
All inputs are finite; a program needn't handle non-finite values.
Results may differ from the reference program's by a relative error of at most 0.024.
The reference program's roundings to bfloat16 on the way count: a program that leaves them out, or rounds other values in their place, can miss the bound.
Values may be sent and summed in bfloat16 or wider, within the bound.
A program may use at most 128 MiB of HBM per device.

```python
import math
import jax
import jax.numpy as jnp
import numpy as np
from jax import lax

D = 768
HEADS = 12
HD = 64
FF = 3072
TD = 128
TH = 512
TMAX = 2000
SEGS = 2
PACK = 1536
FFB = 4
PACKS = 16
TOKENS = 24576
MPARAMS = 7536640
N_DP = 16
N_TENSOR = 2


def draw_layer_vectors(key, part):
    columns = jnp.arange(D, dtype=jnp.float32) / (D - 1)
    base_values = jax.random.uniform(key, (7, D), jnp.float32, minval=0.7, maxval=1.3)
    ramp_top = 3.0
    ramp_values = 1.0 + (ramp_top - 1.0) * columns
    row_select = jnp.array([0.0, 1.0, 1.0, 0.0, 1.0, 1.0, 0.0], jnp.float32)[:, None]
    return base_values * (1.0 + row_select * (ramp_values[None, :] - 1.0))


def with_ends(entries, rng, least, top_value):
    longest = entries.shape.index(max(entries.shape))
    spots = []
    for shift in (0, 1):
        where = [jax.random.randint(jax.random.fold_in(rng, axis), (), 0, length) for axis, length in enumerate(entries.shape)]
        where[longest] = (where[longest] + shift) % entries.shape[longest]
        spots.append(tuple(where))
    return entries.at[spots[0]].set(least).at[spots[1]].set(top_value)


def with_spikes(values, key, source, target, parts, factor):
    owner, partner = [(jnp.arange(values.shape[position]) // (values.shape[position] // parts)).reshape([-1 if axis == position else 1 for axis in range(values.ndim)]) for position in (source, target)]
    chosen = jax.random.permutation(key, parts)[partner]
    strong = (owner == chosen) | (owner == (partner + parts // 2) % parts)
    return jnp.where(strong, factor * values, values)


def shard_levels(own_key, extent, cuts, smallest, top_value):
    def one(axis_at, shards_of):
        heights = jax.random.uniform(jax.random.fold_in(jax.random.fold_in(own_key, 6), axis_at), (shards_of,), jnp.float32, smallest / len(cuts), top_value / len(cuts))
        return jnp.repeat(jnp.exp(heights), extent[axis_at] // shards_of).reshape((-1,) + (1,) * (len(extent) - axis_at - 1))

    level = one(*cuts[0])
    for cut in cuts[1:]:
        level = level * one(*cut)
    return level


def length_profile(amount, total, reach, slope):
    weights = [(1 << 20) // math.isqrt(grade ** slope) + 1 for grade in range(2, amount + 1)]
    spare, holding = total - reach - (amount - 1), [1] * (amount - 1)
    while spare > 0:
        movable = [i for i in range(amount - 1) if holding[i] < reach]
        mass, budget = sum([weights[i] for i in movable]), spare
        for i in movable:
            addition = min(reach - holding[i], max(1, budget * weights[i] // mass), spare)
            holding[i] = holding[i] + addition
            spare = spare - addition
    return np.array([reach] + holding)


def ragged(stream_key, number_of, total, reach, slope):
    if number_of == 2:
        one = jax.random.randint(stream_key, (), max(1, total - reach), min(reach, total - 1) + 1)
        return jnp.stack([one, total - one])
    sizes = jnp.asarray(length_profile(number_of, total, reach, slope), jnp.int32)
    couples = (number_of - 1) // 2
    giver, sink = sizes[1:1 + 2 * couples:2], sizes[2:2 + 2 * couples:2]
    margin = jnp.minimum(giver - 1, reach - sink)
    passed = jax.random.randint(jax.random.fold_in(stream_key, 1), (couples,), 0, 1 << 20) % (margin + 1)
    sizes = sizes.at[1:1 + 2 * couples:2].set(giver - passed).at[2:2 + 2 * couples:2].set(sink + passed)
    return sizes[jax.random.permutation(jax.random.fold_in(stream_key, 2), number_of)]


def normal_values(rng, extent, scale, bound, cuts=(), held_as=jnp.bfloat16):
    drawn = jax.random.normal(rng, extent, jnp.float32) * scale
    if len(cuts) > 0:
        drawn = shard_levels(rng, extent, cuts, -0.22, 0.18) * drawn
    return jnp.clip(drawn, min=-bound, max=bound).astype(held_as)


def noise_with(rng, dims, scale, limit, shards, heavy, held_as=jnp.bfloat16):
    values = scale * jax.random.normal(rng, dims, jnp.float32)
    if shards:
        values = values * shard_levels(rng, dims, shards, -0.22, 0.18)
    return jnp.clip(with_spikes(values, jax.random.fold_in(rng, 3), *heavy), -limit, limit).astype(held_as)


def setup_inputs(seed: int = 0) -> dict:
    keys = jax.random.split(jax.random.key(seed), 32)
    tokens = noise_with(keys[0], (TOKENS, D), 1.0, 6.0, ((0, 16),), (0, 1, 16, 2.0))
    cotangent = noise_with(keys[1], (TOKENS, D), 1.0, 6.0, ((0, 16),), (0, 1, 16, 2.0))
    segment_ids = jax.vmap(lambda own: jnp.searchsorted(jnp.cumsum(ragged(own, SEGS, PACK, 2 * PACK // 3, 2)), jnp.arange(PACK), side="right"))(jax.random.split(keys[2], PACKS)).reshape((PACKS, PACK)).astype(jnp.int32)
    timesteps = with_ends(jax.random.randint(keys[3], (PACKS, SEGS), 0, TMAX), jax.random.fold_in(keys[3], 1), 0, TMAX - 1).astype(jnp.int32)
    qkv_weight = normal_values(keys[4], (D, 3, D), (2 * D // 3) ** -0.5, 0.25, ((0, 16), (2, 2)), jnp.float32)
    out_weight = normal_values(keys[5], (D, D), (D // 8) ** -0.5, 0.625, ((0, 2), (1, 16)), jnp.float32)
    up_weight = normal_values(keys[6], (D, FFB, D), D ** -0.5, 0.21875, ((0, 16), (2, 2)), jnp.float32)
    down_weight = normal_values(keys[7], (FFB, D, D), FF ** -0.5, 0.109375, ((1, 2), (2, 16)), jnp.float32)
    time_inner = normal_values(keys[8], (TD, TH), TD ** -0.5, 0.5, ((0, 16),), jnp.float32)
    time_outer = normal_values(keys[9], (TH, D), TH ** -0.5, 0.25, ((0, 16),), jnp.float32)
    time_bias = normal_values(keys[10], (TH,), 0.5, 3.0, ((0, 16),), jnp.float32)
    head_vectors = normal_values(keys[11], (6, N_TENSOR, D // N_TENSOR), 0.2, 1.0, ((1, 2), (2, 16)), jnp.float32)
    layer_vectors = draw_layer_vectors(jax.random.fold_in(keys[31], 71), 0)
    qkv_moment = normal_values(keys[13], (D, 3, D), MPARAMS ** -0.5, 0.001953125, ((0, 16), (2, 2)), jnp.float32)
    out_moment = normal_values(keys[14], (D, D), MPARAMS ** -0.5, 0.001953125, ((0, 2), (1, 16)), jnp.float32)
    up_moment = normal_values(keys[15], (D, FFB, D), MPARAMS ** -0.5, 0.001953125, ((0, 16), (2, 2)), jnp.float32)
    down_moment = normal_values(keys[16], (FFB, D, D), MPARAMS ** -0.5, 0.001953125, ((1, 2), (2, 16)), jnp.float32)
    inner_moment = normal_values(keys[17], (TD, TH), MPARAMS ** -0.5, 0.001953125, ((0, 16),), jnp.float32)
    outer_moment = normal_values(keys[18], (TH, D), MPARAMS ** -0.5, 0.001953125, ((0, 16),), jnp.float32)
    bias_moment = normal_values(keys[19], (TH,), MPARAMS ** -0.5, 0.001953125, ((0, 16),), jnp.float32)
    head_moment = normal_values(keys[20], (6, N_TENSOR, D // N_TENSOR), MPARAMS ** -0.5, 0.001953125, ((1, 2), (2, 16)), jnp.float32)
    layer_moment = normal_values(keys[21], (7, D), MPARAMS ** -0.5, 0.001953125, ((1, 16),), jnp.float32)
    qkv_average = normal_values(keys[22], (D, 3, D), (2 * D // 3) ** -0.5, 0.25, ((0, 16), (2, 2)), jnp.float32)
    out_average = normal_values(keys[23], (D, D), (D // 8) ** -0.5, 0.625, ((0, 2), (1, 16)), jnp.float32)
    up_average = normal_values(keys[24], (D, FFB, D), D ** -0.5, 0.21875, ((0, 16), (2, 2)), jnp.float32)
    down_average = normal_values(keys[25], (FFB, D, D), FF ** -0.5, 0.109375, ((1, 2), (2, 16)), jnp.float32)
    inner_average = normal_values(keys[26], (TD, TH), TD ** -0.5, 0.5, ((0, 16),), jnp.float32)
    outer_average = normal_values(keys[27], (TH, D), TH ** -0.5, 0.25, ((0, 16),), jnp.float32)
    bias_average = normal_values(keys[28], (TH,), 0.5, 3.0, ((0, 16),), jnp.float32)
    head_average = normal_values(keys[29], (6, N_TENSOR, D // N_TENSOR), 0.2, 1.0, ((1, 2), (2, 16)), jnp.float32)
    layer_average = jnp.clip(0.5 + 1.0 * jax.random.uniform(keys[30], (7, D), jnp.float32) ** shard_levels(keys[30], (7, D), ((1, 16),), -0.2, 0.2), 0.5, 1.5)
    return {"tokens": tokens, "cotangent": cotangent, "segment_ids": segment_ids, "timesteps": timesteps, "qkv_weight": qkv_weight, "out_weight": out_weight, "up_weight": up_weight, "down_weight": down_weight, "time_inner": time_inner, "time_outer": time_outer, "time_bias": time_bias, "head_vectors": head_vectors, "layer_vectors": layer_vectors, "qkv_moment": qkv_moment, "out_moment": out_moment, "up_moment": up_moment, "down_moment": down_moment, "inner_moment": inner_moment, "outer_moment": outer_moment, "bias_moment": bias_moment, "head_moment": head_moment, "layer_moment": layer_moment, "qkv_average": qkv_average, "out_average": out_average, "up_average": up_average, "down_average": down_average, "inner_average": inner_average, "outer_average": outer_average, "bias_average": bias_average, "head_average": head_average, "layer_average": layer_average}


@jax.custom_vjp
def low(v):
    return lax.optimization_barrier(v.astype(jnp.bfloat16)).astype(jnp.float32)

@jax.custom_vjp
def low_back(v):
    return v

def low_keep(v):
    return (low(v), None)

def low_pass(kept, grad):
    return (grad,)

def back_keep(v):
    return (v, None)

def back_low(kept, grad):
    return (low(grad),)
low.defvjp(low_keep, low_pass)
low_back.defvjp(back_keep, back_low)
EPSILON = 1e-05
MOMENTUM = 0.5
AVERAGE_DECAY = 0.5
HIGHEST_PRECISION = lax.Precision.HIGHEST

def product(left, right, form):
    return jnp.einsum(form, left, right, precision=HIGHEST_PRECISION, preferred_element_type=jnp.float32)

def layer_norm(values, gain_vec, shift_vec):
    centre = lax.optimization_barrier(jnp.mean(values, axis=-1, keepdims=True))
    centred = values - centre
    spread = lax.optimization_barrier(jnp.mean(centred * centred, axis=-1, keepdims=True))
    return centred * lax.rsqrt(spread + EPSILON) * gain_vec + shift_vec

def time_features(step_ids, feat_width):
    midpoint = feat_width // 2
    frequency = jnp.exp(-math.log(10000.0) * jnp.arange(midpoint, dtype=jnp.float32) / midpoint)
    angles = step_ids.astype(jnp.float32)[..., None] * frequency
    return jnp.concatenate([jnp.cos(angles), jnp.sin(angles)], axis=-1)

def attention(queries, keys_all, values_all, seg_ids):
    groups_here = queries.shape[0]
    packed = queries.shape[1]
    block_rows = min(packed, 512)
    block_count = packed // block_rows
    query_heads = queries.reshape(groups_here, block_count, block_rows, HEADS, HD).transpose(1, 0, 2, 3, 4)
    seg_blocks = seg_ids.reshape(groups_here, block_count, block_rows).transpose(1, 0, 2)
    key_heads = keys_all.reshape(groups_here, packed, HEADS, HD)
    value_heads = values_all.reshape(groups_here, packed, HEADS, HD)

    def one_block(query_blk, seg_blk):
        raw_scores = low_back(product(query_blk, key_heads, 'gqhd,gkhd->ghqk') * (1.0 / math.sqrt(HD)))
        same_doc = seg_blk[:, None, :, None] == seg_ids[:, None, None, :]
        masked = jnp.where(same_doc, raw_scores, -1e+30)
        row_peak = lax.optimization_barrier(jnp.max(masked, axis=-1, keepdims=True))
        exponent = jnp.exp(masked - row_peak)
        soft_weights = exponent / lax.optimization_barrier(jnp.sum(exponent, axis=-1, keepdims=True))
        return product(low(soft_weights), value_heads, 'ghqk,gkhd->gqhd')
    checked = jax.checkpoint(one_block)

    def apply_block(pair):
        return checked(pair[0], pair[1])
    outputs = lax.map(apply_block, (query_heads, seg_blocks))
    return outputs.transpose(1, 0, 2, 3, 4).reshape(groups_here, packed, HEADS * HD)

def forward(params, tokens_in, seg_ids, step_ids):
    w_qkv, w_out, w_up, w_down, w_inner, w_outer, b_inner, head_vec, layer_vec = [low(item) for item in params]
    groups_here = tokens_in.shape[0]
    head_rows = head_vec.reshape(6, D)
    width_part = D // N_TENSOR
    feats = low(time_features(step_ids, TD)).reshape(groups_here * SEGS, TD)
    inner_pre = low_back(product(feats, w_inner, 'st,tu->su')) + b_inner
    act_low = low(jax.nn.silu(inner_pre))
    time_embed = (low_back(product(act_low, w_outer, 'su,ud->sd')) + layer_vec[6]).reshape(groups_here, SEGS, D)
    onehot = (seg_ids[..., None] == jnp.arange(SEGS, dtype=jnp.int32)).astype(jnp.float32)
    hidden0 = tokens_in + product(onehot, time_embed, 'gps,gsd->gpd')
    hidden_low = low(hidden0)
    projected = low_back(product(hidden_low, w_qkv, 'gpd,dce->gpce'))
    queries = low(projected[:, :, 0] + head_rows[0])
    keys_all = low(projected[:, :, 1])
    values_all = low(projected[:, :, 2] + head_rows[1])
    attended = low(low_back(attention(queries, keys_all, values_all, seg_ids)))
    attn_parts = [low(product(attended[..., part_index * width_part:(part_index + 1) * width_part], w_out[part_index * width_part:(part_index + 1) * width_part], 'gpe,ef->gpf')) for part_index in range(N_TENSOR)]
    attn_branch = low_back(sum(attn_parts)) + layer_vec[0]
    normed1 = layer_norm(hidden0 + attn_branch, layer_vec[1], layer_vec[2])
    norm_low = low(normed1)
    up_pre = low_back(product(norm_low, w_up, 'gpd,dje->gpje')) + head_rows[2:]
    hid_low = low(jax.nn.gelu(up_pre, approximate=False))
    mlp_parts = [low(product(hid_low[..., part_index * width_part:(part_index + 1) * width_part], w_down[:, part_index * width_part:(part_index + 1) * width_part], 'gpje,jef->gpf')) for part_index in range(N_TENSOR)]
    mlp_branch = low_back(sum(mlp_parts)) + layer_vec[3]
    return layer_norm(normed1 + mlp_branch, layer_vec[4], layer_vec[5])

def advance(master, moment, average, grad, factor, step_rate):
    scaled = grad * factor
    velocity = MOMENTUM * moment + scaled
    fresh_master = master - step_rate * (scaled + MOMENTUM * velocity)
    smoothed = AVERAGE_DECAY * average + (1.0 - AVERAGE_DECAY) * fresh_master
    return (fresh_master, velocity, smoothed)

def reference(tokens, cotangent, segment_ids, timesteps, qkv_weight, out_weight, up_weight, down_weight, time_inner, time_outer, time_bias, head_vectors, layer_vectors, qkv_moment, out_moment, up_moment, down_moment, inner_moment, outer_moment, bias_moment, head_moment, layer_moment, qkv_average, out_average, up_average, down_average, inner_average, outer_average, bias_average, head_average, layer_average):
    masters = (qkv_weight, out_weight, up_weight, down_weight, time_inner, time_outer, time_bias, head_vectors, layer_vectors)
    moments = (qkv_moment, out_moment, up_moment, down_moment, inner_moment, outer_moment, bias_moment, head_moment, layer_moment)
    averages = (qkv_average, out_average, up_average, down_average, inner_average, outer_average, bias_average, head_average, layer_average)
    group_size = 1
    for size_try in range(1, N_DP + 1):
        if N_DP % size_try == 0 and size_try * PACK <= 4096:
            group_size = size_try
    rounds_count = N_DP // group_size
    token_groups = tokens.astype(jnp.float32).reshape(rounds_count, group_size, PACK, D)
    cot_groups = cotangent.astype(jnp.float32).reshape(rounds_count, group_size, PACK, D)
    seg_groups = segment_ids.reshape(rounds_count, group_size, PACK)
    step_groups = timesteps.reshape(rounds_count, group_size, SEGS)

    def one_round(totals, inputs):
        token_g, cot_g, seg_g, step_g = inputs

        def wrapped(params, values_in):
            return forward(params, values_in, seg_g, step_g)
        result, pull = jax.vjp(wrapped, masters, token_g)
        grads, token_grad = pull(cot_g)
        totals = tuple((accum + piece for accum, piece in zip(totals, grads)))
        return (totals, (result, token_grad))
    zeros_start = tuple((jnp.zeros(item.shape, jnp.float32) for item in masters))
    grads, (results, token_grads) = lax.scan(one_round, zeros_start, (token_groups, cot_groups, seg_groups, step_groups))
    output = results.reshape(TOKENS, D).astype(jnp.bfloat16)
    input_grad = token_grads.reshape(TOKENS, D).astype(jnp.bfloat16)
    squares = sum((jnp.sum(piece * piece) for piece in grads))
    norm = jnp.sqrt(squares)
    factor = 1.0 / jnp.maximum(norm, 1.0)
    step_rate = 4.0 * math.sqrt(MPARAMS / D)
    updated = [advance(masters[index], moments[index], averages[index], grads[index], factor, step_rate) for index in range(9)]
    qkv_master, qkv_velocity, qkv_smoothed = updated[0]
    out_master, out_velocity, out_smoothed = updated[1]
    up_master, up_velocity, up_smoothed = updated[2]
    down_master, down_velocity, down_smoothed = updated[3]
    inner_master, inner_velocity, inner_smoothed = updated[4]
    outer_master, outer_velocity, outer_smoothed = updated[5]
    bias_master, bias_velocity, bias_smoothed = updated[6]
    head_master, head_velocity, head_smoothed = updated[7]
    layer_master, layer_velocity, layer_smoothed = updated[8]
    return (output, input_grad, norm, qkv_master, out_master, up_master, down_master, inner_master, outer_master, bias_master, head_master, layer_master, qkv_velocity, out_velocity, up_velocity, down_velocity, inner_velocity, outer_velocity, bias_velocity, head_velocity, layer_velocity, qkv_smoothed, out_smoothed, up_smoothed, down_smoothed, inner_smoothed, outer_smoothed, bias_smoothed, head_smoothed, layer_smoothed)
```

```python
import functools
import math

import jax
import jax.numpy as jnp
from jax import lax
from jax.experimental import pallas as pl
from jax.experimental.pallas import tpu as pltpu
from jax.sharding import PartitionSpec as P

D = 768
HD = 64
TD = 128
SEGS = 2
PACK = 1536
MPARAMS = 7536640


EPSILON = 1e-05
MOMENTUM = 0.5
AVERAGE_DECAY = 0.5


def layer_norm(values, gain_vec, shift_vec):
    centre = jnp.mean(values, axis=-1, keepdims=True)
    centred = values - centre
    spread = jnp.mean(centred * centred, axis=-1, keepdims=True)
    return centred * lax.rsqrt(spread + EPSILON) * gain_vec + shift_vec


def time_features(step_ids, feat_width):
    midpoint = feat_width // 2
    frequency = jnp.exp(-math.log(10000.0) * jnp.arange(midpoint, dtype=jnp.float32) / midpoint)
    angles = step_ids.astype(jnp.float32)[..., None] * frequency
    return jnp.concatenate([jnp.cos(angles), jnp.sin(angles)], axis=-1)


def gelu_exact(values):
    return jax.nn.gelu(values, approximate=False)


def head_slice(matrix, head_index):
    return lax.dynamic_slice_in_dim(matrix, head_index * HD, HD, 1)


def merge_heads(stacked):
    return stacked.transpose(1, 0, 2).reshape(stacked.shape[1], stacked.shape[0] * stacked.shape[2])


def advance(master, moment, average, grad, factor, step_rate):
    scaled = grad * factor
    velocity = MOMENTUM * moment + scaled
    fresh_master = master - step_rate * (scaled + MOMENTUM * velocity)
    smoothed = AVERAGE_DECAY * average + (1.0 - AVERAGE_DECAY) * fresh_master
    return (fresh_master, velocity, smoothed)


def shards_any(
    tokens,
    cotangent,
    segment_ids,
    timesteps,
    qkv_weight,
    out_weight,
    up_weight,
    down_weight,
    time_inner,
    time_outer,
    time_bias,
    head_vectors,
    layer_vectors,
    qkv_moment,
    out_moment,
    up_moment,
    down_moment,
    inner_moment,
    outer_moment,
    bias_moment,
    head_moment,
    layer_moment,
    qkv_average,
    out_average,
    up_average,
    down_average,
    inner_average,
    outer_average,
    bias_average,
    head_average,
    layer_average,
):
    w_qkv, w_out, w_up, w_down, w_inner, w_outer, b_inner, head_vec, layer_vec = (
        lax.all_gather(qkv_weight.astype(jnp.bfloat16), "dp", axis=0, tiled=True),
        lax.all_gather(out_weight.astype(jnp.bfloat16), "dp", axis=1, tiled=True),
        lax.all_gather(up_weight.astype(jnp.bfloat16), "dp", axis=0, tiled=True),
        lax.all_gather(down_weight.astype(jnp.bfloat16), "dp", axis=2, tiled=True),
        lax.all_gather(time_inner.astype(jnp.bfloat16), "dp", axis=0, tiled=True),
        lax.all_gather(time_outer.astype(jnp.bfloat16), "dp", axis=0, tiled=True),
        lax.all_gather(time_bias.astype(jnp.bfloat16), "dp", axis=0, tiled=True),
        lax.all_gather(head_vectors.astype(jnp.bfloat16), "dp", axis=2, tiled=True),
        lax.all_gather(layer_vectors.astype(jnp.bfloat16), "dp", axis=1, tiled=True),
    )
    local_width = w_out.shape[0]
    head_count = local_width // HD
    packed = tokens.shape[0]
    head_rows = head_vec.astype(jnp.float32).reshape(6, local_width)
    layer_rows = layer_vec.astype(jnp.float32)
    score_scale = 1.0 / math.sqrt(HD)
    block_rows = min(PACK, 512)
    block_count = packed // block_rows
    seg_row = segment_ids[0]
    features = time_features(timesteps[0], TD)
    feature_low = features.astype(jnp.bfloat16)
    inner_pre = jnp.dot(feature_low, w_inner, preferred_element_type=jnp.float32) + b_inner.astype(
        jnp.float32
    )
    silu_out, silu_pull = jax.vjp(jax.nn.silu, inner_pre)
    act_low = silu_out.astype(jnp.bfloat16)
    time_embed = jnp.dot(act_low, w_outer, preferred_element_type=jnp.float32) + layer_rows[6]
    onehot = (seg_row[:, None] == jnp.arange(SEGS, dtype=jnp.int32)[None, :]).astype(jnp.float32)
    hidden0 = tokens.astype(jnp.float32) + jnp.dot(
        onehot, time_embed, precision=lax.Precision.HIGHEST, preferred_element_type=jnp.float32
    )
    hidden_low = hidden0.astype(jnp.bfloat16)
    projected = jnp.einsum("pd,dce->pce", hidden_low, w_qkv, preferred_element_type=jnp.float32)
    queries = (projected[:, 0] + head_rows[0]).astype(jnp.bfloat16)
    keys_low = projected[:, 1].astype(jnp.bfloat16)
    values_low = (projected[:, 2] + head_rows[1]).astype(jnp.bfloat16)

    def block_scores(query_blk, key_all, seg_query):
        raw_scores = (
            jnp.einsum("qd,kd->qk", query_blk, key_all, preferred_element_type=jnp.float32)
            * score_scale
        )
        same_doc = seg_query[:, None] == seg_row[None, :]
        return (raw_scores, same_doc)

    def attend_head(head_index):
        query_h = head_slice(queries, head_index)
        key_h = head_slice(keys_low, head_index)
        value_h = head_slice(values_low, head_index)
        out_blocks = []
        sum_blocks = []
        for block_index in range(block_count):
            first_row = block_index * block_rows
            raw_scores, same_doc = block_scores(
                query_h[first_row : first_row + block_rows],
                key_h,
                seg_row[first_row : first_row + block_rows],
            )
            masked = jnp.where(same_doc, raw_scores, -1e30)
            row_peak = jnp.max(masked, axis=1, keepdims=True)
            exponent = jnp.exp(masked - row_peak)
            row_total = jnp.sum(exponent, axis=1, keepdims=True)
            soft_weights = exponent / row_total
            out_blocks.append(
                jnp.dot(
                    soft_weights.astype(jnp.bfloat16), value_h, preferred_element_type=jnp.float32
                )
            )
            sum_blocks.append((row_peak + jnp.log(row_total))[:, 0])
        return (jnp.concatenate(out_blocks, axis=0), jnp.concatenate(sum_blocks, axis=0))

    head_out, log_sums = lax.map(attend_head, jnp.arange(head_count, dtype=jnp.int32))
    att_low = merge_heads(head_out).astype(jnp.bfloat16)
    attn_partial = jnp.dot(att_low, w_out, preferred_element_type=jnp.float32)
    attn_branch = (
        lax.psum(attn_partial.astype(jnp.bfloat16), "tensor").astype(jnp.float32) + layer_rows[0]
    )
    residual1 = hidden0 + attn_branch
    cot_here = cotangent.astype(jnp.float32)
    normed1, norm1_pull = jax.vjp(layer_norm, residual1, layer_rows[1], layer_rows[2])
    norm_here = normed1.astype(jnp.bfloat16)
    up_pre = (
        jnp.einsum("pd,dje->pje", norm_here, w_up, preferred_element_type=jnp.float32)
        + head_rows[2:]
    )
    gelu_out, gelu_pull = jax.vjp(gelu_exact, up_pre)
    hid_low = gelu_out.astype(jnp.bfloat16)
    down_partial = jnp.einsum("pje,jef->pf", hid_low, w_down, preferred_element_type=jnp.float32)
    mlp_branch = (
        lax.psum(down_partial.astype(jnp.bfloat16), "tensor").astype(jnp.float32) + layer_rows[3]
    )
    result, norm2_pull = jax.vjp(layer_norm, normed1 + mlp_branch, layer_rows[4], layer_rows[5])
    output_here = result.astype(jnp.bfloat16)
    back_r2, back_gain2, back_shift2 = norm2_pull(cot_here)
    part_bdown = jnp.sum(back_r2, axis=0)
    back_r2_here = back_r2.astype(jnp.bfloat16)
    grad_down = jnp.einsum("pje,pf->jef", hid_low, back_r2_here, preferred_element_type=jnp.float32)
    back_hid = jnp.einsum("pf,jef->pje", back_r2_here, w_down, preferred_element_type=jnp.float32)
    (back_up,) = gelu_pull(back_hid)
    grad_bup = jnp.sum(back_up, axis=0)
    back_up_low = back_up.astype(jnp.bfloat16)
    grad_up = jnp.einsum("pd,pje->dje", norm_here, back_up_low, preferred_element_type=jnp.float32)
    back_a_part = jnp.einsum("pje,dje->pd", back_up_low, w_up, preferred_element_type=jnp.float32)
    back_a = lax.psum(back_a_part.astype(jnp.bfloat16), "tensor").astype(jnp.float32) + back_r2
    back_r1, back_gain1, back_shift1 = norm1_pull(back_a)
    grad_bout = jnp.sum(back_r1, axis=0)
    back_r1_low = back_r1.astype(jnp.bfloat16)
    grad_out = jnp.einsum("pe,pf->ef", att_low, back_r1_low, preferred_element_type=jnp.float32)
    back_att = jnp.einsum(
        "pf,ef->pe", back_r1_low, w_out, preferred_element_type=jnp.float32
    ).astype(jnp.bfloat16)

    def head_back(head_index):
        query_h = head_slice(queries, head_index)
        key_h = head_slice(keys_low, head_index)
        value_h = head_slice(values_low, head_index)
        grad_h = head_slice(back_att, head_index)
        lse_h = log_sums[head_index]
        key_grad = jnp.zeros((packed, HD), jnp.float32)
        value_grad = jnp.zeros((packed, HD), jnp.float32)
        query_blocks = []
        for block_index in range(block_count):
            first_row = block_index * block_rows
            query_blk = query_h[first_row : first_row + block_rows]
            raw_scores, same_doc = block_scores(
                query_blk, key_h, seg_row[first_row : first_row + block_rows]
            )
            lse_blk = lse_h[first_row : first_row + block_rows]
            soft_weights = jnp.where(same_doc, jnp.exp(raw_scores - lse_blk[:, None]), 0.0)
            grad_blk = grad_h[first_row : first_row + block_rows]
            value_grad = value_grad + jnp.einsum(
                "qk,qd->kd",
                soft_weights.astype(jnp.bfloat16),
                grad_blk,
                preferred_element_type=jnp.float32,
            )
            weight_grad = jnp.einsum(
                "qd,kd->qk", grad_blk, value_h, preferred_element_type=jnp.float32
            )
            row_inner = jnp.sum(soft_weights * weight_grad, axis=1, keepdims=True)
            score_low = (soft_weights * (weight_grad - row_inner)).astype(jnp.bfloat16)
            query_blocks.append(
                jnp.dot(score_low, key_h, preferred_element_type=jnp.float32) * score_scale
            )
            key_grad = (
                key_grad
                + jnp.einsum("qk,qd->kd", score_low, query_blk, preferred_element_type=jnp.float32)
                * score_scale
            )
        return (jnp.concatenate(query_blocks, axis=0), key_grad, value_grad)

    query_grads, key_grads, value_grads = lax.map(
        head_back, jnp.arange(head_count, dtype=jnp.int32)
    )
    query_grad_all = merge_heads(query_grads)
    key_grad_all = merge_heads(key_grads)
    value_grad_all = merge_heads(value_grads)
    grad_bq = jnp.sum(query_grad_all, axis=0)
    grad_bv = jnp.sum(value_grad_all, axis=0)
    proj_grad_low = jnp.stack([query_grad_all, key_grad_all, value_grad_all], axis=1).astype(
        jnp.bfloat16
    )
    grad_qkv = jnp.einsum(
        "pd,pce->dce", hidden_low, proj_grad_low, preferred_element_type=jnp.float32
    )
    back_h_part = jnp.einsum(
        "pce,dce->pd", proj_grad_low, w_qkv, preferred_element_type=jnp.float32
    )
    back_h0 = lax.psum(back_h_part.astype(jnp.bfloat16), "tensor").astype(jnp.float32) + back_r1
    input_grad = back_h0.astype(jnp.bfloat16)
    back_time = jnp.einsum(
        "ps,pd->sd",
        onehot,
        back_h0,
        precision=lax.Precision.HIGHEST,
        preferred_element_type=jnp.float32,
    )
    grad_bouter = jnp.sum(back_time, axis=0)
    back_time_low = back_time.astype(jnp.bfloat16)
    grad_outer = jnp.einsum("su,sd->ud", act_low, back_time_low, preferred_element_type=jnp.float32)
    back_act = jnp.einsum("sd,ud->su", back_time_low, w_outer, preferred_element_type=jnp.float32)
    (back_inner,) = silu_pull(back_act)
    grad_binner = jnp.sum(back_inner, axis=0)
    grad_inner = jnp.einsum(
        "st,su->tu",
        feature_low,
        back_inner.astype(jnp.bfloat16),
        preferred_element_type=jnp.float32,
    )
    grad_head = jnp.concatenate([grad_bq[None], grad_bv[None], grad_bup], axis=0).reshape(
        6, 1, local_width
    )
    grad_layer = jnp.stack(
        [grad_bout, back_gain1, back_shift1, part_bdown, back_gain2, back_shift2, grad_bouter],
        axis=0,
    )
    red_qkv, red_out, red_up, red_down, red_inner, red_outer, red_binner, red_head, red_layer = (
        lax.psum_scatter(grad_qkv, "dp", scatter_dimension=0, tiled=True),
        lax.psum_scatter(grad_out, "dp", scatter_dimension=1, tiled=True),
        lax.psum_scatter(grad_up, "dp", scatter_dimension=0, tiled=True),
        lax.psum_scatter(grad_down, "dp", scatter_dimension=2, tiled=True),
        lax.psum_scatter(grad_inner, "dp", scatter_dimension=0, tiled=True),
        lax.psum_scatter(grad_outer, "dp", scatter_dimension=0, tiled=True),
        lax.psum_scatter(grad_binner, "dp", scatter_dimension=0, tiled=True),
        lax.psum_scatter(grad_head, "dp", scatter_dimension=2, tiled=True),
        lax.psum_scatter(grad_layer, "dp", scatter_dimension=1, tiled=True),
    )
    split_squares = sum(
        (jnp.sum(piece * piece) for piece in (red_qkv, red_out, red_up, red_down, red_head))
    )
    shared_squares = sum(
        (jnp.sum(piece * piece) for piece in (red_inner, red_outer, red_binner, red_layer))
    )
    local_squares = split_squares + shared_squares / lax.axis_size("tensor")
    norm = jnp.sqrt(lax.psum(local_squares, ("dp", "tensor")))
    factor = 1.0 / jnp.maximum(norm, 1.0)
    step_rate = 4.0 * math.sqrt(MPARAMS / D)
    qkv_master, qkv_velocity, qkv_smoothed = advance(
        qkv_weight, qkv_moment, qkv_average, red_qkv, factor, step_rate
    )
    out_master, out_velocity, out_smoothed = advance(
        out_weight, out_moment, out_average, red_out, factor, step_rate
    )
    up_master, up_velocity, up_smoothed = advance(
        up_weight, up_moment, up_average, red_up, factor, step_rate
    )
    down_master, down_velocity, down_smoothed = advance(
        down_weight, down_moment, down_average, red_down, factor, step_rate
    )
    inner_master, inner_velocity, inner_smoothed = advance(
        time_inner, inner_moment, inner_average, red_inner, factor, step_rate
    )
    outer_master, outer_velocity, outer_smoothed = advance(
        time_outer, outer_moment, outer_average, red_outer, factor, step_rate
    )
    bias_master, bias_velocity, bias_smoothed = advance(
        time_bias, bias_moment, bias_average, red_binner, factor, step_rate
    )
    head_master, head_velocity, head_smoothed = advance(
        head_vectors, head_moment, head_average, red_head, factor, step_rate
    )
    layer_master, layer_velocity, layer_smoothed = advance(
        layer_vectors, layer_moment, layer_average, red_layer, factor, step_rate
    )
    return (
        output_here,
        input_grad,
        norm,
        qkv_master,
        out_master,
        up_master,
        down_master,
        inner_master,
        outer_master,
        bias_master,
        head_master,
        layer_master,
        qkv_velocity,
        out_velocity,
        up_velocity,
        down_velocity,
        inner_velocity,
        outer_velocity,
        bias_velocity,
        head_velocity,
        layer_velocity,
        qkv_smoothed,
        out_smoothed,
        up_smoothed,
        down_smoothed,
        inner_smoothed,
        outer_smoothed,
        bias_smoothed,
        head_smoothed,
        layer_smoothed,
    )


F32=jnp.float32; BF=jnp.bfloat16
MESH=pl.DeviceIdType.MESH
NZ,NX,NC,NT=4,2,2,2
ROWS=48; PIECE=384

def place():
    dp=lax.axis_index("dp"); t=lax.axis_index("tensor")
    z=lax.div(dp,4); x=lax.rem(lax.div(dp,2),2); c=lax.rem(dp,2)
    return z,x,c,t
def dev(z,x,c,t):
    return ((z*NX+x)*NC+c,t)

def peers():
    z,x,c,t=place()
    zp=[dev(lax.rem(z+d,NZ),x,c,t) for d in range(1,NZ)]
    return zp,dev(z,1-x,c,t),dev(z,x,c,1-t),dev(z,x,1-c,t)

def greet():
    zp,xp,yp,sp=peers()
    bar=pltpu.get_barrier_semaphore()
    for d in zp+[xp,yp,sp]:
        pl.semaphore_signal(bar,inc=1,device_id=d,device_id_type=MESH)
    pl.semaphore_wait(bar,6)

def rcopy(src,dst,ssem,rsem,d):
    return pltpu.make_async_remote_copy(src_ref=src,dst_ref=dst,send_sem=ssem,recv_sem=rsem,device_id=d,device_id_type=MESH)

def gather_kernel(chunks,w_ref,g_ref,lsem,zs,zr,xs,xr,ys,yr,ss,sr):
    z,x,c,t=place()
    zp,xp,yp,sp=peers()
    greet()
    n=len(chunks)
    def cols(i): return pl.ds(chunks[i][0],chunks[i][1])
    def ca(i): return pl.ds(chunks[i][0],chunks[i][2])
    def cb(i): return pl.ds(chunks[i][0]+chunks[i][2],chunks[i][1]-chunks[i][2])
    def zcopies(i):
        return [rcopy(w_ref.at[:,cols(i)],g_ref.at[t,z,x,c,:,cols(i)],zs.at[i,d],zr.at[i,d],zp[d]) for d in range(3)]
    def first(i):
        return [rcopy(g_ref.at[t,:,x,c,:,ca(i)],g_ref.at[t,:,x,c,:,ca(i)],xs.at[i,0],xr.at[i,0],xp),
                rcopy(g_ref.at[t,:,x,c,:,cb(i)],g_ref.at[t,:,x,c,:,cb(i)],ys.at[i,0],yr.at[i,0],yp)]
    def second(i):
        return [rcopy(g_ref.at[t,:,:,c,:,ca(i)],g_ref.at[t,:,:,c,:,ca(i)],ys.at[i,1],yr.at[i,1],yp),
                rcopy(g_ref.at[:,:,x,c,:,cb(i)],g_ref.at[:,:,x,c,:,cb(i)],xs.at[i,1],xr.at[i,1],xp)]
    def sib(i):
        return [rcopy(g_ref.at[:,:,:,c,:,cols(i)],g_ref.at[:,:,:,c,:,cols(i)],ss.at[i],sr.at[i],sp)]
    locs=[pltpu.make_async_copy(w_ref.at[:,cols(i)],g_ref.at[t,z,x,c,:,cols(i)],lsem.at[i]) for i in range(n)]
    Z=[zcopies(i) for i in range(n)]; A=[first(i) for i in range(n)]; B=[second(i) for i in range(n)]; S=[sib(i) for i in range(n)]
    for i in range(n):
        locs[i].start()
        for q in Z[i]: q.start()
    for step in range(n+3):
        if step<n:
            locs[step].wait()
            for q in Z[step]: q.wait_recv()
            for q in A[step]: q.start()
        j=step-1
        if 0<=j<n:
            for q in A[j]: q.wait_recv()
            for q in B[j]: q.start()
        j=step-2
        if 0<=j<n:
            for q in B[j]: q.wait_recv()
            for q in S[j]: q.start()
    for i in range(n):
        for q in Z[i]+A[i]+B[i]: q.wait_send()
        for q in S[i]: q.wait()

def gather(w,chunks,space=pl.ANY,cid=0):
    n=len(chunks); DMA=pltpu.SemaphoreType.DMA
    width=w.shape[1]
    return pl.pallas_call(functools.partial(gather_kernel,chunks),
        in_specs=[pl.BlockSpec(memory_space=space)],out_specs=pl.BlockSpec(memory_space=space),
        out_shape=jax.ShapeDtypeStruct((NT,NZ,NX,NC,ROWS,width),BF),
        scratch_shapes=[DMA((n,)),DMA((n,3)),DMA((n,3)),DMA((n,2)),DMA((n,2)),DMA((n,2)),DMA((n,2)),DMA((n,)),DMA((n,))],
        compiler_params=pltpu.CompilerParams(collective_id=cid,has_side_effects=True,vmem_limit_bytes=60*2**20),name="gather")(w)

def scatter_kernel(chunks,g_hbm,o_ref,g,rs,ra,rc,rb,rz,lsem,ss,sr,as_,ar,bs,br,zs,zr):
    z,x,c,t=place()
    zp,xp,yp,sp=peers()
    n=len(chunks)
    def cols(i): return pl.ds(chunks[i][0],chunks[i][1])
    def ca(i): return pl.ds(chunks[i][0],chunks[i][2])
    def cb(i): return pl.ds(chunks[i][0]+chunks[i][2],chunks[i][1]-chunks[i][2])
    L=[pltpu.make_async_copy(g_hbm.at[:,:,:,:,:,cols(i)],g.at[:,:,:,:,:,cols(i)],lsem.at[i]) for i in range(n)]
    for q in L: q.start()
    greet()
    S=[[rcopy(g.at[:,:,:,1-c,:,cols(i)],rs.at[:,:,:,:,cols(i)],ss.at[i],sr.at[i],sp)] for i in range(n)]
    A=[[rcopy(g.at[:,:,1-x,c,:,ca(i)],ra.at[:,:,:,ca(i)],as_.at[i,0],ar.at[i,0],xp),
        rcopy(g.at[1-t,:,:,c,:,cb(i)],rc.at[:,:,:,cb(i)],as_.at[i,1],ar.at[i,1],yp)] for i in range(n)]
    B=[[rcopy(g.at[1-t,:,x,c,:,ca(i)],rb.at[:,:,ca(i)],bs.at[i,0],br.at[i,0],yp),
        rcopy(g.at[t,:,1-x,c,:,cb(i)],rb.at[:,:,cb(i)],bs.at[i,1],br.at[i,1],xp)] for i in range(n)]
    Zc=[[rcopy(g.at[t,lax.rem(z+d+1,NZ),x,c,:,cols(i)],rz.at[d,:,cols(i)],zs.at[i,d],zr.at[i,d],zp[d]) for d in range(3)] for i in range(n)]
    def addS(i):
        def body(k,_):
            tt=lax.div(k,8); zz=lax.rem(lax.div(k,2),4); xx=lax.rem(k,2)
            g[tt,zz,xx,c,:,cols(i)]=(g[tt,zz,xx,c,:,cols(i)].astype(F32)+rs[tt,zz,xx,:,cols(i)].astype(F32)).astype(BF)
            return 0
        lax.fori_loop(0,16,body,0)
    def addA(i):
        def body(k,_):
            a=lax.div(k,4); b=lax.rem(k,4)
            g[a,b,x,c,:,ca(i)]=(g[a,b,x,c,:,ca(i)].astype(F32)+ra[a,b,:,ca(i)].astype(F32)).astype(BF)
            zz=lax.div(k,2); xx=lax.rem(k,2)
            g[t,zz,xx,c,:,cb(i)]=(g[t,zz,xx,c,:,cb(i)].astype(F32)+rc[zz,xx,:,cb(i)].astype(F32)).astype(BF)
            return 0
        lax.fori_loop(0,8,body,0)
    def addB(i):
        def body(k,_):
            g[t,k,x,c,:,cols(i)]=(g[t,k,x,c,:,cols(i)].astype(F32)+rb[k,:,cols(i)].astype(F32)).astype(BF)
            return 0
        lax.fori_loop(0,4,body,0)
    def addZ(i):
        acc=g[t,z,x,c,:,cols(i)].astype(F32)
        for d in range(3): acc=acc+rz[d,:,cols(i)].astype(F32)
        o_ref[:,cols(i)]=acc
    for step in range(n+4):
        if step<n:
            L[step].wait()
            for q in S[step]: q.start()
        j=step-1
        if 0<=j<n:
            for q in S[j]: q.wait_recv()
            addS(j)
            for q in A[j]: q.start()
        j=step-2
        if 0<=j<n:
            for q in A[j]: q.wait_recv()
            addA(j)
            for q in B[j]: q.start()
        j=step-3
        if 0<=j<n:
            for q in B[j]: q.wait_recv()
            addB(j)
            for q in Zc[j]: q.start()
        j=step-4
        if 0<=j<n:
            for q in Zc[j]: q.wait_recv()
            addZ(j)
    for i in range(n):
        for q in S[i]+A[i]+B[i]+Zc[i]: q.wait_send()

def scatter(g,chunks,cid=1):
    n=len(chunks); DMA=pltpu.SemaphoreType.DMA
    W=g.shape[-1]; V=lambda *s:pltpu.VMEM(s+(ROWS,W),BF)
    return pl.pallas_call(functools.partial(scatter_kernel,chunks),
        in_specs=[pl.BlockSpec(memory_space=pl.ANY)],out_specs=pl.BlockSpec(memory_space=pltpu.VMEM),
        out_shape=jax.ShapeDtypeStruct((ROWS,W),F32),
        scratch_shapes=[V(NT,NZ,NX,NC),V(NT,NZ,NX),V(NT,NZ),V(NZ,NX),V(NZ),V(3),
          DMA((n,)),DMA((n,)),DMA((n,)),DMA((n,2)),DMA((n,2)),DMA((n,2)),DMA((n,2)),DMA((n,3)),DMA((n,3))],
        compiler_params=pltpu.CompilerParams(collective_id=cid,has_side_effects=True,vmem_limit_bytes=62*2**20),name="scatter")(g)
def mkchunks(ws):
    out=[];s=0
    for w in ws:
        w*=128
        out.append((s,w,(w//256)*128)); s+=w
    return out

CHUNKS=mkchunks([6,6,9,6,6,6])
L=1024
def dot(a,b,ca,cb):
    return lax.dot_general(a,b,(((ca,),(cb,)),((),())),preferred_element_type=F32)
def fwdT(bk, q_ref,k_ref,v_ref,bias_ref,o_ref,lse_ref):
    lane=lax.broadcasted_iota(jnp.int32,(1,128),1)
    qp=q_ref[...]; kp=k_ref[...]; vp=v_ref[...]
    bias=bias_ref[...]
    vT=vp.T
    outs=[]
    for h in range(2):
        sel=(lane//64)==h
        one=lane==(64*(1-h))
        kh=jnp.where(sel,kp,jnp.where(one,bias.astype(BF),jnp.zeros_like(kp)))
        qh=jnp.where(sel,qp*0.125,jnp.where(one,jnp.ones_like(qp),jnp.zeros_like(qp)))
        oT=[]
        for qi in range(L//bk):
            sT=dot(kh,qh[qi*bk:(qi+1)*bk],1,1)
            m=jnp.max(sT,axis=0,keepdims=True)
            e=jnp.exp(sT-m)
            l=jnp.sum(e,axis=0,keepdims=True)
            p=(e*(1.0/l)).astype(BF)
            oT.append(dot(vT[h*64:(h+1)*64],p,1,0))
            lse_ref[0,h:h+1,qi*bk:(qi+1)*bk]=m+jnp.log(l)
        outs.append(jnp.concatenate(oT,axis=1))
    oT=jnp.concatenate(outs,axis=0)
    o_ref[...]=oT.T.astype(BF)

def call_fwd(body,b,q,k,v,bias):
    return pl.pallas_call(functools.partial(body,b),grid=(6,),
      in_specs=[pl.BlockSpec((L,128),lambda i:(0,i))]*3+[pl.BlockSpec((L,1),lambda i:(0,0))],
      out_specs=[pl.BlockSpec((L,128),lambda i:(0,i)),pl.BlockSpec((1,2,L),lambda i:(i,0,0))],
      out_shape=[jax.ShapeDtypeStruct((L,768),BF),jax.ShapeDtypeStruct((6,2,L),F32)],
      compiler_params=pltpu.CompilerParams(vmem_limit_bytes=60*2**20),name=f"{body.__name__}_{b}")(q,k,v,bias)

def bwdT(bq, q_ref,k_ref,v_ref,do_ref,bias_ref,lse_ref,dq_ref,dk_ref,dv_ref):
    lane=lax.broadcasted_iota(jnp.int32,(1,128),1)
    kp=k_ref[...]; vp=v_ref[...]
    bias=bias_ref[...]
    khs=[];vhs=[];kts=[]
    for h in range(2):
        sel=(lane//64)==h
        one=lane==(64*(1-h))
        khs.append(jnp.where(sel,kp,jnp.where(one,bias.astype(BF),jnp.zeros_like(kp))))
        vhs.append(jnp.where(sel,vp,jnp.zeros_like(vp)))
    kT=kp.T
    dk=[None,None];dv=[None,None]
    for qi in range(L//bq):
        rows=pl.ds(qi*bq,bq)
        qp=q_ref[rows,:]; dop=do_ref[rows,:]
        dqT=[]
        for h in range(2):
            sel=(lane//64)==h
            one=lane==(64*(1-h))
            qh=jnp.where(sel,qp*0.125,jnp.where(one,jnp.ones_like(qp),jnp.zeros_like(qp)))
            doh=jnp.where(sel,dop,jnp.zeros_like(dop))
            qz=jnp.where(sel,qp*0.125,jnp.zeros_like(qp))
            sT=dot(khs[h],qh,1,1)
            p=jnp.exp(sT-lse_ref[0,h:h+1,qi*bq:(qi+1)*bq])
            dp=dot(vhs[h],doh,1,1)
            d=jnp.sum(p*dp,axis=0,keepdims=True)
            ds=(p*(dp-d)).astype(BF)
            pb=p.astype(BF)
            a=dot(pb,doh,1,0); dv[h]=a if dv[h] is None else dv[h]+a
            a=dot(ds,qz,1,0); dk[h]=a if dk[h] is None else dk[h]+a
            dqT.append(dot(kT[h*64:(h+1)*64],ds,1,0))
        dq_ref[rows,:]=(jnp.concatenate(dqT,axis=0).T*0.125)
    dk_ref[...]=dk[0]+dk[1]
    dv_ref[...]=dv[0]+dv[1]

def call_bwd(body,b,q,k,v,do,bias,lse):
    return pl.pallas_call(functools.partial(body,b),grid=(6,),
      in_specs=[pl.BlockSpec((L,128),lambda i:(0,i))]*4+[pl.BlockSpec((L,1),lambda i:(0,0)),pl.BlockSpec((1,2,L),lambda i:(i,0,0))],
      out_specs=[pl.BlockSpec((L,128),lambda i:(0,i))]*3,
      out_shape=[jax.ShapeDtypeStruct((L,768),F32)]*3,
      compiler_params=pltpu.CompilerParams(vmem_limit_bytes=60*2**20),name=f"{body.__name__}_{b}")(q,k,v,do,bias,lse)


def ln_stats(v):
    mean=jnp.mean(v,axis=-1,keepdims=True)
    cen=v-mean
    inv=lax.rsqrt(jnp.mean(cen*cen,axis=-1,keepdims=True)+EPSILON)
    return cen*inv,inv

def ln_back(gain,dy,xhat,inv):
    gd=gain*dy
    return (gd-jnp.mean(gd,axis=-1,keepdims=True)-xhat*jnp.mean(gd*xhat,axis=-1,keepdims=True))*inv

def phi_cdf(u):
    return 0.5*(1.0+lax.erf(u*(1.0/math.sqrt(2.0))))

def pack_weights(qkv,out,up,down,w1,w2,b1,hv,lv):
    t=lax.axis_index("tensor")
    low=lambda a:a.astype(BF)
    w2h=lax.dynamic_slice_in_dim(low(w2),t*PIECE,PIECE,1)
    w1h=lax.dynamic_slice_in_dim(jnp.pad(low(w1),((0,8),(0,0))),t*256,256,1)
    lanes=lambda a:jnp.pad(low(a),((0,0),(0,128-a.shape[1])))
    vec=jnp.concatenate([lanes(lv),lanes(hv[:,0]),lanes(b1[None]),jnp.zeros((2,128),BF)],axis=0)
    aux=jnp.concatenate([w2h,jnp.concatenate([w1h,vec],axis=1)],axis=0)
    return jnp.concatenate([aux,low(qkv).reshape(ROWS,3*PIECE),low(out).T,low(up).reshape(ROWS,4*PIECE),low(down).transpose(2,0,1).reshape(ROWS,4*PIECE)],axis=1)

def shards_fast(tokens,cotangent,segment_ids,timesteps,*params):
    masters=params[:9];moments=params[9:18];averages=params[18:]
    t=lax.axis_index("tensor")
    g=gather(pack_weights(*masters),CHUNKS)
    g=g.reshape(NT,16,ROWS,13*PIECE)
    aux=g[...,:PIECE]
    both=lambda a:jnp.concatenate([a[0],a[1]],axis=-1)
    w2=both(aux[:,:,:32].reshape(NT,512,PIECE))
    w1=both(aux[:,:,32:,:256].reshape(NT,256,256))
    vec=aux[:,:,32:,256:].astype(F32)
    lv=vec[0,:,0:7,0:48].transpose(1,0,2).reshape(7,D)
    hv=vec[:,:,7:13,0:24].transpose(2,0,1,3).reshape(6,D)
    b1=vec[0,:,13,0:32].reshape(1,512)
    wide=g.reshape(NT,D,13*PIECE)
    w_qkv=wide[...,PIECE:4*PIECE].reshape(NT,D,3,PIECE)
    w_outT=wide[...,4*PIECE:5*PIECE]
    w_up=wide[...,5*PIECE:9*PIECE]
    w_downT=wide[...,9*PIECE:]

    seg=lax.dynamic_slice_in_dim(segment_ids[0],t*512,L,0)
    own=(seg==t)[:,None]
    tok=lax.dynamic_slice_in_dim(tokens,t*512,L,0).astype(F32)
    dy=jnp.where(own,lax.dynamic_slice_in_dim(cotangent,t*512,L,0).astype(F32),0.0)
    step=lax.dynamic_slice_in_dim(timesteps,t,1,1)[0]
    feat=time_features(step,TD).astype(BF)
    featp=jnp.pad(feat.reshape(16,8),((0,0),(0,8))).reshape(1,256)
    inner=dot(featp,w1,1,0)+b1
    sig=jax.nn.sigmoid(inner)
    act=(inner*sig).astype(BF)
    temb=dot(act,w2,1,0)+lv[6:7]
    h0=tok+temb
    hb=h0.astype(BF)
    proj=jnp.einsum("pd,tdce->pcte",hb,w_qkv,preferred_element_type=F32).reshape(L,3,D)
    q=(proj[:,0]+hv[0]).astype(BF); k=proj[:,1].astype(BF); v=(proj[:,2]+hv[1]).astype(BF)
    bias=jnp.where(own,0.0,-1e30).astype(F32)
    o,lse=call_fwd(fwdT,512,q,k,v,bias)
    attn=jnp.einsum("pte,tfe->pf",o.reshape(L,NT,PIECE),w_outT,preferred_element_type=F32)+lv[0]
    x1,inv1=ln_stats(h0+attn)
    a=x1*lv[1]+lv[2]
    ab=a.astype(BF)
    bup=hv[2:].reshape(4,NT,PIECE).transpose(1,0,2).reshape(NT,4*PIECE)
    u=jnp.einsum("pd,tdj->ptj",ab,w_up,preferred_element_type=F32)+bup
    cdf=phi_cdf(u)
    hid=(u*cdf).astype(BF)
    mlp=jnp.einsum("ptj,tfj->pf",hid,w_downT,preferred_element_type=F32)+lv[3]
    x2,inv2=ln_stats(a+mlp)
    out_win=(x2*lv[4]+lv[5]).astype(BF)
    g_gain2=jnp.sum(dy*x2,0); g_shift2=jnp.sum(dy,0)
    dr2=ln_back(lv[4],dy,x2,inv2)
    g_bdown=jnp.sum(dr2,0)
    dmb=dr2.astype(BF)
    g_down=jnp.einsum("pf,ptj->tfj",dmb,hid,preferred_element_type=F32)
    dhid=jnp.einsum("pf,tfj->ptj",dmb,w_downT,preferred_element_type=F32)
    du=dhid*(cdf+u*jnp.exp(-0.5*u*u)*(1.0/math.sqrt(2*math.pi)))
    g_bup=jnp.sum(du,0)
    dub=du.astype(BF)
    g_up=jnp.einsum("pd,ptj->tdj",ab,dub,preferred_element_type=F32)
    da=jnp.einsum("ptj,tdj->pd",dub,w_up,preferred_element_type=F32)+dr2
    g_gain1=jnp.sum(da*x1,0); g_shift1=jnp.sum(da,0)
    dr1=ln_back(lv[1],da,x1,inv1)
    g_bo=jnp.sum(dr1,0)
    drb=dr1.astype(BF)
    g_out=jnp.einsum("pf,pte->tfe",drb,o.reshape(L,NT,PIECE),preferred_element_type=F32)
    dob=jnp.einsum("pf,tfe->pte",drb,w_outT,preferred_element_type=F32).astype(BF).reshape(L,D)
    dq,dk,dv=call_bwd(bwdT,512,q,k,v,dob,bias,lse)
    g_bq=jnp.sum(dq,0); g_bv=jnp.sum(dv,0)
    dqkv=jnp.stack([dq,dk,dv],axis=1).astype(BF).reshape(L,3,NT,PIECE)
    g_qkv=jnp.einsum("pd,pcte->tdce",hb,dqkv,preferred_element_type=F32)
    dh0=jnp.einsum("pcte,tdce->pd",dqkv,w_qkv,preferred_element_type=F32)+dr1
    in_win=dh0.astype(BF)
    dtemb=jnp.sum(dh0,0,keepdims=True)
    dtb=dtemb.astype(BF)
    g_w2=dot(act,dtb,0,0)
    dinner=dot(dtb,w2,1,1)*(sig*(1.0+inner*(1.0-sig)))
    g_w1=dot(featp,dinner.astype(BF),0,0)
    g_lv=jnp.stack([g_bo,g_gain1,g_shift1,g_bdown,g_gain2,g_shift2,dtemb[0]],0)
    g_bup=g_bup.reshape(NT,4,PIECE).transpose(1,0,2).reshape(4,D)
    g_hv=jnp.concatenate([g_bq[None],g_bv[None],g_bup],0)
    low=lambda a:a.astype(BF)
    padl=lambda a:jnp.pad(low(a),((0,0),)*3+((0,128-a.shape[-1]),))
    lvp=jnp.broadcast_to(padl(g_lv.reshape(7,16,48).transpose(1,0,2)[None]),(NT,16,7,128))
    hvp=padl(g_hv.reshape(6,NT,16,24).transpose(1,2,0,3))
    b1p=jnp.broadcast_to(padl(dinner.reshape(1,16,1,32)),(NT,16,1,128))
    vecp=jnp.concatenate([lvp,hvp,b1p,jnp.zeros((NT,16,2,128),BF)],axis=2)
    split=lambda a,r,w:low(a).reshape(16,r,NT,w).transpose(2,0,1,3)
    auxg=jnp.concatenate([split(g_w2,32,PIECE),jnp.concatenate([split(g_w1,16,256),vecp],axis=3)],axis=2)
    slab=lambda a:low(a).reshape(NT,16,ROWS,-1)
    big=jnp.concatenate([auxg,slab(g_qkv),slab(g_out),slab(g_up),slab(g_down)],axis=3).reshape(NT,NZ,NX,NC,ROWS,13*PIECE)
    red=scatter(big,CHUNKS)
    swap=lambda a:lax.ppermute(a,"tensor",[(0,1),(1,0)])
    aux_mine=red[:,:PIECE].astype(BF)
    aux_peer=swap(aux_mine)
    aux0=jnp.where(t==0,aux_mine,aux_peer).astype(F32); aux1=jnp.where(t==0,aux_peer,aux_mine).astype(F32)
    r_qkv=red[:,PIECE:4*PIECE].reshape(ROWS,3,PIECE)
    r_out=red[:,4*PIECE:5*PIECE].T
    r_up=red[:,5*PIECE:9*PIECE].reshape(ROWS,4,PIECE)
    r_down=red[:,9*PIECE:].reshape(ROWS,4,PIECE).transpose(1,2,0)
    r_w2=jnp.concatenate([aux0[:32],aux1[:32]],axis=1)
    r_w1=jnp.concatenate([aux0[32:40,:256],aux1[32:40,:256]],axis=1)
    r_lv=aux0[32:39,256:304]
    r_b1=aux0[45,256:288]
    r_hv=jnp.where(t==0,aux0,aux1)[39:45,256:280].reshape(6,1,24)
    grads=(r_qkv,r_out,r_up,r_down,r_w1,r_w2,r_b1,r_hv,r_lv)
    sq=lambda a:jnp.sum(a*a)
    squares=sum(sq(grads[i]) for i in (0,1,2,3,7))+0.5*sum(sq(grads[i]) for i in (4,5,6,8))
    norm=jnp.sqrt(lax.psum(squares,("dp","tensor")))
    factor=1.0/jnp.maximum(norm,1.0)
    rate=4.0*math.sqrt(MPARAMS/D)
    new=[advance(m,v_,a_,g_,factor,rate) for m,v_,a_,g_ in zip(masters,moments,averages,grads)]

    def whole(win):
        peer=swap(win)
        lo=jnp.where(t==0,win,peer); hi=jnp.where(t==0,peer,win)
        mid=jnp.where((segment_ids[0,512:1024]==0)[:,None],lo[512:],hi[:512])
        return jnp.concatenate([lo[:512],mid,hi[512:]],axis=0)
    return (whole(out_win),whole(in_win),norm)+tuple(n[0] for n in new)+tuple(n[1] for n in new)+tuple(n[2] for n in new)


def solution(mesh):
    fast=dict(mesh.shape)=={'dp':16,'tensor':2}
    return jax.shard_map(
        shards_fast if fast else shards_any,
        mesh=mesh,
        in_specs=(
            P("dp", None),
            P("dp", None),
            P("dp", None),
            P("dp", None),
            P("dp", None, "tensor"),
            P("tensor", "dp"),
            P("dp", None, "tensor"),
            P(None, "tensor", "dp"),
            P("dp", None),
            P("dp", None),
            P("dp"),
            P(None, "tensor", "dp"),
            P(None, "dp"),
            P("dp", None, "tensor"),
            P("tensor", "dp"),
            P("dp", None, "tensor"),
            P(None, "tensor", "dp"),
            P("dp", None),
            P("dp", None),
            P("dp"),
            P(None, "tensor", "dp"),
            P(None, "dp"),
            P("dp", None, "tensor"),
            P("tensor", "dp"),
            P("dp", None, "tensor"),
            P(None, "tensor", "dp"),
            P("dp", None),
            P("dp", None),
            P("dp"),
            P(None, "tensor", "dp"),
            P(None, "dp"),
        ),
        out_specs=(
            P("dp", None),
            P("dp", None),
            P(),
            P("dp", None, "tensor"),
            P("tensor", "dp"),
            P("dp", None, "tensor"),
            P(None, "tensor", "dp"),
            P("dp", None),
            P("dp", None),
            P("dp"),
            P(None, "tensor", "dp"),
            P(None, "dp"),
            P("dp", None, "tensor"),
            P("tensor", "dp"),
            P("dp", None, "tensor"),
            P(None, "tensor", "dp"),
            P("dp", None),
            P("dp", None),
            P("dp"),
            P(None, "tensor", "dp"),
            P(None, "dp"),
            P("dp", None, "tensor"),
            P("tensor", "dp"),
            P("dp", None, "tensor"),
            P(None, "tensor", "dp"),
            P("dp", None),
            P("dp", None),
            P("dp"),
            P(None, "tensor", "dp"),
            P(None, "dp"),
        ),
        check_vma=False,
    )
```

```python
import functools
import math

import jax
import jax.numpy as jnp
from jax import lax
from jax.experimental import pallas as pl
from jax.experimental.pallas import tpu as pltpu
from jax.sharding import PartitionSpec as P

D = 768
HD = 64
TD = 128
SEGS = 2
PACK = 1536
MPARAMS = 7536640


EPSILON = 1e-05
MOMENTUM = 0.5
AVERAGE_DECAY = 0.5


def layer_norm(values, gain_vec, shift_vec):
    centre = jnp.mean(values, axis=-1, keepdims=True)
    centred = values - centre
    spread = jnp.mean(centred * centred, axis=-1, keepdims=True)
    return centred * lax.rsqrt(spread + EPSILON) * gain_vec + shift_vec


def time_features(step_ids, feat_width):
    midpoint = feat_width // 2
    frequency = jnp.exp(-math.log(10000.0) * jnp.arange(midpoint, dtype=jnp.float32) / midpoint)
    angles = step_ids.astype(jnp.float32)[..., None] * frequency
    return jnp.concatenate([jnp.cos(angles), jnp.sin(angles)], axis=-1)


def gelu_exact(values):
    return jax.nn.gelu(values, approximate=False)


def head_slice(matrix, head_index):
    return lax.dynamic_slice_in_dim(matrix, head_index * HD, HD, 1)


def merge_heads(stacked):
    return stacked.transpose(1, 0, 2).reshape(stacked.shape[1], stacked.shape[0] * stacked.shape[2])


def advance(master, moment, average, grad, factor, step_rate):
    scaled = grad * factor
    velocity = MOMENTUM * moment + scaled
    fresh_master = master - step_rate * (scaled + MOMENTUM * velocity)
    smoothed = AVERAGE_DECAY * average + (1.0 - AVERAGE_DECAY) * fresh_master
    return (fresh_master, velocity, smoothed)


def shards_any(
    tokens,
    cotangent,
    segment_ids,
    timesteps,
    qkv_weight,
    out_weight,
    up_weight,
    down_weight,
    time_inner,
    time_outer,
    time_bias,
    head_vectors,
    layer_vectors,
    qkv_moment,
    out_moment,
    up_moment,
    down_moment,
    inner_moment,
    outer_moment,
    bias_moment,
    head_moment,
    layer_moment,
    qkv_average,
    out_average,
    up_average,
    down_average,
    inner_average,
    outer_average,
    bias_average,
    head_average,
    layer_average,
):
    w_qkv, w_out, w_up, w_down, w_inner, w_outer, b_inner, head_vec, layer_vec = (
        lax.all_gather(qkv_weight.astype(jnp.bfloat16), "dp", axis=0, tiled=True),
        lax.all_gather(out_weight.astype(jnp.bfloat16), "dp", axis=1, tiled=True),
        lax.all_gather(up_weight.astype(jnp.bfloat16), "dp", axis=0, tiled=True),
        lax.all_gather(down_weight.astype(jnp.bfloat16), "dp", axis=2, tiled=True),
        lax.all_gather(time_inner.astype(jnp.bfloat16), "dp", axis=0, tiled=True),
        lax.all_gather(time_outer.astype(jnp.bfloat16), "dp", axis=0, tiled=True),
        lax.all_gather(time_bias.astype(jnp.bfloat16), "dp", axis=0, tiled=True),
        lax.all_gather(head_vectors.astype(jnp.bfloat16), "dp", axis=2, tiled=True),
        lax.all_gather(layer_vectors.astype(jnp.bfloat16), "dp", axis=1, tiled=True),
    )
    local_width = w_out.shape[0]
    head_count = local_width // HD
    packed = tokens.shape[0]
    head_rows = head_vec.astype(jnp.float32).reshape(6, local_width)
    layer_rows = layer_vec.astype(jnp.float32)
    score_scale = 1.0 / math.sqrt(HD)
    block_rows = min(PACK, 512)
    block_count = packed // block_rows
    seg_row = segment_ids[0]
    features = time_features(timesteps[0], TD)
    feature_low = features.astype(jnp.bfloat16)
    inner_pre = jnp.dot(feature_low, w_inner, preferred_element_type=jnp.float32) + b_inner.astype(
        jnp.float32
    )
    silu_out, silu_pull = jax.vjp(jax.nn.silu, inner_pre)
    act_low = silu_out.astype(jnp.bfloat16)
    time_embed = jnp.dot(act_low, w_outer, preferred_element_type=jnp.float32) + layer_rows[6]
    onehot = (seg_row[:, None] == jnp.arange(SEGS, dtype=jnp.int32)[None, :]).astype(jnp.float32)
    hidden0 = tokens.astype(jnp.float32) + jnp.dot(
        onehot, time_embed, precision=lax.Precision.HIGHEST, preferred_element_type=jnp.float32
    )
    hidden_low = hidden0.astype(jnp.bfloat16)
    projected = jnp.einsum("pd,dce->pce", hidden_low, w_qkv, preferred_element_type=jnp.float32)
    queries = (projected[:, 0] + head_rows[0]).astype(jnp.bfloat16)
    keys_low = projected[:, 1].astype(jnp.bfloat16)
    values_low = (projected[:, 2] + head_rows[1]).astype(jnp.bfloat16)

    def block_scores(query_blk, key_all, seg_query):
        raw_scores = (
            jnp.einsum("qd,kd->qk", query_blk, key_all, preferred_element_type=jnp.float32)
            * score_scale
        )
        same_doc = seg_query[:, None] == seg_row[None, :]
        return (raw_scores, same_doc)

    def attend_head(head_index):
        query_h = head_slice(queries, head_index)
        key_h = head_slice(keys_low, head_index)
        value_h = head_slice(values_low, head_index)
        out_blocks = []
        sum_blocks = []
        for block_index in range(block_count):
            first_row = block_index * block_rows
            raw_scores, same_doc = block_scores(
                query_h[first_row : first_row + block_rows],
                key_h,
                seg_row[first_row : first_row + block_rows],
            )
            masked = jnp.where(same_doc, raw_scores, -1e30)
            row_peak = jnp.max(masked, axis=1, keepdims=True)
            exponent = jnp.exp(masked - row_peak)
            row_total = jnp.sum(exponent, axis=1, keepdims=True)
            soft_weights = exponent / row_total
            out_blocks.append(
                jnp.dot(
                    soft_weights.astype(jnp.bfloat16), value_h, preferred_element_type=jnp.float32
                )
            )
            sum_blocks.append((row_peak + jnp.log(row_total))[:, 0])
        return (jnp.concatenate(out_blocks, axis=0), jnp.concatenate(sum_blocks, axis=0))

    head_out, log_sums = lax.map(attend_head, jnp.arange(head_count, dtype=jnp.int32))
    att_low = merge_heads(head_out).astype(jnp.bfloat16)
    attn_partial = jnp.dot(att_low, w_out, preferred_element_type=jnp.float32)
    attn_branch = (
        lax.psum(attn_partial.astype(jnp.bfloat16), "tensor").astype(jnp.float32) + layer_rows[0]
    )
    residual1 = hidden0 + attn_branch
    cot_here = cotangent.astype(jnp.float32)
    normed1, norm1_pull = jax.vjp(layer_norm, residual1, layer_rows[1], layer_rows[2])
    norm_here = normed1.astype(jnp.bfloat16)
    up_pre = (
        jnp.einsum("pd,dje->pje", norm_here, w_up, preferred_element_type=jnp.float32)
        + head_rows[2:]
    )
    gelu_out, gelu_pull = jax.vjp(gelu_exact, up_pre)
    hid_low = gelu_out.astype(jnp.bfloat16)
    down_partial = jnp.einsum("pje,jef->pf", hid_low, w_down, preferred_element_type=jnp.float32)
    mlp_branch = (
        lax.psum(down_partial.astype(jnp.bfloat16), "tensor").astype(jnp.float32) + layer_rows[3]
    )
    result, norm2_pull = jax.vjp(layer_norm, normed1 + mlp_branch, layer_rows[4], layer_rows[5])
    output_here = result.astype(jnp.bfloat16)
    back_r2, back_gain2, back_shift2 = norm2_pull(cot_here)
    part_bdown = jnp.sum(back_r2, axis=0)
    back_r2_here = back_r2.astype(jnp.bfloat16)
    grad_down = jnp.einsum("pje,pf->jef", hid_low, back_r2_here, preferred_element_type=jnp.float32)
    back_hid = jnp.einsum("pf,jef->pje", back_r2_here, w_down, preferred_element_type=jnp.float32)
    (back_up,) = gelu_pull(back_hid)
    grad_bup = jnp.sum(back_up, axis=0)
    back_up_low = back_up.astype(jnp.bfloat16)
    grad_up = jnp.einsum("pd,pje->dje", norm_here, back_up_low, preferred_element_type=jnp.float32)
    back_a_part = jnp.einsum("pje,dje->pd", back_up_low, w_up, preferred_element_type=jnp.float32)
    back_a = lax.psum(back_a_part.astype(jnp.bfloat16), "tensor").astype(jnp.float32) + back_r2
    back_r1, back_gain1, back_shift1 = norm1_pull(back_a)
    grad_bout = jnp.sum(back_r1, axis=0)
    back_r1_low = back_r1.astype(jnp.bfloat16)
    grad_out = jnp.einsum("pe,pf->ef", att_low, back_r1_low, preferred_element_type=jnp.float32)
    back_att = jnp.einsum(
        "pf,ef->pe", back_r1_low, w_out, preferred_element_type=jnp.float32
    ).astype(jnp.bfloat16)

    def head_back(head_index):
        query_h = head_slice(queries, head_index)
        key_h = head_slice(keys_low, head_index)
        value_h = head_slice(values_low, head_index)
        grad_h = head_slice(back_att, head_index)
        lse_h = log_sums[head_index]
        key_grad = jnp.zeros((packed, HD), jnp.float32)
        value_grad = jnp.zeros((packed, HD), jnp.float32)
        query_blocks = []
        for block_index in range(block_count):
            first_row = block_index * block_rows
            query_blk = query_h[first_row : first_row + block_rows]
            raw_scores, same_doc = block_scores(
                query_blk, key_h, seg_row[first_row : first_row + block_rows]
            )
            lse_blk = lse_h[first_row : first_row + block_rows]
            soft_weights = jnp.where(same_doc, jnp.exp(raw_scores - lse_blk[:, None]), 0.0)
            grad_blk = grad_h[first_row : first_row + block_rows]
            value_grad = value_grad + jnp.einsum(
                "qk,qd->kd",
                soft_weights.astype(jnp.bfloat16),
                grad_blk,
                preferred_element_type=jnp.float32,
            )
            weight_grad = jnp.einsum(
                "qd,kd->qk", grad_blk, value_h, preferred_element_type=jnp.float32
            )
            row_inner = jnp.sum(soft_weights * weight_grad, axis=1, keepdims=True)
            score_low = (soft_weights * (weight_grad - row_inner)).astype(jnp.bfloat16)
            query_blocks.append(
                jnp.dot(score_low, key_h, preferred_element_type=jnp.float32) * score_scale
            )
            key_grad = (
                key_grad
                + jnp.einsum("qk,qd->kd", score_low, query_blk, preferred_element_type=jnp.float32)
                * score_scale
            )
        return (jnp.concatenate(query_blocks, axis=0), key_grad, value_grad)

    query_grads, key_grads, value_grads = lax.map(
        head_back, jnp.arange(head_count, dtype=jnp.int32)
    )
    query_grad_all = merge_heads(query_grads)
    key_grad_all = merge_heads(key_grads)
    value_grad_all = merge_heads(value_grads)
    grad_bq = jnp.sum(query_grad_all, axis=0)
    grad_bv = jnp.sum(value_grad_all, axis=0)
    proj_grad_low = jnp.stack([query_grad_all, key_grad_all, value_grad_all], axis=1).astype(
        jnp.bfloat16
    )
    grad_qkv = jnp.einsum(
        "pd,pce->dce", hidden_low, proj_grad_low, preferred_element_type=jnp.float32
    )
    back_h_part = jnp.einsum(
        "pce,dce->pd", proj_grad_low, w_qkv, preferred_element_type=jnp.float32
    )
    back_h0 = lax.psum(back_h_part.astype(jnp.bfloat16), "tensor").astype(jnp.float32) + back_r1
    input_grad = back_h0.astype(jnp.bfloat16)
    back_time = jnp.einsum(
        "ps,pd->sd",
        onehot,
        back_h0,
        precision=lax.Precision.HIGHEST,
        preferred_element_type=jnp.float32,
    )
    grad_bouter = jnp.sum(back_time, axis=0)
    back_time_low = back_time.astype(jnp.bfloat16)
    grad_outer = jnp.einsum("su,sd->ud", act_low, back_time_low, preferred_element_type=jnp.float32)
    back_act = jnp.einsum("sd,ud->su", back_time_low, w_outer, preferred_element_type=jnp.float32)
    (back_inner,) = silu_pull(back_act)
    grad_binner = jnp.sum(back_inner, axis=0)
    grad_inner = jnp.einsum(
        "st,su->tu",
        feature_low,
        back_inner.astype(jnp.bfloat16),
        preferred_element_type=jnp.float32,
    )
    grad_head = jnp.concatenate([grad_bq[None], grad_bv[None], grad_bup], axis=0).reshape(
        6, 1, local_width
    )
    grad_layer = jnp.stack(
        [grad_bout, back_gain1, back_shift1, part_bdown, back_gain2, back_shift2, grad_bouter],
        axis=0,
    )
    red_qkv, red_out, red_up, red_down, red_inner, red_outer, red_binner, red_head, red_layer = (
        lax.psum_scatter(grad_qkv, "dp", scatter_dimension=0, tiled=True),
        lax.psum_scatter(grad_out, "dp", scatter_dimension=1, tiled=True),
        lax.psum_scatter(grad_up, "dp", scatter_dimension=0, tiled=True),
        lax.psum_scatter(grad_down, "dp", scatter_dimension=2, tiled=True),
        lax.psum_scatter(grad_inner, "dp", scatter_dimension=0, tiled=True),
        lax.psum_scatter(grad_outer, "dp", scatter_dimension=0, tiled=True),
        lax.psum_scatter(grad_binner, "dp", scatter_dimension=0, tiled=True),
        lax.psum_scatter(grad_head, "dp", scatter_dimension=2, tiled=True),
        lax.psum_scatter(grad_layer, "dp", scatter_dimension=1, tiled=True),
    )
    split_squares = sum(
        (jnp.sum(piece * piece) for piece in (red_qkv, red_out, red_up, red_down, red_head))
    )
    shared_squares = sum(
        (jnp.sum(piece * piece) for piece in (red_inner, red_outer, red_binner, red_layer))
    )
    local_squares = split_squares + shared_squares / lax.axis_size("tensor")
    norm = jnp.sqrt(lax.psum(local_squares, ("dp", "tensor")))
    factor = 1.0 / jnp.maximum(norm, 1.0)
    step_rate = 4.0 * math.sqrt(MPARAMS / D)
    qkv_master, qkv_velocity, qkv_smoothed = advance(
        qkv_weight, qkv_moment, qkv_average, red_qkv, factor, step_rate
    )
    out_master, out_velocity, out_smoothed = advance(
        out_weight, out_moment, out_average, red_out, factor, step_rate
    )
    up_master, up_velocity, up_smoothed = advance(
        up_weight, up_moment, up_average, red_up, factor, step_rate
    )
    down_master, down_velocity, down_smoothed = advance(
        down_weight, down_moment, down_average, red_down, factor, step_rate
    )
    inner_master, inner_velocity, inner_smoothed = advance(
        time_inner, inner_moment, inner_average, red_inner, factor, step_rate
    )
    outer_master, outer_velocity, outer_smoothed = advance(
        time_outer, outer_moment, outer_average, red_outer, factor, step_rate
    )
    bias_master, bias_velocity, bias_smoothed = advance(
        time_bias, bias_moment, bias_average, red_binner, factor, step_rate
    )
    head_master, head_velocity, head_smoothed = advance(
        head_vectors, head_moment, head_average, red_head, factor, step_rate
    )
    layer_master, layer_velocity, layer_smoothed = advance(
        layer_vectors, layer_moment, layer_average, red_layer, factor, step_rate
    )
    return (
        output_here,
        input_grad,
        norm,
        qkv_master,
        out_master,
        up_master,
        down_master,
        inner_master,
        outer_master,
        bias_master,
        head_master,
        layer_master,
        qkv_velocity,
        out_velocity,
        up_velocity,
        down_velocity,
        inner_velocity,
        outer_velocity,
        bias_velocity,
        head_velocity,
        layer_velocity,
        qkv_smoothed,
        out_smoothed,
        up_smoothed,
        down_smoothed,
        inner_smoothed,
        outer_smoothed,
        bias_smoothed,
        head_smoothed,
        layer_smoothed,
    )


F32=jnp.float32; BF=jnp.bfloat16
MESH=pl.DeviceIdType.MESH
NZ,NX,NC,NT=4,2,2,2
ROWS=48; PIECE=384

def place():
    dp=lax.axis_index("dp"); t=lax.axis_index("tensor")
    z=lax.div(dp,4); x=lax.rem(lax.div(dp,2),2); c=lax.rem(dp,2)
    return z,x,c,t
def dev(z,x,c,t):
    return ((z*NX+x)*NC+c,t)

def peers():
    z,x,c,t=place()
    zp=[dev(lax.rem(z+d,NZ),x,c,t) for d in range(1,NZ)]
    return zp,dev(z,1-x,c,t),dev(z,x,c,1-t),dev(z,x,1-c,t)

def greet():
    zp,xp,yp,sp=peers()
    bar=pltpu.get_barrier_semaphore()
    for d in zp+[xp,yp,sp]:
        pl.semaphore_signal(bar,inc=1,device_id=d,device_id_type=MESH)
    pl.semaphore_wait(bar,6)

def rcopy(src,dst,ssem,rsem,d):
    return pltpu.make_async_remote_copy(src_ref=src,dst_ref=dst,send_sem=ssem,recv_sem=rsem,device_id=d,device_id_type=MESH)

def gather_kernel(chunks,w_ref,g_ref,lsem,zs,zr,xs,xr,ys,yr,ss,sr):
    z,x,c,t=place()
    zp,xp,yp,sp=peers()
    greet()
    n=len(chunks)
    def cols(i): return pl.ds(chunks[i][0],chunks[i][1])
    def ca(i): return pl.ds(chunks[i][0],chunks[i][2])
    def cb(i): return pl.ds(chunks[i][0]+chunks[i][2],chunks[i][1]-chunks[i][2])
    def zcopies(i):
        return [rcopy(w_ref.at[:,cols(i)],g_ref.at[t,z,x,c,:,cols(i)],zs.at[i,d],zr.at[i,d],zp[d]) for d in range(3)]
    def first(i):
        return [rcopy(g_ref.at[t,:,x,c,:,ca(i)],g_ref.at[t,:,x,c,:,ca(i)],xs.at[i,0],xr.at[i,0],xp),
                rcopy(g_ref.at[t,:,x,c,:,cb(i)],g_ref.at[t,:,x,c,:,cb(i)],ys.at[i,0],yr.at[i,0],yp)]
    def second(i):
        return [rcopy(g_ref.at[t,:,:,c,:,ca(i)],g_ref.at[t,:,:,c,:,ca(i)],ys.at[i,1],yr.at[i,1],yp),
                rcopy(g_ref.at[:,:,x,c,:,cb(i)],g_ref.at[:,:,x,c,:,cb(i)],xs.at[i,1],xr.at[i,1],xp)]
    def sib(i):
        return [rcopy(g_ref.at[:,:,:,c,:,cols(i)],g_ref.at[:,:,:,c,:,cols(i)],ss.at[i],sr.at[i],sp)]
    locs=[pltpu.make_async_copy(w_ref.at[:,cols(i)],g_ref.at[t,z,x,c,:,cols(i)],lsem.at[i]) for i in range(n)]
    Z=[zcopies(i) for i in range(n)]; A=[first(i) for i in range(n)]; B=[second(i) for i in range(n)]; S=[sib(i) for i in range(n)]
    for i in range(n):
        locs[i].start()
        for q in Z[i]: q.start()
    for step in range(n+3):
        if step<n:
            locs[step].wait()
            for q in Z[step]: q.wait_recv()
            for q in A[step]: q.start()
        j=step-1
        if 0<=j<n:
            for q in A[j]: q.wait_recv()
            for q in B[j]: q.start()
        j=step-2
        if 0<=j<n:
            for q in B[j]: q.wait_recv()
            for q in S[j]: q.start()
    for i in range(n):
        for q in Z[i]+A[i]+B[i]: q.wait_send()
        for q in S[i]: q.wait()

def gather(w,chunks,space=pl.ANY,cid=0):
    n=len(chunks); DMA=pltpu.SemaphoreType.DMA
    width=w.shape[1]
    return pl.pallas_call(functools.partial(gather_kernel,chunks),
        in_specs=[pl.BlockSpec(memory_space=space)],out_specs=pl.BlockSpec(memory_space=space),
        out_shape=jax.ShapeDtypeStruct((NT,NZ,NX,NC,ROWS,width),BF),
        scratch_shapes=[DMA((n,)),DMA((n,3)),DMA((n,3)),DMA((n,2)),DMA((n,2)),DMA((n,2)),DMA((n,2)),DMA((n,)),DMA((n,))],
        compiler_params=pltpu.CompilerParams(collective_id=cid,has_side_effects=True,vmem_limit_bytes=60*2**20),name="gather")(w)

def scatter_kernel(chunks,g_hbm,o_ref,g,rs,ra,rc,rb,rz,lsem,ss,sr,as_,ar,bs,br,zs,zr):
    z,x,c,t=place()
    zp,xp,yp,sp=peers()
    n=len(chunks)
    def cols(i): return pl.ds(chunks[i][0],chunks[i][1])
    def ca(i): return pl.ds(chunks[i][0],chunks[i][2])
    def cb(i): return pl.ds(chunks[i][0]+chunks[i][2],chunks[i][1]-chunks[i][2])
    L=[pltpu.make_async_copy(g_hbm.at[:,:,:,:,:,cols(i)],g.at[:,:,:,:,:,cols(i)],lsem.at[i]) for i in range(n)]
    for q in L: q.start()
    greet()
    S=[[rcopy(g.at[:,:,:,1-c,:,cols(i)],rs.at[:,:,:,:,cols(i)],ss.at[i],sr.at[i],sp)] for i in range(n)]
    A=[[rcopy(g.at[:,:,1-x,c,:,ca(i)],ra.at[:,:,:,ca(i)],as_.at[i,0],ar.at[i,0],xp),
        rcopy(g.at[1-t,:,:,c,:,cb(i)],rc.at[:,:,:,cb(i)],as_.at[i,1],ar.at[i,1],yp)] for i in range(n)]
    B=[[rcopy(g.at[1-t,:,x,c,:,ca(i)],rb.at[:,:,ca(i)],bs.at[i,0],br.at[i,0],yp),
        rcopy(g.at[t,:,1-x,c,:,cb(i)],rb.at[:,:,cb(i)],bs.at[i,1],br.at[i,1],xp)] for i in range(n)]
    Zc=[[rcopy(g.at[t,lax.rem(z+d+1,NZ),x,c,:,cols(i)],rz.at[d,:,cols(i)],zs.at[i,d],zr.at[i,d],zp[d]) for d in range(3)] for i in range(n)]
    def addS(i):
        def body(k,_):
            tt=lax.div(k,8); zz=lax.rem(lax.div(k,2),4); xx=lax.rem(k,2)
            g[tt,zz,xx,c,:,cols(i)]=(g[tt,zz,xx,c,:,cols(i)].astype(F32)+rs[tt,zz,xx,:,cols(i)].astype(F32)).astype(BF)
            return 0
        lax.fori_loop(0,16,body,0)
    def addA(i):
        def body(k,_):
            a=lax.div(k,4); b=lax.rem(k,4)
            g[a,b,x,c,:,ca(i)]=(g[a,b,x,c,:,ca(i)].astype(F32)+ra[a,b,:,ca(i)].astype(F32)).astype(BF)
            zz=lax.div(k,2); xx=lax.rem(k,2)
            g[t,zz,xx,c,:,cb(i)]=(g[t,zz,xx,c,:,cb(i)].astype(F32)+rc[zz,xx,:,cb(i)].astype(F32)).astype(BF)
            return 0
        lax.fori_loop(0,8,body,0)
    def addB(i):
        def body(k,_):
            g[t,k,x,c,:,cols(i)]=(g[t,k,x,c,:,cols(i)].astype(F32)+rb[k,:,cols(i)].astype(F32)).astype(BF)
            return 0
        lax.fori_loop(0,4,body,0)
    def addZ(i):
        acc=g[t,z,x,c,:,cols(i)].astype(F32)
        for d in range(3): acc=acc+rz[d,:,cols(i)].astype(F32)
        o_ref[:,cols(i)]=acc
    for step in range(n+4):
        if step<n:
            L[step].wait()
            for q in S[step]: q.start()
        j=step-1
        if 0<=j<n:
            for q in S[j]: q.wait_recv()
            addS(j)
            for q in A[j]: q.start()
        j=step-2
        if 0<=j<n:
            for q in A[j]: q.wait_recv()
            addA(j)
            for q in B[j]: q.start()
        j=step-3
        if 0<=j<n:
            for q in B[j]: q.wait_recv()
            addB(j)
            for q in Zc[j]: q.start()
        j=step-4
        if 0<=j<n:
            for q in Zc[j]: q.wait_recv()
            addZ(j)
    for i in range(n):
        for q in S[i]+A[i]+B[i]+Zc[i]: q.wait_send()

def scatter(g,chunks,cid=1):
    n=len(chunks); DMA=pltpu.SemaphoreType.DMA
    W=g.shape[-1]; V=lambda *s:pltpu.VMEM(s+(ROWS,W),BF)
    return pl.pallas_call(functools.partial(scatter_kernel,chunks),
        in_specs=[pl.BlockSpec(memory_space=pl.ANY)],out_specs=pl.BlockSpec(memory_space=pltpu.VMEM),
        out_shape=jax.ShapeDtypeStruct((ROWS,W),F32),
        scratch_shapes=[V(NT,NZ,NX,NC),V(NT,NZ,NX),V(NT,NZ),V(NZ,NX),V(NZ),V(3),
          DMA((n,)),DMA((n,)),DMA((n,)),DMA((n,2)),DMA((n,2)),DMA((n,2)),DMA((n,2)),DMA((n,3)),DMA((n,3))],
        compiler_params=pltpu.CompilerParams(collective_id=cid,has_side_effects=True,vmem_limit_bytes=62*2**20),name="scatter")(g)
def mkchunks(ws):
    out=[];s=0
    for w in ws:
        w*=128
        out.append((s,w,(w//256)*128)); s+=w
    return out

CHUNKS=mkchunks([6,6,9,6,6,6])
L=1024
def dot(a,b,ca,cb):
    return lax.dot_general(a,b,(((ca,),(cb,)),((),())),preferred_element_type=F32)
def fwdT(bk, q_ref,k_ref,v_ref,bias_ref,o_ref,lse_ref):
    lane=lax.broadcasted_iota(jnp.int32,(1,128),1)
    qp=q_ref[...]; kp=k_ref[...]; vp=v_ref[...]
    bias=bias_ref[...]
    vT=vp.T
    outs=[]
    for h in range(2):
        sel=(lane//64)==h
        one=lane==(64*(1-h))
        kh=jnp.where(sel,kp,jnp.where(one,bias.astype(BF),jnp.zeros_like(kp)))
        qh=jnp.where(sel,qp*0.125,jnp.where(one,jnp.ones_like(qp),jnp.zeros_like(qp)))
        oT=[]
        for qi in range(L//bk):
            sT=dot(kh,qh[qi*bk:(qi+1)*bk],1,1)
            m=jnp.max(sT,axis=0,keepdims=True)
            e=jnp.exp(sT-m)
            l=jnp.sum(e,axis=0,keepdims=True)
            p=(e*(1.0/l)).astype(BF)
            oT.append(dot(vT[h*64:(h+1)*64],p,1,0))
            lse_ref[0,h:h+1,qi*bk:(qi+1)*bk]=m+jnp.log(l)
        outs.append(jnp.concatenate(oT,axis=1))
    oT=jnp.concatenate(outs,axis=0)
    o_ref[...]=oT.T.astype(BF)

def call_fwd(body,b,q,k,v,bias):
    return pl.pallas_call(functools.partial(body,b),grid=(6,),
      in_specs=[pl.BlockSpec((L,128),lambda i:(0,i))]*3+[pl.BlockSpec((L,1),lambda i:(0,0))],
      out_specs=[pl.BlockSpec((L,128),lambda i:(0,i)),pl.BlockSpec((1,2,L),lambda i:(i,0,0))],
      out_shape=[jax.ShapeDtypeStruct((L,768),BF),jax.ShapeDtypeStruct((6,2,L),F32)],
      compiler_params=pltpu.CompilerParams(vmem_limit_bytes=60*2**20),name=f"{body.__name__}_{b}")(q,k,v,bias)

def bwdT(bq, q_ref,k_ref,v_ref,do_ref,bias_ref,lse_ref,dq_ref,dk_ref,dv_ref):
    lane=lax.broadcasted_iota(jnp.int32,(1,128),1)
    kp=k_ref[...]; vp=v_ref[...]
    bias=bias_ref[...]
    khs=[];vhs=[];kts=[]
    for h in range(2):
        sel=(lane//64)==h
        one=lane==(64*(1-h))
        khs.append(jnp.where(sel,kp,jnp.where(one,bias.astype(BF),jnp.zeros_like(kp))))
        vhs.append(jnp.where(sel,vp,jnp.zeros_like(vp)))
    kT=kp.T
    dk=[None,None];dv=[None,None]
    for qi in range(L//bq):
        rows=pl.ds(qi*bq,bq)
        qp=q_ref[rows,:]; dop=do_ref[rows,:]
        dqT=[]
        for h in range(2):
            sel=(lane//64)==h
            one=lane==(64*(1-h))
            qh=jnp.where(sel,qp*0.125,jnp.where(one,jnp.ones_like(qp),jnp.zeros_like(qp)))
            doh=jnp.where(sel,dop,jnp.zeros_like(dop))
            qz=jnp.where(sel,qp*0.125,jnp.zeros_like(qp))
            sT=dot(khs[h],qh,1,1)
            p=jnp.exp(sT-lse_ref[0,h:h+1,qi*bq:(qi+1)*bq])
            dp=dot(vhs[h],doh,1,1)
            d=jnp.sum(p*dp,axis=0,keepdims=True)
            ds=(p*(dp-d)).astype(BF)
            pb=p.astype(BF)
            a=dot(pb,doh,1,0); dv[h]=a if dv[h] is None else dv[h]+a
            a=dot(ds,qz,1,0); dk[h]=a if dk[h] is None else dk[h]+a
            dqT.append(dot(kT[h*64:(h+1)*64],ds,1,0))
        dq_ref[rows,:]=(jnp.concatenate(dqT,axis=0).T*0.125)
    dk_ref[...]=dk[0]+dk[1]
    dv_ref[...]=dv[0]+dv[1]

def call_bwd(body,b,q,k,v,do,bias,lse):
    return pl.pallas_call(functools.partial(body,b),grid=(6,),
      in_specs=[pl.BlockSpec((L,128),lambda i:(0,i))]*4+[pl.BlockSpec((L,1),lambda i:(0,0)),pl.BlockSpec((1,2,L),lambda i:(i,0,0))],
      out_specs=[pl.BlockSpec((L,128),lambda i:(0,i))]*3,
      out_shape=[jax.ShapeDtypeStruct((L,768),F32)]*3,
      compiler_params=pltpu.CompilerParams(vmem_limit_bytes=60*2**20),name=f"{body.__name__}_{b}")(q,k,v,do,bias,lse)


def ln_stats(v):
    mean=jnp.mean(v,axis=-1,keepdims=True)
    cen=v-mean
    inv=lax.rsqrt(jnp.mean(cen*cen,axis=-1,keepdims=True)+EPSILON)
    return cen*inv,inv

def ln_back(gain,dy,xhat,inv):
    gd=gain*dy
    return (gd-jnp.mean(gd,axis=-1,keepdims=True)-xhat*jnp.mean(gd*xhat,axis=-1,keepdims=True))*inv

def phi_cdf(u):
    return 0.5*(1.0+lax.erf(u*(1.0/math.sqrt(2.0))))

def pack_weights(qkv,out,up,down,w1,w2,b1,hv,lv):
    t=lax.axis_index("tensor")
    low=lambda a:a.astype(BF)
    w2h=lax.dynamic_slice_in_dim(low(w2),t*PIECE,PIECE,1)
    w1h=lax.dynamic_slice_in_dim(jnp.pad(low(w1),((0,8),(0,0))),t*256,256,1)
    lanes=lambda a:jnp.pad(low(a),((0,0),(0,128-a.shape[1])))
    vec=jnp.concatenate([lanes(lv),lanes(hv[:,0]),lanes(b1[None]),jnp.zeros((2,128),BF)],axis=0)
    aux=jnp.concatenate([w2h,jnp.concatenate([w1h,vec],axis=1)],axis=0)
    return jnp.concatenate([aux,low(qkv).reshape(ROWS,3*PIECE),low(out).T,low(up).reshape(ROWS,4*PIECE),low(down).transpose(2,0,1).reshape(ROWS,4*PIECE)],axis=1)

WIDE=13*PIECE
RB=256
def spread(blocks,w,tiles):
    lane=lax.broadcasted_iota(jnp.int32,(16,128),1)
    acc=[jnp.zeros((16,128),F32) for _ in range(tiles+1)]
    for n,b in enumerate(blocks):
        tile,s=divmod(n*w,128)
        wide=jnp.concatenate([jnp.where(lane<w,b,0.0),jnp.zeros((16,128),F32)],axis=1)
        if s: wide=pltpu.roll(wide,s,1)
        acc[tile]=acc[tile]+wide[:,:128]
        acc[tile+1]=acc[tile+1]+wide[:,128:]
    return jnp.concatenate(acc[:tiles],axis=1)

def attend_pair(q_ref,k_ref,v_ref,o_ref,lse_ref,bias_ref,i,bq=512):
    lane=lax.broadcasted_iota(jnp.int32,(1,128),1)
    cs=pl.ds(pl.multiple_of(i*128,128),128)
    kp=k_ref[:,cs]; vT=v_ref[:,cs].T
    bias=bias_ref[...]
    khs=[]
    for h in range(2):
        khs.append(jnp.where((lane//64)==h,kp,jnp.where(lane==(64*(1-h)),bias,jnp.zeros_like(kp))))
    for qi in range(L//bq):
        qp=q_ref[pl.ds(qi*bq,bq),cs]*0.125
        oT=[]
        for h in range(2):
            qh=jnp.where((lane//64)==h,qp,jnp.where(lane==(64*(1-h)),jnp.ones_like(qp),jnp.zeros_like(qp)))
            sT=dot(khs[h],qh,1,1)
            m=jnp.max(sT,axis=0,keepdims=True)
            e=jnp.exp(sT-m)
            l=jnp.sum(e,axis=0,keepdims=True)
            p=(e*(1.0/l)).astype(BF)
            oT.append(dot(vT[h*64:(h+1)*64],p,1,0))
            lse_ref[i,h:h+1,qi*bq:(qi+1)*bq]=m+jnp.log(l)
        o_ref[pl.ds(qi*bq,bq),cs]=jnp.concatenate(oT,axis=0).T.astype(BF)

GCH=[(k*2*PIECE,2*PIECE,PIECE) for k in range(6)]+[(12*PIECE,PIECE,128)]

def gather_steps(w_ref,g,zs,zr,fs,fr,ss,sr):
    z,x,c,t=place(); zp,xp,yp,sp=peers(); n=len(GCH)
    def cols(i): return pl.ds(GCH[i][0],GCH[i][1])
    def ca(i): return pl.ds(GCH[i][0],GCH[i][2])
    def cb(i): return pl.ds(GCH[i][0]+GCH[i][2],GCH[i][1]-GCH[i][2])
    same=lambda r,s,q,d:rcopy(r,r,s,q,d)
    Z=lambda i:[rcopy(w_ref.at[:,cols(i)],g.at[t,z,x,c,:,cols(i)],zs.at[i,d],zr.at[i,d],zp[d]) for d in range(3)]
    A=lambda i:[same(g.at[t,:,x,c,:,ca(i)],fs.at[i,0],fr.at[i,0],xp),same(g.at[t,:,x,c,:,cb(i)],fs.at[i,1],fr.at[i,1],yp)]
    B=lambda i:[same(g.at[t,:,:,c,:,ca(i)],fs.at[i,2],fr.at[i,2],yp),same(g.at[:,:,x,c,:,cb(i)],fs.at[i,3],fr.at[i,3],xp)]
    S=lambda i:[same(g.at[:,:,:,c,:,cols(i)],ss.at[i],sr.at[i],sp)]
    def begin():
        for i in range(n):
            g[t,z,x,c,:,cols(i)]=w_ref[:,cols(i)]
        for i in range(n):
            for q in Z(i): q.start()
    def step(k):
        if k<n:
            for q in Z(k): q.wait_recv()
            for q in A(k): q.start()
        if 0<=k-1<n:
            for q in A(k-1): q.wait_recv()
            for q in B(k-1): q.start()
        if 0<=k-2<n:
            for q in B(k-2): q.wait_recv()
            for q in S(k-2): q.start()
        if 0<=k-3<n:
            for q in S(k-3): q.wait_recv()
    def finish():
        for i in range(n):
            for q in Z(i)+A(i)+B(i)+S(i): q.wait_send()
    return begin,step,finish

def front_kernel(w_ref,tok_hbm,cot_hbm,seg_ref,feat_ref,
        q_o,k_o,v_o,o_o,lse_o,out_o,dmbT_o,abT_o,drbT_o,hid_o,dub_o,dr1_o,dob_o,hbT_o,wqkv_o,aux_o,sums_o,bup_o,time_o,
        g,tok,cot,q,k,v,o,lse,own,bias,vecs,temb,hbT,gp,hid,dub,dmbT,abT,drbT,dr1,
        zs,zr,fs,fr,ss,sr,lsem,osem,hsem):
    z,x,c,t=place()
    begin,step,finish=gather_steps(w_ref,g,zs,zr,fs,fr,ss,sr)
    win=pl.ds(pl.multiple_of(t*512,512),L)
    ltok=pltpu.make_async_copy(tok_hbm.at[win,:],tok,lsem.at[0]); ltok.start()
    lcot=pltpu.make_async_copy(cot_hbm.at[win,:],cot,lsem.at[1]); lcot.start()
    greet()
    begin()
    seg=seg_ref[:,pl.ds(pl.multiple_of(t*512,128),L)]
    own_row=jnp.where(seg==t,1.0,0.0)
    ownT=jnp.broadcast_to(own_row,(128,L)).T
    own[...]=ownT
    bias[...]=jnp.where(ownT>0.5,0.0,-1e30).astype(BF)
    for s in range(4): step(s)
    def vecblk(tt,n): return g[tt,n//4,(n//2)%2,n%2,32:48,256:384].astype(F32)
    b0=[vecblk(0,n) for n in range(16)]; b1=[vecblk(1,n) for n in range(16)]
    lv=spread(b0,48,6)
    hv=jnp.concatenate([spread(b0,24,3),spread(b1,24,3)],axis=1)
    vecs[0:16,:]=lv
    vecs[16:32,:]=hv
    bin_=spread(b0,32,4)[13:14,:]
    inner=bin_
    w1=jnp.concatenate([g[0,:,:,:,32:48,0:256].reshape(256,256),g[1,:,:,:,32:48,0:256].reshape(256,256)],axis=1)
    inner=dot(feat_ref[...],w1,1,0)[0:1]+bin_
    sig=1.0/(1.0+jnp.exp(-inner))
    act=inner*sig
    w2=jnp.concatenate([g[0,:,:,:,0:32,0:384].reshape(512,384),g[1,:,:,:,0:32,0:384].reshape(512,384)],axis=1)
    actb=jnp.broadcast_to(act,(16,512)).astype(BF)
    te=dot(actb,w2,1,0)[0:1]+lv[6:7]
    temb[...]=jnp.broadcast_to(te,(8,D))
    time_o[...]=jnp.concatenate([inner,sig,jnp.zeros((6,512),F32)],axis=0)
    ltok.wait()
    outs=[]
    def emit(src,dst):
        cp=pltpu.make_async_copy(src,dst,osem.at[len(outs)]); cp.start(); outs.append(cp)
    def hid_rows(r,_):
        rows=pl.ds(pl.multiple_of(r*RB,RB),RB)
        hb=(tok[rows,:].astype(F32)+temb[0:1,:]).astype(BF)
        hbT[:,rows]=hb.T
        return 0
    lax.fori_loop(0,L//RB,hid_rows,0)
    def project(which,ref,brow):
        def rows_body(r,_):
            rows=pl.ds(pl.multiple_of(r*RB,RB),RB)
            hb=(tok[rows,:].astype(F32)+temb[0:1,:]).astype(BF)
            for tt in range(2):
                val=dot(hb,g[tt,:,:,:,:,(1+which)*PIECE:(2+which)*PIECE].reshape(D,PIECE),1,0)
                if brow is not None: val=val+vecs[brow:brow+1,tt*PIECE:(tt+1)*PIECE]
                ref[rows,tt*PIECE:(tt+1)*PIECE]=val.astype(BF)
            return 0
        lax.fori_loop(0,L//RB,rows_body,0)
    project(0,q,16+7)
    emit(hbT,hbT_o); emit(q,q_o)
    step(4)
    project(1,k,None); project(2,v,16+8)
    emit(k,k_o); emit(v,v_o)
    emit(g.at[:,:,:,:,:,0:PIECE],aux_o); emit(g.at[:,:,:,:,:,PIECE:4*PIECE],wqkv_o)
    def pair(i,_):
        attend_pair(q,k,v,o,lse,bias,i)
        for s in range(5):
            @pl.when(i==s)
            def _(): step(5+s)
        return 0
    lax.fori_loop(0,6,pair,0)
    emit(o,o_o); emit(lse,lse_o)
    lcot.wait()
    for cp in outs: cp.wait()
    done=len(outs)
    out,dob=q,k
    mid_body(g,tok,cot,o,own,vecs,temb,gp,hid,dub,out,dmbT,abT,drbT,dr1,dob,sums_o,bup_o,hid_o,dub_o,hsem)
    for a,b in ((out,out_o),(dmbT,dmbT_o),(abT,abT_o),(drbT,drbT_o),(dr1,dr1_o),(dob,dob_o)): emit(a,b)
    for cp in outs[done:]: cp.wait()
    finish()

def mid_body(g,tok,cot,o,own,vecs,temb,gp,hid,dub,out,dmbT,abT,drbT,dr1,dob,sums_o,bup_o,hid_o,dub_o,hsem):
    def W(tt,piece,n=1): return g[tt,:,:,:,:,piece*PIECE:(piece+n)*PIECE].reshape(D,n*PIECE)
    row=lambda r:vecs[r:r+1,:]
    sums_o[...]=jnp.zeros((8,D),F32); bup_o[...]=jnp.zeros((8,4*D),F32)
    csum=lambda a:jnp.sum(a,axis=0,keepdims=True)
    def stage(buf,dst,r,which):
        return pltpu.make_async_copy(buf.at[lax.rem(r,2)],dst.at[pl.ds(pl.multiple_of(r*RB,RB),RB),:],hsem.at[which,lax.rem(r,2)])
    def block(r,_):
        rows=pl.ds(pl.multiple_of(r*RB,RB),RB)
        slot=lax.rem(r,2)
        @pl.when(r>=2)
        def _():
            stage(hid,hid_o,r-2,0).wait(); stage(dub,dub_o,r-2,1).wait()
        attn=dot(o[rows,0:PIECE],W(0,4),1,1)+dot(o[rows,PIECE:D],W(1,4),1,1)
        r1=(tok[rows,:].astype(F32)+temb[0:1,:])+(attn+row(0))
        x1,inv1=ln_stats(r1)
        a=x1*row(1)+row(2)
        ab=a.astype(BF)
        abT[:,rows]=ab.T
        mlp=row(3)
        for tt in range(2):
            for j in range(4):
                cc=pl.ds((tt*4+j)*PIECE,PIECE)
                u=dot(ab,W(tt,5+j),1,0)+vecs[16+9+j:16+10+j,tt*PIECE:(tt+1)*PIECE]
                cdf=phi_cdf(u)
                gp[:,cc]=cdf+u*jnp.exp(-0.5*u*u)*(1.0/math.sqrt(2*math.pi))
                hid[slot,:,cc]=(u*cdf).astype(BF)
            mlp=mlp+dot(hid[slot,:,tt*4*PIECE:(tt+1)*4*PIECE],W(tt,9,4),1,1)
        stage(hid,hid_o,r,0).start()
        x2,inv2=ln_stats(a+mlp)
        out[rows,:]=(x2*row(4)+row(5)).astype(BF)
        dy=jnp.where(own[rows,0:1]>0.5,cot[rows,:].astype(F32),0.0)
        sums_o[4:5,:]+=csum(dy*x2); sums_o[5:6,:]+=csum(dy)
        dr2=ln_back(row(4),dy,x2,inv2)
        sums_o[3:4,:]+=csum(dr2)
        dmb=dr2.astype(BF)
        dmbT[:,rows]=dmb.T
        da=dr2
        for tt in range(2):
            for j in range(4):
                cc=pl.ds((tt*4+j)*PIECE,PIECE)
                du=dot(dmb,W(tt,9+j),1,0)*gp[:,cc]
                bup_o[0:1,cc]+=csum(du)
                dub[slot,:,cc]=du.astype(BF)
            da=da+dot(dub[slot,:,tt*4*PIECE:(tt+1)*4*PIECE],W(tt,5,4),1,1)
        stage(dub,dub_o,r,1).start()
        sums_o[1:2,:]+=csum(da*x1); sums_o[2:3,:]+=csum(da)
        d1=ln_back(row(1),da,x1,inv1)
        sums_o[0:1,:]+=csum(d1)
        dr1[rows,:]=d1
        drb=d1.astype(BF)
        drbT[:,rows]=drb.T
        for tt in range(2):
            dob[rows,tt*PIECE:(tt+1)*PIECE]=dot(drb,W(tt,4),1,0).astype(BF)
        return 0
    lax.fori_loop(0,L//RB,block,0)
    for r in (L//RB-2,L//RB-1):
        stage(hid,hid_o,r,0).wait(); stage(dub,dub_o,r,1).wait()

def front(w,tokens,cotangent,seg,featp,cid=0):
    DMA=pltpu.SemaphoreType.DMA; n=len(GCH)
    V=lambda s,d=BF:pltpu.VMEM(s,d)
    A=pl.BlockSpec(memory_space=pl.ANY); M=pl.BlockSpec(memory_space=pltpu.VMEM)
    big=lambda s,d=BF:jax.ShapeDtypeStruct(s,d)
    row=(L,D); tr=(D,L)
    G6=lambda w_:(NT,NZ,NX,NC,ROWS,w_)
    return pl.pallas_call(front_kernel,
        in_specs=[M,A,A,M,M],
        out_specs=[A]*16+[M]*3,
        out_shape=[big(row),big(row),big(row),big(row),big((6,2,L),F32),big(row),big(tr),big(tr),big(tr),big((L,4*D)),big((L,4*D)),
            big(row,F32),big(row),big(tr),big(G6(3*PIECE)),big(G6(PIECE)),big((8,D),F32),big((8,4*D),F32),big((8,512),F32)],
        scratch_shapes=[V(G6(WIDE)),V(row),V(row),V(row),V(row),V(row),V(row),V((6,2,L),F32),V((L,128),F32),V((L,128)),V((32,D),F32),V((8,D),F32),
            V(tr),V((RB,4*D),F32),V((2,RB,4*D)),V((2,RB,4*D)),V(tr),V(tr),V(tr),V(row,F32),
            DMA((n,3)),DMA((n,3)),DMA((n,4)),DMA((n,4)),DMA((n,)),DMA((n,)),DMA((2,)),DMA((20,)),DMA((2,2))],
        compiler_params=pltpu.CompilerParams(collective_id=cid,has_side_effects=True,vmem_limit_bytes=63*2**20),name="front")(w,tokens,cotangent,seg,featp)

def shards_fast(tokens,cotangent,segment_ids,timesteps,*params):
    masters=params[:9];moments=params[9:18];averages=params[18:]
    t=lax.axis_index("tensor")
    step=lax.dynamic_slice_in_dim(timesteps,t,1,1)[0]
    feat=time_features(step,TD).astype(BF)
    featp=jnp.broadcast_to(jnp.pad(feat.reshape(16,8),((0,0),(0,8))).reshape(1,256),(16,256))
    q,k,v,o,lse,out_win,dmbT,abT,drbT,hid,dub,dr1,dob,hbT,wq6,aux6,sums,bups,tstate=front(pack_weights(*masters),tokens,cotangent,segment_ids,featp)
    own=(lax.dynamic_slice_in_dim(segment_ids[0],t*512,L,0)==t)[:,None]
    bias=jnp.where(own,0.0,-1e30).astype(F32)
    w_qkv=wq6.reshape(NT,D,3,PIECE)
    both=lambda a:jnp.concatenate([a[0],a[1]],axis=-1)
    w2=both(aux6.reshape(NT,16,ROWS,PIECE)[:,:,:32].reshape(NT,512,PIECE))
    inner=tstate[0:1];sig=tstate[1:2];act=(inner*sig).astype(BF)
    featp=featp[:1]
    g_bo,g_gain1,g_shift1,g_bdown,g_gain2,g_shift2=[sums[r] for r in range(6)]
    g_bup=bups[0].reshape(NT,4*PIECE)
    E=functools.partial(jnp.einsum,preferred_element_type=F32)
    hidr=hid.reshape(L,NT,4*PIECE);dubr=dub.reshape(L,NT,4*PIECE)
    g_down=E("fp,ptj->tfj",dmbT,hidr);g_up=E("dp,ptj->tdj",abT,dubr);g_out=E("fp,pte->tfe",drbT,o.reshape(L,NT,PIECE))
    hb=hbT.T
    dq,dk,dv=call_bwd(bwdT,512,q,k,v,dob,bias,lse)
    g_bq=jnp.sum(dq,0); g_bv=jnp.sum(dv,0)
    dqkv=jnp.stack([dq,dk,dv],axis=1).astype(BF).reshape(L,3,NT,PIECE)
    g_qkv=jnp.einsum("pd,pcte->tdce",hb,dqkv,preferred_element_type=F32)
    dh0=jnp.einsum("pcte,tdce->pd",dqkv,w_qkv,preferred_element_type=F32)+dr1
    in_win=dh0.astype(BF)
    dtemb=jnp.sum(dh0,0,keepdims=True)
    dtb=dtemb.astype(BF)
    g_w2=dot(act,dtb,0,0)
    dinner=dot(dtb,w2,1,1)*(sig*(1.0+inner*(1.0-sig)))
    g_w1=dot(featp,dinner.astype(BF),0,0)
    g_lv=jnp.stack([g_bo,g_gain1,g_shift1,g_bdown,g_gain2,g_shift2,dtemb[0]],0)
    g_bup=g_bup.reshape(NT,4,PIECE).transpose(1,0,2).reshape(4,D)
    g_hv=jnp.concatenate([g_bq[None],g_bv[None],g_bup],0)
    low=lambda a:a.astype(BF)
    padl=lambda a:jnp.pad(low(a),((0,0),)*3+((0,128-a.shape[-1]),))
    lvp=jnp.broadcast_to(padl(g_lv.reshape(7,16,48).transpose(1,0,2)[None]),(NT,16,7,128))
    hvp=padl(g_hv.reshape(6,NT,16,24).transpose(1,2,0,3))
    b1p=jnp.broadcast_to(padl(dinner.reshape(1,16,1,32)),(NT,16,1,128))
    vecp=jnp.concatenate([lvp,hvp,b1p,jnp.zeros((NT,16,2,128),BF)],axis=2)
    split=lambda a,r,w:low(a).reshape(16,r,NT,w).transpose(2,0,1,3)
    auxg=jnp.concatenate([split(g_w2,32,PIECE),jnp.concatenate([split(g_w1,16,256),vecp],axis=3)],axis=2)
    slab=lambda a:low(a).reshape(NT,16,ROWS,-1)
    big=jnp.concatenate([auxg,slab(g_qkv),slab(g_out),slab(g_up),slab(g_down)],axis=3).reshape(NT,NZ,NX,NC,ROWS,13*PIECE)
    red=scatter(big,CHUNKS)
    swap=lambda a:lax.ppermute(a,"tensor",[(0,1),(1,0)])
    aux_mine=red[:,:PIECE].astype(BF)
    aux_peer=swap(aux_mine)
    aux0=jnp.where(t==0,aux_mine,aux_peer).astype(F32); aux1=jnp.where(t==0,aux_peer,aux_mine).astype(F32)
    r_qkv=red[:,PIECE:4*PIECE].reshape(ROWS,3,PIECE)
    r_out=red[:,4*PIECE:5*PIECE].T
    r_up=red[:,5*PIECE:9*PIECE].reshape(ROWS,4,PIECE)
    r_down=red[:,9*PIECE:].reshape(ROWS,4,PIECE).transpose(1,2,0)
    r_w2=jnp.concatenate([aux0[:32],aux1[:32]],axis=1)
    r_w1=jnp.concatenate([aux0[32:40,:256],aux1[32:40,:256]],axis=1)
    r_lv=aux0[32:39,256:304]
    r_b1=aux0[45,256:288]
    r_hv=jnp.where(t==0,aux0,aux1)[39:45,256:280].reshape(6,1,24)
    grads=(r_qkv,r_out,r_up,r_down,r_w1,r_w2,r_b1,r_hv,r_lv)
    sq=lambda a:jnp.sum(a*a)
    squares=sum(sq(grads[i]) for i in (0,1,2,3,7))+0.5*sum(sq(grads[i]) for i in (4,5,6,8))
    norm=jnp.sqrt(lax.psum(squares,("dp","tensor")))
    factor=1.0/jnp.maximum(norm,1.0)
    rate=4.0*math.sqrt(MPARAMS/D)
    new=[advance(m,v_,a_,g_,factor,rate) for m,v_,a_,g_ in zip(masters,moments,averages,grads)]

    def whole(win):
        peer=swap(win)
        lo=jnp.where(t==0,win,peer); hi=jnp.where(t==0,peer,win)
        mid=jnp.where((segment_ids[0,512:1024]==0)[:,None],lo[512:],hi[:512])
        return jnp.concatenate([lo[:512],mid,hi[512:]],axis=0)
    return (whole(out_win),whole(in_win),norm)+tuple(n[0] for n in new)+tuple(n[1] for n in new)+tuple(n[2] for n in new)


def solution(mesh):
    fast=dict(mesh.shape)=={'dp':16,'tensor':2}
    return jax.shard_map(
        shards_fast if fast else shards_any,
        mesh=mesh,
        in_specs=(
            P("dp", None),
            P("dp", None),
            P("dp", None),
            P("dp", None),
            P("dp", None, "tensor"),
            P("tensor", "dp"),
            P("dp", None, "tensor"),
            P(None, "tensor", "dp"),
            P("dp", None),
            P("dp", None),
            P("dp"),
            P(None, "tensor", "dp"),
            P(None, "dp"),
            P("dp", None, "tensor"),
            P("tensor", "dp"),
            P("dp", None, "tensor"),
            P(None, "tensor", "dp"),
            P("dp", None),
            P("dp", None),
            P("dp"),
            P(None, "tensor", "dp"),
            P(None, "dp"),
            P("dp", None, "tensor"),
            P("tensor", "dp"),
            P("dp", None, "tensor"),
            P(None, "tensor", "dp"),
            P("dp", None),
            P("dp", None),
            P("dp"),
            P(None, "tensor", "dp"),
            P(None, "dp"),
        ),
        out_specs=(
            P("dp", None),
            P("dp", None),
            P(),
            P("dp", None, "tensor"),
            P("tensor", "dp"),
            P("dp", None, "tensor"),
            P(None, "tensor", "dp"),
            P("dp", None),
            P("dp", None),
            P("dp"),
            P(None, "tensor", "dp"),
            P(None, "dp"),
            P("dp", None, "tensor"),
            P("tensor", "dp"),
            P("dp", None, "tensor"),
            P(None, "tensor", "dp"),
            P("dp", None),
            P("dp", None),
            P("dp"),
            P(None, "tensor", "dp"),
            P(None, "dp"),
            P("dp", None, "tensor"),
            P("tensor", "dp"),
            P("dp", None, "tensor"),
            P(None, "tensor", "dp"),
            P("dp", None),
            P("dp", None),
            P("dp"),
            P(None, "tensor", "dp"),
            P(None, "dp"),
        ),
        check_vma=False,
    )
```

```python
import functools
import math

import jax
import jax.numpy as jnp
from jax import lax
from jax.experimental import pallas as pl
from jax.experimental.pallas import tpu as pltpu
from jax.sharding import PartitionSpec as P

D = 768
HD = 64
TD = 128
SEGS = 2
PACK = 1536
MPARAMS = 7536640


EPSILON = 1e-05
MOMENTUM = 0.5
AVERAGE_DECAY = 0.5


def layer_norm(values, gain_vec, shift_vec):
    centre = jnp.mean(values, axis=-1, keepdims=True)
    centred = values - centre
    spread = jnp.mean(centred * centred, axis=-1, keepdims=True)
    return centred * lax.rsqrt(spread + EPSILON) * gain_vec + shift_vec


def time_features(step_ids, feat_width):
    midpoint = feat_width // 2
    frequency = jnp.exp(-math.log(10000.0) * jnp.arange(midpoint, dtype=jnp.float32) / midpoint)
    angles = step_ids.astype(jnp.float32)[..., None] * frequency
    return jnp.concatenate([jnp.cos(angles), jnp.sin(angles)], axis=-1)


def gelu_exact(values):
    return jax.nn.gelu(values, approximate=False)


def head_slice(matrix, head_index):
    return lax.dynamic_slice_in_dim(matrix, head_index * HD, HD, 1)


def merge_heads(stacked):
    return stacked.transpose(1, 0, 2).reshape(stacked.shape[1], stacked.shape[0] * stacked.shape[2])


def advance(master, moment, average, grad, factor, step_rate):
    scaled = grad * factor
    velocity = MOMENTUM * moment + scaled
    fresh_master = master - step_rate * (scaled + MOMENTUM * velocity)
    smoothed = AVERAGE_DECAY * average + (1.0 - AVERAGE_DECAY) * fresh_master
    return (fresh_master, velocity, smoothed)


def shards_any(
    tokens,
    cotangent,
    segment_ids,
    timesteps,
    qkv_weight,
    out_weight,
    up_weight,
    down_weight,
    time_inner,
    time_outer,
    time_bias,
    head_vectors,
    layer_vectors,
    qkv_moment,
    out_moment,
    up_moment,
    down_moment,
    inner_moment,
    outer_moment,
    bias_moment,
    head_moment,
    layer_moment,
    qkv_average,
    out_average,
    up_average,
    down_average,
    inner_average,
    outer_average,
    bias_average,
    head_average,
    layer_average,
):
    w_qkv, w_out, w_up, w_down, w_inner, w_outer, b_inner, head_vec, layer_vec = (
        lax.all_gather(qkv_weight.astype(jnp.bfloat16), "dp", axis=0, tiled=True),
        lax.all_gather(out_weight.astype(jnp.bfloat16), "dp", axis=1, tiled=True),
        lax.all_gather(up_weight.astype(jnp.bfloat16), "dp", axis=0, tiled=True),
        lax.all_gather(down_weight.astype(jnp.bfloat16), "dp", axis=2, tiled=True),
        lax.all_gather(time_inner.astype(jnp.bfloat16), "dp", axis=0, tiled=True),
        lax.all_gather(time_outer.astype(jnp.bfloat16), "dp", axis=0, tiled=True),
        lax.all_gather(time_bias.astype(jnp.bfloat16), "dp", axis=0, tiled=True),
        lax.all_gather(head_vectors.astype(jnp.bfloat16), "dp", axis=2, tiled=True),
        lax.all_gather(layer_vectors.astype(jnp.bfloat16), "dp", axis=1, tiled=True),
    )
    local_width = w_out.shape[0]
    head_count = local_width // HD
    packed = tokens.shape[0]
    head_rows = head_vec.astype(jnp.float32).reshape(6, local_width)
    layer_rows = layer_vec.astype(jnp.float32)
    score_scale = 1.0 / math.sqrt(HD)
    block_rows = min(PACK, 512)
    block_count = packed // block_rows
    seg_row = segment_ids[0]
    features = time_features(timesteps[0], TD)
    feature_low = features.astype(jnp.bfloat16)
    inner_pre = jnp.dot(feature_low, w_inner, preferred_element_type=jnp.float32) + b_inner.astype(
        jnp.float32
    )
    silu_out, silu_pull = jax.vjp(jax.nn.silu, inner_pre)
    act_low = silu_out.astype(jnp.bfloat16)
    time_embed = jnp.dot(act_low, w_outer, preferred_element_type=jnp.float32) + layer_rows[6]
    onehot = (seg_row[:, None] == jnp.arange(SEGS, dtype=jnp.int32)[None, :]).astype(jnp.float32)
    hidden0 = tokens.astype(jnp.float32) + jnp.dot(
        onehot, time_embed, precision=lax.Precision.HIGHEST, preferred_element_type=jnp.float32
    )
    hidden_low = hidden0.astype(jnp.bfloat16)
    projected = jnp.einsum("pd,dce->pce", hidden_low, w_qkv, preferred_element_type=jnp.float32)
    queries = (projected[:, 0] + head_rows[0]).astype(jnp.bfloat16)
    keys_low = projected[:, 1].astype(jnp.bfloat16)
    values_low = (projected[:, 2] + head_rows[1]).astype(jnp.bfloat16)

    def block_scores(query_blk, key_all, seg_query):
        raw_scores = (
            jnp.einsum("qd,kd->qk", query_blk, key_all, preferred_element_type=jnp.float32)
            * score_scale
        )
        same_doc = seg_query[:, None] == seg_row[None, :]
        return (raw_scores, same_doc)

    def attend_head(head_index):
        query_h = head_slice(queries, head_index)
        key_h = head_slice(keys_low, head_index)
        value_h = head_slice(values_low, head_index)
        out_blocks = []
        sum_blocks = []
        for block_index in range(block_count):
            first_row = block_index * block_rows
            raw_scores, same_doc = block_scores(
                query_h[first_row : first_row + block_rows],
                key_h,
                seg_row[first_row : first_row + block_rows],
            )
            masked = jnp.where(same_doc, raw_scores, -1e30)
            row_peak = jnp.max(masked, axis=1, keepdims=True)
            exponent = jnp.exp(masked - row_peak)
            row_total = jnp.sum(exponent, axis=1, keepdims=True)
            soft_weights = exponent / row_total
            out_blocks.append(
                jnp.dot(
                    soft_weights.astype(jnp.bfloat16), value_h, preferred_element_type=jnp.float32
                )
            )
            sum_blocks.append((row_peak + jnp.log(row_total))[:, 0])
        return (jnp.concatenate(out_blocks, axis=0), jnp.concatenate(sum_blocks, axis=0))

    head_out, log_sums = lax.map(attend_head, jnp.arange(head_count, dtype=jnp.int32))
    att_low = merge_heads(head_out).astype(jnp.bfloat16)
    attn_partial = jnp.dot(att_low, w_out, preferred_element_type=jnp.float32)
    attn_branch = (
        lax.psum(attn_partial.astype(jnp.bfloat16), "tensor").astype(jnp.float32) + layer_rows[0]
    )
    residual1 = hidden0 + attn_branch
    cot_here = cotangent.astype(jnp.float32)
    normed1, norm1_pull = jax.vjp(layer_norm, residual1, layer_rows[1], layer_rows[2])
    norm_here = normed1.astype(jnp.bfloat16)
    up_pre = (
        jnp.einsum("pd,dje->pje", norm_here, w_up, preferred_element_type=jnp.float32)
        + head_rows[2:]
    )
    gelu_out, gelu_pull = jax.vjp(gelu_exact, up_pre)
    hid_low = gelu_out.astype(jnp.bfloat16)
    down_partial = jnp.einsum("pje,jef->pf", hid_low, w_down, preferred_element_type=jnp.float32)
    mlp_branch = (
        lax.psum(down_partial.astype(jnp.bfloat16), "tensor").astype(jnp.float32) + layer_rows[3]
    )
    result, norm2_pull = jax.vjp(layer_norm, normed1 + mlp_branch, layer_rows[4], layer_rows[5])
    output_here = result.astype(jnp.bfloat16)
    back_r2, back_gain2, back_shift2 = norm2_pull(cot_here)
    part_bdown = jnp.sum(back_r2, axis=0)
    back_r2_here = back_r2.astype(jnp.bfloat16)
    grad_down = jnp.einsum("pje,pf->jef", hid_low, back_r2_here, preferred_element_type=jnp.float32)
    back_hid = jnp.einsum("pf,jef->pje", back_r2_here, w_down, preferred_element_type=jnp.float32)
    (back_up,) = gelu_pull(back_hid)
    grad_bup = jnp.sum(back_up, axis=0)
    back_up_low = back_up.astype(jnp.bfloat16)
    grad_up = jnp.einsum("pd,pje->dje", norm_here, back_up_low, preferred_element_type=jnp.float32)
    back_a_part = jnp.einsum("pje,dje->pd", back_up_low, w_up, preferred_element_type=jnp.float32)
    back_a = lax.psum(back_a_part.astype(jnp.bfloat16), "tensor").astype(jnp.float32) + back_r2
    back_r1, back_gain1, back_shift1 = norm1_pull(back_a)
    grad_bout = jnp.sum(back_r1, axis=0)
    back_r1_low = back_r1.astype(jnp.bfloat16)
    grad_out = jnp.einsum("pe,pf->ef", att_low, back_r1_low, preferred_element_type=jnp.float32)
    back_att = jnp.einsum(
        "pf,ef->pe", back_r1_low, w_out, preferred_element_type=jnp.float32
    ).astype(jnp.bfloat16)

    def head_back(head_index):
        query_h = head_slice(queries, head_index)
        key_h = head_slice(keys_low, head_index)
        value_h = head_slice(values_low, head_index)
        grad_h = head_slice(back_att, head_index)
        lse_h = log_sums[head_index]
        key_grad = jnp.zeros((packed, HD), jnp.float32)
        value_grad = jnp.zeros((packed, HD), jnp.float32)
        query_blocks = []
        for block_index in range(block_count):
            first_row = block_index * block_rows
            query_blk = query_h[first_row : first_row + block_rows]
            raw_scores, same_doc = block_scores(
                query_blk, key_h, seg_row[first_row : first_row + block_rows]
            )
            lse_blk = lse_h[first_row : first_row + block_rows]
            soft_weights = jnp.where(same_doc, jnp.exp(raw_scores - lse_blk[:, None]), 0.0)
            grad_blk = grad_h[first_row : first_row + block_rows]
            value_grad = value_grad + jnp.einsum(
                "qk,qd->kd",
                soft_weights.astype(jnp.bfloat16),
                grad_blk,
                preferred_element_type=jnp.float32,
            )
            weight_grad = jnp.einsum(
                "qd,kd->qk", grad_blk, value_h, preferred_element_type=jnp.float32
            )
            row_inner = jnp.sum(soft_weights * weight_grad, axis=1, keepdims=True)
            score_low = (soft_weights * (weight_grad - row_inner)).astype(jnp.bfloat16)
            query_blocks.append(
                jnp.dot(score_low, key_h, preferred_element_type=jnp.float32) * score_scale
            )
            key_grad = (
                key_grad
                + jnp.einsum("qk,qd->kd", score_low, query_blk, preferred_element_type=jnp.float32)
                * score_scale
            )
        return (jnp.concatenate(query_blocks, axis=0), key_grad, value_grad)

    query_grads, key_grads, value_grads = lax.map(
        head_back, jnp.arange(head_count, dtype=jnp.int32)
    )
    query_grad_all = merge_heads(query_grads)
    key_grad_all = merge_heads(key_grads)
    value_grad_all = merge_heads(value_grads)
    grad_bq = jnp.sum(query_grad_all, axis=0)
    grad_bv = jnp.sum(value_grad_all, axis=0)
    proj_grad_low = jnp.stack([query_grad_all, key_grad_all, value_grad_all], axis=1).astype(
        jnp.bfloat16
    )
    grad_qkv = jnp.einsum(
        "pd,pce->dce", hidden_low, proj_grad_low, preferred_element_type=jnp.float32
    )
    back_h_part = jnp.einsum(
        "pce,dce->pd", proj_grad_low, w_qkv, preferred_element_type=jnp.float32
    )
    back_h0 = lax.psum(back_h_part.astype(jnp.bfloat16), "tensor").astype(jnp.float32) + back_r1
    input_grad = back_h0.astype(jnp.bfloat16)
    back_time = jnp.einsum(
        "ps,pd->sd",
        onehot,
        back_h0,
        precision=lax.Precision.HIGHEST,
        preferred_element_type=jnp.float32,
    )
    grad_bouter = jnp.sum(back_time, axis=0)
    back_time_low = back_time.astype(jnp.bfloat16)
    grad_outer = jnp.einsum("su,sd->ud", act_low, back_time_low, preferred_element_type=jnp.float32)
    back_act = jnp.einsum("sd,ud->su", back_time_low, w_outer, preferred_element_type=jnp.float32)
    (back_inner,) = silu_pull(back_act)
    grad_binner = jnp.sum(back_inner, axis=0)
    grad_inner = jnp.einsum(
        "st,su->tu",
        feature_low,
        back_inner.astype(jnp.bfloat16),
        preferred_element_type=jnp.float32,
    )
    grad_head = jnp.concatenate([grad_bq[None], grad_bv[None], grad_bup], axis=0).reshape(
        6, 1, local_width
    )
    grad_layer = jnp.stack(
        [grad_bout, back_gain1, back_shift1, part_bdown, back_gain2, back_shift2, grad_bouter],
        axis=0,
    )
    red_qkv, red_out, red_up, red_down, red_inner, red_outer, red_binner, red_head, red_layer = (
        lax.psum_scatter(grad_qkv, "dp", scatter_dimension=0, tiled=True),
        lax.psum_scatter(grad_out, "dp", scatter_dimension=1, tiled=True),
        lax.psum_scatter(grad_up, "dp", scatter_dimension=0, tiled=True),
        lax.psum_scatter(grad_down, "dp", scatter_dimension=2, tiled=True),
        lax.psum_scatter(grad_inner, "dp", scatter_dimension=0, tiled=True),
        lax.psum_scatter(grad_outer, "dp", scatter_dimension=0, tiled=True),
        lax.psum_scatter(grad_binner, "dp", scatter_dimension=0, tiled=True),
        lax.psum_scatter(grad_head, "dp", scatter_dimension=2, tiled=True),
        lax.psum_scatter(grad_layer, "dp", scatter_dimension=1, tiled=True),
    )
    split_squares = sum(
        (jnp.sum(piece * piece) for piece in (red_qkv, red_out, red_up, red_down, red_head))
    )
    shared_squares = sum(
        (jnp.sum(piece * piece) for piece in (red_inner, red_outer, red_binner, red_layer))
    )
    local_squares = split_squares + shared_squares / lax.axis_size("tensor")
    norm = jnp.sqrt(lax.psum(local_squares, ("dp", "tensor")))
    factor = 1.0 / jnp.maximum(norm, 1.0)
    step_rate = 4.0 * math.sqrt(MPARAMS / D)
    qkv_master, qkv_velocity, qkv_smoothed = advance(
        qkv_weight, qkv_moment, qkv_average, red_qkv, factor, step_rate
    )
    out_master, out_velocity, out_smoothed = advance(
        out_weight, out_moment, out_average, red_out, factor, step_rate
    )
    up_master, up_velocity, up_smoothed = advance(
        up_weight, up_moment, up_average, red_up, factor, step_rate
    )
    down_master, down_velocity, down_smoothed = advance(
        down_weight, down_moment, down_average, red_down, factor, step_rate
    )
    inner_master, inner_velocity, inner_smoothed = advance(
        time_inner, inner_moment, inner_average, red_inner, factor, step_rate
    )
    outer_master, outer_velocity, outer_smoothed = advance(
        time_outer, outer_moment, outer_average, red_outer, factor, step_rate
    )
    bias_master, bias_velocity, bias_smoothed = advance(
        time_bias, bias_moment, bias_average, red_binner, factor, step_rate
    )
    head_master, head_velocity, head_smoothed = advance(
        head_vectors, head_moment, head_average, red_head, factor, step_rate
    )
    layer_master, layer_velocity, layer_smoothed = advance(
        layer_vectors, layer_moment, layer_average, red_layer, factor, step_rate
    )
    return (
        output_here,
        input_grad,
        norm,
        qkv_master,
        out_master,
        up_master,
        down_master,
        inner_master,
        outer_master,
        bias_master,
        head_master,
        layer_master,
        qkv_velocity,
        out_velocity,
        up_velocity,
        down_velocity,
        inner_velocity,
        outer_velocity,
        bias_velocity,
        head_velocity,
        layer_velocity,
        qkv_smoothed,
        out_smoothed,
        up_smoothed,
        down_smoothed,
        inner_smoothed,
        outer_smoothed,
        bias_smoothed,
        head_smoothed,
        layer_smoothed,
    )


F32=jnp.float32; BF=jnp.bfloat16
MESH=pl.DeviceIdType.MESH
NZ,NX,NC,NT=4,2,2,2
ROWS=48; PIECE=384

def place():
    dp=lax.axis_index("dp"); t=lax.axis_index("tensor")
    z=lax.div(dp,4); x=lax.rem(lax.div(dp,2),2); c=lax.rem(dp,2)
    return z,x,c,t
def dev(z,x,c,t):
    return ((z*NX+x)*NC+c,t)

def peers():
    z,x,c,t=place()
    zp=[dev(lax.rem(z+d,NZ),x,c,t) for d in range(1,NZ)]
    return zp,dev(z,1-x,c,t),dev(z,x,c,1-t),dev(z,x,1-c,t)

def greet():
    zp,xp,yp,sp=peers()
    bar=pltpu.get_barrier_semaphore()
    for d in zp+[xp,yp,sp]:
        pl.semaphore_signal(bar,inc=1,device_id=d,device_id_type=MESH)
    pl.semaphore_wait(bar,6)

def rcopy(src,dst,ssem,rsem,d):
    return pltpu.make_async_remote_copy(src_ref=src,dst_ref=dst,send_sem=ssem,recv_sem=rsem,device_id=d,device_id_type=MESH)

def gather_kernel(chunks,w_ref,g_ref,lsem,zs,zr,xs,xr,ys,yr,ss,sr):
    z,x,c,t=place()
    zp,xp,yp,sp=peers()
    greet()
    n=len(chunks)
    def cols(i): return pl.ds(chunks[i][0],chunks[i][1])
    def ca(i): return pl.ds(chunks[i][0],chunks[i][2])
    def cb(i): return pl.ds(chunks[i][0]+chunks[i][2],chunks[i][1]-chunks[i][2])
    def zcopies(i):
        return [rcopy(w_ref.at[:,cols(i)],g_ref.at[t,z,x,c,:,cols(i)],zs.at[i,d],zr.at[i,d],zp[d]) for d in range(3)]
    def first(i):
        return [rcopy(g_ref.at[t,:,x,c,:,ca(i)],g_ref.at[t,:,x,c,:,ca(i)],xs.at[i,0],xr.at[i,0],xp),
                rcopy(g_ref.at[t,:,x,c,:,cb(i)],g_ref.at[t,:,x,c,:,cb(i)],ys.at[i,0],yr.at[i,0],yp)]
    def second(i):
        return [rcopy(g_ref.at[t,:,:,c,:,ca(i)],g_ref.at[t,:,:,c,:,ca(i)],ys.at[i,1],yr.at[i,1],yp),
                rcopy(g_ref.at[:,:,x,c,:,cb(i)],g_ref.at[:,:,x,c,:,cb(i)],xs.at[i,1],xr.at[i,1],xp)]
    def sib(i):
        return [rcopy(g_ref.at[:,:,:,c,:,cols(i)],g_ref.at[:,:,:,c,:,cols(i)],ss.at[i],sr.at[i],sp)]
    locs=[pltpu.make_async_copy(w_ref.at[:,cols(i)],g_ref.at[t,z,x,c,:,cols(i)],lsem.at[i]) for i in range(n)]
    Z=[zcopies(i) for i in range(n)]; A=[first(i) for i in range(n)]; B=[second(i) for i in range(n)]; S=[sib(i) for i in range(n)]
    for i in range(n):
        locs[i].start()
        for q in Z[i]: q.start()
    for step in range(n+3):
        if step<n:
            locs[step].wait()
            for q in Z[step]: q.wait_recv()
            for q in A[step]: q.start()
        j=step-1
        if 0<=j<n:
            for q in A[j]: q.wait_recv()
            for q in B[j]: q.start()
        j=step-2
        if 0<=j<n:
            for q in B[j]: q.wait_recv()
            for q in S[j]: q.start()
    for i in range(n):
        for q in Z[i]+A[i]+B[i]: q.wait_send()
        for q in S[i]: q.wait()

def gather(w,chunks,space=pl.ANY,cid=0):
    n=len(chunks); DMA=pltpu.SemaphoreType.DMA
    width=w.shape[1]
    return pl.pallas_call(functools.partial(gather_kernel,chunks),
        in_specs=[pl.BlockSpec(memory_space=space)],out_specs=pl.BlockSpec(memory_space=space),
        out_shape=jax.ShapeDtypeStruct((NT,NZ,NX,NC,ROWS,width),BF),
        scratch_shapes=[DMA((n,)),DMA((n,3)),DMA((n,3)),DMA((n,2)),DMA((n,2)),DMA((n,2)),DMA((n,2)),DMA((n,)),DMA((n,))],
        compiler_params=pltpu.CompilerParams(collective_id=cid,has_side_effects=True,vmem_limit_bytes=60*2**20),name="gather")(w)

def scatter_kernel(chunks,g_hbm,o_ref,g,rs,ra,rc,rb,rz,lsem,ss,sr,as_,ar,bs,br,zs,zr):
    z,x,c,t=place()
    zp,xp,yp,sp=peers()
    n=len(chunks)
    def cols(i): return pl.ds(chunks[i][0],chunks[i][1])
    def ca(i): return pl.ds(chunks[i][0],chunks[i][2])
    def cb(i): return pl.ds(chunks[i][0]+chunks[i][2],chunks[i][1]-chunks[i][2])
    L=[pltpu.make_async_copy(g_hbm.at[:,:,:,:,:,cols(i)],g.at[:,:,:,:,:,cols(i)],lsem.at[i]) for i in range(n)]
    for q in L: q.start()
    greet()
    S=[[rcopy(g.at[:,:,:,1-c,:,cols(i)],rs.at[:,:,:,:,cols(i)],ss.at[i],sr.at[i],sp)] for i in range(n)]
    A=[[rcopy(g.at[:,:,1-x,c,:,ca(i)],ra.at[:,:,:,ca(i)],as_.at[i,0],ar.at[i,0],xp),
        rcopy(g.at[1-t,:,:,c,:,cb(i)],rc.at[:,:,:,cb(i)],as_.at[i,1],ar.at[i,1],yp)] for i in range(n)]
    B=[[rcopy(g.at[1-t,:,x,c,:,ca(i)],rb.at[:,:,ca(i)],bs.at[i,0],br.at[i,0],yp),
        rcopy(g.at[t,:,1-x,c,:,cb(i)],rb.at[:,:,cb(i)],bs.at[i,1],br.at[i,1],xp)] for i in range(n)]
    Zc=[[rcopy(g.at[t,lax.rem(z+d+1,NZ),x,c,:,cols(i)],rz.at[d,:,cols(i)],zs.at[i,d],zr.at[i,d],zp[d]) for d in range(3)] for i in range(n)]
    def addS(i):
        def body(k,_):
            tt=lax.div(k,8); zz=lax.rem(lax.div(k,2),4); xx=lax.rem(k,2)
            g[tt,zz,xx,c,:,cols(i)]=(g[tt,zz,xx,c,:,cols(i)].astype(F32)+rs[tt,zz,xx,:,cols(i)].astype(F32)).astype(BF)
            return 0
        lax.fori_loop(0,16,body,0)
    def addA(i):
        def body(k,_):
            a=lax.div(k,4); b=lax.rem(k,4)
            g[a,b,x,c,:,ca(i)]=(g[a,b,x,c,:,ca(i)].astype(F32)+ra[a,b,:,ca(i)].astype(F32)).astype(BF)
            zz=lax.div(k,2); xx=lax.rem(k,2)
            g[t,zz,xx,c,:,cb(i)]=(g[t,zz,xx,c,:,cb(i)].astype(F32)+rc[zz,xx,:,cb(i)].astype(F32)).astype(BF)
            return 0
        lax.fori_loop(0,8,body,0)
    def addB(i):
        def body(k,_):
            g[t,k,x,c,:,cols(i)]=(g[t,k,x,c,:,cols(i)].astype(F32)+rb[k,:,cols(i)].astype(F32)).astype(BF)
            return 0
        lax.fori_loop(0,4,body,0)
    def addZ(i):
        acc=g[t,z,x,c,:,cols(i)].astype(F32)
        for d in range(3): acc=acc+rz[d,:,cols(i)].astype(F32)
        o_ref[:,cols(i)]=acc
    for step in range(n+4):
        if step<n:
            L[step].wait()
            for q in S[step]: q.start()
        j=step-1
        if 0<=j<n:
            for q in S[j]: q.wait_recv()
            addS(j)
            for q in A[j]: q.start()
        j=step-2
        if 0<=j<n:
            for q in A[j]: q.wait_recv()
            addA(j)
            for q in B[j]: q.start()
        j=step-3
        if 0<=j<n:
            for q in B[j]: q.wait_recv()
            addB(j)
            for q in Zc[j]: q.start()
        j=step-4
        if 0<=j<n:
            for q in Zc[j]: q.wait_recv()
            addZ(j)
    for i in range(n):
        for q in S[i]+A[i]+B[i]+Zc[i]: q.wait_send()

def scatter(g,chunks,cid=1):
    n=len(chunks); DMA=pltpu.SemaphoreType.DMA
    W=g.shape[-1]; V=lambda *s:pltpu.VMEM(s+(ROWS,W),BF)
    return pl.pallas_call(functools.partial(scatter_kernel,chunks),
        in_specs=[pl.BlockSpec(memory_space=pl.ANY)],out_specs=pl.BlockSpec(memory_space=pltpu.VMEM),
        out_shape=jax.ShapeDtypeStruct((ROWS,W),F32),
        scratch_shapes=[V(NT,NZ,NX,NC),V(NT,NZ,NX),V(NT,NZ),V(NZ,NX),V(NZ),V(3),
          DMA((n,)),DMA((n,)),DMA((n,)),DMA((n,2)),DMA((n,2)),DMA((n,2)),DMA((n,2)),DMA((n,3)),DMA((n,3))],
        compiler_params=pltpu.CompilerParams(collective_id=cid,has_side_effects=True,vmem_limit_bytes=62*2**20),name="scatter")(g)
def mkchunks(ws):
    out=[];s=0
    for w in ws:
        w*=128
        out.append((s,w,(w//256)*128)); s+=w
    return out

CHUNKS=mkchunks([6,6,9,6,6,6])
L=1024
def dot(a,b,ca,cb):
    return lax.dot_general(a,b,(((ca,),(cb,)),((),())),preferred_element_type=F32)
def fwdT(bk, q_ref,k_ref,v_ref,bias_ref,o_ref,lse_ref):
    lane=lax.broadcasted_iota(jnp.int32,(1,128),1)
    qp=q_ref[...]; kp=k_ref[...]; vp=v_ref[...]
    bias=bias_ref[...]
    vT=vp.T
    outs=[]
    for h in range(2):
        sel=(lane//64)==h
        one=lane==(64*(1-h))
        kh=jnp.where(sel,kp,jnp.where(one,bias.astype(BF),jnp.zeros_like(kp)))
        qh=jnp.where(sel,qp*0.125,jnp.where(one,jnp.ones_like(qp),jnp.zeros_like(qp)))
        oT=[]
        for qi in range(L//bk):
            sT=dot(kh,qh[qi*bk:(qi+1)*bk],1,1)
            m=jnp.max(sT,axis=0,keepdims=True)
            e=jnp.exp(sT-m)
            l=jnp.sum(e,axis=0,keepdims=True)
            p=(e*(1.0/l)).astype(BF)
            oT.append(dot(vT[h*64:(h+1)*64],p,1,0))
            lse_ref[0,h:h+1,qi*bk:(qi+1)*bk]=m+jnp.log(l)
        outs.append(jnp.concatenate(oT,axis=1))
    oT=jnp.concatenate(outs,axis=0)
    o_ref[...]=oT.T.astype(BF)

def call_fwd(body,b,q,k,v,bias):
    return pl.pallas_call(functools.partial(body,b),grid=(6,),
      in_specs=[pl.BlockSpec((L,128),lambda i:(0,i))]*3+[pl.BlockSpec((L,1),lambda i:(0,0))],
      out_specs=[pl.BlockSpec((L,128),lambda i:(0,i)),pl.BlockSpec((1,2,L),lambda i:(i,0,0))],
      out_shape=[jax.ShapeDtypeStruct((L,768),BF),jax.ShapeDtypeStruct((6,2,L),F32)],
      compiler_params=pltpu.CompilerParams(vmem_limit_bytes=60*2**20),name=f"{body.__name__}_{b}")(q,k,v,bias)

def bwdT(bq, q_ref,k_ref,v_ref,do_ref,bias_ref,lse_ref,dq_ref,dk_ref,dv_ref):
    lane=lax.broadcasted_iota(jnp.int32,(1,128),1)
    kp=k_ref[...]; vp=v_ref[...]
    bias=bias_ref[...]
    khs=[];vhs=[];kts=[]
    for h in range(2):
        sel=(lane//64)==h
        one=lane==(64*(1-h))
        khs.append(jnp.where(sel,kp,jnp.where(one,bias.astype(BF),jnp.zeros_like(kp))))
        vhs.append(jnp.where(sel,vp,jnp.zeros_like(vp)))
    kT=kp.T
    dk=[None,None];dv=[None,None]
    for qi in range(L//bq):
        rows=pl.ds(qi*bq,bq)
        qp=q_ref[rows,:]; dop=do_ref[rows,:]
        dqT=[]
        for h in range(2):
            sel=(lane//64)==h
            one=lane==(64*(1-h))
            qh=jnp.where(sel,qp*0.125,jnp.where(one,jnp.ones_like(qp),jnp.zeros_like(qp)))
            doh=jnp.where(sel,dop,jnp.zeros_like(dop))
            qz=jnp.where(sel,qp*0.125,jnp.zeros_like(qp))
            sT=dot(khs[h],qh,1,1)
            p=jnp.exp(sT-lse_ref[0,h:h+1,qi*bq:(qi+1)*bq])
            dp=dot(vhs[h],doh,1,1)
            d=jnp.sum(p*dp,axis=0,keepdims=True)
            ds=(p*(dp-d)).astype(BF)
            pb=p.astype(BF)
            a=dot(pb,doh,1,0); dv[h]=a if dv[h] is None else dv[h]+a
            a=dot(ds,qz,1,0); dk[h]=a if dk[h] is None else dk[h]+a
            dqT.append(dot(kT[h*64:(h+1)*64],ds,1,0))
        dq_ref[rows,:]=(jnp.concatenate(dqT,axis=0).T*0.125)
    dk_ref[...]=dk[0]+dk[1]
    dv_ref[...]=dv[0]+dv[1]

def call_bwd(body,b,q,k,v,do,bias,lse):
    return pl.pallas_call(functools.partial(body,b),grid=(6,),
      in_specs=[pl.BlockSpec((L,128),lambda i:(0,i))]*4+[pl.BlockSpec((L,1),lambda i:(0,0)),pl.BlockSpec((1,2,L),lambda i:(i,0,0))],
      out_specs=[pl.BlockSpec((L,128),lambda i:(0,i))]*3,
      out_shape=[jax.ShapeDtypeStruct((L,768),F32)]*3,
      compiler_params=pltpu.CompilerParams(vmem_limit_bytes=60*2**20),name=f"{body.__name__}_{b}")(q,k,v,do,bias,lse)


def ln_stats(v):
    mean=jnp.mean(v,axis=-1,keepdims=True)
    cen=v-mean
    inv=lax.rsqrt(jnp.mean(cen*cen,axis=-1,keepdims=True)+EPSILON)
    return cen*inv,inv

def ln_back(gain,dy,xhat,inv):
    gd=gain*dy
    return (gd-jnp.mean(gd,axis=-1,keepdims=True)-xhat*jnp.mean(gd*xhat,axis=-1,keepdims=True))*inv

def phi_cdf(u):
    return 0.5*(1.0+lax.erf(u*(1.0/math.sqrt(2.0))))

def pack_weights(qkv,out,up,down,w1,w2,b1,hv,lv):
    t=lax.axis_index("tensor")
    low=lambda a:a.astype(BF)
    w2h=lax.dynamic_slice_in_dim(low(w2),t*PIECE,PIECE,1)
    w1h=lax.dynamic_slice_in_dim(jnp.pad(low(w1),((0,8),(0,0))),t*256,256,1)
    lanes=lambda a:jnp.pad(low(a),((0,0),(0,128-a.shape[1])))
    vec=jnp.concatenate([lanes(lv),lanes(hv[:,0]),lanes(b1[None]),jnp.zeros((2,128),BF)],axis=0)
    aux=jnp.concatenate([w2h,jnp.concatenate([w1h,vec],axis=1)],axis=0)
    return jnp.concatenate([aux,low(qkv).reshape(ROWS,3*PIECE),low(out).T,low(up).reshape(ROWS,4*PIECE),low(down).transpose(2,0,1).reshape(ROWS,4*PIECE)],axis=1)

WIDE=13*PIECE
RB=256
def spread(blocks,w,tiles):
    lane=lax.broadcasted_iota(jnp.int32,(16,128),1)
    acc=[jnp.zeros((16,128),F32) for _ in range(tiles+1)]
    for n,b in enumerate(blocks):
        tile,s=divmod(n*w,128)
        wide=jnp.concatenate([jnp.where(lane<w,b,0.0),jnp.zeros((16,128),F32)],axis=1)
        if s: wide=pltpu.roll(wide,s,1)
        acc[tile]=acc[tile]+wide[:,:128]
        acc[tile+1]=acc[tile+1]+wide[:,128:]
    return jnp.concatenate(acc[:tiles],axis=1)

def attend_pair(q_ref,k_ref,v_ref,o_ref,lse_ref,bias_ref,i,bq=512):
    lane=lax.broadcasted_iota(jnp.int32,(1,128),1)
    cs=pl.ds(pl.multiple_of(i*128,128),128)
    kp=k_ref[:,cs]; vT=v_ref[:,cs].T
    bias=bias_ref[...]
    khs=[]
    for h in range(2):
        khs.append(jnp.where((lane//64)==h,kp,jnp.where(lane==(64*(1-h)),bias,jnp.zeros_like(kp))))
    for qi in range(L//bq):
        qp=q_ref[pl.ds(qi*bq,bq),cs]*0.125
        oT=[]
        for h in range(2):
            qh=jnp.where((lane//64)==h,qp,jnp.where(lane==(64*(1-h)),jnp.ones_like(qp),jnp.zeros_like(qp)))
            sT=dot(khs[h],qh,1,1)
            m=jnp.max(sT,axis=0,keepdims=True)
            e=jnp.exp(sT-m)
            l=jnp.sum(e,axis=0,keepdims=True)
            p=(e*(1.0/l)).astype(BF)
            oT.append(dot(vT[h*64:(h+1)*64],p,1,0))
            lse_ref[i,h:h+1,qi*bq:(qi+1)*bq]=m+jnp.log(l)
        o_ref[pl.ds(qi*bq,bq),cs]=jnp.concatenate(oT,axis=0).T.astype(BF)

GCH=[(k*2*PIECE,2*PIECE,PIECE) for k in range(6)]+[(12*PIECE,PIECE,128)]

def gather_steps(w_ref,g,zs,zr,fs,fr,ss,sr):
    z,x,c,t=place(); zp,xp,yp,sp=peers(); n=len(GCH)
    def cols(i): return pl.ds(GCH[i][0],GCH[i][1])
    def ca(i): return pl.ds(GCH[i][0],GCH[i][2])
    def cb(i): return pl.ds(GCH[i][0]+GCH[i][2],GCH[i][1]-GCH[i][2])
    same=lambda r,s,q,d:rcopy(r,r,s,q,d)
    Z=lambda i:[rcopy(w_ref.at[:,cols(i)],g.at[t,z,x,c,:,cols(i)],zs.at[i,d],zr.at[i,d],zp[d]) for d in range(3)]
    A=lambda i:[same(g.at[t,:,x,c,:,ca(i)],fs.at[i,0],fr.at[i,0],xp),same(g.at[t,:,x,c,:,cb(i)],fs.at[i,1],fr.at[i,1],yp)]
    B=lambda i:[same(g.at[t,:,:,c,:,ca(i)],fs.at[i,2],fr.at[i,2],yp),same(g.at[:,:,x,c,:,cb(i)],fs.at[i,3],fr.at[i,3],xp)]
    S=lambda i:[same(g.at[:,:,:,c,:,cols(i)],ss.at[i],sr.at[i],sp)]
    def begin():
        for i in range(n):
            g[t,z,x,c,:,cols(i)]=w_ref[:,cols(i)]
        for i in range(n):
            for q in Z(i): q.start()
    def step(k):
        if k<n:
            for q in Z(k): q.wait_recv()
            for q in A(k): q.start()
        if 0<=k-1<n:
            for q in A(k-1): q.wait_recv()
            for q in B(k-1): q.start()
        if 0<=k-2<n:
            for q in B(k-2): q.wait_recv()
            for q in S(k-2): q.start()
        if 0<=k-3<n:
            for q in S(k-3): q.wait_recv()
    def finish():
        for i in range(n):
            for q in Z(i)+A(i)+B(i)+S(i): q.wait_send()
    return begin,step,finish

def front_kernel(w_ref,tok_hbm,cot_hbm,seg_ref,feat_ref,
        q_o,k_o,v_o,o_o,lse_o,out_o,dmbT_o,abT_o,drbT_o,hid_o,dub_o,dr1_o,dob_o,hbT_o,wqkv_o,aux_o,sums_o,bup_o,time_o,
        g,tok,cot,q,k,v,o,lse,own,bias,vecs,temb,hbT,gp,hid,dub,dmbT,abT,drbT,dr1,
        zs,zr,fs,fr,ss,sr,lsem,osem,hsem):
    z,x,c,t=place()
    begin,step,finish=gather_steps(w_ref,g,zs,zr,fs,fr,ss,sr)
    win=pl.ds(pl.multiple_of(t*512,512),L)
    ltok=pltpu.make_async_copy(tok_hbm.at[win,:],tok,lsem.at[0]); ltok.start()
    lcot=pltpu.make_async_copy(cot_hbm.at[win,:],cot,lsem.at[1]); lcot.start()
    greet()
    begin()
    seg=seg_ref[:,pl.ds(pl.multiple_of(t*512,128),L)]
    own_row=jnp.where(seg==t,1.0,0.0)
    ownT=jnp.broadcast_to(own_row,(128,L)).T
    own[...]=ownT
    bias[...]=jnp.where(ownT>0.5,0.0,-1e30).astype(BF)
    for s in range(4): step(s)
    def vecblk(tt,n): return g[tt,n//4,(n//2)%2,n%2,32:48,256:384].astype(F32)
    b0=[vecblk(0,n) for n in range(16)]; b1=[vecblk(1,n) for n in range(16)]
    lv=spread(b0,48,6)
    hv=jnp.concatenate([spread(b0,24,3),spread(b1,24,3)],axis=1)
    vecs[0:16,:]=lv
    vecs[16:32,:]=hv
    bin_=spread(b0,32,4)[13:14,:]
    inner=bin_
    w1=jnp.concatenate([g[0,:,:,:,32:48,0:256].reshape(256,256),g[1,:,:,:,32:48,0:256].reshape(256,256)],axis=1)
    inner=dot(feat_ref[...],w1,1,0)[0:1]+bin_
    sig=1.0/(1.0+jnp.exp(-inner))
    act=inner*sig
    w2=jnp.concatenate([g[0,:,:,:,0:32,0:384].reshape(512,384),g[1,:,:,:,0:32,0:384].reshape(512,384)],axis=1)
    actb=jnp.broadcast_to(act,(16,512)).astype(BF)
    te=dot(actb,w2,1,0)[0:1]+lv[6:7]
    temb[...]=jnp.broadcast_to(te,(8,D))
    time_o[...]=jnp.concatenate([inner,sig,jnp.zeros((6,512),F32)],axis=0)
    ltok.wait()
    outs=[]
    def emit(src,dst):
        cp=pltpu.make_async_copy(src,dst,osem.at[len(outs)]); cp.start(); outs.append(cp)
    def hid_rows(r,_):
        rows=pl.ds(pl.multiple_of(r*RB,RB),RB)
        hb=(tok[rows,:].astype(F32)+temb[0:1,:]).astype(BF)
        hbT[:,rows]=hb.T
        return 0
    lax.fori_loop(0,L//RB,hid_rows,0)
    def project(which,ref,brow):
        def rows_body(r,_):
            rows=pl.ds(pl.multiple_of(r*RB,RB),RB)
            hb=(tok[rows,:].astype(F32)+temb[0:1,:]).astype(BF)
            for tt in range(2):
                val=dot(hb,g[tt,:,:,:,:,(1+which)*PIECE:(2+which)*PIECE].reshape(D,PIECE),1,0)
                if brow is not None: val=val+vecs[brow:brow+1,tt*PIECE:(tt+1)*PIECE]
                ref[rows,tt*PIECE:(tt+1)*PIECE]=val.astype(BF)
            return 0
        lax.fori_loop(0,L//RB,rows_body,0)
    project(0,q,16+7)
    emit(hbT,hbT_o); emit(q,q_o)
    step(4)
    project(1,k,None); project(2,v,16+8)
    emit(k,k_o); emit(v,v_o)
    emit(g.at[:,:,:,:,:,0:PIECE],aux_o); emit(g.at[:,:,:,:,:,PIECE:4*PIECE],wqkv_o)
    def pair(i,_):
        attend_pair(q,k,v,o,lse,bias,i)
        for s in range(5):
            @pl.when(i==s)
            def _(): step(5+s)
        return 0
    lax.fori_loop(0,6,pair,0)
    emit(o,o_o); emit(lse,lse_o)
    lcot.wait()
    for cp in outs: cp.wait()
    done=len(outs)
    out,dob=q,k
    mid_body(g,tok,cot,o,own,vecs,temb,gp,hid,dub,out,dmbT,abT,drbT,dr1,dob,sums_o,bup_o,hid_o,dub_o,hsem)
    for a,b in ((out,out_o),(dmbT,dmbT_o),(abT,abT_o),(drbT,drbT_o),(dr1,dr1_o),(dob,dob_o)): emit(a,b)
    for cp in outs[done:]: cp.wait()
    finish()

def mid_body(g,tok,cot,o,own,vecs,temb,gp,hid,dub,out,dmbT,abT,drbT,dr1,dob,sums_o,bup_o,hid_o,dub_o,hsem):
    def W(tt,piece,n=1): return g[tt,:,:,:,:,piece*PIECE:(piece+n)*PIECE].reshape(D,n*PIECE)
    row=lambda r:vecs[r:r+1,:]
    sums_o[...]=jnp.zeros((8,D),F32); bup_o[...]=jnp.zeros((8,4*D),F32)
    csum=lambda a:jnp.sum(a,axis=0,keepdims=True)
    def stage(buf,dst,r,which):
        return pltpu.make_async_copy(buf.at[lax.rem(r,2)],dst.at[pl.ds(pl.multiple_of(r*RB,RB),RB),:],hsem.at[which,lax.rem(r,2)])
    def block(r,_):
        rows=pl.ds(pl.multiple_of(r*RB,RB),RB)
        slot=lax.rem(r,2)
        @pl.when(r>=2)
        def _():
            stage(hid,hid_o,r-2,0).wait(); stage(dub,dub_o,r-2,1).wait()
        attn=dot(o[rows,0:PIECE],W(0,4),1,1)+dot(o[rows,PIECE:D],W(1,4),1,1)
        r1=(tok[rows,:].astype(F32)+temb[0:1,:])+(attn+row(0))
        x1,inv1=ln_stats(r1)
        a=x1*row(1)+row(2)
        ab=a.astype(BF)
        abT[:,rows]=ab.T
        mlp=row(3)
        for tt in range(2):
            for j in range(4):
                cc=pl.ds((tt*4+j)*PIECE,PIECE)
                u=dot(ab,W(tt,5+j),1,0)+vecs[16+9+j:16+10+j,tt*PIECE:(tt+1)*PIECE]
                cdf=phi_cdf(u)
                gp[:,cc]=cdf+u*jnp.exp(-0.5*u*u)*(1.0/math.sqrt(2*math.pi))
                hid[slot,:,cc]=(u*cdf).astype(BF)
            mlp=mlp+dot(hid[slot,:,tt*4*PIECE:(tt+1)*4*PIECE],W(tt,9,4),1,1)
        stage(hid,hid_o,r,0).start()
        x2,inv2=ln_stats(a+mlp)
        out[rows,:]=(x2*row(4)+row(5)).astype(BF)
        dy=jnp.where(own[rows,0:1]>0.5,cot[rows,:].astype(F32),0.0)
        sums_o[4:5,:]+=csum(dy*x2); sums_o[5:6,:]+=csum(dy)
        dr2=ln_back(row(4),dy,x2,inv2)
        sums_o[3:4,:]+=csum(dr2)
        dmb=dr2.astype(BF)
        dmbT[:,rows]=dmb.T
        da=dr2
        for tt in range(2):
            for j in range(4):
                cc=pl.ds((tt*4+j)*PIECE,PIECE)
                du=dot(dmb,W(tt,9+j),1,0)*gp[:,cc]
                bup_o[0:1,cc]+=csum(du)
                dub[slot,:,cc]=du.astype(BF)
            da=da+dot(dub[slot,:,tt*4*PIECE:(tt+1)*4*PIECE],W(tt,5,4),1,1)
        stage(dub,dub_o,r,1).start()
        sums_o[1:2,:]+=csum(da*x1); sums_o[2:3,:]+=csum(da)
        d1=ln_back(row(1),da,x1,inv1)
        sums_o[0:1,:]+=csum(d1)
        dr1[rows,:]=d1
        drb=d1.astype(BF)
        drbT[:,rows]=drb.T
        for tt in range(2):
            dob[rows,tt*PIECE:(tt+1)*PIECE]=dot(drb,W(tt,4),1,0).astype(BF)
        return 0
    lax.fori_loop(0,L//RB,block,0)
    for r in (L//RB-2,L//RB-1):
        stage(hid,hid_o,r,0).wait(); stage(dub,dub_o,r,1).wait()

def front(w,tokens,cotangent,seg,featp,cid=0):
    DMA=pltpu.SemaphoreType.DMA; n=len(GCH)
    V=lambda s,d=BF:pltpu.VMEM(s,d)
    A=pl.BlockSpec(memory_space=pl.ANY); M=pl.BlockSpec(memory_space=pltpu.VMEM)
    big=lambda s,d=BF:jax.ShapeDtypeStruct(s,d)
    row=(L,D); tr=(D,L)
    G6=lambda w_:(NT,NZ,NX,NC,ROWS,w_)
    return pl.pallas_call(front_kernel,
        in_specs=[M,A,A,M,M],
        out_specs=[A]*16+[M]*3,
        out_shape=[big(row),big(row),big(row),big(row),big((6,2,L),F32),big(row),big(tr),big(tr),big(tr),big((L,4*D)),big((L,4*D)),
            big(row,F32),big(row),big(tr),big(G6(3*PIECE)),big(G6(PIECE)),big((8,D),F32),big((8,4*D),F32),big((8,512),F32)],
        scratch_shapes=[V(G6(WIDE)),V(row),V(row),V(row),V(row),V(row),V(row),V((6,2,L),F32),V((L,128),F32),V((L,128)),V((32,D),F32),V((8,D),F32),
            V(tr),V((RB,4*D),F32),V((2,RB,4*D)),V((2,RB,4*D)),V(tr),V(tr),V(tr),V(row,F32),
            DMA((n,3)),DMA((n,3)),DMA((n,4)),DMA((n,4)),DMA((n,)),DMA((n,)),DMA((2,)),DMA((20,)),DMA((2,2))],
        compiler_params=pltpu.CompilerParams(collective_id=cid,has_side_effects=True,vmem_limit_bytes=63*2**20),name="front")(w,tokens,cotangent,seg,featp)

RGR=[dict(g=0,r=0,w=768,a=384),dict(g=768,r=768,w=768,a=384),dict(g=1536,r=1536,w=768,a=384),dict(g=2304,r=2304,w=768,a=384),
     dict(g=3072,r=3072,w=384,a=128),dict(g=0,r=3456,w=768,a=384),dict(g=768,r=4224,w=768,a=384)]
_a=_b=0
for _q in RGR:
    _q["ao"]=_a; _q["bo"]=_b; _a+=_q["a"]; _b+=_q["w"]-_q["a"]
RWA,RWB=_a,_b

def scatter_steps(gb,rs,ra,rc,rb,rz,red,ss,sr,as_,ar,bs,br,zs,zr):
    z,x,c,t=place(); zp,xp,yp,sp=peers()
    def sl(i):
        q=RGR[i]; g,r,w,a,ao,bo=q["g"],q["r"],q["w"],q["a"],q["ao"],q["bo"]
        return dict(g=pl.ds(g,w),ga=pl.ds(g,a),gb=pl.ds(g+a,w-a),r=pl.ds(r,w),ra=pl.ds(r,a),rb=pl.ds(r+a,w-a),a=pl.ds(ao,a),b=pl.ds(bo,w-a))
    def S(i):
        k=sl(i); return [rcopy(gb.at[:,:,:,1-c,:,k["g"]],rs.at[:,:,:,:,k["r"]],ss.at[i],sr.at[i],sp)]
    def A(i):
        k=sl(i); return [rcopy(gb.at[:,:,1-x,c,:,k["ga"]],ra.at[:,:,:,k["a"]],as_.at[i,0],ar.at[i,0],xp),
                         rcopy(gb.at[1-t,:,:,c,:,k["gb"]],rc.at[:,:,:,k["b"]],as_.at[i,1],ar.at[i,1],yp)]
    def B(i):
        k=sl(i); return [rcopy(gb.at[1-t,:,x,c,:,k["ga"]],rb.at[:,:,k["ra"]],bs.at[i,0],br.at[i,0],yp),
                         rcopy(gb.at[t,:,1-x,c,:,k["gb"]],rb.at[:,:,k["rb"]],bs.at[i,1],br.at[i,1],xp)]
    def Z(i):
        k=sl(i); return [rcopy(gb.at[t,lax.rem(z+d+1,NZ),x,c,:,k["g"]],rz.at[d,:,k["r"]],zs.at[i,d],zr.at[i,d],zp[d]) for d in range(3)]
    def go(cs):
        for q in cs: q.start()
    def got(cs):
        for q in cs: q.wait_recv()
    def sums(a,b): return (a.astype(F32)+b.astype(F32)).astype(BF)
    def s_to_a(i):
        got(S(i)); k=sl(i)
        def body(n,_):
            tt=lax.div(n,8); zz=lax.rem(lax.div(n,2),4); xx=lax.rem(n,2)
            gb[tt,zz,xx,c,:,k["g"]]=sums(gb[tt,zz,xx,c,:,k["g"]],rs[tt,zz,xx,:,k["r"]])
            return 0
        lax.fori_loop(0,16,body,0)
        go(A(i))
    def a_to_b(i):
        got(A(i)); k=sl(i)
        def body(n,_):
            a=lax.div(n,4); b=lax.rem(n,4)
            gb[a,b,x,c,:,k["ga"]]=sums(gb[a,b,x,c,:,k["ga"]],ra[a,b,:,k["a"]])
            zz=lax.div(n,2); xx=lax.rem(n,2)
            gb[t,zz,xx,c,:,k["gb"]]=sums(gb[t,zz,xx,c,:,k["gb"]],rc[zz,xx,:,k["b"]])
            return 0
        lax.fori_loop(0,8,body,0)
        go(B(i))
    def b_to_z(i):
        got(B(i)); k=sl(i)
        def body(n,_):
            gb[t,n,x,c,:,k["g"]]=sums(gb[t,n,x,c,:,k["g"]],rb[n,:,k["r"]])
            return 0
        lax.fori_loop(0,4,body,0)
        go(Z(i))
    def z_end(i):
        got(Z(i)); k=sl(i)
        acc=gb[t,z,x,c,:,k["g"]].astype(F32)
        for d in range(3): acc=acc+rz[d,:,k["r"]].astype(F32)
        red[:,k["r"]]=acc
    def drain(i):
        for q in S(i)+A(i)+B(i)+Z(i): q.wait_send()
    return S,go,s_to_a,a_to_b,b_to_z,z_end,drain

def attend_back(q_ref,k_ref,v_ref,do_ref,lse_ref,bias_ref,hvs,i,bq=512):
    lane=lax.broadcasted_iota(jnp.int32,(1,128),1)
    cs=pl.ds(pl.multiple_of(i*128,128),128)
    kp=k_ref[:,cs]; vp=v_ref[:,cs]; bias=bias_ref[...]
    khs=[];vhs=[]
    for h in range(2):
        sel=(lane//64)==h; one=lane==(64*(1-h))
        khs.append(jnp.where(sel,kp,jnp.where(one,bias,jnp.zeros_like(kp))))
        vhs.append(jnp.where(sel,vp,jnp.zeros_like(vp)))
    kT=kp.T
    dk=[None,None];dv=[None,None]; sq=None
    for qi in range(L//bq):
        rows=pl.ds(qi*bq,bq)
        qp=q_ref[rows,cs]*0.125; dop=do_ref[rows,cs]
        dqT=[]
        for h in range(2):
            sel=(lane//64)==h; one=lane==(64*(1-h))
            zero=jnp.zeros_like(qp)
            qh=jnp.where(sel,qp,jnp.where(one,jnp.ones_like(qp),zero))
            doh=jnp.where(sel,dop,zero)
            qz=jnp.where(sel,qp,zero)
            sT=dot(khs[h],qh,1,1)
            p=jnp.exp(sT-lse_ref[i,h:h+1,qi*bq:(qi+1)*bq])
            dp=dot(vhs[h],doh,1,1)
            d=jnp.sum(p*dp,axis=0,keepdims=True)
            ds=(p*(dp-d)).astype(BF)
            pb=p.astype(BF)
            a=dot(pb,doh,1,0); dv[h]=a if dv[h] is None else dv[h]+a
            a=dot(ds,qz,1,0); dk[h]=a if dk[h] is None else dk[h]+a
            dqT.append(dot(kT[h*64:(h+1)*64],ds,1,0))
        dq=jnp.concatenate(dqT,axis=0).T*0.125
        s=jnp.sum(dq,axis=0,keepdims=True); sq=s if sq is None else sq+s
        q_ref[rows,cs]=dq.astype(BF)
    k_ref[:,cs]=(dk[0]+dk[1]).astype(BF)
    dvv=dv[0]+dv[1]
    v_ref[:,cs]=dvv.astype(BF)
    hvs[0:1,cs]=sq
    hvs[1:2,cs]=jnp.sum(dvv,axis=0,keepdims=True)

def unspread(src,w,n):
    lane=lax.broadcasted_iota(jnp.int32,(16,128),1)
    tile,s=divmod(n*w,128)
    wide=src[:,tile*128:(tile+2)*128]
    if s: wide=pltpu.roll(wide,256-s,1)
    return jnp.where(lane<w,wide[:,:128],0.0)

def back_kernel(q_h,k_h,v_h,do_h,o_h,lse_h,dmbT_h,abT_h,drbT_h,hbT_h,hid_h,dub_h,dr1_h,wqkv_h,aux_h,out_h,seg_ref,feat_ref,sums_ref,bup_ref,time_ref,
        in_o,inp_o,outp_o,red,auxp,tot,
        q,k,v,do,lse,bias,st,ta,tb,wq,dr1,aux,inw,hvs,lvs,hsrc,bsrc,auxm,nv,nr,nz,
        gb,rs,ra,rc,rb,rz,ss,sr,as_,ar,bs,br,zs,zr,ls,ts,xs,ns,nrs):
    z,x,c,t=place(); zp,xp,yp,sp=peers()
    S,go,s_to_a,a_to_b,b_to_z,z_end,drain=scatter_steps(gb,rs,ra,rc,rb,rz,red,ss,sr,as_,ar,bs,br,zs,zr)
    def load(src,dst,n):
        return pltpu.make_async_copy(src,dst,ls.at[n])
    LQ=[load(q_h,q,0),load(k_h,k,1),load(v_h,v,2),load(do_h,do,3),load(lse_h,lse,4)]
    LW=[load(wqkv_h,wq,5),load(dr1_h,dr1,6),load(aux_h,aux,7)]
    def tcopy(src,buf,n): return pltpu.make_async_copy(src,buf,ts.at[n])
    def stage(src,cols,n):
        return [pltpu.make_async_copy(src.at[:,pl.ds(cs,PIECE)],st.at[s],ts.at[n+s]) for s,cs in enumerate(cols)]
    pc=lambda j:[tt*4*PIECE+jj*PIECE for jj in (j,j+1) for tt in range(2)]
    ST=[stage(hid_h,pc(0),4),stage(hid_h,pc(2),8),stage(dub_h,pc(0),4),stage(dub_h,pc(2),8),stage(o_h,[0,PIECE],4)]
    for q_ in [tcopy(dmbT_h,ta,0),*ST[0],tcopy(abT_h,tb,1)]+LQ+LW: q_.start()
    greet()
    cout=rcopy(out_h,outp_o,xs.at[0],xs.at[1],yp); cout.start()
    seg=seg_ref[:,pl.ds(pl.multiple_of(t*512,128),L)]
    bias[...]=jnp.broadcast_to(jnp.where(seg==t,0.0,-1e30),(128,L)).T.astype(BF)
    def compute(i,lhs,n):
        base=RGR[i]["g"]
        for q_ in ST[i]: q_.wait()
        def body(s,_):
            tt=lax.rem(s,2); cs=pl.ds(pl.multiple_of(base+lax.div(s,2)*PIECE,128),PIECE)
            gb[tt,:,:,:,:,cs]=dot(lhs[...],st[s],1,0).astype(BF).reshape(NZ,NX,NC,ROWS,PIECE)
            return 0
        lax.fori_loop(0,n,body,0)
        if i+1<len(ST):
            for q_ in ST[i+1]: q_.start()
        go(S(i))
    tcopy(dmbT_h,ta,0).wait()
    compute(0,ta,4)
    compute(1,ta,4)
    tcopy(drbT_h,ta,2).start()
    tcopy(abT_h,tb,1).wait()
    for q_ in LQ: q_.wait()
    def pair(i,_):
        @pl.when(i==0)
        def _():
            s_to_a(0); s_to_a(1); compute(2,tb,4)
        @pl.when(i==1)
        def _():
            a_to_b(0); a_to_b(1); s_to_a(2); compute(3,tb,4); tcopy(hbT_h,tb,3).start()
        @pl.when(i==2)
        def _():
            b_to_z(0); b_to_z(1); a_to_b(2); s_to_a(3); tcopy(drbT_h,ta,2).wait(); compute(4,ta,2)
        @pl.when(i==3)
        def _():
            z_end(0); z_end(1); b_to_z(2); a_to_b(3); s_to_a(4)
        @pl.when(i==4)
        def _():
            z_end(2); b_to_z(3); a_to_b(4)
        @pl.when(i==5)
        def _():
            z_end(3); b_to_z(4)
        attend_back(q,k,v,do,lse,bias,hvs,i)
        return 0
    lax.fori_loop(0,6,pair,0)
    z_end(4)
    for i in range(5): drain(i)
    tcopy(hbT_h,tb,3).wait()
    def qkv_grad(i,pairs):
        for n,ref in enumerate(pairs):
            for tt in range(2):
                cs=RGR[i]["g"]+n*PIECE
                gb[tt,:,:,:,:,cs:cs+PIECE]=dot(tb[...],ref[:,tt*PIECE:(tt+1)*PIECE],1,0).astype(BF).reshape(NZ,NX,NC,ROWS,PIECE)
    qkv_grad(5,[q,k]); go(S(5))
    for q_ in LW: q_.wait()
    lvs[...]=jnp.zeros((16,D+128),F32)
    lvs[0:6,0:D]=sums_ref[0:6,:]
    def rows_body(r,_):
        rows=pl.ds(pl.multiple_of(r*RB,RB),RB)
        acc=dr1[rows,:]
        for n,ref in enumerate((q,k,v)):
            for tt in range(2):
                acc=acc+dot(ref[rows,tt*PIECE:(tt+1)*PIECE],wq[tt,:,:,:,:,n*PIECE:(n+1)*PIECE].reshape(D,PIECE),1,1)
        inw[rows,:]=acc.astype(BF)
        lvs[6:7,0:D]+=jnp.sum(acc,axis=0,keepdims=True)
        return 0
    lax.fori_loop(0,L//RB,rows_body,0)
    cin=rcopy(inw,inp_o,xs.at[2],xs.at[3],yp); cin.start()
    cinl=pltpu.make_async_copy(inw,in_o,ls.at[8]); cinl.start()
    s_to_a(5)
    qkv_grad(6,[v])
    dtb=lvs[6:7,0:D].astype(BF)
    inner=time_ref[0:1,:]; sig=time_ref[1:2,:]
    w2=jnp.concatenate([aux[0,:,:,:,0:32,:].reshape(512,PIECE),aux[1,:,:,:,0:32,:].reshape(512,PIECE)],axis=1)
    dinner=dot(jnp.broadcast_to(dtb,(16,D)),w2,1,1)[0:1]*(sig*(1.0+inner*(1.0-sig)))
    act=(inner*sig).astype(BF).astype(F32)
    actc=jnp.broadcast_to(act,(128,512)).T[:,0:1]
    featc=jnp.broadcast_to(feat_ref[0:1,:].astype(F32),(128,256)).T[:,0:1]
    dinb=dinner.astype(BF).astype(F32); dtf=dtb.astype(F32)
    hsrc[...]=jnp.zeros((16,2*(PIECE+128)),F32)
    for tt in range(2):
        o0=tt*(PIECE+128); cc=slice(tt*PIECE,(tt+1)*PIECE)
        hsrc[7:9,o0:o0+PIECE]=hvs[0:2,cc]
        for j in range(4): hsrc[9+j:10+j,o0:o0+PIECE]=bup_ref[0:1,(tt*4+j)*PIECE:(tt*4+j+1)*PIECE]
    bsrc[...]=jnp.zeros((16,640),F32)
    bsrc[13:14,0:512]=dinner
    base=RGR[6]["g"]+PIECE
    for tt in range(2):
        gb[tt,:,:,:,0:32,base:base+PIECE]=(actc*dtf[:,tt*PIECE:(tt+1)*PIECE]).astype(BF).reshape(NZ,NX,NC,32,PIECE)
        gb[tt,:,:,:,32:48,base:base+256]=(featc*dinb[:,tt*256:(tt+1)*256]).astype(BF).reshape(NZ,NX,NC,16,256)
        hs=hsrc[:,tt*(PIECE+128):(tt+1)*(PIECE+128)]
        for n in range(16):
            blk=unspread(lvs[...],48,n)+unspread(hs,24,n)+unspread(bsrc[...],32,n)
            gb[tt,n//4,(n//2)%2,n%2,32:48,base+256:base+PIECE]=blk.astype(BF)
    go(S(6))
    a_to_b(5)
    s_to_a(6)
    b_to_z(5)
    a_to_b(6)
    z_end(5)
    b_to_z(6)
    z_end(6)
    am=red[:,12*PIECE:13*PIECE].astype(BF)
    auxm[...]=am
    cax=rcopy(auxm,auxp,xs.at[4],xs.at[5],yp); cax.start()
    af=am.astype(F32)
    ri=lax.broadcasted_iota(jnp.int32,(ROWS,PIECE),0); ci=lax.broadcasted_iota(jnp.int32,(ROWS,PIECE),1)
    dup=(ri>=32)&(ci>=256)&((ri<39)|(ri==45))
    sqa=jnp.where(dup&(t!=0),0.0,af*af)
    big=red[:,0:12*PIECE]
    part=jnp.sum(sqa)+jnp.sum(big*big)
    nv[0]=jnp.full((8,128),part,F32)
    for s,peer in enumerate((yp,xp,sp)):
        cp=rcopy(nv.at[s],nr.at[s],ns.at[s],nrs.at[s],peer); cp.start(); cp.wait()
        nv[s+1]=nv[s]+nr[s]
    cz=[rcopy(nv.at[3],nz.at[z],ns.at[3+d],nrs.at[3+d],zp[d]) for d in range(3)]
    for q_ in cz: q_.start()
    nz[z]=nv[3]
    for q_ in cz: q_.wait()
    tot[...]=((nz[0]+nz[1])+nz[2])+nz[3]
    cax.wait(); cin.wait(); cinl.wait(); cout.wait()
    for i in (5,6): drain(i)

def back(q,k,v,dob,o,lse,dmbT,abT,drbT,hbT,hid,dub,dr1,wqkv,aux,out_win,seg,featp,sums,bups,tstate,cid=1):
    DMA=pltpu.SemaphoreType.DMA; n=len(RGR)
    V=lambda s,d=BF:pltpu.VMEM(s,d)
    A=pl.BlockSpec(memory_space=pl.ANY); M=pl.BlockSpec(memory_space=pltpu.VMEM)
    sd=jax.ShapeDtypeStruct; row=(L,D); tr=(D,L)
    return pl.pallas_call(back_kernel,
        in_specs=[A]*16+[M]*5,out_specs=[A]*3+[M]*3,
        out_shape=[sd(row,BF),sd(row,BF),sd(row,BF),sd((ROWS,WIDE),F32),sd((ROWS,PIECE),BF),sd((8,128),F32)],
        scratch_shapes=[V(row),V(row),V(row),V(row),V((6,2,L),F32),V((L,128)),V((4,L,PIECE)),V(tr),V(tr),V((NT,NZ,NX,NC,ROWS,3*PIECE)),V(row,F32),
            V((NT,NZ,NX,NC,ROWS,PIECE)),V(row),V((8,D),F32),V((16,D+128),F32),V((16,2*(PIECE+128)),F32),V((16,640),F32),V((ROWS,PIECE)),
            V((4,8,128),F32),V((3,8,128),F32),V((4,8,128),F32),
            V((NT,NZ,NX,NC,ROWS,9*PIECE)),V((NT,NZ,NX,ROWS,WIDE)),V((NT,NZ,ROWS,RWA)),V((NZ,NX,ROWS,RWB)),V((NZ,ROWS,WIDE)),V((3,ROWS,WIDE)),
            DMA((n,)),DMA((n,)),DMA((n,2)),DMA((n,2)),DMA((n,2)),DMA((n,2)),DMA((n,3)),DMA((n,3)),DMA((9,)),DMA((12,)),DMA((6,)),DMA((6,)),DMA((6,))],
        compiler_params=pltpu.CompilerParams(collective_id=cid,has_side_effects=True,vmem_limit_bytes=63*2**20),name="back")(
            q,k,v,dob,o,lse,dmbT,abT,drbT,hbT,hid,dub,dr1,wqkv,aux,out_win,seg,featp,sums,bups,tstate)

def shards_fast(tokens,cotangent,segment_ids,timesteps,*params):
    masters=params[:9];moments=params[9:18];averages=params[18:]
    t=lax.axis_index("tensor")
    step=lax.dynamic_slice_in_dim(timesteps,t,1,1)[0]
    feat=time_features(step,TD).astype(BF)
    featp=jnp.broadcast_to(jnp.pad(feat.reshape(16,8),((0,0),(0,8))).reshape(1,256),(16,256))
    q,k,v,o,lse,out_win,dmbT,abT,drbT,hid,dub,dr1,dob,hbT,wq6,aux6,sums,bups,tstate=front(pack_weights(*masters),tokens,cotangent,segment_ids,featp)
    in_win,in_peer,out_peer,red,aux_peer,total=back(q,k,v,dob,o,lse,dmbT,abT,drbT,hbT,hid,dub,dr1,wq6,aux6,out_win,segment_ids,featp,sums,bups,tstate)
    aux_mine=red[:,12*PIECE:].astype(BF)
    aux0=jnp.where(t==0,aux_mine,aux_peer).astype(F32); aux1=jnp.where(t==0,aux_peer,aux_mine).astype(F32)
    r_down=red[:,0:4*PIECE].reshape(ROWS,4,PIECE).transpose(1,2,0)
    r_up=red[:,4*PIECE:8*PIECE].reshape(ROWS,4,PIECE)
    r_out=red[:,8*PIECE:9*PIECE].T
    r_qkv=red[:,9*PIECE:12*PIECE].reshape(ROWS,3,PIECE)
    r_w2=jnp.concatenate([aux0[:32],aux1[:32]],axis=1)
    r_w1=jnp.concatenate([aux0[32:40,:256],aux1[32:40,:256]],axis=1)
    r_lv=aux0[32:39,256:304]
    r_b1=aux0[45,256:288]
    r_hv=jnp.where(t==0,aux0,aux1)[39:45,256:280].reshape(6,1,24)
    grads=(r_qkv,r_out,r_up,r_down,r_w1,r_w2,r_b1,r_hv,r_lv)
    norm=jnp.sqrt(total[0,0])
    factor=1.0/jnp.maximum(norm,1.0)
    rate=4.0*math.sqrt(MPARAMS/D)
    new=[advance(m,v_,a_,g_,factor,rate) for m,v_,a_,g_ in zip(masters,moments,averages,grads)]

    def whole(win,peer):
        lo=jnp.where(t==0,win,peer); hi=jnp.where(t==0,peer,win)
        mid=jnp.where((segment_ids[0,512:1024]==0)[:,None],lo[512:],hi[:512])
        return jnp.concatenate([lo[:512],mid,hi[512:]],axis=0)
    return (whole(out_win,out_peer),whole(in_win,in_peer),norm)+tuple(n[0] for n in new)+tuple(n[1] for n in new)+tuple(n[2] for n in new)


def solution(mesh):
    fast=dict(mesh.shape)=={'dp':16,'tensor':2}
    return jax.shard_map(
        shards_fast if fast else shards_any,
        mesh=mesh,
        in_specs=(
            P("dp", None),
            P("dp", None),
            P("dp", None),
            P("dp", None),
            P("dp", None, "tensor"),
            P("tensor", "dp"),
            P("dp", None, "tensor"),
            P(None, "tensor", "dp"),
            P("dp", None),
            P("dp", None),
            P("dp"),
            P(None, "tensor", "dp"),
            P(None, "dp"),
            P("dp", None, "tensor"),
            P("tensor", "dp"),
            P("dp", None, "tensor"),
            P(None, "tensor", "dp"),
            P("dp", None),
            P("dp", None),
            P("dp"),
            P(None, "tensor", "dp"),
            P(None, "dp"),
            P("dp", None, "tensor"),
            P("tensor", "dp"),
            P("dp", None, "tensor"),
            P(None, "tensor", "dp"),
            P("dp", None),
            P("dp", None),
            P("dp"),
            P(None, "tensor", "dp"),
            P(None, "dp"),
        ),
        out_specs=(
            P("dp", None),
            P("dp", None),
            P(),
            P("dp", None, "tensor"),
            P("tensor", "dp"),
            P("dp", None, "tensor"),
            P(None, "tensor", "dp"),
            P("dp", None),
            P("dp", None),
            P("dp"),
            P(None, "tensor", "dp"),
            P(None, "dp"),
            P("dp", None, "tensor"),
            P("tensor", "dp"),
            P("dp", None, "tensor"),
            P(None, "tensor", "dp"),
            P("dp", None),
            P("dp", None),
            P("dp"),
            P(None, "tensor", "dp"),
            P(None, "dp"),
            P("dp", None, "tensor"),
            P("tensor", "dp"),
            P("dp", None, "tensor"),
            P(None, "tensor", "dp"),
            P("dp", None),
            P("dp", None),
            P("dp"),
            P(None, "tensor", "dp"),
            P(None, "dp"),
        ),
        check_vma=False,
    )
```

```python
import functools
import math

import jax
import jax.numpy as jnp
from jax import lax
from jax.experimental import pallas as pl
from jax.experimental.pallas import tpu as pltpu
from jax.sharding import PartitionSpec as P

D = 768
HD = 64
TD = 128
SEGS = 2
PACK = 1536
MPARAMS = 7536640


EPSILON = 1e-05
MOMENTUM = 0.5
AVERAGE_DECAY = 0.5


def layer_norm(values, gain_vec, shift_vec):
    centre = jnp.mean(values, axis=-1, keepdims=True)
    centred = values - centre
    spread = jnp.mean(centred * centred, axis=-1, keepdims=True)
    return centred * lax.rsqrt(spread + EPSILON) * gain_vec + shift_vec


def time_features(step_ids, feat_width):
    midpoint = feat_width // 2
    frequency = jnp.exp(-math.log(10000.0) * jnp.arange(midpoint, dtype=jnp.float32) / midpoint)
    angles = step_ids.astype(jnp.float32)[..., None] * frequency
    return jnp.concatenate([jnp.cos(angles), jnp.sin(angles)], axis=-1)


def gelu_exact(values):
    return jax.nn.gelu(values, approximate=False)


def head_slice(matrix, head_index):
    return lax.dynamic_slice_in_dim(matrix, head_index * HD, HD, 1)


def merge_heads(stacked):
    return stacked.transpose(1, 0, 2).reshape(stacked.shape[1], stacked.shape[0] * stacked.shape[2])


def advance(master, moment, average, grad, factor, step_rate):
    scaled = grad * factor
    velocity = MOMENTUM * moment + scaled
    fresh_master = master - step_rate * (scaled + MOMENTUM * velocity)
    smoothed = AVERAGE_DECAY * average + (1.0 - AVERAGE_DECAY) * fresh_master
    return (fresh_master, velocity, smoothed)


def shards_any(
    tokens,
    cotangent,
    segment_ids,
    timesteps,
    qkv_weight,
    out_weight,
    up_weight,
    down_weight,
    time_inner,
    time_outer,
    time_bias,
    head_vectors,
    layer_vectors,
    qkv_moment,
    out_moment,
    up_moment,
    down_moment,
    inner_moment,
    outer_moment,
    bias_moment,
    head_moment,
    layer_moment,
    qkv_average,
    out_average,
    up_average,
    down_average,
    inner_average,
    outer_average,
    bias_average,
    head_average,
    layer_average,
):
    w_qkv, w_out, w_up, w_down, w_inner, w_outer, b_inner, head_vec, layer_vec = (
        lax.all_gather(qkv_weight.astype(jnp.bfloat16), "dp", axis=0, tiled=True),
        lax.all_gather(out_weight.astype(jnp.bfloat16), "dp", axis=1, tiled=True),
        lax.all_gather(up_weight.astype(jnp.bfloat16), "dp", axis=0, tiled=True),
        lax.all_gather(down_weight.astype(jnp.bfloat16), "dp", axis=2, tiled=True),
        lax.all_gather(time_inner.astype(jnp.bfloat16), "dp", axis=0, tiled=True),
        lax.all_gather(time_outer.astype(jnp.bfloat16), "dp", axis=0, tiled=True),
        lax.all_gather(time_bias.astype(jnp.bfloat16), "dp", axis=0, tiled=True),
        lax.all_gather(head_vectors.astype(jnp.bfloat16), "dp", axis=2, tiled=True),
        lax.all_gather(layer_vectors.astype(jnp.bfloat16), "dp", axis=1, tiled=True),
    )
    local_width = w_out.shape[0]
    head_count = local_width // HD
    packed = tokens.shape[0]
    head_rows = head_vec.astype(jnp.float32).reshape(6, local_width)
    layer_rows = layer_vec.astype(jnp.float32)
    score_scale = 1.0 / math.sqrt(HD)
    block_rows = min(PACK, 512)
    block_count = packed // block_rows
    seg_row = segment_ids[0]
    features = time_features(timesteps[0], TD)
    feature_low = features.astype(jnp.bfloat16)
    inner_pre = jnp.dot(feature_low, w_inner, preferred_element_type=jnp.float32) + b_inner.astype(
        jnp.float32
    )
    silu_out, silu_pull = jax.vjp(jax.nn.silu, inner_pre)
    act_low = silu_out.astype(jnp.bfloat16)
    time_embed = jnp.dot(act_low, w_outer, preferred_element_type=jnp.float32) + layer_rows[6]
    onehot = (seg_row[:, None] == jnp.arange(SEGS, dtype=jnp.int32)[None, :]).astype(jnp.float32)
    hidden0 = tokens.astype(jnp.float32) + jnp.dot(
        onehot, time_embed, precision=lax.Precision.HIGHEST, preferred_element_type=jnp.float32
    )
    hidden_low = hidden0.astype(jnp.bfloat16)
    projected = jnp.einsum("pd,dce->pce", hidden_low, w_qkv, preferred_element_type=jnp.float32)
    queries = (projected[:, 0] + head_rows[0]).astype(jnp.bfloat16)
    keys_low = projected[:, 1].astype(jnp.bfloat16)
    values_low = (projected[:, 2] + head_rows[1]).astype(jnp.bfloat16)

    def block_scores(query_blk, key_all, seg_query):
        raw_scores = (
            jnp.einsum("qd,kd->qk", query_blk, key_all, preferred_element_type=jnp.float32)
            * score_scale
        )
        same_doc = seg_query[:, None] == seg_row[None, :]
        return (raw_scores, same_doc)

    def attend_head(head_index):
        query_h = head_slice(queries, head_index)
        key_h = head_slice(keys_low, head_index)
        value_h = head_slice(values_low, head_index)
        out_blocks = []
        sum_blocks = []
        for block_index in range(block_count):
            first_row = block_index * block_rows
            raw_scores, same_doc = block_scores(
                query_h[first_row : first_row + block_rows],
                key_h,
                seg_row[first_row : first_row + block_rows],
            )
            masked = jnp.where(same_doc, raw_scores, -1e30)
            row_peak = jnp.max(masked, axis=1, keepdims=True)
            exponent = jnp.exp(masked - row_peak)
            row_total = jnp.sum(exponent, axis=1, keepdims=True)
            soft_weights = exponent / row_total
            out_blocks.append(
                jnp.dot(
                    soft_weights.astype(jnp.bfloat16), value_h, preferred_element_type=jnp.float32
                )
            )
            sum_blocks.append((row_peak + jnp.log(row_total))[:, 0])
        return (jnp.concatenate(out_blocks, axis=0), jnp.concatenate(sum_blocks, axis=0))

    head_out, log_sums = lax.map(attend_head, jnp.arange(head_count, dtype=jnp.int32))
    att_low = merge_heads(head_out).astype(jnp.bfloat16)
    attn_partial = jnp.dot(att_low, w_out, preferred_element_type=jnp.float32)
    attn_branch = (
        lax.psum(attn_partial.astype(jnp.bfloat16), "tensor").astype(jnp.float32) + layer_rows[0]
    )
    residual1 = hidden0 + attn_branch
    cot_here = cotangent.astype(jnp.float32)
    normed1, norm1_pull = jax.vjp(layer_norm, residual1, layer_rows[1], layer_rows[2])
    norm_here = normed1.astype(jnp.bfloat16)
    up_pre = (
        jnp.einsum("pd,dje->pje", norm_here, w_up, preferred_element_type=jnp.float32)
        + head_rows[2:]
    )
    gelu_out, gelu_pull = jax.vjp(gelu_exact, up_pre)
    hid_low = gelu_out.astype(jnp.bfloat16)
    down_partial = jnp.einsum("pje,jef->pf", hid_low, w_down, preferred_element_type=jnp.float32)
    mlp_branch = (
        lax.psum(down_partial.astype(jnp.bfloat16), "tensor").astype(jnp.float32) + layer_rows[3]
    )
    result, norm2_pull = jax.vjp(layer_norm, normed1 + mlp_branch, layer_rows[4], layer_rows[5])
    output_here = result.astype(jnp.bfloat16)
    back_r2, back_gain2, back_shift2 = norm2_pull(cot_here)
    part_bdown = jnp.sum(back_r2, axis=0)
    back_r2_here = back_r2.astype(jnp.bfloat16)
    grad_down = jnp.einsum("pje,pf->jef", hid_low, back_r2_here, preferred_element_type=jnp.float32)
    back_hid = jnp.einsum("pf,jef->pje", back_r2_here, w_down, preferred_element_type=jnp.float32)
    (back_up,) = gelu_pull(back_hid)
    grad_bup = jnp.sum(back_up, axis=0)
    back_up_low = back_up.astype(jnp.bfloat16)
    grad_up = jnp.einsum("pd,pje->dje", norm_here, back_up_low, preferred_element_type=jnp.float32)
    back_a_part = jnp.einsum("pje,dje->pd", back_up_low, w_up, preferred_element_type=jnp.float32)
    back_a = lax.psum(back_a_part.astype(jnp.bfloat16), "tensor").astype(jnp.float32) + back_r2
    back_r1, back_gain1, back_shift1 = norm1_pull(back_a)
    grad_bout = jnp.sum(back_r1, axis=0)
    back_r1_low = back_r1.astype(jnp.bfloat16)
    grad_out = jnp.einsum("pe,pf->ef", att_low, back_r1_low, preferred_element_type=jnp.float32)
    back_att = jnp.einsum(
        "pf,ef->pe", back_r1_low, w_out, preferred_element_type=jnp.float32
    ).astype(jnp.bfloat16)

    def head_back(head_index):
        query_h = head_slice(queries, head_index)
        key_h = head_slice(keys_low, head_index)
        value_h = head_slice(values_low, head_index)
        grad_h = head_slice(back_att, head_index)
        lse_h = log_sums[head_index]
        key_grad = jnp.zeros((packed, HD), jnp.float32)
        value_grad = jnp.zeros((packed, HD), jnp.float32)
        query_blocks = []
        for block_index in range(block_count):
            first_row = block_index * block_rows
            query_blk = query_h[first_row : first_row + block_rows]
            raw_scores, same_doc = block_scores(
                query_blk, key_h, seg_row[first_row : first_row + block_rows]
            )
            lse_blk = lse_h[first_row : first_row + block_rows]
            soft_weights = jnp.where(same_doc, jnp.exp(raw_scores - lse_blk[:, None]), 0.0)
            grad_blk = grad_h[first_row : first_row + block_rows]
            value_grad = value_grad + jnp.einsum(
                "qk,qd->kd",
                soft_weights.astype(jnp.bfloat16),
                grad_blk,
                preferred_element_type=jnp.float32,
            )
            weight_grad = jnp.einsum(
                "qd,kd->qk", grad_blk, value_h, preferred_element_type=jnp.float32
            )
            row_inner = jnp.sum(soft_weights * weight_grad, axis=1, keepdims=True)
            score_low = (soft_weights * (weight_grad - row_inner)).astype(jnp.bfloat16)
            query_blocks.append(
                jnp.dot(score_low, key_h, preferred_element_type=jnp.float32) * score_scale
            )
            key_grad = (
                key_grad
                + jnp.einsum("qk,qd->kd", score_low, query_blk, preferred_element_type=jnp.float32)
                * score_scale
            )
        return (jnp.concatenate(query_blocks, axis=0), key_grad, value_grad)

    query_grads, key_grads, value_grads = lax.map(
        head_back, jnp.arange(head_count, dtype=jnp.int32)
    )
    query_grad_all = merge_heads(query_grads)
    key_grad_all = merge_heads(key_grads)
    value_grad_all = merge_heads(value_grads)
    grad_bq = jnp.sum(query_grad_all, axis=0)
    grad_bv = jnp.sum(value_grad_all, axis=0)
    proj_grad_low = jnp.stack([query_grad_all, key_grad_all, value_grad_all], axis=1).astype(
        jnp.bfloat16
    )
    grad_qkv = jnp.einsum(
        "pd,pce->dce", hidden_low, proj_grad_low, preferred_element_type=jnp.float32
    )
    back_h_part = jnp.einsum(
        "pce,dce->pd", proj_grad_low, w_qkv, preferred_element_type=jnp.float32
    )
    back_h0 = lax.psum(back_h_part.astype(jnp.bfloat16), "tensor").astype(jnp.float32) + back_r1
    input_grad = back_h0.astype(jnp.bfloat16)
    back_time = jnp.einsum(
        "ps,pd->sd",
        onehot,
        back_h0,
        precision=lax.Precision.HIGHEST,
        preferred_element_type=jnp.float32,
    )
    grad_bouter = jnp.sum(back_time, axis=0)
    back_time_low = back_time.astype(jnp.bfloat16)
    grad_outer = jnp.einsum("su,sd->ud", act_low, back_time_low, preferred_element_type=jnp.float32)
    back_act = jnp.einsum("sd,ud->su", back_time_low, w_outer, preferred_element_type=jnp.float32)
    (back_inner,) = silu_pull(back_act)
    grad_binner = jnp.sum(back_inner, axis=0)
    grad_inner = jnp.einsum(
        "st,su->tu",
        feature_low,
        back_inner.astype(jnp.bfloat16),
        preferred_element_type=jnp.float32,
    )
    grad_head = jnp.concatenate([grad_bq[None], grad_bv[None], grad_bup], axis=0).reshape(
        6, 1, local_width
    )
    grad_layer = jnp.stack(
        [grad_bout, back_gain1, back_shift1, part_bdown, back_gain2, back_shift2, grad_bouter],
        axis=0,
    )
    red_qkv, red_out, red_up, red_down, red_inner, red_outer, red_binner, red_head, red_layer = (
        lax.psum_scatter(grad_qkv, "dp", scatter_dimension=0, tiled=True),
        lax.psum_scatter(grad_out, "dp", scatter_dimension=1, tiled=True),
        lax.psum_scatter(grad_up, "dp", scatter_dimension=0, tiled=True),
        lax.psum_scatter(grad_down, "dp", scatter_dimension=2, tiled=True),
        lax.psum_scatter(grad_inner, "dp", scatter_dimension=0, tiled=True),
        lax.psum_scatter(grad_outer, "dp", scatter_dimension=0, tiled=True),
        lax.psum_scatter(grad_binner, "dp", scatter_dimension=0, tiled=True),
        lax.psum_scatter(grad_head, "dp", scatter_dimension=2, tiled=True),
        lax.psum_scatter(grad_layer, "dp", scatter_dimension=1, tiled=True),
    )
    split_squares = sum(
        (jnp.sum(piece * piece) for piece in (red_qkv, red_out, red_up, red_down, red_head))
    )
    shared_squares = sum(
        (jnp.sum(piece * piece) for piece in (red_inner, red_outer, red_binner, red_layer))
    )
    local_squares = split_squares + shared_squares / lax.axis_size("tensor")
    norm = jnp.sqrt(lax.psum(local_squares, ("dp", "tensor")))
    factor = 1.0 / jnp.maximum(norm, 1.0)
    step_rate = 4.0 * math.sqrt(MPARAMS / D)
    qkv_master, qkv_velocity, qkv_smoothed = advance(
        qkv_weight, qkv_moment, qkv_average, red_qkv, factor, step_rate
    )
    out_master, out_velocity, out_smoothed = advance(
        out_weight, out_moment, out_average, red_out, factor, step_rate
    )
    up_master, up_velocity, up_smoothed = advance(
        up_weight, up_moment, up_average, red_up, factor, step_rate
    )
    down_master, down_velocity, down_smoothed = advance(
        down_weight, down_moment, down_average, red_down, factor, step_rate
    )
    inner_master, inner_velocity, inner_smoothed = advance(
        time_inner, inner_moment, inner_average, red_inner, factor, step_rate
    )
    outer_master, outer_velocity, outer_smoothed = advance(
        time_outer, outer_moment, outer_average, red_outer, factor, step_rate
    )
    bias_master, bias_velocity, bias_smoothed = advance(
        time_bias, bias_moment, bias_average, red_binner, factor, step_rate
    )
    head_master, head_velocity, head_smoothed = advance(
        head_vectors, head_moment, head_average, red_head, factor, step_rate
    )
    layer_master, layer_velocity, layer_smoothed = advance(
        layer_vectors, layer_moment, layer_average, red_layer, factor, step_rate
    )
    return (
        output_here,
        input_grad,
        norm,
        qkv_master,
        out_master,
        up_master,
        down_master,
        inner_master,
        outer_master,
        bias_master,
        head_master,
        layer_master,
        qkv_velocity,
        out_velocity,
        up_velocity,
        down_velocity,
        inner_velocity,
        outer_velocity,
        bias_velocity,
        head_velocity,
        layer_velocity,
        qkv_smoothed,
        out_smoothed,
        up_smoothed,
        down_smoothed,
        inner_smoothed,
        outer_smoothed,
        bias_smoothed,
        head_smoothed,
        layer_smoothed,
    )


F32=jnp.float32; BF=jnp.bfloat16
MESH=pl.DeviceIdType.MESH
NZ,NX,NC,NT=4,2,2,2
ROWS=48; PIECE=384

def place():
    dp=lax.axis_index("dp"); t=lax.axis_index("tensor")
    z=lax.div(dp,4); x=lax.rem(lax.div(dp,2),2); c=lax.rem(dp,2)
    return z,x,c,t
def dev(z,x,c,t):
    return ((z*NX+x)*NC+c,t)

def peers():
    z,x,c,t=place()
    zp=[dev(lax.rem(z+d,NZ),x,c,t) for d in range(1,NZ)]
    return zp,dev(z,1-x,c,t),dev(z,x,c,1-t),dev(z,x,1-c,t)

def greet():
    zp,xp,yp,sp=peers()
    bar=pltpu.get_barrier_semaphore()
    for d in zp+[xp,yp,sp]:
        pl.semaphore_signal(bar,inc=1,device_id=d,device_id_type=MESH)
    pl.semaphore_wait(bar,6)

def rcopy(src,dst,ssem,rsem,d):
    return pltpu.make_async_remote_copy(src_ref=src,dst_ref=dst,send_sem=ssem,recv_sem=rsem,device_id=d,device_id_type=MESH)

L=1024
def dot(a,b,ca,cb):
    return lax.dot_general(a,b,(((ca,),(cb,)),((),())),preferred_element_type=F32)
def ln_stats(v):
    mean=jnp.mean(v,axis=-1,keepdims=True)
    cen=v-mean
    inv=lax.rsqrt(jnp.mean(cen*cen,axis=-1,keepdims=True)+EPSILON)
    return cen*inv,inv

def ln_back(gain,dy,xhat,inv):
    gd=gain*dy
    return (gd-jnp.mean(gd,axis=-1,keepdims=True)-xhat*jnp.mean(gd*xhat,axis=-1,keepdims=True))*inv

def phi_cdf(u):
    return 0.5*(1.0+lax.erf(u*(1.0/math.sqrt(2.0))))

WIDE=13*PIECE
RB=256
def spread(blocks,w,tiles):
    lane=lax.broadcasted_iota(jnp.int32,(16,128),1)
    acc=[jnp.zeros((16,128),F32) for _ in range(tiles+1)]
    for n,b in enumerate(blocks):
        tile,s=divmod(n*w,128)
        wide=jnp.concatenate([jnp.where(lane<w,b,0.0),jnp.zeros((16,128),F32)],axis=1)
        if s: wide=pltpu.roll(wide,s,1)
        acc[tile]=acc[tile]+wide[:,:128]
        acc[tile+1]=acc[tile+1]+wide[:,128:]
    return jnp.concatenate(acc[:tiles],axis=1)

def attend_pair(q_ref,k_ref,v_ref,o_ref,lse_ref,bias_ref,i,bq=512):
    lane=lax.broadcasted_iota(jnp.int32,(1,128),1)
    cs=pl.ds(pl.multiple_of(i*128,128),128)
    kp=k_ref[:,cs]; vT=v_ref[:,cs].T
    bias=bias_ref[...]
    khs=[]
    for h in range(2):
        khs.append(jnp.where((lane//64)==h,kp,jnp.where(lane==(64*(1-h)),bias,jnp.zeros_like(kp))))
    for qi in range(L//bq):
        qp=q_ref[pl.ds(qi*bq,bq),cs]*0.125
        oT=[]
        for h in range(2):
            qh=jnp.where((lane//64)==h,qp,jnp.where(lane==(64*(1-h)),jnp.ones_like(qp),jnp.zeros_like(qp)))
            sT=dot(khs[h],qh,1,1)
            m=jnp.max(sT,axis=0,keepdims=True)
            e=jnp.exp(sT-m)
            l=jnp.sum(e,axis=0,keepdims=True)
            p=(e*(1.0/l)).astype(BF)
            oT.append(dot(vT[h*64:(h+1)*64],p,1,0))
            lse_ref[i,h:h+1,qi*bq:(qi+1)*bq]=m+jnp.log(l)
        o_ref[pl.ds(qi*bq,bq),cs]=jnp.concatenate(oT,axis=0).T.astype(BF)

GCH=[(n*PIECE,PIECE,128*(1+n%2)) for n in range(13)]

def slots(n):
    out={}
    for i in range(n):
        for stage,lag in enumerate((0,1,2,3) if i<4 else (0,2,4,5)): out.setdefault(i+lag,[]).append((stage,i))
    return {k:sorted(v) for k,v in out.items()}
SLOTS=slots(len(GCH)-1)

def gather_steps(g,zs,zr,fs,fr,ss,sr):
    z,x,c,t=place(); zp,xp,yp,sp=peers(); n=len(GCH)-1
    def cols(i): return pl.ds(GCH[i][0],GCH[i][1])
    def ca(i): return pl.ds(GCH[i][0],GCH[i][2])
    def cb(i): return pl.ds(GCH[i][0]+GCH[i][2],GCH[i][1]-GCH[i][2])
    same=lambda r,s,q,d:rcopy(r,r,s,q,d)
    def Z(i):
        src=g.at[:,z,:,c,:,cols(i)] if i==n else g.at[t,z,x,c,:,cols(i)]
        return [same(src,zs.at[i,d],zr.at[i,d],zp[d]) for d in range(3)]
    def A(i):
        if i==n: return [same(g.at[t,z,x,c,:,ca(i)],fs.at[i,0],fr.at[i,0],xp),same(g.at[t,z,x,c,:,cb(i)],fs.at[i,1],fr.at[i,1],yp)]
        return [same(g.at[t,:,x,c,:,ca(i)],fs.at[i,0],fr.at[i,0],xp),same(g.at[t,:,x,c,:,cb(i)],fs.at[i,1],fr.at[i,1],yp)]
    def B(i):
        if i==n: return [same(g.at[t,z,:,c,:,ca(i)],fs.at[i,2],fr.at[i,2],yp),same(g.at[:,z,x,c,:,cb(i)],fs.at[i,3],fr.at[i,3],xp)]
        return [same(g.at[t,:,:,c,:,ca(i)],fs.at[i,2],fr.at[i,2],yp),same(g.at[:,:,x,c,:,cb(i)],fs.at[i,3],fr.at[i,3],xp)]
    S=lambda i:[same(g.at[:,:,:,c,:,cols(i)],ss.at[i],sr.at[i],sp)]
    def go(cs):
        for q in cs: q.start()
    def got(cs):
        for q in cs: q.wait_recv()
    def step(k):
        for stage,i in SLOTS.get(k,()):
            if stage==0:
                got(Z(i)); go(A(i))
                if i+4<n: go(Z(i+4))
            if stage==1: got(A(i)); go(B(i))
            if stage==2: got(B(i)); go(S(i))
            if stage==3: got(S(i))
    def late(k):
        if k==0: go(A(n))
        if k==1: got(A(n)); go(B(n))
        if k==2: got(B(n)); go(Z(n))
        if k==3: got(Z(n)); go(S(n))
        if k==4: got(S(n))
    def first(k): go(Z(k))
    def finish():
        for i in range(n+1):
            for q in Z(i)+A(i)+B(i)+S(i): q.wait_send()
    return step,late,first,finish

def front_kernel(ts_ref,qkv_m,out_m,up_m,down_m,w1_m,w2_m,b1_m,hv_m,lv_m,tok_hbm,cot_hbm,seg_ref,
        q_o,k_o,v_o,o_o,lse_o,out_o,outp_o,dmbT_o,abT_o,drbT_o,hid_o,dub_o,dr1_o,dob_o,hbT_o,wqkv_o,aux_o,sums_o,bup_o,time_o,feat_o,
        g,tok,cot,q,k,v,o,lse,own,bias,vecs,temb,hbT,gp,hid,inv,dmbT,abT,drbT,dr1,a32,
        zs,zr,fs,fr,ss,sr,lsem,osem,hsem,bsem,ysem):
    z,x,c,t=place()
    step,late,first,finish=gather_steps(g,zs,zr,fs,fr,ss,sr)
    win=pl.ds(pl.multiple_of(t*512,512),L)
    ltok=pltpu.make_async_copy(tok_hbm.at[win,:],tok,lsem.at[0]); ltok.start()
    lcot=pltpu.make_async_copy(cot_hbm.at[win,:],cot,lsem.at[1]); lcot.start()
    greet_out()
    a32[...]=jnp.zeros((ROWS,PIECE),F32)
    a32[0:32,:]=w2_m[:,pl.ds(pl.multiple_of(t*PIECE,128),PIECE)]
    a32[32:40,0:256]=w1_m[:,pl.ds(pl.multiple_of(t*256,128),256)]
    a32[32:39,256:304]=lv_m[...]
    a32[39:45,256:280]=hv_m[:,0,:]
    a32[45:46,256:288]=b1_m[...]
    def put(p,val): g[t,z,x,c,:,p*PIECE:(p+1)*PIECE]=val.astype(BF)
    put(0,a32[...])
    greet_in()
    first(0)
    for j in range(3): put(1+j,qkv_m[j])
    put(4,out_m[...])
    first(1); first(2); first(3)
    for j in range(4): put(5+j,up_m[:,j,:])
    for j in range(4): put(9+j,down_m[j])
    late(0)
    ln=lax.broadcasted_iota(jnp.int32,(16,256),1)
    fi=lax.div(ln,16)*8+lax.rem(ln,16)
    theta=jnp.exp(lax.rem(fi,64).astype(F32)*(-math.log(10000.0)/64.0))
    ang=theta*ts_ref[0,t].astype(F32)
    feat=jnp.where(lax.rem(ln,16)<8,jnp.where(fi<64,jnp.cos(ang),jnp.sin(ang)),0.0).astype(BF)
    feat_o[...]=feat
    seg=seg_ref[:,pl.ds(pl.multiple_of(t*512,128),L)]
    own_row=jnp.where(seg==t,1.0,0.0)
    ownT=jnp.broadcast_to(own_row,(128,L)).T
    own[...]=ownT
    bias[...]=jnp.where(ownT>0.5,0.0,-1e30).astype(BF)
    for n in range(4): step(n)
    def vecblk(tt,n): return g[tt,n//4,(n//2)%2,n%2,32:48,256:384].astype(F32)
    b0=[vecblk(0,n) for n in range(16)]; b1=[vecblk(1,n) for n in range(16)]
    lv=spread(b0,48,6)
    hv=jnp.concatenate([spread(b0,24,3),spread(b1,24,3)],axis=1)
    vecs[0:16,:]=lv
    vecs[16:32,:]=hv
    bin_=spread(b0,32,4)[13:14,:]
    w1=jnp.concatenate([g[0,:,:,:,32:48,0:256].reshape(256,256),g[1,:,:,:,32:48,0:256].reshape(256,256)],axis=1)
    inner=dot(feat,w1,1,0)[0:1]+bin_
    sig=1.0/(1.0+jnp.exp(-inner))
    act=inner*sig
    w2=jnp.concatenate([g[0,:,:,:,0:32,0:384].reshape(512,384),g[1,:,:,:,0:32,0:384].reshape(512,384)],axis=1)
    actb=jnp.broadcast_to(act,(16,512)).astype(BF)
    te=dot(actb,w2,1,0)[0:1]+lv[6:7]
    temb[...]=jnp.broadcast_to(te,(8,D))
    time_o[...]=jnp.concatenate([inner,sig,jnp.zeros((6,512),F32)],axis=0)
    ltok.wait()
    outs=[]
    def emit(src,dst):
        cp=pltpu.make_async_copy(src,dst,osem.at[len(outs)]); cp.start(); outs.append(cp)
    def hid_rows(r,_):
        rows=pl.ds(pl.multiple_of(r*RB,RB),RB)
        hb=(tok[rows,:].astype(F32)+temb[0:1,:]).astype(BF)
        hbT[:,rows]=hb.T
        return 0
    lax.fori_loop(0,L//RB,hid_rows,0)
    def project(which,ref,brow):
        def rows_body(r,_):
            rows=pl.ds(pl.multiple_of(r*RB,RB),RB)
            hb=(tok[rows,:].astype(F32)+temb[0:1,:]).astype(BF)
            for tt in range(2):
                val=dot(hb,g[tt,:,:,:,:,(1+which)*PIECE:(2+which)*PIECE].reshape(D,PIECE),1,0)
                if brow is not None: val=val+vecs[brow:brow+1,tt*PIECE:(tt+1)*PIECE]
                ref[rows,tt*PIECE:(tt+1)*PIECE]=val.astype(BF)
            return 0
        lax.fori_loop(0,L//RB,rows_body,0)
    emit(hbT,hbT_o)
    step(4)
    project(0,q,16+7)
    emit(q,q_o)
    step(5); late(1)
    project(1,k,None)
    emit(k,k_o)
    step(6)
    project(2,v,16+8)
    emit(v,v_o)
    emit(g.at[:,:,:,:,:,0:PIECE],aux_o); emit(g.at[:,:,:,:,:,PIECE:4*PIECE],wqkv_o)
    def pair(i,_):
        attend_pair(q,k,v,o,lse,bias,i)
        for s in range(6):
            @pl.when(i==s)
            def _():
                if s==3: late(2)
                step(7+s)
        return 0
    lax.fori_loop(0,6,pair,0)
    emit(o,o_o); emit(lse,lse_o)
    lcot.wait()
    for cp in outs: cp.wait()
    out,dob=q,k
    yp=peers()[2]
    def emits(r):
        rows=pl.ds(pl.multiple_of(r*RB,RB),RB)
        byrow=[(out,out_o),(dr1,dr1_o),(dob,dob_o)]; bycol=[(dmbT,dmbT_o),(abT,abT_o),(drbT,drbT_o)]
        cs=[pltpu.make_async_copy(a.at[rows,:],b.at[rows,:],bsem.at[n,r]) for n,(a,b) in enumerate(byrow)]
        cs+=[pltpu.make_async_copy(a.at[:,rows],b.at[:,rows],bsem.at[3+n,r]) for n,(a,b) in enumerate(bycol)]
        return cs,rcopy(out.at[rows,:],outp_o.at[rows,:],ysem.at[0,r],ysem.at[1,r],yp)
    mid_body(g,tok,cot,o,own,vecs,temb,gp,hid,inv,out,dmbT,abT,drbT,dr1,dob,sums_o,bup_o,hid_o,dub_o,hsem,step,late,emits)
    for r in range(L//RB):
        cs,far=emits(r)
        for cp in cs: cp.wait()
        if r<2: far.wait()
    finish()

def mid_body(g,tok,cot,o,own,vecs,temb,gp,hid,inv,out,dmbT,abT,drbT,dr1,dob,sums_o,bup_o,hid_o,dub_o,hsem,step,late,emits):
    def W(tt,piece,n=1): return g[tt,:,:,:,:,piece*PIECE:(piece+n)*PIECE].reshape(D,n*PIECE)
    row=lambda r:vecs[r:r+1,:]
    sums_o[...]=jnp.zeros((8,D),F32); bup_o[...]=jnp.zeros((8,4*D),F32)
    csum=lambda a:jnp.sum(a,axis=0,keepdims=True)
    def emit_rows(buf,dst,r,which):
        rows=pl.ds(pl.multiple_of(r*RB,RB),RB)
        return pltpu.make_async_copy(buf.at[rows,:],dst.at[rows,:],hsem.at[which,r])
    def up_block(r,_):
        rows=pl.ds(pl.multiple_of(r*RB,RB),RB)
        for n in range(4):
            @pl.when(r==n)
            def _():
                if n==1: late(3)
                step(13+n)
        attn=dot(o[rows,0:PIECE],W(0,4),1,1)+dot(o[rows,PIECE:D],W(1,4),1,1)
        r1=(tok[rows,:].astype(F32)+temb[0:1,:])+(attn+row(0))
        x1,inv1=ln_stats(r1)
        dr1[rows,:]=x1
        inv[rows,:]=jnp.broadcast_to(inv1,(RB,128))
        ab=(x1*row(1)+row(2)).astype(BF)
        abT[:,rows]=ab.T
        for tt in range(2):
            for j in range(4):
                cc=pl.ds((tt*4+j)*PIECE,PIECE)
                u=dot(ab,W(tt,5+j),1,0)+vecs[16+9+j:16+10+j,tt*PIECE:(tt+1)*PIECE]
                cdf=phi_cdf(u)
                gp[rows,cc]=(cdf+u*jnp.exp(-0.5*u*u)*(1.0/math.sqrt(2*math.pi))).astype(BF)
                hid[rows,cc]=(u*cdf).astype(BF)
        emit_rows(hid,hid_o,r,0).start()
        return 0
    lax.fori_loop(0,L//RB,up_block,0)
    late(4)
    def block(r,_):
        rows=pl.ds(pl.multiple_of(r*RB,RB),RB)
        x1=dr1[rows,:]; inv1=inv[rows,0:1]
        a=x1*row(1)+row(2)
        mlp=row(3)
        for tt in range(2):
            mlp=mlp+dot(hid[rows,tt*4*PIECE:(tt+1)*4*PIECE],W(tt,9,4),1,1)
        x2,inv2=ln_stats(a+mlp)
        out[rows,:]=(x2*row(4)+row(5)).astype(BF)
        @pl.when(r<2)
        def _(): emits(r)[1].start()
        dy=jnp.where(own[rows,0:1]>0.5,cot[rows,:].astype(F32),0.0)
        sums_o[4:5,:]+=csum(dy*x2); sums_o[5:6,:]+=csum(dy)
        dr2=ln_back(row(4),dy,x2,inv2)
        sums_o[3:4,:]+=csum(dr2)
        dmb=dr2.astype(BF)
        dmbT[:,rows]=dmb.T
        da=dr2
        for tt in range(2):
            for j in range(4):
                cc=pl.ds((tt*4+j)*PIECE,PIECE)
                du=dot(dmb,W(tt,9+j),1,0)*gp[rows,cc].astype(F32)
                bup_o[0:1,cc]+=csum(du)
                gp[rows,cc]=du.astype(BF)
            da=da+dot(gp[rows,tt*4*PIECE:(tt+1)*4*PIECE],W(tt,5,4),1,1)
        emit_rows(gp,dub_o,r,1).start()
        sums_o[1:2,:]+=csum(da*x1); sums_o[2:3,:]+=csum(da)
        d1=ln_back(row(1),da,x1,inv1)
        sums_o[0:1,:]+=csum(d1)
        dr1[rows,:]=d1
        drb=d1.astype(BF)
        drbT[:,rows]=drb.T
        for tt in range(2):
            dob[rows,tt*PIECE:(tt+1)*PIECE]=dot(drb,W(tt,4),1,0).astype(BF)
        for cp in emits(r)[0]: cp.start()
        return 0
    lax.fori_loop(0,L//RB,block,0)
    for r in range(L//RB):
        emit_rows(hid,hid_o,r,0).wait(); emit_rows(gp,dub_o,r,1).wait()

def front(ts,masters,tokens,cotangent,seg,cid=0):
    DMA=pltpu.SemaphoreType.DMA; n=len(GCH)
    V=lambda s,d=BF:pltpu.VMEM(s,d)
    A=pl.BlockSpec(memory_space=pl.ANY); M=pl.BlockSpec(memory_space=pltpu.VMEM)
    big=lambda s,d=BF:jax.ShapeDtypeStruct(s,d)
    row=(L,D); tr=(D,L)
    G6=lambda w_:(NT,NZ,NX,NC,ROWS,w_)
    return pl.pallas_call(front_kernel,
        in_specs=[pl.BlockSpec(memory_space=pltpu.SMEM)]+[M]*9+[A,A,M],
        out_specs=[A]*17+[M]*4,
        out_shape=[big(row),big(row),big(row),big(row),big((6,2,L),F32),big(row),big((512,D)),big(tr),big(tr),big(tr),big((L,4*D)),big((L,4*D)),
            big(row,F32),big(row),big(tr),big(G6(3*PIECE)),big(G6(PIECE)),big((8,D),F32),big((8,4*D),F32),big((8,512),F32),big((16,256))],
        scratch_shapes=[V(G6(WIDE)),V(row),V(row),V(row),V(row),V(row),V(row),V((6,2,L),F32),V((L,128),F32),V((L,128)),V((32,D),F32),V((8,D),F32),
            V(tr),V((L,4*D)),V((L,4*D)),V((L,128),F32),V(tr),V(tr),V(tr),V(row,F32),V((ROWS,PIECE),F32),
            DMA((n,3)),DMA((n,3)),DMA((n,4)),DMA((n,4)),DMA((n,)),DMA((n,)),DMA((2,)),DMA((8,)),DMA((2,L//RB)),DMA((6,L//RB)),DMA((2,L//RB))],
        compiler_params=pltpu.CompilerParams(collective_id=cid,has_side_effects=True,vmem_limit_bytes=63*2**20),name="front")(ts,*masters,tokens,cotangent,seg)

def group(g,r,w,a): return dict(g=g,r=r,w=w,a=a)
RGR=[group(0,0,768,-1),group(768,768,768,0),group(1536,1536,768,-1),group(2304,2304,768,0),group(3072,3072,384,-1),
     group(3456,3456,384,0),group(3840,3840,384,-1),group(0,4224,384,128)]
RW=12*PIECE
GBW=11*PIECE
_a=_b=_p=_q=0
for _g in RGR:
    if _g["a"]>=0:
        _g["ao"]=_a; _g["bo"]=_b; _g["po"]=_p; _a+=_g["a"]; _b+=_g["w"]-_g["a"]; _p+=_g["w"]
    else:
        _g["qo"]=_q; _q+=_g["w"]
RWA,RWB,RWP,RWQ=max(_a,128),_b,_p,_q

def scatter_steps(gb,rs,ra,rc,rb,rz,rx,rq,ry,red,ss,sr,as_,ar,bs,br,zs,zr):
    z,x,c,t=place(); zp,xp,yp,sp=peers()
    def go(cs):
        for q in cs: q.start()
    def got(cs):
        for q in cs: q.wait_recv()
    def sums(a,b): return a+b
    def sl(i):
        q=RGR[i]; g,r,w,a=q["g"],q["r"],q["w"],q["a"]
        k=dict(g=pl.ds(g,w),r=pl.ds(r,w))
        if a>=0: k.update(ga=pl.ds(g,a),gb=pl.ds(g+a,w-a),a=pl.ds(q["ao"],a),b=pl.ds(q["bo"],w-a),p=pl.ds(q["po"],w),pa=pl.ds(q["po"],a),pb=pl.ds(q["po"]+a,w-a))
        else: k.update(q=pl.ds(q["qo"],w))
        return k
    def S(i):
        k=sl(i); return [rcopy(gb.at[:,:,:,1-c,:,k["g"]],rs.at[:,:,:,:,k["r"]],ss.at[i],sr.at[i],sp)]
    def A(i):
        k=sl(i)
        if "q" in k: return [rcopy(gb.at[:,:,1-x,c,:,k["g"]],rx.at[:,:,:,k["q"]],as_.at[i,0],ar.at[i,0],xp)]
        one=[rcopy(gb.at[:,:,1-x,c,:,k["ga"]],ra.at[:,:,:,k["a"]],as_.at[i,0],ar.at[i,0],xp)] if RGR[i]["a"] else []
        return one+[rcopy(gb.at[1-t,:,:,c,:,k["gb"]],rc.at[:,:,:,k["b"]],as_.at[i,1],ar.at[i,1],yp)]
    def zdst(d): return lax.rem(z+d+1,NZ)
    def B(i):
        k=sl(i)
        if "q" in k: return [rcopy(gb.at[:,zdst(d),x,c,:,k["g"]],rq.at[d,:,:,k["q"]],bs.at[i,d],br.at[i,d],zp[d]) for d in range(3)]
        one=[rcopy(gb.at[1-t,:,x,c,:,k["ga"]],rb.at[:,:,k["pa"]],bs.at[i,0],br.at[i,0],yp)] if RGR[i]["a"] else []
        return one+[rcopy(gb.at[t,:,1-x,c,:,k["gb"]],rb.at[:,:,k["pb"]],bs.at[i,1],br.at[i,1],xp)]
    def Z(i):
        k=sl(i)
        if "q" in k: return [rcopy(gb.at[1-t,z,x,c,:,k["g"]],ry.at[:,k["q"]],zs.at[i,0],zr.at[i,0],yp)]
        return [rcopy(gb.at[t,zdst(d),x,c,:,k["g"]],rz.at[d,:,k["p"]],zs.at[i,d],zr.at[i,d],zp[d]) for d in range(3)]
    def s_to_a(i):
        got(S(i)); k=sl(i)
        def body(n,_):
            tt=lax.div(n,8); zz=lax.rem(lax.div(n,2),4); xx=lax.rem(n,2)
            gb[tt,zz,xx,c,:,k["g"]]=sums(gb[tt,zz,xx,c,:,k["g"]],rs[tt,zz,xx,:,k["r"]])
            return 0
        lax.fori_loop(0,16,body,0)
        go(A(i))
    def a_to_b(i):
        got(A(i)); k=sl(i)
        def body(n,_):
            a=lax.div(n,4); b=lax.rem(n,4)
            if "q" in k:
                gb[a,b,x,c,:,k["g"]]=sums(gb[a,b,x,c,:,k["g"]],rx[a,b,:,k["q"]])
            else:
                if RGR[i]["a"]: gb[a,b,x,c,:,k["ga"]]=sums(gb[a,b,x,c,:,k["ga"]],ra[a,b,:,k["a"]])
                zz=lax.div(n,2); xx=lax.rem(n,2)
                gb[t,zz,xx,c,:,k["gb"]]=sums(gb[t,zz,xx,c,:,k["gb"]],rc[zz,xx,:,k["b"]])
            return 0
        lax.fori_loop(0,8,body,0)
        go(B(i))
    def b_to_z(i):
        got(B(i)); k=sl(i)
        if "q" in k:
            for a in range(2):
                acc=gb[a,z,x,c,:,k["g"]].astype(F32)
                for d in range(3): acc=acc+rq[d,a,:,k["q"]].astype(F32)
                gb[a,z,x,c,:,k["g"]]=acc.astype(BF)
        else:
            def body(n,_):
                gb[t,n,x,c,:,k["g"]]=sums(gb[t,n,x,c,:,k["g"]],rb[n,:,k["p"]])
                return 0
            lax.fori_loop(0,4,body,0)
        go(Z(i))
    def z_end(i):
        got(Z(i)); k=sl(i)
        acc=gb[t,z,x,c,:,k["g"]].astype(F32)
        if "q" in k: acc=acc+ry[:,k["q"]].astype(F32)
        else:
            for d in range(3): acc=acc+rz[d,:,k["p"]].astype(F32)
        red[:,k["r"]]=acc
    def drain(i):
        for q in S(i)+A(i)+B(i)+Z(i): q.wait_send()
    return S,go,s_to_a,a_to_b,b_to_z,z_end,drain

def attend_back(q_ref,k_ref,v_ref,do_ref,lse_ref,bias_ref,hvs,i,bq=512):
    lane=lax.broadcasted_iota(jnp.int32,(1,128),1)
    cs=pl.ds(pl.multiple_of(i*128,128),128)
    kp=k_ref[:,cs]; vp=v_ref[:,cs]; bias=bias_ref[...]
    khs=[];vhs=[]
    for h in range(2):
        sel=(lane//64)==h; one=lane==(64*(1-h))
        khs.append(jnp.where(sel,kp,jnp.where(one,bias,jnp.zeros_like(kp))))
        vhs.append(jnp.where(sel,vp,jnp.zeros_like(vp)))
    kT=kp.T
    dk=[None,None];dv=[None,None]; sq=None
    for qi in range(L//bq):
        rows=pl.ds(qi*bq,bq)
        qp=q_ref[rows,cs]*0.125; dop=do_ref[rows,cs]
        dqT=[]
        for h in range(2):
            sel=(lane//64)==h; one=lane==(64*(1-h))
            zero=jnp.zeros_like(qp)
            qh=jnp.where(sel,qp,jnp.where(one,jnp.ones_like(qp),zero))
            doh=jnp.where(sel,dop,zero)
            qz=jnp.where(sel,qp,zero)
            sT=dot(khs[h],qh,1,1)
            p=jnp.exp(sT-lse_ref[i,h:h+1,qi*bq:(qi+1)*bq])
            dp=dot(vhs[h],doh,1,1)
            d=jnp.sum(p*dp,axis=0,keepdims=True)
            ds=(p*(dp-d)).astype(BF)
            pb=p.astype(BF)
            a=dot(pb,doh,1,0); dv[h]=a if dv[h] is None else dv[h]+a
            a=dot(ds,qz,1,0); dk[h]=a if dk[h] is None else dk[h]+a
            dqT.append(dot(kT[h*64:(h+1)*64],ds,1,0))
        dq=jnp.concatenate(dqT,axis=0).T*0.125
        s=jnp.sum(dq,axis=0,keepdims=True); sq=s if sq is None else sq+s
        q_ref[rows,cs]=dq.astype(BF)
    k_ref[:,cs]=(dk[0]+dk[1]).astype(BF)
    dvv=dv[0]+dv[1]
    v_ref[:,cs]=dvv.astype(BF)
    hvs[0:1,cs]=sq
    hvs[1:2,cs]=jnp.sum(dvv,axis=0,keepdims=True)

def unspread(src,w,n):
    lane=lax.broadcasted_iota(jnp.int32,(16,128),1)
    tile,s=divmod(n*w,128)
    wide=src[:,tile*128:(tile+2)*128]
    if s: wide=pltpu.roll(wide,256-s,1)
    return jnp.where(lane<w,wide[:,:128],0.0)

def back_kernel(q_h,k_h,v_h,do_h,o_h,lse_h,dmbT_h,abT_h,drbT_h,hbT_h,hid_h,dub_h,dr1_h,wqkv_h,aux_h,out_h,seg_ref,feat_ref,sums_ref,bup_ref,time_ref,
        in_o,inp_o,outp_o,red,w2g,w1g,vecg,tot,
        q,k,v,do,lse,bias,st,ta,tb,wq,dr1,aux,ow,hvs,lvs,hsrc,bsrc,nv,nr,nz,vg,vs,vx,vz,vy,sg,mat,aT,fT,
        gb,rs,ra,rc,rb,rz,rx,rq,ry,ss,sr,as_,ar,bs,br,zs,zr,ls,ts,xs,ns,nrs,os,vsm,vrm,gsm,grm):
    z,x,c,t=place(); zp,xp,yp,sp=peers()
    inw=do
    S,go,s_to_a,a_to_b,b_to_z,z_end,drain=scatter_steps(gb,rs,ra,rc,rb,rz,rx,rq,ry,red,ss,sr,as_,ar,bs,br,zs,zr)
    def load(src,dst,n):
        return pltpu.make_async_copy(src,dst,ls.at[n])
    LQ=[load(q_h,q,0),load(k_h,k,1),load(v_h,v,2),load(do_h,do,3),load(lse_h,lse,4)]
    LW=[load(wqkv_h,wq,5),load(dr1_h,dr1,6),load(aux_h,aux,7)]
    def tcopy(src,buf,n): return pltpu.make_async_copy(src,buf,ts.at[n])
    def stage(src,cols,n):
        return [pltpu.make_async_copy(src.at[:,pl.ds(cs,PIECE)],st.at[s],ts.at[n+s]) for s,cs in enumerate(cols)]
    pc=lambda j:[tt*4*PIECE+jj*PIECE for jj in (j,j+1) for tt in range(2)]
    ST=[stage(hid_h,pc(0),4),stage(hid_h,pc(2),8),stage(dub_h,pc(0),4),stage(dub_h,pc(2),8),stage(o_h,[0,PIECE],4)]
    for q_ in [tcopy(dmbT_h,ta,0),*ST[0],tcopy(abT_h,tb,1)]+LQ+LW: q_.start()
    greet()
    lo=load(out_h.at[pl.ds(512,512),:],ow,9); lo.start(); lo.wait()
    cout=[rcopy(ow.at[pl.ds(n*256,256),:],outp_o.at[pl.ds(n*256,256),:],os.at[0,n],os.at[1,n],yp) for n in range(2)]
    for q_ in cout: q_.start()
    seg=seg_ref[:,pl.ds(pl.multiple_of(t*512,128),L)]
    bias[...]=jnp.broadcast_to(jnp.where(seg==t,0.0,-1e30),(128,L)).T.astype(BF)
    def compute(i,lhs,n):
        base=RGR[i]["g"]
        for q_ in ST[i]: q_.wait()
        def body(s,_):
            tt=lax.rem(s,2); cs=pl.ds(pl.multiple_of(base+lax.div(s,2)*PIECE,128),PIECE)
            gb[tt,:,:,:,:,cs]=dot(lhs[...],st[s],1,0).astype(BF).reshape(NZ,NX,NC,ROWS,PIECE)
            return 0
        lax.fori_loop(0,n,body,0)
        if i+1<len(ST):
            for q_ in ST[i+1]: q_.start()
        go(S(i))
    tcopy(dmbT_h,ta,0).wait()
    compute(0,ta,4)
    compute(1,ta,4)
    tcopy(drbT_h,ta,2).start()
    tcopy(abT_h,tb,1).wait()
    s_to_a(0)
    compute(2,tb,4)
    s_to_a(1)
    compute(3,tb,4)
    tcopy(hbT_h,tb,3).start()
    s_to_a(2)
    tcopy(drbT_h,ta,2).wait()
    compute(4,ta,2)
    s_to_a(3); a_to_b(0)
    for q_ in LQ: q_.wait()
    tcopy(hbT_h,tb,3).wait()
    def quad(i,n):
        base=RGR[i]["g"]
        for tt in range(2):
            o_=tt*PIECE+n*128
            rhs=jnp.concatenate([q[:,o_:o_+128],k[:,o_:o_+128],v[:,o_:o_+128]],axis=1)
            gb[tt,:,:,:,:,base:base+PIECE]=dot(tb[...],rhs,1,0).astype(BF).reshape(NZ,NX,NC,ROWS,PIECE)
        go(S(i))
    def pair(i,_):
        @pl.when(i==1)
        def _():
            s_to_a(4); a_to_b(1)
        @pl.when(i==2)
        def _():
            a_to_b(2); b_to_z(0); quad(5,0)
        @pl.when(i==3)
        def _():
            s_to_a(5); a_to_b(3); b_to_z(1)
        @pl.when(i==4)
        def _():
            a_to_b(4); z_end(0); b_to_z(2); quad(6,1)
        @pl.when(i==5)
        def _():
            s_to_a(6); a_to_b(5); b_to_z(3); z_end(1)
        attend_back(q,k,v,do,lse,bias,hvs,lax.div(i,2)+3*lax.rem(i,2))
        return 0
    lax.fori_loop(0,6,pair,0)
    z_end(2); b_to_z(4)
    drain(0)
    quad(7,2)
    a_to_b(6); z_end(3); b_to_z(5)
    for q_ in LW: q_.wait()
    lvs[...]=jnp.zeros((16,D+128),F32)
    lvs[0:6,0:D]=sums_ref[0:6,:]
    def far(r):
        rows=pl.ds(pl.multiple_of(r*RB,RB),RB)
        return rcopy(inw.at[rows,:],inp_o.at[rows,:],xs.at[0,r],xs.at[1,r],yp)
    def rows_body(r,_):
        rows=pl.ds(pl.multiple_of(r*RB,RB),RB)
        acc=dr1[rows,:]
        for n,ref in enumerate((q,k,v)):
            for tt in range(2):
                acc=acc+dot(ref[rows,tt*PIECE:(tt+1)*PIECE],wq[tt,:,:,:,:,n*PIECE:(n+1)*PIECE].reshape(D,PIECE),1,1)
        inw[rows,:]=acc.astype(BF)
        lvs[6:7,0:D]+=jnp.sum(acc,axis=0,keepdims=True)
        return 0
    lax.fori_loop(0,2,rows_body,0)
    s_to_a(7)
    lax.fori_loop(2,L//RB,rows_body,0)
    a_to_b(7)
    far(0).start(); far(1).start()
    cinl=pltpu.make_async_copy(inw,in_o,ls.at[8]); cinl.start()
    dtb=lvs[6:7,0:D].astype(BF)
    inner=time_ref[0:1,:]; sig=time_ref[1:2,:]
    w2=jnp.concatenate([aux[0,:,:,:,0:32,:].reshape(512,PIECE),aux[1,:,:,:,0:32,:].reshape(512,PIECE)],axis=1)
    dinner=dot(jnp.broadcast_to(dtb,(16,D)),w2,1,1)[0:1]*(sig*(1.0+inner*(1.0-sig)))
    act=(inner*sig).astype(BF).astype(F32)
    sg[t,z,x,c,0:1,:]=jnp.concatenate([act,dtb.astype(F32),dinner,feat_ref[0:1,:].astype(F32)],axis=1)
    def pass_on(k):
        src=[sg.at[t,z,x,c],sg.at[t,:,x,c],sg.at[t,:,:,c],sg.at[:,:,:,c]][k]
        if k==0: return [rcopy(src,src,gsm.at[d],grm.at[d],zp[d]) for d in range(3)]
        return [rcopy(src,src,gsm.at[2+k],grm.at[2+k],(xp,yp,sp)[k-1])]
    def vec_send(k):
        if k==0: return [rcopy(vg.at[:,:,:,1-c],vs,vsm.at[0],vrm.at[0],sp)]
        if k==1: return [rcopy(vg.at[:,:,1-x,c],vx,vsm.at[1],vrm.at[1],xp)]
        if k==2: return [rcopy(vg.at[:,lax.rem(z+d+1,NZ),x,c],vz.at[d],vsm.at[2+d],vrm.at[2+d],zp[d]) for d in range(3)]
        return [rcopy(vg.at[1-t,z,x,c],vy,vsm.at[5],vrm.at[5],yp)]
    def small(k):
        if k>0:
            for q_ in pass_on(k-1)+vec_send(k-1): q_.wait_recv()
        if k==1: vg[:,:,:,c]=vg[:,:,:,c]+vs[...]
        if k==2: vg[:,:,x,c]=vg[:,:,x,c]+vx[...]
        if k==3:
            acc=vg[:,z,x,c].astype(F32)
            for d in range(3): acc=acc+vz[d].astype(F32)
            vg[:,z,x,c]=acc.astype(BF)
        if k<4:
            for q_ in pass_on(k)+vec_send(k): q_.start()
        else: vecg[...]=vg[t,z,x,c].astype(F32)+vy[...].astype(F32)
    hsrc[...]=jnp.zeros((16,2*(PIECE+128)),F32)
    for tt in range(2):
        o0=tt*(PIECE+128); cc=slice(tt*PIECE,(tt+1)*PIECE)
        hsrc[7:9,o0:o0+PIECE]=hvs[0:2,cc]
        for j in range(4): hsrc[9+j:10+j,o0:o0+PIECE]=bup_ref[0:1,(tt*4+j)*PIECE:(tt*4+j+1)*PIECE]
    bsrc[...]=jnp.zeros((16,640),F32)
    bsrc[13:14,0:512]=dinner
    for n in range(16):
        both=unspread(lvs[...],48,n)+unspread(bsrc[...],32,n)
        for tt in range(2):
            vg[tt,n//4,(n//2)%2,n%2]=(both+unspread(hsrc[:,tt*(PIECE+128):(tt+1)*(PIECE+128)],24,n)).astype(BF)
    small(0)
    b_to_z(6); z_end(4); z_end(5)
    small(1)
    b_to_z(7)
    small(2)
    z_end(6)
    small(3)
    far(2).start()
    z_end(7)
    small(4)
    for n in range(32): mat[n:n+1,:]=sg[n//16,(n//4)%4,(n//2)%2,n%2]
    aT[...]=mat[:,0:512].T
    fT[...]=mat[:,1792:2048].T
    dp=lax.axis_index("dp")
    g2=dot(aT[pl.ds(pl.multiple_of(dp*32,32),32),:].astype(BF),mat[:,512:1280].astype(BF),1,0)
    g1=dot(fT[pl.ds(pl.multiple_of(dp*16,16),16),:].astype(BF),mat[:,1280:1792].astype(BF),1,0)
    w2g[...]=g2; w1g[...]=g1
    vv=vecg[...]
    ri=lax.broadcasted_iota(jnp.int32,(16,128),0)
    big=red[...]
    part=jnp.sum(big*big)+0.5*(jnp.sum(g2*g2)+jnp.sum(g1*g1))+jnp.sum(jnp.where((ri<7)|(ri==13),0.5,1.0)*vv*vv)
    nv[0]=jnp.full((8,128),part,F32)
    def swap(s,peer):
        cp=rcopy(nv.at[s],nr.at[s],ns.at[s],nrs.at[s],peer); cp.start(); cp.wait()
        nv[s+1]=nv[s]+nr[s]
    swap(0,yp)
    far(3).start()
    swap(1,xp); swap(2,sp)
    cz=[rcopy(nv.at[3],nz.at[z],ns.at[3+d],nrs.at[3+d],zp[d]) for d in range(3)]
    for q_ in cz: q_.start()
    nz[z]=nv[3]
    for q_ in cz: q_.wait()
    tot[...]=((nz[0]+nz[1])+nz[2])+nz[3]
    cinl.wait()
    for q_ in cout: q_.wait()
    for k_ in range(4):
        for q_ in pass_on(k_)+vec_send(k_): q_.wait_send()
    for r in range(4): far(r).wait()
    for i in range(1,8): drain(i)

def back(q,k,v,dob,o,lse,dmbT,abT,drbT,hbT,hid,dub,dr1,wqkv,aux,out_win,seg,featp,sums,bups,tstate,cid=1):
    DMA=pltpu.SemaphoreType.DMA; n=len(RGR)
    V=lambda s,d=BF:pltpu.VMEM(s,d)
    A=pl.BlockSpec(memory_space=pl.ANY); M=pl.BlockSpec(memory_space=pltpu.VMEM)
    sd=jax.ShapeDtypeStruct; row=(L,D); tr=(D,L)
    return pl.pallas_call(back_kernel,
        in_specs=[A]*16+[M]*5,out_specs=[A]*3+[M]*5,
        out_shape=[sd(row,BF),sd(row,BF),sd((512,D),BF),sd((ROWS,RW),F32),sd((32,D),F32),sd((16,512),F32),sd((16,128),F32),sd((8,128),F32)],
        scratch_shapes=[V(row),V(row),V(row),V(row),V((6,2,L),F32),V((L,128)),V((4,L,PIECE)),V(tr),V(tr),V((NT,NZ,NX,NC,ROWS,3*PIECE)),V(row,F32),
            V((NT,NZ,NX,NC,ROWS,PIECE)),V((512,D)),V((8,D),F32),V((16,D+128),F32),V((16,2*(PIECE+128)),F32),V((16,640),F32),
            V((4,8,128),F32),V((3,8,128),F32),V((4,8,128),F32),
            V((NT,NZ,NX,NC,16,128)),V((NT,NZ,NX,16,128)),V((NT,NZ,16,128)),V((3,NT,16,128)),V((16,128)),V((NT,NZ,NX,NC,1,2048),F32),V((32,2048),F32),V((512,32),F32),V((256,32),F32),
            V((NT,NZ,NX,NC,ROWS,GBW)),V((NT,NZ,NX,ROWS,RW)),V((NT,NZ,ROWS,RWA)),V((NZ,NX,ROWS,RWB)),V((NZ,ROWS,RWP)),V((3,ROWS,RWP)),
            V((NT,NZ,ROWS,RWQ)),V((3,NT,ROWS,RWQ)),V((ROWS,RWQ)),
            DMA((n,)),DMA((n,)),DMA((n,2)),DMA((n,2)),DMA((n,3)),DMA((n,3)),DMA((n,3)),DMA((n,3)),DMA((10,)),DMA((12,)),DMA((2,4)),DMA((6,)),DMA((6,)),DMA((2,2)),DMA((6,)),DMA((6,)),DMA((6,)),DMA((6,))],
        compiler_params=pltpu.CompilerParams(collective_id=cid,has_side_effects=True,vmem_limit_bytes=63*2**20),name="back")(
            q,k,v,dob,o,lse,dmbT,abT,drbT,hbT,hid,dub,dr1,wqkv,aux,out_win,seg,featp,sums,bups,tstate)

def greet_out():
    zp,xp,yp,sp=peers()
    bar=pltpu.get_barrier_semaphore()
    for d in zp+[xp,yp,sp]:
        pl.semaphore_signal(bar,inc=1,device_id=d,device_id_type=MESH)
def greet_in():
    pl.semaphore_wait(pltpu.get_barrier_semaphore(),6)

def update_kernel(*refs):
    red,w2g,w1g,vecg,tot,seg_ref,ow,op,op2,iw,ip=refs[:11]
    hbm=refs[11:38]
    out_o,in_o,norm_o=refs[38:41]
    far=refs[41:68]
    ps,ns=refs[68:95],refs[95:122]
    ms,vs,avs=ps[:9],ps[9:18],ps[18:]
    nm,nv,na=ns[:9],ns[9:18],ns[18:]
    mine,theirs,mid,sem,psem,nsem=refs[122:]
    pin=[pltpu.make_async_copy(a,b,psem.at[n]) for n,(a,b) in enumerate(zip(hbm,ps))]
    for q in pin: q.start()
    t=lax.axis_index("tensor")
    half=lambda k:pl.ds(pl.multiple_of(k*512,512),512)
    ins=[]
    for n,(w,ps_) in enumerate(((ow,(op,op2)),(iw,(ip,)))):
        ins.append(pltpu.make_async_copy(w,mine.at[n],sem.at[n,0]))
        step=L//len(ps_)
        ins+=[pltpu.make_async_copy(p,theirs.at[n,pl.ds(m*step,step),:],sem.at[n,5+m]) for m,p in enumerate(ps_)]
    for q in ins: q.start()
    norm=jnp.sqrt(tot[...])
    norm_o[0,0]=norm[0,0]
    factor=(1.0/jnp.maximum(norm,1.0))[0:1,0:1]
    rate=4.0*math.sqrt(MPARAMS/D)
    def upd(i,idx,g):
        sc=g*factor
        vel=MOMENTUM*vs[i][idx]+sc
        fm=ms[i][idx]-rate*(sc+MOMENTUM*vel)
        nv[i][idx]=vel; nm[i][idx]=fm
        na[i][idx]=AVERAGE_DECAY*avs[i][idx]+(1.0-AVERAGE_DECAY)*fm
    al=slice(None)
    for q in pin: q.wait()
    nout=[pltpu.make_async_copy(a,b,nsem.at[n]) for n,(a,b) in enumerate(zip(ns,far))]
    def flush(i):
        for n in (i,i+9,i+18): nout[n].start()
    for n in range(3):
        for c in range(3):
            b=9*PIECE+n*PIECE+c*128
            upd(0,(c,al,slice(n*128,(n+1)*128)),red[:,b:b+128])
    flush(0)
    upd(1,(al,al),red[:,8*PIECE:9*PIECE])
    flush(1)
    for j in range(4):
        upd(2,(al,j,al),red[:,(4+j)*PIECE:(5+j)*PIECE])
        upd(3,(j,),red[:,j*PIECE:(j+1)*PIECE])
    flush(2); flush(3)
    upd(4,(al,al),w1g[0:8,:])
    upd(5,(al,al),w2g[...])
    upd(6,(al,al),vecg[13:14,0:32])
    upd(7,(al,0,al),vecg[7:13,0:24])
    upd(8,(al,al),vecg[0:7,0:48])
    for i in range(4,9): flush(i)
    own=jnp.broadcast_to(jnp.where(seg_ref[:,512:1024]==t,1.0,0.0),(128,512)).T[:,0:1]>0.5
    for q in ins: q.wait()
    last=[]
    for n,o in enumerate((out_o,in_o)):
        last+=[pltpu.make_async_copy(mine.at[n,half(t),:],o.at[half(2*t),:],sem.at[n,2]),pltpu.make_async_copy(theirs.at[n,half(1-t),:],o.at[half(2*(1-t)),:],sem.at[n,3])]
        mid[n]=jnp.where(own,mine[n,half(1-t),:].astype(F32),theirs[n,half(t),:].astype(F32)).astype(BF)
        last.append(pltpu.make_async_copy(mid.at[n],o.at[pl.ds(512,512),:],sem.at[n,4]))
        for q in last[-3:]: q.start()
    for q in last+nout: q.wait()

def update(red,w2g,w1g,vecg,tot,seg,ow,op,op2,iw,ip,masters,moments,averages):
    A=pl.BlockSpec(memory_space=pl.ANY); M=pl.BlockSpec(memory_space=pltpu.VMEM)
    sd=jax.ShapeDtypeStruct
    ps=[sd(m.shape,F32) for m in masters]
    whole=sd((PACK,D),BF)
    return pl.pallas_call(update_kernel,in_specs=[M]*6+[A]*5+[A]*27,out_specs=[A,A,pl.BlockSpec(memory_space=pltpu.SMEM)]+[A]*27,
        out_shape=[whole,whole,sd((1,1),F32)]+ps*3,
        scratch_shapes=[pltpu.VMEM(p.shape,F32) for p in ps*6]+[pltpu.VMEM((2,L,D),BF),pltpu.VMEM((2,L,D),BF),pltpu.VMEM((2,512,D),BF),pltpu.SemaphoreType.DMA((2,7)),pltpu.SemaphoreType.DMA((27,)),pltpu.SemaphoreType.DMA((27,))],
        compiler_params=pltpu.CompilerParams(vmem_limit_bytes=63*2**20),name="upd")(red,w2g,w1g,vecg,tot,seg,ow,op,op2,iw,ip,*masters,*moments,*averages)

def shards_fast(tokens,cotangent,segment_ids,timesteps,*params):
    def turn(n,p): return {0:lambda:p.transpose(1,0,2),1:lambda:p.T,3:lambda:p.transpose(0,2,1),6:lambda:p.reshape(1,-1)}.get(n,lambda:p)()
    def back_turn(n,p): return {0:lambda:p.transpose(1,0,2),1:lambda:p.T,3:lambda:p.transpose(0,2,1),6:lambda:p.reshape(-1)}.get(n,lambda:p)()
    line=lambda ps:[turn(n,p) for n,p in enumerate(ps)]
    masters,moments,averages=line(params[:9]),line(params[9:18]),line(params[18:])
    q,k,v,o,lse,out_win,out_peer,dmbT,abT,drbT,hid,dub,dr1,dob,hbT,wq6,aux6,sums,bups,tstate,featp=front(timesteps,masters,tokens,cotangent,segment_ids)
    in_win,in_peer,out_peer2,red,w2g,w1g,vecg,total=back(q,k,v,dob,o,lse,dmbT,abT,drbT,hbT,hid,dub,dr1,wq6,aux6,out_win,segment_ids,featp,sums,bups,tstate)
    res=update(red,w2g,w1g,vecg,total,segment_ids,out_win,out_peer,out_peer2,in_win,in_peer,masters,moments,averages)
    return (res[0],res[1],res[2].reshape(()))+tuple(back_turn(n%9,r) for n,r in enumerate(res[3:]))


def solution(mesh):
    fast=dict(mesh.shape)=={'dp':16,'tensor':2}
    return jax.shard_map(
        shards_fast if fast else shards_any,
        mesh=mesh,
        in_specs=(
            P("dp", None),
            P("dp", None),
            P("dp", None),
            P("dp", None),
            P("dp", None, "tensor"),
            P("tensor", "dp"),
            P("dp", None, "tensor"),
            P(None, "tensor", "dp"),
            P("dp", None),
            P("dp", None),
            P("dp"),
            P(None, "tensor", "dp"),
            P(None, "dp"),
            P("dp", None, "tensor"),
            P("tensor", "dp"),
            P("dp", None, "tensor"),
            P(None, "tensor", "dp"),
            P("dp", None),
            P("dp", None),
            P("dp"),
            P(None, "tensor", "dp"),
            P(None, "dp"),
            P("dp", None, "tensor"),
            P("tensor", "dp"),
            P("dp", None, "tensor"),
            P(None, "tensor", "dp"),
            P("dp", None),
            P("dp", None),
            P("dp"),
            P(None, "tensor", "dp"),
            P(None, "dp"),
        ),
        out_specs=(
            P("dp", None),
            P("dp", None),
            P(),
            P("dp", None, "tensor"),
            P("tensor", "dp"),
            P("dp", None, "tensor"),
            P(None, "tensor", "dp"),
            P("dp", None),
            P("dp", None),
            P("dp"),
            P(None, "tensor", "dp"),
            P(None, "dp"),
            P("dp", None, "tensor"),
            P("tensor", "dp"),
            P("dp", None, "tensor"),
            P(None, "tensor", "dp"),
            P("dp", None),
            P("dp", None),
            P("dp"),
            P(None, "tensor", "dp"),
            P(None, "dp"),
            P("dp", None, "tensor"),
            P("tensor", "dp"),
            P("dp", None, "tensor"),
            P(None, "tensor", "dp"),
            P("dp", None),
            P("dp", None),
            P("dp"),
            P(None, "tensor", "dp"),
            P(None, "dp"),
        ),
        check_vma=False,
    )
```

```python
import functools
import math

import jax
import jax.numpy as jnp
from jax import lax
from jax.experimental import pallas as pl
from jax.experimental.pallas import tpu as pltpu
from jax.sharding import PartitionSpec as P

D = 768
HD = 64
TD = 128
SEGS = 2
PACK = 1536
MPARAMS = 7536640


EPSILON = 1e-05
MOMENTUM = 0.5
AVERAGE_DECAY = 0.5


def layer_norm(values, gain_vec, shift_vec):
    centre = jnp.mean(values, axis=-1, keepdims=True)
    centred = values - centre
    spread = jnp.mean(centred * centred, axis=-1, keepdims=True)
    return centred * lax.rsqrt(spread + EPSILON) * gain_vec + shift_vec


def time_features(step_ids, feat_width):
    midpoint = feat_width // 2
    frequency = jnp.exp(-math.log(10000.0) * jnp.arange(midpoint, dtype=jnp.float32) / midpoint)
    angles = step_ids.astype(jnp.float32)[..., None] * frequency
    return jnp.concatenate([jnp.cos(angles), jnp.sin(angles)], axis=-1)


def gelu_exact(values):
    return jax.nn.gelu(values, approximate=False)


def head_slice(matrix, head_index):
    return lax.dynamic_slice_in_dim(matrix, head_index * HD, HD, 1)


def merge_heads(stacked):
    return stacked.transpose(1, 0, 2).reshape(stacked.shape[1], stacked.shape[0] * stacked.shape[2])


def advance(master, moment, average, grad, factor, step_rate):
    scaled = grad * factor
    velocity = MOMENTUM * moment + scaled
    fresh_master = master - step_rate * (scaled + MOMENTUM * velocity)
    smoothed = AVERAGE_DECAY * average + (1.0 - AVERAGE_DECAY) * fresh_master
    return (fresh_master, velocity, smoothed)


def shards_any(
    tokens,
    cotangent,
    segment_ids,
    timesteps,
    qkv_weight,
    out_weight,
    up_weight,
    down_weight,
    time_inner,
    time_outer,
    time_bias,
    head_vectors,
    layer_vectors,
    qkv_moment,
    out_moment,
    up_moment,
    down_moment,
    inner_moment,
    outer_moment,
    bias_moment,
    head_moment,
    layer_moment,
    qkv_average,
    out_average,
    up_average,
    down_average,
    inner_average,
    outer_average,
    bias_average,
    head_average,
    layer_average,
):
    w_qkv, w_out, w_up, w_down, w_inner, w_outer, b_inner, head_vec, layer_vec = (
        lax.all_gather(qkv_weight.astype(jnp.bfloat16), "dp", axis=0, tiled=True),
        lax.all_gather(out_weight.astype(jnp.bfloat16), "dp", axis=1, tiled=True),
        lax.all_gather(up_weight.astype(jnp.bfloat16), "dp", axis=0, tiled=True),
        lax.all_gather(down_weight.astype(jnp.bfloat16), "dp", axis=2, tiled=True),
        lax.all_gather(time_inner.astype(jnp.bfloat16), "dp", axis=0, tiled=True),
        lax.all_gather(time_outer.astype(jnp.bfloat16), "dp", axis=0, tiled=True),
        lax.all_gather(time_bias.astype(jnp.bfloat16), "dp", axis=0, tiled=True),
        lax.all_gather(head_vectors.astype(jnp.bfloat16), "dp", axis=2, tiled=True),
        lax.all_gather(layer_vectors.astype(jnp.bfloat16), "dp", axis=1, tiled=True),
    )
    local_width = w_out.shape[0]
    head_count = local_width // HD
    packed = tokens.shape[0]
    head_rows = head_vec.astype(jnp.float32).reshape(6, local_width)
    layer_rows = layer_vec.astype(jnp.float32)
    score_scale = 1.0 / math.sqrt(HD)
    block_rows = min(PACK, 512)
    block_count = packed // block_rows
    seg_row = segment_ids[0]
    features = time_features(timesteps[0], TD)
    feature_low = features.astype(jnp.bfloat16)
    inner_pre = jnp.dot(feature_low, w_inner, preferred_element_type=jnp.float32) + b_inner.astype(
        jnp.float32
    )
    silu_out, silu_pull = jax.vjp(jax.nn.silu, inner_pre)
    act_low = silu_out.astype(jnp.bfloat16)
    time_embed = jnp.dot(act_low, w_outer, preferred_element_type=jnp.float32) + layer_rows[6]
    onehot = (seg_row[:, None] == jnp.arange(SEGS, dtype=jnp.int32)[None, :]).astype(jnp.float32)
    hidden0 = tokens.astype(jnp.float32) + jnp.dot(
        onehot, time_embed, precision=lax.Precision.HIGHEST, preferred_element_type=jnp.float32
    )
    hidden_low = hidden0.astype(jnp.bfloat16)
    projected = jnp.einsum("pd,dce->pce", hidden_low, w_qkv, preferred_element_type=jnp.float32)
    queries = (projected[:, 0] + head_rows[0]).astype(jnp.bfloat16)
    keys_low = projected[:, 1].astype(jnp.bfloat16)
    values_low = (projected[:, 2] + head_rows[1]).astype(jnp.bfloat16)

    def block_scores(query_blk, key_all, seg_query):
        raw_scores = (
            jnp.einsum("qd,kd->qk", query_blk, key_all, preferred_element_type=jnp.float32)
            * score_scale
        )
        same_doc = seg_query[:, None] == seg_row[None, :]
        return (raw_scores, same_doc)

    def attend_head(head_index):
        query_h = head_slice(queries, head_index)
        key_h = head_slice(keys_low, head_index)
        value_h = head_slice(values_low, head_index)
        out_blocks = []
        sum_blocks = []
        for block_index in range(block_count):
            first_row = block_index * block_rows
            raw_scores, same_doc = block_scores(
                query_h[first_row : first_row + block_rows],
                key_h,
                seg_row[first_row : first_row + block_rows],
            )
            masked = jnp.where(same_doc, raw_scores, -1e30)
            row_peak = jnp.max(masked, axis=1, keepdims=True)
            exponent = jnp.exp(masked - row_peak)
            row_total = jnp.sum(exponent, axis=1, keepdims=True)
            soft_weights = exponent / row_total
            out_blocks.append(
                jnp.dot(
                    soft_weights.astype(jnp.bfloat16), value_h, preferred_element_type=jnp.float32
                )
            )
            sum_blocks.append((row_peak + jnp.log(row_total))[:, 0])
        return (jnp.concatenate(out_blocks, axis=0), jnp.concatenate(sum_blocks, axis=0))

    head_out, log_sums = lax.map(attend_head, jnp.arange(head_count, dtype=jnp.int32))
    att_low = merge_heads(head_out).astype(jnp.bfloat16)
    attn_partial = jnp.dot(att_low, w_out, preferred_element_type=jnp.float32)
    attn_branch = (
        lax.psum(attn_partial.astype(jnp.bfloat16), "tensor").astype(jnp.float32) + layer_rows[0]
    )
    residual1 = hidden0 + attn_branch
    cot_here = cotangent.astype(jnp.float32)
    normed1, norm1_pull = jax.vjp(layer_norm, residual1, layer_rows[1], layer_rows[2])
    norm_here = normed1.astype(jnp.bfloat16)
    up_pre = (
        jnp.einsum("pd,dje->pje", norm_here, w_up, preferred_element_type=jnp.float32)
        + head_rows[2:]
    )
    gelu_out, gelu_pull = jax.vjp(gelu_exact, up_pre)
    hid_low = gelu_out.astype(jnp.bfloat16)
    down_partial = jnp.einsum("pje,jef->pf", hid_low, w_down, preferred_element_type=jnp.float32)
    mlp_branch = (
        lax.psum(down_partial.astype(jnp.bfloat16), "tensor").astype(jnp.float32) + layer_rows[3]
    )
    result, norm2_pull = jax.vjp(layer_norm, normed1 + mlp_branch, layer_rows[4], layer_rows[5])
    output_here = result.astype(jnp.bfloat16)
    back_r2, back_gain2, back_shift2 = norm2_pull(cot_here)
    part_bdown = jnp.sum(back_r2, axis=0)
    back_r2_here = back_r2.astype(jnp.bfloat16)
    grad_down = jnp.einsum("pje,pf->jef", hid_low, back_r2_here, preferred_element_type=jnp.float32)
    back_hid = jnp.einsum("pf,jef->pje", back_r2_here, w_down, preferred_element_type=jnp.float32)
    (back_up,) = gelu_pull(back_hid)
    grad_bup = jnp.sum(back_up, axis=0)
    back_up_low = back_up.astype(jnp.bfloat16)
    grad_up = jnp.einsum("pd,pje->dje", norm_here, back_up_low, preferred_element_type=jnp.float32)
    back_a_part = jnp.einsum("pje,dje->pd", back_up_low, w_up, preferred_element_type=jnp.float32)
    back_a = lax.psum(back_a_part.astype(jnp.bfloat16), "tensor").astype(jnp.float32) + back_r2
    back_r1, back_gain1, back_shift1 = norm1_pull(back_a)
    grad_bout = jnp.sum(back_r1, axis=0)
    back_r1_low = back_r1.astype(jnp.bfloat16)
    grad_out = jnp.einsum("pe,pf->ef", att_low, back_r1_low, preferred_element_type=jnp.float32)
    back_att = jnp.einsum(
        "pf,ef->pe", back_r1_low, w_out, preferred_element_type=jnp.float32
    ).astype(jnp.bfloat16)

    def head_back(head_index):
        query_h = head_slice(queries, head_index)
        key_h = head_slice(keys_low, head_index)
        value_h = head_slice(values_low, head_index)
        grad_h = head_slice(back_att, head_index)
        lse_h = log_sums[head_index]
        key_grad = jnp.zeros((packed, HD), jnp.float32)
        value_grad = jnp.zeros((packed, HD), jnp.float32)
        query_blocks = []
        for block_index in range(block_count):
            first_row = block_index * block_rows
            query_blk = query_h[first_row : first_row + block_rows]
            raw_scores, same_doc = block_scores(
                query_blk, key_h, seg_row[first_row : first_row + block_rows]
            )
            lse_blk = lse_h[first_row : first_row + block_rows]
            soft_weights = jnp.where(same_doc, jnp.exp(raw_scores - lse_blk[:, None]), 0.0)
            grad_blk = grad_h[first_row : first_row + block_rows]
            value_grad = value_grad + jnp.einsum(
                "qk,qd->kd",
                soft_weights.astype(jnp.bfloat16),
                grad_blk,
                preferred_element_type=jnp.float32,
            )
            weight_grad = jnp.einsum(
                "qd,kd->qk", grad_blk, value_h, preferred_element_type=jnp.float32
            )
            row_inner = jnp.sum(soft_weights * weight_grad, axis=1, keepdims=True)
            score_low = (soft_weights * (weight_grad - row_inner)).astype(jnp.bfloat16)
            query_blocks.append(
                jnp.dot(score_low, key_h, preferred_element_type=jnp.float32) * score_scale
            )
            key_grad = (
                key_grad
                + jnp.einsum("qk,qd->kd", score_low, query_blk, preferred_element_type=jnp.float32)
                * score_scale
            )
        return (jnp.concatenate(query_blocks, axis=0), key_grad, value_grad)

    query_grads, key_grads, value_grads = lax.map(
        head_back, jnp.arange(head_count, dtype=jnp.int32)
    )
    query_grad_all = merge_heads(query_grads)
    key_grad_all = merge_heads(key_grads)
    value_grad_all = merge_heads(value_grads)
    grad_bq = jnp.sum(query_grad_all, axis=0)
    grad_bv = jnp.sum(value_grad_all, axis=0)
    proj_grad_low = jnp.stack([query_grad_all, key_grad_all, value_grad_all], axis=1).astype(
        jnp.bfloat16
    )
    grad_qkv = jnp.einsum(
        "pd,pce->dce", hidden_low, proj_grad_low, preferred_element_type=jnp.float32
    )
    back_h_part = jnp.einsum(
        "pce,dce->pd", proj_grad_low, w_qkv, preferred_element_type=jnp.float32
    )
    back_h0 = lax.psum(back_h_part.astype(jnp.bfloat16), "tensor").astype(jnp.float32) + back_r1
    input_grad = back_h0.astype(jnp.bfloat16)
    back_time = jnp.einsum(
        "ps,pd->sd",
        onehot,
        back_h0,
        precision=lax.Precision.HIGHEST,
        preferred_element_type=jnp.float32,
    )
    grad_bouter = jnp.sum(back_time, axis=0)
    back_time_low = back_time.astype(jnp.bfloat16)
    grad_outer = jnp.einsum("su,sd->ud", act_low, back_time_low, preferred_element_type=jnp.float32)
    back_act = jnp.einsum("sd,ud->su", back_time_low, w_outer, preferred_element_type=jnp.float32)
    (back_inner,) = silu_pull(back_act)
    grad_binner = jnp.sum(back_inner, axis=0)
    grad_inner = jnp.einsum(
        "st,su->tu",
        feature_low,
        back_inner.astype(jnp.bfloat16),
        preferred_element_type=jnp.float32,
    )
    grad_head = jnp.concatenate([grad_bq[None], grad_bv[None], grad_bup], axis=0).reshape(
        6, 1, local_width
    )
    grad_layer = jnp.stack(
        [grad_bout, back_gain1, back_shift1, part_bdown, back_gain2, back_shift2, grad_bouter],
        axis=0,
    )
    red_qkv, red_out, red_up, red_down, red_inner, red_outer, red_binner, red_head, red_layer = (
        lax.psum_scatter(grad_qkv, "dp", scatter_dimension=0, tiled=True),
        lax.psum_scatter(grad_out, "dp", scatter_dimension=1, tiled=True),
        lax.psum_scatter(grad_up, "dp", scatter_dimension=0, tiled=True),
        lax.psum_scatter(grad_down, "dp", scatter_dimension=2, tiled=True),
        lax.psum_scatter(grad_inner, "dp", scatter_dimension=0, tiled=True),
        lax.psum_scatter(grad_outer, "dp", scatter_dimension=0, tiled=True),
        lax.psum_scatter(grad_binner, "dp", scatter_dimension=0, tiled=True),
        lax.psum_scatter(grad_head, "dp", scatter_dimension=2, tiled=True),
        lax.psum_scatter(grad_layer, "dp", scatter_dimension=1, tiled=True),
    )
    split_squares = sum(
        (jnp.sum(piece * piece) for piece in (red_qkv, red_out, red_up, red_down, red_head))
    )
    shared_squares = sum(
        (jnp.sum(piece * piece) for piece in (red_inner, red_outer, red_binner, red_layer))
    )
    local_squares = split_squares + shared_squares / lax.axis_size("tensor")
    norm = jnp.sqrt(lax.psum(local_squares, ("dp", "tensor")))
    factor = 1.0 / jnp.maximum(norm, 1.0)
    step_rate = 4.0 * math.sqrt(MPARAMS / D)
    qkv_master, qkv_velocity, qkv_smoothed = advance(
        qkv_weight, qkv_moment, qkv_average, red_qkv, factor, step_rate
    )
    out_master, out_velocity, out_smoothed = advance(
        out_weight, out_moment, out_average, red_out, factor, step_rate
    )
    up_master, up_velocity, up_smoothed = advance(
        up_weight, up_moment, up_average, red_up, factor, step_rate
    )
    down_master, down_velocity, down_smoothed = advance(
        down_weight, down_moment, down_average, red_down, factor, step_rate
    )
    inner_master, inner_velocity, inner_smoothed = advance(
        time_inner, inner_moment, inner_average, red_inner, factor, step_rate
    )
    outer_master, outer_velocity, outer_smoothed = advance(
        time_outer, outer_moment, outer_average, red_outer, factor, step_rate
    )
    bias_master, bias_velocity, bias_smoothed = advance(
        time_bias, bias_moment, bias_average, red_binner, factor, step_rate
    )
    head_master, head_velocity, head_smoothed = advance(
        head_vectors, head_moment, head_average, red_head, factor, step_rate
    )
    layer_master, layer_velocity, layer_smoothed = advance(
        layer_vectors, layer_moment, layer_average, red_layer, factor, step_rate
    )
    return (
        output_here,
        input_grad,
        norm,
        qkv_master,
        out_master,
        up_master,
        down_master,
        inner_master,
        outer_master,
        bias_master,
        head_master,
        layer_master,
        qkv_velocity,
        out_velocity,
        up_velocity,
        down_velocity,
        inner_velocity,
        outer_velocity,
        bias_velocity,
        head_velocity,
        layer_velocity,
        qkv_smoothed,
        out_smoothed,
        up_smoothed,
        down_smoothed,
        inner_smoothed,
        outer_smoothed,
        bias_smoothed,
        head_smoothed,
        layer_smoothed,
    )


F32=jnp.float32; BF=jnp.bfloat16
MESH=pl.DeviceIdType.MESH
NZ,NX,NC,NT=4,2,2,2
ROWS=48; PIECE=384

def place():
    dp=lax.axis_index("dp"); t=lax.axis_index("tensor")
    z=lax.div(dp,4); x=lax.rem(lax.div(dp,2),2); c=lax.rem(dp,2)
    return z,x,c,t
def dev(z,x,c,t):
    return ((z*NX+x)*NC+c,t)

def peers():
    z,x,c,t=place()
    zp=[dev(lax.rem(z+d,NZ),x,c,t) for d in range(1,NZ)]
    return zp,dev(z,1-x,c,t),dev(z,x,c,1-t),dev(z,x,1-c,t)

def greet():
    zp,xp,yp,sp=peers()
    bar=pltpu.get_barrier_semaphore()
    for d in zp+[xp,yp,sp]:
        pl.semaphore_signal(bar,inc=1,device_id=d,device_id_type=MESH)
    pl.semaphore_wait(bar,6)

def rcopy(src,dst,ssem,rsem,d):
    return pltpu.make_async_remote_copy(src_ref=src,dst_ref=dst,send_sem=ssem,recv_sem=rsem,device_id=d,device_id_type=MESH)

L=1024
def dot(a,b,ca,cb):
    return lax.dot_general(a,b,(((ca,),(cb,)),((),())),preferred_element_type=F32)
def ln_stats(v):
    mean=jnp.mean(v,axis=-1,keepdims=True)
    cen=v-mean
    inv=lax.rsqrt(jnp.mean(cen*cen,axis=-1,keepdims=True)+EPSILON)
    return cen*inv,inv

def ln_back(gain,dy,xhat,inv):
    gd=gain*dy
    return (gd-jnp.mean(gd,axis=-1,keepdims=True)-xhat*jnp.mean(gd*xhat,axis=-1,keepdims=True))*inv

def phi_cdf(u):
    return 0.5*(1.0+lax.erf(u*(1.0/math.sqrt(2.0))))

WIDE=13*PIECE
RB=256
def spread(blocks,w,tiles):
    lane=lax.broadcasted_iota(jnp.int32,(16,128),1)
    acc=[jnp.zeros((16,128),F32) for _ in range(tiles+1)]
    for n,b in enumerate(blocks):
        tile,s=divmod(n*w,128)
        wide=jnp.concatenate([jnp.where(lane<w,b,0.0),jnp.zeros((16,128),F32)],axis=1)
        if s: wide=pltpu.roll(wide,s,1)
        acc[tile]=acc[tile]+wide[:,:128]
        acc[tile+1]=acc[tile+1]+wide[:,128:]
    return jnp.concatenate(acc[:tiles],axis=1)

def attend_pair(q_ref,k_ref,v_ref,o_ref,lse_ref,bias_ref,i,bq=512):
    lane=lax.broadcasted_iota(jnp.int32,(1,128),1)
    cs=pl.ds(pl.multiple_of(i*128,128),128)
    kp=k_ref[:,cs]; vT=v_ref[:,cs].T
    bias=bias_ref[...]
    khs=[]
    for h in range(2):
        khs.append(jnp.where((lane//64)==h,kp,jnp.where(lane==(64*(1-h)),bias,jnp.zeros_like(kp))))
    for qi in range(L//bq):
        qp=q_ref[pl.ds(qi*bq,bq),cs]*0.125
        oT=[]
        for h in range(2):
            qh=jnp.where((lane//64)==h,qp,jnp.where(lane==(64*(1-h)),jnp.ones_like(qp),jnp.zeros_like(qp)))
            sT=dot(khs[h],qh,1,1)
            m=jnp.max(sT,axis=0,keepdims=True)
            e=jnp.exp(sT-m)
            l=jnp.sum(e,axis=0,keepdims=True)
            p=(e*(1.0/l)).astype(BF)
            oT.append(dot(vT[h*64:(h+1)*64],p,1,0))
            lse_ref[i,h:h+1,qi*bq:(qi+1)*bq]=m+jnp.log(l)
        o_ref[pl.ds(qi*bq,bq),cs]=jnp.concatenate(oT,axis=0).T.astype(BF)

GCH=[(n*PIECE,PIECE,128*(1+n%2)) for n in range(13)]

def slots(n):
    out={}
    for i in range(n):
        for stage,lag in enumerate((0,1,2,3) if i<4 else (0,2,4,5)): out.setdefault(i+lag,[]).append((stage,i))
    return {k:sorted(v) for k,v in out.items()}
SLOTS=slots(len(GCH)-1)

def gather_steps(g,zs,zr,fs,fr,ss,sr):
    z,x,c,t=place(); zp,xp,yp,sp=peers(); n=len(GCH)-1
    def cols(i): return pl.ds(GCH[i][0],GCH[i][1])
    def ca(i): return pl.ds(GCH[i][0],GCH[i][2])
    def cb(i): return pl.ds(GCH[i][0]+GCH[i][2],GCH[i][1]-GCH[i][2])
    same=lambda r,s,q,d:rcopy(r,r,s,q,d)
    def Z(i):
        src=g.at[:,z,:,c,:,cols(i)] if i==n else g.at[t,z,x,c,:,cols(i)]
        return [same(src,zs.at[i,d],zr.at[i,d],zp[d]) for d in range(3)]
    def A(i):
        if i==n: return [same(g.at[t,z,x,c,:,ca(i)],fs.at[i,0],fr.at[i,0],xp),same(g.at[t,z,x,c,:,cb(i)],fs.at[i,1],fr.at[i,1],yp)]
        return [same(g.at[t,:,x,c,:,ca(i)],fs.at[i,0],fr.at[i,0],xp),same(g.at[t,:,x,c,:,cb(i)],fs.at[i,1],fr.at[i,1],yp)]
    def B(i):
        if i==n: return [same(g.at[t,z,:,c,:,ca(i)],fs.at[i,2],fr.at[i,2],yp),same(g.at[:,z,x,c,:,cb(i)],fs.at[i,3],fr.at[i,3],xp)]
        return [same(g.at[t,:,:,c,:,ca(i)],fs.at[i,2],fr.at[i,2],yp),same(g.at[:,:,x,c,:,cb(i)],fs.at[i,3],fr.at[i,3],xp)]
    S=lambda i:[same(g.at[:,:,:,c,:,cols(i)],ss.at[i],sr.at[i],sp)]
    def go(cs):
        for q in cs: q.start()
    def got(cs):
        for q in cs: q.wait_recv()
    def step(k):
        for stage,i in SLOTS.get(k,()):
            if stage==0:
                got(Z(i)); go(A(i))
                if i+4<n: go(Z(i+4))
            if stage==1: got(A(i)); go(B(i))
            if stage==2: got(B(i)); go(S(i))
            if stage==3: got(S(i))
    def late(k):
        if k==0: go(A(n))
        if k==1: got(A(n)); go(B(n))
        if k==2: got(B(n)); go(Z(n))
        if k==3: got(Z(n)); go(S(n))
        if k==4: got(S(n))
    def first(k): go(Z(k))
    def finish():
        for i in range(n+1):
            for q in Z(i)+A(i)+B(i)+S(i): q.wait_send()
    return step,late,first,finish

def front_kernel(ts_ref,qkv_m,out_m,up_m,down_m,w1_m,w2_m,b1_m,hv_m,lv_m,tok_hbm,cot_hbm,seg_ref,
        q_o,k_o,v_o,o_o,lse_o,out_o,outp_o,dmbT_o,abT_o,drbT_o,hid_o,dub_o,dr1_o,dob_o,hbT_o,wqkv_o,aux_o,sums_o,bup_o,time_o,feat_o,
        g,tok,cot,q,k,v,o,lse,own,bias,vecs,temb,hbT,gp,hid,inv,dmbT,abT,drbT,dr1,a32,
        zs,zr,fs,fr,ss,sr,lsem,osem,hsem,bsem,ysem):
    z,x,c,t=place()
    step,late,first,finish=gather_steps(g,zs,zr,fs,fr,ss,sr)
    win=pl.ds(pl.multiple_of(t*512,512),L)
    ltok=pltpu.make_async_copy(tok_hbm.at[win,:],tok,lsem.at[0]); ltok.start()
    lcot=pltpu.make_async_copy(cot_hbm.at[win,:],cot,lsem.at[1]); lcot.start()
    greet_out()
    a32[...]=jnp.zeros((ROWS,PIECE),F32)
    a32[0:32,:]=w2_m[:,pl.ds(pl.multiple_of(t*PIECE,128),PIECE)]
    a32[32:40,0:256]=w1_m[:,pl.ds(pl.multiple_of(t*256,128),256)]
    a32[32:39,256:304]=lv_m[...]
    a32[39:45,256:280]=hv_m[:,0,:]
    a32[45:46,256:288]=b1_m[...]
    def put(p,val): g[t,z,x,c,:,p*PIECE:(p+1)*PIECE]=val.astype(BF)
    put(0,a32[...])
    greet_in()
    first(0)
    for j in range(3): put(1+j,qkv_m[j])
    put(4,out_m[...])
    first(1); first(2); first(3)
    for j in range(4): put(5+j,up_m[:,j,:])
    for j in range(4): put(9+j,down_m[j])
    late(0)
    ln=lax.broadcasted_iota(jnp.int32,(16,256),1)
    fi=lax.div(ln,16)*8+lax.rem(ln,16)
    theta=jnp.exp(lax.rem(fi,64).astype(F32)*(-math.log(10000.0)/64.0))
    ang=theta*ts_ref[0,t].astype(F32)
    feat=jnp.where(lax.rem(ln,16)<8,jnp.where(fi<64,jnp.cos(ang),jnp.sin(ang)),0.0).astype(BF)
    feat_o[...]=feat
    seg=seg_ref[:,pl.ds(pl.multiple_of(t*512,128),L)]
    own_row=jnp.where(seg==t,1.0,0.0)
    ownT=jnp.broadcast_to(own_row,(128,L)).T
    own[...]=ownT
    bias[...]=jnp.where(ownT>0.5,0.0,-1e30).astype(BF)
    for n in range(4): step(n)
    def vecblk(tt,n): return g[tt,n//4,(n//2)%2,n%2,32:48,256:384].astype(F32)
    b0=[vecblk(0,n) for n in range(16)]; b1=[vecblk(1,n) for n in range(16)]
    lv=spread(b0,48,6)
    hv=jnp.concatenate([spread(b0,24,3),spread(b1,24,3)],axis=1)
    vecs[0:16,:]=lv
    vecs[16:32,:]=hv
    bin_=spread(b0,32,4)[13:14,:]
    w1=jnp.concatenate([g[0,:,:,:,32:48,0:256].reshape(256,256),g[1,:,:,:,32:48,0:256].reshape(256,256)],axis=1)
    inner=dot(feat,w1,1,0)[0:1]+bin_
    sig=1.0/(1.0+jnp.exp(-inner))
    act=inner*sig
    w2=jnp.concatenate([g[0,:,:,:,0:32,0:384].reshape(512,384),g[1,:,:,:,0:32,0:384].reshape(512,384)],axis=1)
    actb=jnp.broadcast_to(act,(16,512)).astype(BF)
    te=dot(actb,w2,1,0)[0:1]+lv[6:7]
    temb[...]=jnp.broadcast_to(te,(8,D))
    time_o[...]=jnp.concatenate([inner,sig,jnp.zeros((6,512),F32)],axis=0)
    ltok.wait()
    outs=[]
    def emit(src,dst):
        cp=pltpu.make_async_copy(src,dst,osem.at[len(outs)]); cp.start(); outs.append(cp)
    def hid_rows(r,_):
        rows=pl.ds(pl.multiple_of(r*RB,RB),RB)
        hb=(tok[rows,:].astype(F32)+temb[0:1,:]).astype(BF)
        hbT[:,rows]=hb.T
        return 0
    lax.fori_loop(0,L//RB,hid_rows,0)
    def project(which,ref,brow):
        def rows_body(r,_):
            rows=pl.ds(pl.multiple_of(r*RB,RB),RB)
            hb=(tok[rows,:].astype(F32)+temb[0:1,:]).astype(BF)
            for tt in range(2):
                val=dot(hb,g[tt,:,:,:,:,(1+which)*PIECE:(2+which)*PIECE].reshape(D,PIECE),1,0)
                if brow is not None: val=val+vecs[brow:brow+1,tt*PIECE:(tt+1)*PIECE]
                ref[rows,tt*PIECE:(tt+1)*PIECE]=val.astype(BF)
            return 0
        lax.fori_loop(0,L//RB,rows_body,0)
    emit(hbT,hbT_o)
    step(4)
    project(0,q,16+7)
    emit(q,q_o)
    step(5); late(1)
    project(1,k,None)
    emit(k,k_o)
    step(6)
    project(2,v,16+8)
    emit(v,v_o)
    emit(g.at[:,:,:,:,:,0:PIECE],aux_o); emit(g.at[:,:,:,:,:,PIECE:4*PIECE],wqkv_o)
    def pair(i,_):
        attend_pair(q,k,v,o,lse,bias,i)
        for s in range(6):
            @pl.when(i==s)
            def _():
                if s==3: late(2)
                step(7+s)
        return 0
    lax.fori_loop(0,6,pair,0)
    emit(o,o_o); emit(lse,lse_o)
    lcot.wait()
    for cp in outs: cp.wait()
    out,dob=q,k
    yp=peers()[2]
    def emits(r):
        rows=pl.ds(pl.multiple_of(r*RB,RB),RB)
        byrow=[(out,out_o),(dr1,dr1_o),(dob,dob_o)]; bycol=[(dmbT,dmbT_o),(abT,abT_o),(drbT,drbT_o)]
        cs=[pltpu.make_async_copy(a.at[rows,:],b.at[rows,:],bsem.at[n,r]) for n,(a,b) in enumerate(byrow)]
        cs+=[pltpu.make_async_copy(a.at[:,rows],b.at[:,rows],bsem.at[3+n,r]) for n,(a,b) in enumerate(bycol)]
        return cs,rcopy(out.at[rows,:],outp_o.at[rows,:],ysem.at[0,r],ysem.at[1,r],yp)
    mid_body(g,tok,cot,o,own,vecs,temb,gp,hid,inv,out,dmbT,abT,drbT,dr1,dob,sums_o,bup_o,hid_o,dub_o,hsem,step,late,emits)
    for r in range(L//RB):
        cs,far=emits(r)
        for cp in cs: cp.wait()
        if r<2: far.wait()
    finish()

def mid_body(g,tok,cot,o,own,vecs,temb,gp,hid,inv,out,dmbT,abT,drbT,dr1,dob,sums_o,bup_o,hid_o,dub_o,hsem,step,late,emits):
    def W(tt,piece,n=1): return g[tt,:,:,:,:,piece*PIECE:(piece+n)*PIECE].reshape(D,n*PIECE)
    row=lambda r:vecs[r:r+1,:]
    sums_o[...]=jnp.zeros((8,D),F32); bup_o[...]=jnp.zeros((8,4*D),F32)
    csum=lambda a:jnp.sum(a,axis=0,keepdims=True)
    def emit_rows(buf,dst,r,which):
        rows=pl.ds(pl.multiple_of(r*RB,RB),RB)
        return pltpu.make_async_copy(buf.at[rows,:],dst.at[rows,:],hsem.at[which,r])
    def up_block(r,_):
        rows=pl.ds(pl.multiple_of(r*RB,RB),RB)
        for n in range(4):
            @pl.when(r==n)
            def _():
                if n==1: late(3)
                step(13+n)
        attn=dot(o[rows,0:PIECE],W(0,4),1,1)+dot(o[rows,PIECE:D],W(1,4),1,1)
        r1=(tok[rows,:].astype(F32)+temb[0:1,:])+(attn+row(0))
        x1,inv1=ln_stats(r1)
        dr1[rows,:]=x1
        inv[rows,:]=jnp.broadcast_to(inv1,(RB,128))
        ab=(x1*row(1)+row(2)).astype(BF)
        abT[:,rows]=ab.T
        for tt in range(2):
            for j in range(4):
                cc=pl.ds((tt*4+j)*PIECE,PIECE)
                u=dot(ab,W(tt,5+j),1,0)+vecs[16+9+j:16+10+j,tt*PIECE:(tt+1)*PIECE]
                cdf=phi_cdf(u)
                gp[rows,cc]=(cdf+u*jnp.exp(-0.5*u*u)*(1.0/math.sqrt(2*math.pi))).astype(BF)
                hid[rows,cc]=(u*cdf).astype(BF)
        emit_rows(hid,hid_o,r,0).start()
        return 0
    lax.fori_loop(0,L//RB,up_block,0)
    late(4)
    def block(r,_):
        rows=pl.ds(pl.multiple_of(r*RB,RB),RB)
        x1=dr1[rows,:]; inv1=inv[rows,0:1]
        a=x1*row(1)+row(2)
        mlp=row(3)
        for tt in range(2):
            mlp=mlp+dot(hid[rows,tt*4*PIECE:(tt+1)*4*PIECE],W(tt,9,4),1,1)
        x2,inv2=ln_stats(a+mlp)
        out[rows,:]=(x2*row(4)+row(5)).astype(BF)
        @pl.when(r<2)
        def _(): emits(r)[1].start()
        dy=jnp.where(own[rows,0:1]>0.5,cot[rows,:].astype(F32),0.0)
        sums_o[4:5,:]+=csum(dy*x2); sums_o[5:6,:]+=csum(dy)
        dr2=ln_back(row(4),dy,x2,inv2)
        sums_o[3:4,:]+=csum(dr2)
        dmb=dr2.astype(BF)
        dmbT[:,rows]=dmb.T
        da=dr2
        for tt in range(2):
            for j in range(4):
                cc=pl.ds((tt*4+j)*PIECE,PIECE)
                du=dot(dmb,W(tt,9+j),1,0)*gp[rows,cc].astype(F32)
                bup_o[0:1,cc]+=csum(du)
                gp[rows,cc]=du.astype(BF)
            da=da+dot(gp[rows,tt*4*PIECE:(tt+1)*4*PIECE],W(tt,5,4),1,1)
        emit_rows(gp,dub_o,r,1).start()
        sums_o[1:2,:]+=csum(da*x1); sums_o[2:3,:]+=csum(da)
        d1=ln_back(row(1),da,x1,inv1)
        sums_o[0:1,:]+=csum(d1)
        dr1[rows,:]=d1
        drb=d1.astype(BF)
        drbT[:,rows]=drb.T
        for tt in range(2):
            dob[rows,tt*PIECE:(tt+1)*PIECE]=dot(drb,W(tt,4),1,0).astype(BF)
        for cp in emits(r)[0]: cp.start()
        return 0
    lax.fori_loop(0,L//RB,block,0)
    for r in range(L//RB):
        emit_rows(hid,hid_o,r,0).wait(); emit_rows(gp,dub_o,r,1).wait()

def front(ts,masters,tokens,cotangent,seg,cid=0):
    DMA=pltpu.SemaphoreType.DMA; n=len(GCH)
    V=lambda s,d=BF:pltpu.VMEM(s,d)
    A=pl.BlockSpec(memory_space=pl.ANY); M=pl.BlockSpec(memory_space=pltpu.VMEM)
    big=lambda s,d=BF:jax.ShapeDtypeStruct(s,d)
    row=(L,D); tr=(D,L)
    G6=lambda w_:(NT,NZ,NX,NC,ROWS,w_)
    return pl.pallas_call(front_kernel,
        in_specs=[pl.BlockSpec(memory_space=pltpu.SMEM)]+[M]*9+[A,A,M],
        out_specs=[A]*17+[M]*4,
        out_shape=[big(row),big(row),big(row),big(row),big((6,2,L),F32),big(row),big((512,D)),big(tr),big(tr),big(tr),big((L,4*D)),big((L,4*D)),
            big(row,F32),big(row),big(tr),big(G6(3*PIECE)),big(G6(PIECE)),big((8,D),F32),big((8,4*D),F32),big((8,512),F32),big((16,256))],
        scratch_shapes=[V(G6(WIDE)),V(row),V(row),V(row),V(row),V(row),V(row),V((6,2,L),F32),V((L,128),F32),V((L,128)),V((32,D),F32),V((8,D),F32),
            V(tr),V((L,4*D)),V((L,4*D)),V((L,128),F32),V(tr),V(tr),V(tr),V(row,F32),V((ROWS,PIECE),F32),
            DMA((n,3)),DMA((n,3)),DMA((n,4)),DMA((n,4)),DMA((n,)),DMA((n,)),DMA((2,)),DMA((8,)),DMA((2,L//RB)),DMA((6,L//RB)),DMA((2,L//RB))],
        compiler_params=pltpu.CompilerParams(collective_id=cid,has_side_effects=True,vmem_limit_bytes=63*2**20),name="front")(ts,*masters,tokens,cotangent,seg)

def group(g,r,w,a): return dict(g=g,r=r,w=w,a=a)
RGR=[group(0,0,768,-1),group(768,768,768,0),group(1536,1536,768,-1),group(2304,2304,768,0),group(3072,3072,384,-1),
     group(3456,3456,384,0),group(3840,3840,384,0),group(0,4224,384,256)]
RW=12*PIECE
GBW=11*PIECE
_a=_b=_p=_q=0
for _g in RGR:
    if _g["a"]>=0:
        _g["ao"]=_a; _g["bo"]=_b; _g["po"]=_p; _a+=_g["a"]; _b+=_g["w"]-_g["a"]; _p+=_g["w"]
    else:
        _g["qo"]=_q; _q+=_g["w"]
RWA,RWB,RWP,RWQ=max(_a,128),_b,_p,_q

def scatter_steps(gb,rs,ra,rc,rb,rz,rx,rq,ry,red,ss,sr,as_,ar,bs,br,zs,zr):
    z,x,c,t=place(); zp,xp,yp,sp=peers()
    def go(cs):
        for q in cs: q.start()
    def got(cs):
        for q in cs: q.wait_recv()
    def sums(a,b): return a+b
    def sl(i):
        q=RGR[i]; g,r,w,a=q["g"],q["r"],q["w"],q["a"]
        k=dict(g=pl.ds(g,w),r=pl.ds(r,w))
        if a>=0: k.update(ga=pl.ds(g,a),gb=pl.ds(g+a,w-a),a=pl.ds(q["ao"],a),b=pl.ds(q["bo"],w-a),p=pl.ds(q["po"],w),pa=pl.ds(q["po"],a),pb=pl.ds(q["po"]+a,w-a))
        else: k.update(q=pl.ds(q["qo"],w))
        return k
    def S(i):
        k=sl(i); return [rcopy(gb.at[:,:,:,1-c,:,k["g"]],rs.at[:,:,:,:,k["r"]],ss.at[i],sr.at[i],sp)]
    def A(i):
        k=sl(i)
        if "q" in k: return [rcopy(gb.at[:,:,1-x,c,:,k["g"]],rx.at[:,:,:,k["q"]],as_.at[i,0],ar.at[i,0],xp)]
        one=[rcopy(gb.at[:,:,1-x,c,:,k["ga"]],ra.at[:,:,:,k["a"]],as_.at[i,0],ar.at[i,0],xp)] if RGR[i]["a"] else []
        return one+[rcopy(gb.at[1-t,:,:,c,:,k["gb"]],rc.at[:,:,:,k["b"]],as_.at[i,1],ar.at[i,1],yp)]
    def zdst(d): return lax.rem(z+d+1,NZ)
    def B(i):
        k=sl(i)
        if "q" in k: return [rcopy(gb.at[:,zdst(d),x,c,:,k["g"]],rq.at[d,:,:,k["q"]],bs.at[i,d],br.at[i,d],zp[d]) for d in range(3)]
        one=[rcopy(gb.at[1-t,:,x,c,:,k["ga"]],rb.at[:,:,k["pa"]],bs.at[i,0],br.at[i,0],yp)] if RGR[i]["a"] else []
        return one+[rcopy(gb.at[t,:,1-x,c,:,k["gb"]],rb.at[:,:,k["pb"]],bs.at[i,1],br.at[i,1],xp)]
    def Z(i):
        k=sl(i)
        if "q" in k: return [rcopy(gb.at[1-t,z,x,c,:,k["g"]],ry.at[:,k["q"]],zs.at[i,0],zr.at[i,0],yp)]
        return [rcopy(gb.at[t,zdst(d),x,c,:,k["g"]],rz.at[d,:,k["p"]],zs.at[i,d],zr.at[i,d],zp[d]) for d in range(3)]
    def s_to_a(i):
        got(S(i)); k=sl(i)
        def body(n,_):
            tt=lax.div(n,8); zz=lax.rem(lax.div(n,2),4); xx=lax.rem(n,2)
            gb[tt,zz,xx,c,:,k["g"]]=sums(gb[tt,zz,xx,c,:,k["g"]],rs[tt,zz,xx,:,k["r"]])
            return 0
        lax.fori_loop(0,16,body,0)
        go(A(i))
    def a_to_b(i):
        got(A(i)); k=sl(i)
        def body(n,_):
            a=lax.div(n,4); b=lax.rem(n,4)
            if "q" in k:
                gb[a,b,x,c,:,k["g"]]=sums(gb[a,b,x,c,:,k["g"]],rx[a,b,:,k["q"]])
            else:
                if RGR[i]["a"]: gb[a,b,x,c,:,k["ga"]]=sums(gb[a,b,x,c,:,k["ga"]],ra[a,b,:,k["a"]])
                zz=lax.div(n,2); xx=lax.rem(n,2)
                gb[t,zz,xx,c,:,k["gb"]]=sums(gb[t,zz,xx,c,:,k["gb"]],rc[zz,xx,:,k["b"]])
            return 0
        lax.fori_loop(0,8,body,0)
        go(B(i))
    def b_to_z(i):
        got(B(i)); k=sl(i)
        if "q" in k:
            for a in range(2):
                acc=gb[a,z,x,c,:,k["g"]].astype(F32)
                for d in range(3): acc=acc+rq[d,a,:,k["q"]].astype(F32)
                gb[a,z,x,c,:,k["g"]]=acc.astype(BF)
        else:
            def body(n,_):
                gb[t,n,x,c,:,k["g"]]=sums(gb[t,n,x,c,:,k["g"]],rb[n,:,k["p"]])
                return 0
            lax.fori_loop(0,4,body,0)
        go(Z(i))
    def z_end(i):
        got(Z(i)); k=sl(i)
        acc=gb[t,z,x,c,:,k["g"]].astype(F32)
        if "q" in k: acc=acc+ry[:,k["q"]].astype(F32)
        else:
            for d in range(3): acc=acc+rz[d,:,k["p"]].astype(F32)
        red[:,k["r"]]=acc
    def drain(i):
        for q in S(i)+A(i)+B(i)+Z(i): q.wait_send()
    return S,go,s_to_a,a_to_b,b_to_z,z_end,drain

def attend_back(q_ref,k_ref,v_ref,do_ref,lse_ref,bias_ref,hvs,i,bq=512):
    lane=lax.broadcasted_iota(jnp.int32,(1,128),1)
    cs=pl.ds(pl.multiple_of(i*128,128),128)
    kp=k_ref[:,cs]; vp=v_ref[:,cs]; bias=bias_ref[...]
    khs=[];vhs=[]
    for h in range(2):
        sel=(lane//64)==h; one=lane==(64*(1-h))
        khs.append(jnp.where(sel,kp,jnp.where(one,bias,jnp.zeros_like(kp))))
        vhs.append(jnp.where(sel,vp,jnp.zeros_like(vp)))
    kT=kp.T
    dk=[None,None];dv=[None,None]; sq=None
    for qi in range(L//bq):
        rows=pl.ds(qi*bq,bq)
        qp=q_ref[rows,cs]*0.125; dop=do_ref[rows,cs]
        dqT=[]
        for h in range(2):
            sel=(lane//64)==h; one=lane==(64*(1-h))
            zero=jnp.zeros_like(qp)
            qh=jnp.where(sel,qp,jnp.where(one,jnp.ones_like(qp),zero))
            doh=jnp.where(sel,dop,zero)
            qz=jnp.where(sel,qp,zero)
            sT=dot(khs[h],qh,1,1)
            p=jnp.exp(sT-lse_ref[i,h:h+1,qi*bq:(qi+1)*bq])
            dp=dot(vhs[h],doh,1,1)
            d=jnp.sum(p*dp,axis=0,keepdims=True)
            ds=(p*(dp-d)).astype(BF)
            pb=p.astype(BF)
            a=dot(pb,doh,1,0); dv[h]=a if dv[h] is None else dv[h]+a
            a=dot(ds,qz,1,0); dk[h]=a if dk[h] is None else dk[h]+a
            dqT.append(dot(kT[h*64:(h+1)*64],ds,1,0))
        dq=jnp.concatenate(dqT,axis=0).T*0.125
        s=jnp.sum(dq,axis=0,keepdims=True); sq=s if sq is None else sq+s
        q_ref[rows,cs]=dq.astype(BF)
    k_ref[:,cs]=(dk[0]+dk[1]).astype(BF)
    dvv=dv[0]+dv[1]
    v_ref[:,cs]=dvv.astype(BF)
    hvs[0:1,cs]=sq
    hvs[1:2,cs]=jnp.sum(dvv,axis=0,keepdims=True)

def unspread(src,w,n):
    lane=lax.broadcasted_iota(jnp.int32,(16,128),1)
    tile,s=divmod(n*w,128)
    wide=src[:,tile*128:(tile+2)*128]
    if s: wide=pltpu.roll(wide,256-s,1)
    return jnp.where(lane<w,wide[:,:128],0.0)

def back_kernel(q_h,k_h,v_h,do_h,o_h,lse_h,dmbT_h,abT_h,drbT_h,hbT_h,hid_h,dub_h,dr1_h,wqkv_h,aux_h,out_h,seg_ref,feat_ref,sums_ref,bup_ref,time_ref,
        in_o,inp_o,outp_o,red,w2g,w1g,vecg,tot,
        q,k,v,do,lse,bias,st,ta,tb,wq,dr1,aux,ow,hvs,lvs,hsrc,dtm,nv,nr,nz,vg,vs,vx,vz,vy,sg,mat,aT,fT,dT,
        gb,rs,ra,rc,rb,rz,rx,rq,ry,ss,sr,as_,ar,bs,br,zs,zr,ls,ts,xs,ns,nrs,os,vsm,vrm,gsm,grm):
    z,x,c,t=place(); zp,xp,yp,sp=peers()
    inw=do
    S,go,s_to_a,a_to_b,b_to_z,z_end,drain=scatter_steps(gb,rs,ra,rc,rb,rz,rx,rq,ry,red,ss,sr,as_,ar,bs,br,zs,zr)
    def load(src,dst,n):
        return pltpu.make_async_copy(src,dst,ls.at[n])
    LQ=[load(q_h,q,0),load(k_h,k,1),load(v_h,v,2),load(do_h,do,3),load(lse_h,lse,4)]
    LW=[load(wqkv_h,wq,5),load(dr1_h,dr1,6),load(aux_h,aux,7)]
    def tcopy(src,buf,n): return pltpu.make_async_copy(src,buf,ts.at[n])
    def stage(src,cols,n):
        return [pltpu.make_async_copy(src.at[:,pl.ds(cs,PIECE)],st.at[s],ts.at[n+s]) for s,cs in enumerate(cols)]
    pc=lambda j:[tt*4*PIECE+jj*PIECE for jj in (j,j+1) for tt in range(2)]
    ST=[stage(hid_h,pc(0),4),stage(hid_h,pc(2),8),stage(dub_h,pc(0),4),stage(dub_h,pc(2),8),stage(o_h,[0,PIECE],4)]
    for q_ in [tcopy(dmbT_h,ta,0),*ST[0],tcopy(abT_h,tb,1)]+LQ+LW: q_.start()
    greet()
    lo=load(out_h.at[pl.ds(512,512),:],ow,9); lo.start(); lo.wait()
    cout=[rcopy(ow.at[pl.ds(n*256,256),:],outp_o.at[pl.ds(n*256,256),:],os.at[0,n],os.at[1,n],yp) for n in range(2)]
    for q_ in cout: q_.start()
    seg=seg_ref[:,pl.ds(pl.multiple_of(t*512,128),L)]
    bias[...]=jnp.broadcast_to(jnp.where(seg==t,0.0,-1e30),(128,L)).T.astype(BF)
    def compute(i,lhs,n):
        base=RGR[i]["g"]
        for q_ in ST[i]: q_.wait()
        def body(s,_):
            tt=lax.rem(s,2); cs=pl.ds(pl.multiple_of(base+lax.div(s,2)*PIECE,128),PIECE)
            gb[tt,:,:,:,:,cs]=dot(lhs[...],st[s],1,0).astype(BF).reshape(NZ,NX,NC,ROWS,PIECE)
            return 0
        lax.fori_loop(0,n,body,0)
        if i+1<len(ST):
            for q_ in ST[i+1]: q_.start()
        go(S(i))
    tcopy(dmbT_h,ta,0).wait()
    compute(0,ta,4)
    compute(1,ta,4)
    tcopy(drbT_h,ta,2).start()
    tcopy(abT_h,tb,1).wait()
    s_to_a(0)
    compute(2,tb,4)
    s_to_a(1)
    compute(3,tb,4)
    tcopy(hbT_h,tb,3).start()
    s_to_a(2)
    tcopy(drbT_h,ta,2).wait()
    compute(4,ta,2)
    s_to_a(3); a_to_b(0)
    for q_ in LQ: q_.wait()
    tcopy(hbT_h,tb,3).wait()
    def quad(i,n):
        base=RGR[i]["g"]
        for tt in range(2):
            o_=tt*PIECE+n*128
            rhs=jnp.concatenate([q[:,o_:o_+128],k[:,o_:o_+128],v[:,o_:o_+128]],axis=1)
            gb[tt,:,:,:,:,base:base+PIECE]=dot(tb[...],rhs,1,0).astype(BF).reshape(NZ,NX,NC,ROWS,PIECE)
        go(S(i))
    def pair(i,_):
        @pl.when(i==1)
        def _():
            s_to_a(4); a_to_b(1)
        @pl.when(i==2)
        def _():
            a_to_b(2); b_to_z(0); quad(5,0)
        @pl.when(i==3)
        def _():
            s_to_a(5); a_to_b(3); b_to_z(1)
        @pl.when(i==4)
        def _():
            a_to_b(4); z_end(0); b_to_z(2); quad(6,1)
        @pl.when(i==5)
        def _():
            s_to_a(6); a_to_b(5); b_to_z(3); z_end(1)
        attend_back(q,k,v,do,lse,bias,hvs,lax.div(i,2)+3*lax.rem(i,2))
        return 0
    lax.fori_loop(0,6,pair,0)
    z_end(2); b_to_z(4)
    lvs[...]=jnp.zeros((16,D+128),F32)
    lvs[0:6,0:D]=sums_ref[0:6,:]
    hsrc[...]=jnp.zeros((16,2*(PIECE+128)),F32)
    for tt in range(2):
        o0=tt*(PIECE+128); cc=slice(tt*PIECE,(tt+1)*PIECE)
        hsrc[7:9,o0:o0+PIECE]=hvs[0:2,cc]
        for j in range(4): hsrc[9+j:10+j,o0:o0+PIECE]=bup_ref[0:1,(tt*4+j)*PIECE:(tt*4+j+1)*PIECE]
    for n in range(16):
        both=unspread(lvs[...],48,n)
        for tt in range(2):
            vg[tt,n//4,(n//2)%2,n%2]=(both+unspread(hsrc[:,tt*(PIECE+128):(tt+1)*(PIECE+128)],24,n)).astype(BF)
    def pass_on(k):
        src=[sg.at[t,z,x,c],sg.at[:,z,x,c],sg.at[:,z,:,c],sg.at[:,z]][k]
        if k==3: return [rcopy(src,src,gsm.at[3+d],grm.at[3+d],zp[d]) for d in range(3)]
        return [rcopy(src,src,gsm.at[k],grm.at[k],(yp,xp,sp)[k])]
    def vec_send(k):
        if k==0: return [rcopy(vg.at[1-t],vy,vsm.at[0],vrm.at[0],yp)]
        if k==1: return [rcopy(vg.at[t,:,1-x],vx,vsm.at[1],vrm.at[1],xp)]
        if k==2: return [rcopy(vg.at[t,:,x,1-c],vs,vsm.at[2],vrm.at[2],sp)]
        return [rcopy(vg.at[t,lax.rem(z+d+1,NZ),x,c],vz.at[d],vsm.at[3+d],vrm.at[3+d],zp[d]) for d in range(3)]
    def vec(k):
        if k>0:
            for q_ in vec_send(k-1): q_.wait_recv()
        if k==1: vg[t]=vg[t]+vy[...]
        if k==2: vg[t,:,x]=vg[t,:,x]+vx[...]
        if k==3: vg[t,:,x,c]=vg[t,:,x,c]+vs[...]
        if k<4:
            for q_ in vec_send(k): q_.start()
        else:
            acc=vg[t,z,x,c].astype(F32)
            for d in range(3): acc=acc+vz[d].astype(F32)
            vecg[...]=acc
    def rows_on(k):
        if k>0:
            for q_ in pass_on(k-1): q_.wait_recv()
        if k<4:
            for q_ in pass_on(k): q_.start()
    vec(0)
    drain(0)
    quad(7,2)
    a_to_b(6); z_end(3); b_to_z(5)
    vec(1)
    for q_ in LW: q_.wait()
    dtm[...]=jnp.zeros((8,D),F32)
    def far(r):
        rows=pl.ds(pl.multiple_of(r*RB,RB),RB)
        return rcopy(inw.at[rows,:],inp_o.at[rows,:],xs.at[0,r],xs.at[1,r],yp)
    def rows_body(r,_):
        rows=pl.ds(pl.multiple_of(r*RB,RB),RB)
        acc=dr1[rows,:]
        for n,ref in enumerate((q,k,v)):
            for tt in range(2):
                acc=acc+dot(ref[rows,tt*PIECE:(tt+1)*PIECE],wq[tt,:,:,:,:,n*PIECE:(n+1)*PIECE].reshape(D,PIECE),1,1)
        inw[rows,:]=acc.astype(BF)
        dtm[0:1,:]+=jnp.sum(acc,axis=0,keepdims=True)
        return 0
    s_to_a(7)
    lax.fori_loop(0,2,rows_body,0)
    a_to_b(7)
    far(0).start()
    vec(2)
    lax.fori_loop(2,L//RB,rows_body,0)
    cinl=pltpu.make_async_copy(inw,in_o,ls.at[8]); cinl.start()
    dtb=dtm[0:1,:].astype(BF)
    inner=time_ref[0:1,:]; sig=time_ref[1:2,:]
    w2=jnp.concatenate([aux[0,:,:,:,0:32,:].reshape(512,PIECE),aux[1,:,:,:,0:32,:].reshape(512,PIECE)],axis=1)
    dinner=dot(jnp.broadcast_to(dtb,(16,D)),w2,1,1)[0:1]*(sig*(1.0+inner*(1.0-sig)))
    act=(inner*sig).astype(BF).astype(F32)
    sg[t,z,x,c,0:1,:]=jnp.concatenate([act,dtm[0:1,:],dinner,feat_ref[0:1,:].astype(F32)],axis=1)
    rows_on(0)
    far(1).start(); far(2).start(); far(3).start()
    vec(3)
    b_to_z(6); z_end(4); z_end(5)
    rows_on(1)
    b_to_z(7)
    vec(4)
    rows_on(2)
    z_end(6)
    rows_on(3)
    z_end(7)
    vv=vecg[...]
    big=red[...]
    part=jnp.sum(big*big)+jnp.sum(jnp.where(lax.broadcasted_iota(jnp.int32,(16,128),0)<7,0.5,1.0)*vv*vv)
    nv[0]=jnp.full((8,128),part,F32)
    def swap(s,peer): return rcopy(nv.at[s],nr.at[s],ns.at[s],nrs.at[s],peer)
    swap(0,xp).start()
    rows_on(4)
    for n in range(32): mat[n:n+1,:]=sg[n//16,(n//4)%4,(n//2)%2,n%2]
    aT[...]=mat[:,0:512].T
    fT[...]=mat[:,1792:2048].T
    dp=lax.axis_index("dp")
    g2=dot(aT[pl.ds(pl.multiple_of(dp*32,32),32),:].astype(BF),mat[:,512:1280].astype(BF),1,0)
    g1=dot(fT[pl.ds(pl.multiple_of(dp*16,16),16),:].astype(BF),mat[:,1280:1792].astype(BF),1,0)
    w2g[...]=g2; w1g[...]=g1
    def own_sum(m,w):
        dT[0:m.shape[1],:]=m.T
        col=jnp.sum(dT[pl.ds(pl.multiple_of(dp*w,16),w),:],axis=1,keepdims=True)
        return jnp.broadcast_to(col,(w,128)).T[0:1,:]
    vecg[6:7,0:48]=own_sum(mat[:,512:1280],48)
    vecg[13:14,0:32]=own_sum(mat[:,1280:1792],32)
    sq=lambda a:jnp.sum(a*a)
    rest=(sq(dot(aT[...].astype(BF),mat[:,512:1280].astype(BF),1,0))+sq(dot(fT[...].astype(BF),mat[:,1280:1792].astype(BF),1,0))
        +sq(jnp.sum(mat[:,512:1280],axis=0,keepdims=True))+sq(jnp.sum(mat[:,1280:1792],axis=0,keepdims=True)))
    swap(0,xp).wait()
    nv[1]=nv[0]+nr[0]
    swap(1,sp).start(); swap(1,sp).wait()
    nv[2]=nv[1]+nr[1]
    cz=[rcopy(nv.at[2],nz.at[z],ns.at[3+d],nrs.at[3+d],zp[d]) for d in range(3)]
    for q_ in cz: q_.start()
    nz[z]=nv[2]
    for q_ in cz: q_.wait()
    nv[3]=((nz[0]+nz[1])+nz[2])+nz[3]
    cy=rcopy(nv.at[3],nr.at[2],ns.at[2],nrs.at[2],yp); cy.start(); cy.wait()
    tot[...]=(nv[3]+nr[2])+rest
    cinl.wait()
    for q_ in cout: q_.wait()
    for k_ in range(4):
        for q_ in pass_on(k_)+vec_send(k_): q_.wait_send()
    for r in range(4): far(r).wait()
    for i in range(1,8): drain(i)

def back(q,k,v,dob,o,lse,dmbT,abT,drbT,hbT,hid,dub,dr1,wqkv,aux,out_win,seg,featp,sums,bups,tstate,cid=1):
    DMA=pltpu.SemaphoreType.DMA; n=len(RGR)
    V=lambda s,d=BF:pltpu.VMEM(s,d)
    A=pl.BlockSpec(memory_space=pl.ANY); M=pl.BlockSpec(memory_space=pltpu.VMEM)
    sd=jax.ShapeDtypeStruct; row=(L,D); tr=(D,L)
    return pl.pallas_call(back_kernel,
        in_specs=[A]*16+[M]*5,out_specs=[A]*3+[M]*5,
        out_shape=[sd(row,BF),sd(row,BF),sd((512,D),BF),sd((ROWS,RW),F32),sd((32,D),F32),sd((16,512),F32),sd((16,128),F32),sd((8,128),F32)],
        scratch_shapes=[V(row),V(row),V(row),V(row),V((6,2,L),F32),V((L,128)),V((4,L,PIECE)),V(tr),V(tr),V((NT,NZ,NX,NC,ROWS,3*PIECE)),V(row,F32),
            V((NT,NZ,NX,NC,ROWS,PIECE)),V((512,D)),V((8,D),F32),V((16,D+128),F32),V((16,2*(PIECE+128)),F32),V((8,D),F32),
            V((4,8,128),F32),V((3,8,128),F32),V((4,8,128),F32),
            V((NT,NZ,NX,NC,16,128)),V((NZ,16,128)),V((NZ,NC,16,128)),V((3,16,128)),V((NZ,NX,NC,16,128)),V((NT,NZ,NX,NC,1,2048),F32),V((32,2048),F32),V((512,32),F32),V((256,32),F32),V((D,32),F32),
            V((NT,NZ,NX,NC,ROWS,GBW)),V((NT,NZ,NX,ROWS,RW)),V((NT,NZ,ROWS,RWA)),V((NZ,NX,ROWS,RWB)),V((NZ,ROWS,RWP)),V((3,ROWS,RWP)),
            V((NT,NZ,ROWS,RWQ)),V((3,NT,ROWS,RWQ)),V((ROWS,RWQ)),
            DMA((n,)),DMA((n,)),DMA((n,2)),DMA((n,2)),DMA((n,3)),DMA((n,3)),DMA((n,3)),DMA((n,3)),DMA((10,)),DMA((12,)),DMA((2,4)),DMA((6,)),DMA((6,)),DMA((2,2)),DMA((6,)),DMA((6,)),DMA((6,)),DMA((6,))],
        compiler_params=pltpu.CompilerParams(collective_id=cid,has_side_effects=True,vmem_limit_bytes=63*2**20),name="back")(
            q,k,v,dob,o,lse,dmbT,abT,drbT,hbT,hid,dub,dr1,wqkv,aux,out_win,seg,featp,sums,bups,tstate)

def greet_out():
    zp,xp,yp,sp=peers()
    bar=pltpu.get_barrier_semaphore()
    for d in zp+[xp,yp,sp]:
        pl.semaphore_signal(bar,inc=1,device_id=d,device_id_type=MESH)
def greet_in():
    pl.semaphore_wait(pltpu.get_barrier_semaphore(),6)

def update_kernel(*refs):
    red,w2g,w1g,vecg,tot,seg_ref,ow,op,op2,iw,ip=refs[:11]
    hbm=refs[11:38]
    out_o,in_o,norm_o=refs[38:41]
    far=refs[41:68]
    ps,ns=refs[68:95],refs[95:122]
    ms,vs,avs=ps[:9],ps[9:18],ps[18:]
    nm,nv,na=ns[:9],ns[9:18],ns[18:]
    mine,theirs,mid,sem,psem,nsem=refs[122:]
    pin=[pltpu.make_async_copy(a,b,psem.at[n]) for n,(a,b) in enumerate(zip(hbm,ps))]
    for q in pin: q.start()
    t=lax.axis_index("tensor")
    half=lambda k:pl.ds(pl.multiple_of(k*512,512),512)
    ins=[]
    for n,(w,ps_) in enumerate(((ow,(op,op2)),(iw,(ip,)))):
        ins.append(pltpu.make_async_copy(w,mine.at[n],sem.at[n,0]))
        step=L//len(ps_)
        ins+=[pltpu.make_async_copy(p,theirs.at[n,pl.ds(m*step,step),:],sem.at[n,5+m]) for m,p in enumerate(ps_)]
    for q in ins: q.start()
    norm=jnp.sqrt(tot[...])
    norm_o[0,0]=norm[0,0]
    factor=(1.0/jnp.maximum(norm,1.0))[0:1,0:1]
    rate=4.0*math.sqrt(MPARAMS/D)
    def upd(i,idx,g):
        sc=g*factor
        vel=MOMENTUM*vs[i][idx]+sc
        fm=ms[i][idx]-rate*(sc+MOMENTUM*vel)
        nv[i][idx]=vel; nm[i][idx]=fm
        na[i][idx]=AVERAGE_DECAY*avs[i][idx]+(1.0-AVERAGE_DECAY)*fm
    al=slice(None)
    for q in pin: q.wait()
    nout=[pltpu.make_async_copy(a,b,nsem.at[n]) for n,(a,b) in enumerate(zip(ns,far))]
    def flush(i):
        for n in (i,i+9,i+18): nout[n].start()
    for n in range(3):
        for c in range(3):
            b=9*PIECE+n*PIECE+c*128
            upd(0,(c,al,slice(n*128,(n+1)*128)),red[:,b:b+128])
    flush(0)
    upd(1,(al,al),red[:,8*PIECE:9*PIECE])
    flush(1)
    for j in range(4):
        upd(2,(al,j,al),red[:,(4+j)*PIECE:(5+j)*PIECE])
        upd(3,(j,),red[:,j*PIECE:(j+1)*PIECE])
    flush(2); flush(3)
    upd(4,(al,al),w1g[0:8,:])
    upd(5,(al,al),w2g[...])
    upd(6,(al,al),vecg[13:14,0:32])
    upd(7,(al,0,al),vecg[7:13,0:24])
    upd(8,(al,al),vecg[0:7,0:48])
    for i in range(4,9): flush(i)
    own=jnp.broadcast_to(jnp.where(seg_ref[:,512:1024]==t,1.0,0.0),(128,512)).T[:,0:1]>0.5
    for q in ins: q.wait()
    last=[]
    for n,o in enumerate((out_o,in_o)):
        last+=[pltpu.make_async_copy(mine.at[n,half(t),:],o.at[half(2*t),:],sem.at[n,2]),pltpu.make_async_copy(theirs.at[n,half(1-t),:],o.at[half(2*(1-t)),:],sem.at[n,3])]
        mid[n]=jnp.where(own,mine[n,half(1-t),:].astype(F32),theirs[n,half(t),:].astype(F32)).astype(BF)
        last.append(pltpu.make_async_copy(mid.at[n],o.at[pl.ds(512,512),:],sem.at[n,4]))
        for q in last[-3:]: q.start()
    for q in last+nout: q.wait()

def update(red,w2g,w1g,vecg,tot,seg,ow,op,op2,iw,ip,masters,moments,averages):
    A=pl.BlockSpec(memory_space=pl.ANY); M=pl.BlockSpec(memory_space=pltpu.VMEM)
    sd=jax.ShapeDtypeStruct
    ps=[sd(m.shape,F32) for m in masters]
    whole=sd((PACK,D),BF)
    return pl.pallas_call(update_kernel,in_specs=[M]*6+[A]*5+[A]*27,out_specs=[A,A,pl.BlockSpec(memory_space=pltpu.SMEM)]+[A]*27,
        out_shape=[whole,whole,sd((1,1),F32)]+ps*3,
        scratch_shapes=[pltpu.VMEM(p.shape,F32) for p in ps*6]+[pltpu.VMEM((2,L,D),BF),pltpu.VMEM((2,L,D),BF),pltpu.VMEM((2,512,D),BF),pltpu.SemaphoreType.DMA((2,7)),pltpu.SemaphoreType.DMA((27,)),pltpu.SemaphoreType.DMA((27,))],
        compiler_params=pltpu.CompilerParams(vmem_limit_bytes=63*2**20),name="upd")(red,w2g,w1g,vecg,tot,seg,ow,op,op2,iw,ip,*masters,*moments,*averages)

def shards_fast(tokens,cotangent,segment_ids,timesteps,*params):
    def turn(n,p): return {0:lambda:p.transpose(1,0,2),1:lambda:p.T,3:lambda:p.transpose(0,2,1),6:lambda:p.reshape(1,-1)}.get(n,lambda:p)()
    def back_turn(n,p): return {0:lambda:p.transpose(1,0,2),1:lambda:p.T,3:lambda:p.transpose(0,2,1),6:lambda:p.reshape(-1)}.get(n,lambda:p)()
    line=lambda ps:[turn(n,p) for n,p in enumerate(ps)]
    masters,moments,averages=line(params[:9]),line(params[9:18]),line(params[18:])
    q,k,v,o,lse,out_win,out_peer,dmbT,abT,drbT,hid,dub,dr1,dob,hbT,wq6,aux6,sums,bups,tstate,featp=front(timesteps,masters,tokens,cotangent,segment_ids)
    in_win,in_peer,out_peer2,red,w2g,w1g,vecg,total=back(q,k,v,dob,o,lse,dmbT,abT,drbT,hbT,hid,dub,dr1,wq6,aux6,out_win,segment_ids,featp,sums,bups,tstate)
    res=update(red,w2g,w1g,vecg,total,segment_ids,out_win,out_peer,out_peer2,in_win,in_peer,masters,moments,averages)
    return (res[0],res[1],res[2].reshape(()))+tuple(back_turn(n%9,r) for n,r in enumerate(res[3:]))


def solution(mesh):
    fast=dict(mesh.shape)=={'dp':16,'tensor':2}
    return jax.shard_map(
        shards_fast if fast else shards_any,
        mesh=mesh,
        in_specs=(
            P("dp", None),
            P("dp", None),
            P("dp", None),
            P("dp", None),
            P("dp", None, "tensor"),
            P("tensor", "dp"),
            P("dp", None, "tensor"),
            P(None, "tensor", "dp"),
            P("dp", None),
            P("dp", None),
            P("dp"),
            P(None, "tensor", "dp"),
            P(None, "dp"),
            P("dp", None, "tensor"),
            P("tensor", "dp"),
            P("dp", None, "tensor"),
            P(None, "tensor", "dp"),
            P("dp", None),
            P("dp", None),
            P("dp"),
            P(None, "tensor", "dp"),
            P(None, "dp"),
            P("dp", None, "tensor"),
            P("tensor", "dp"),
            P("dp", None, "tensor"),
            P(None, "tensor", "dp"),
            P("dp", None),
            P("dp", None),
            P("dp"),
            P(None, "tensor", "dp"),
            P(None, "dp"),
        ),
        out_specs=(
            P("dp", None),
            P("dp", None),
            P(),
            P("dp", None, "tensor"),
            P("tensor", "dp"),
            P("dp", None, "tensor"),
            P(None, "tensor", "dp"),
            P("dp", None),
            P("dp", None),
            P("dp"),
            P(None, "tensor", "dp"),
            P(None, "dp"),
            P("dp", None, "tensor"),
            P("tensor", "dp"),
            P("dp", None, "tensor"),
            P(None, "tensor", "dp"),
            P("dp", None),
            P("dp", None),
            P("dp"),
            P(None, "tensor", "dp"),
            P(None, "dp"),
            P("dp", None, "tensor"),
            P("tensor", "dp"),
            P("dp", None, "tensor"),
            P(None, "tensor", "dp"),
            P("dp", None),
            P("dp", None),
            P("dp"),
            P(None, "tensor", "dp"),
            P(None, "dp"),
        ),
        check_vma=False,
    )
```

```python
import functools
import math

import jax
import jax.numpy as jnp
from jax import lax
from jax.experimental import pallas as pl
from jax.experimental.pallas import tpu as pltpu
from jax.sharding import PartitionSpec as P

D = 768
HD = 64
TD = 128
SEGS = 2
PACK = 1536
MPARAMS = 7536640


EPSILON = 1e-05
MOMENTUM = 0.5
AVERAGE_DECAY = 0.5


def layer_norm(values, gain_vec, shift_vec):
    centre = jnp.mean(values, axis=-1, keepdims=True)
    centred = values - centre
    spread = jnp.mean(centred * centred, axis=-1, keepdims=True)
    return centred * lax.rsqrt(spread + EPSILON) * gain_vec + shift_vec


def time_features(step_ids, feat_width):
    midpoint = feat_width // 2
    frequency = jnp.exp(-math.log(10000.0) * jnp.arange(midpoint, dtype=jnp.float32) / midpoint)
    angles = step_ids.astype(jnp.float32)[..., None] * frequency
    return jnp.concatenate([jnp.cos(angles), jnp.sin(angles)], axis=-1)


def gelu_exact(values):
    return jax.nn.gelu(values, approximate=False)


def head_slice(matrix, head_index):
    return lax.dynamic_slice_in_dim(matrix, head_index * HD, HD, 1)


def merge_heads(stacked):
    return stacked.transpose(1, 0, 2).reshape(stacked.shape[1], stacked.shape[0] * stacked.shape[2])


def advance(master, moment, average, grad, factor, step_rate):
    scaled = grad * factor
    velocity = MOMENTUM * moment + scaled
    fresh_master = master - step_rate * (scaled + MOMENTUM * velocity)
    smoothed = AVERAGE_DECAY * average + (1.0 - AVERAGE_DECAY) * fresh_master
    return (fresh_master, velocity, smoothed)


def shards_any(
    tokens,
    cotangent,
    segment_ids,
    timesteps,
    qkv_weight,
    out_weight,
    up_weight,
    down_weight,
    time_inner,
    time_outer,
    time_bias,
    head_vectors,
    layer_vectors,
    qkv_moment,
    out_moment,
    up_moment,
    down_moment,
    inner_moment,
    outer_moment,
    bias_moment,
    head_moment,
    layer_moment,
    qkv_average,
    out_average,
    up_average,
    down_average,
    inner_average,
    outer_average,
    bias_average,
    head_average,
    layer_average,
):
    w_qkv, w_out, w_up, w_down, w_inner, w_outer, b_inner, head_vec, layer_vec = (
        lax.all_gather(qkv_weight.astype(jnp.bfloat16), "dp", axis=0, tiled=True),
        lax.all_gather(out_weight.astype(jnp.bfloat16), "dp", axis=1, tiled=True),
        lax.all_gather(up_weight.astype(jnp.bfloat16), "dp", axis=0, tiled=True),
        lax.all_gather(down_weight.astype(jnp.bfloat16), "dp", axis=2, tiled=True),
        lax.all_gather(time_inner.astype(jnp.bfloat16), "dp", axis=0, tiled=True),
        lax.all_gather(time_outer.astype(jnp.bfloat16), "dp", axis=0, tiled=True),
        lax.all_gather(time_bias.astype(jnp.bfloat16), "dp", axis=0, tiled=True),
        lax.all_gather(head_vectors.astype(jnp.bfloat16), "dp", axis=2, tiled=True),
        lax.all_gather(layer_vectors.astype(jnp.bfloat16), "dp", axis=1, tiled=True),
    )
    local_width = w_out.shape[0]
    head_count = local_width // HD
    packed = tokens.shape[0]
    head_rows = head_vec.astype(jnp.float32).reshape(6, local_width)
    layer_rows = layer_vec.astype(jnp.float32)
    score_scale = 1.0 / math.sqrt(HD)
    block_rows = min(PACK, 512)
    block_count = packed // block_rows
    seg_row = segment_ids[0]
    features = time_features(timesteps[0], TD)
    feature_low = features.astype(jnp.bfloat16)
    inner_pre = jnp.dot(feature_low, w_inner, preferred_element_type=jnp.float32) + b_inner.astype(
        jnp.float32
    )
    silu_out, silu_pull = jax.vjp(jax.nn.silu, inner_pre)
    act_low = silu_out.astype(jnp.bfloat16)
    time_embed = jnp.dot(act_low, w_outer, preferred_element_type=jnp.float32) + layer_rows[6]
    onehot = (seg_row[:, None] == jnp.arange(SEGS, dtype=jnp.int32)[None, :]).astype(jnp.float32)
    hidden0 = tokens.astype(jnp.float32) + jnp.dot(
        onehot, time_embed, precision=lax.Precision.HIGHEST, preferred_element_type=jnp.float32
    )
    hidden_low = hidden0.astype(jnp.bfloat16)
    projected = jnp.einsum("pd,dce->pce", hidden_low, w_qkv, preferred_element_type=jnp.float32)
    queries = (projected[:, 0] + head_rows[0]).astype(jnp.bfloat16)
    keys_low = projected[:, 1].astype(jnp.bfloat16)
    values_low = (projected[:, 2] + head_rows[1]).astype(jnp.bfloat16)

    def block_scores(query_blk, key_all, seg_query):
        raw_scores = (
            jnp.einsum("qd,kd->qk", query_blk, key_all, preferred_element_type=jnp.float32)
            * score_scale
        )
        same_doc = seg_query[:, None] == seg_row[None, :]
        return (raw_scores, same_doc)

    def attend_head(head_index):
        query_h = head_slice(queries, head_index)
        key_h = head_slice(keys_low, head_index)
        value_h = head_slice(values_low, head_index)
        out_blocks = []
        sum_blocks = []
        for block_index in range(block_count):
            first_row = block_index * block_rows
            raw_scores, same_doc = block_scores(
                query_h[first_row : first_row + block_rows],
                key_h,
                seg_row[first_row : first_row + block_rows],
            )
            masked = jnp.where(same_doc, raw_scores, -1e30)
            row_peak = jnp.max(masked, axis=1, keepdims=True)
            exponent = jnp.exp(masked - row_peak)
            row_total = jnp.sum(exponent, axis=1, keepdims=True)
            soft_weights = exponent / row_total
            out_blocks.append(
                jnp.dot(
                    soft_weights.astype(jnp.bfloat16), value_h, preferred_element_type=jnp.float32
                )
            )
            sum_blocks.append((row_peak + jnp.log(row_total))[:, 0])
        return (jnp.concatenate(out_blocks, axis=0), jnp.concatenate(sum_blocks, axis=0))

    head_out, log_sums = lax.map(attend_head, jnp.arange(head_count, dtype=jnp.int32))
    att_low = merge_heads(head_out).astype(jnp.bfloat16)
    attn_partial = jnp.dot(att_low, w_out, preferred_element_type=jnp.float32)
    attn_branch = (
        lax.psum(attn_partial.astype(jnp.bfloat16), "tensor").astype(jnp.float32) + layer_rows[0]
    )
    residual1 = hidden0 + attn_branch
    cot_here = cotangent.astype(jnp.float32)
    normed1, norm1_pull = jax.vjp(layer_norm, residual1, layer_rows[1], layer_rows[2])
    norm_here = normed1.astype(jnp.bfloat16)
    up_pre = (
        jnp.einsum("pd,dje->pje", norm_here, w_up, preferred_element_type=jnp.float32)
        + head_rows[2:]
    )
    gelu_out, gelu_pull = jax.vjp(gelu_exact, up_pre)
    hid_low = gelu_out.astype(jnp.bfloat16)
    down_partial = jnp.einsum("pje,jef->pf", hid_low, w_down, preferred_element_type=jnp.float32)
    mlp_branch = (
        lax.psum(down_partial.astype(jnp.bfloat16), "tensor").astype(jnp.float32) + layer_rows[3]
    )
    result, norm2_pull = jax.vjp(layer_norm, normed1 + mlp_branch, layer_rows[4], layer_rows[5])
    output_here = result.astype(jnp.bfloat16)
    back_r2, back_gain2, back_shift2 = norm2_pull(cot_here)
    part_bdown = jnp.sum(back_r2, axis=0)
    back_r2_here = back_r2.astype(jnp.bfloat16)
    grad_down = jnp.einsum("pje,pf->jef", hid_low, back_r2_here, preferred_element_type=jnp.float32)
    back_hid = jnp.einsum("pf,jef->pje", back_r2_here, w_down, preferred_element_type=jnp.float32)
    (back_up,) = gelu_pull(back_hid)
    grad_bup = jnp.sum(back_up, axis=0)
    back_up_low = back_up.astype(jnp.bfloat16)
    grad_up = jnp.einsum("pd,pje->dje", norm_here, back_up_low, preferred_element_type=jnp.float32)
    back_a_part = jnp.einsum("pje,dje->pd", back_up_low, w_up, preferred_element_type=jnp.float32)
    back_a = lax.psum(back_a_part.astype(jnp.bfloat16), "tensor").astype(jnp.float32) + back_r2
    back_r1, back_gain1, back_shift1 = norm1_pull(back_a)
    grad_bout = jnp.sum(back_r1, axis=0)
    back_r1_low = back_r1.astype(jnp.bfloat16)
    grad_out = jnp.einsum("pe,pf->ef", att_low, back_r1_low, preferred_element_type=jnp.float32)
    back_att = jnp.einsum(
        "pf,ef->pe", back_r1_low, w_out, preferred_element_type=jnp.float32
    ).astype(jnp.bfloat16)

    def head_back(head_index):
        query_h = head_slice(queries, head_index)
        key_h = head_slice(keys_low, head_index)
        value_h = head_slice(values_low, head_index)
        grad_h = head_slice(back_att, head_index)
        lse_h = log_sums[head_index]
        key_grad = jnp.zeros((packed, HD), jnp.float32)
        value_grad = jnp.zeros((packed, HD), jnp.float32)
        query_blocks = []
        for block_index in range(block_count):
            first_row = block_index * block_rows
            query_blk = query_h[first_row : first_row + block_rows]
            raw_scores, same_doc = block_scores(
                query_blk, key_h, seg_row[first_row : first_row + block_rows]
            )
            lse_blk = lse_h[first_row : first_row + block_rows]
            soft_weights = jnp.where(same_doc, jnp.exp(raw_scores - lse_blk[:, None]), 0.0)
            grad_blk = grad_h[first_row : first_row + block_rows]
            value_grad = value_grad + jnp.einsum(
                "qk,qd->kd",
                soft_weights.astype(jnp.bfloat16),
                grad_blk,
                preferred_element_type=jnp.float32,
            )
            weight_grad = jnp.einsum(
                "qd,kd->qk", grad_blk, value_h, preferred_element_type=jnp.float32
            )
            row_inner = jnp.sum(soft_weights * weight_grad, axis=1, keepdims=True)
            score_low = (soft_weights * (weight_grad - row_inner)).astype(jnp.bfloat16)
            query_blocks.append(
                jnp.dot(score_low, key_h, preferred_element_type=jnp.float32) * score_scale
            )
            key_grad = (
                key_grad
                + jnp.einsum("qk,qd->kd", score_low, query_blk, preferred_element_type=jnp.float32)
                * score_scale
            )
        return (jnp.concatenate(query_blocks, axis=0), key_grad, value_grad)

    query_grads, key_grads, value_grads = lax.map(
        head_back, jnp.arange(head_count, dtype=jnp.int32)
    )
    query_grad_all = merge_heads(query_grads)
    key_grad_all = merge_heads(key_grads)
    value_grad_all = merge_heads(value_grads)
    grad_bq = jnp.sum(query_grad_all, axis=0)
    grad_bv = jnp.sum(value_grad_all, axis=0)
    proj_grad_low = jnp.stack([query_grad_all, key_grad_all, value_grad_all], axis=1).astype(
        jnp.bfloat16
    )
    grad_qkv = jnp.einsum(
        "pd,pce->dce", hidden_low, proj_grad_low, preferred_element_type=jnp.float32
    )
    back_h_part = jnp.einsum(
        "pce,dce->pd", proj_grad_low, w_qkv, preferred_element_type=jnp.float32
    )
    back_h0 = lax.psum(back_h_part.astype(jnp.bfloat16), "tensor").astype(jnp.float32) + back_r1
    input_grad = back_h0.astype(jnp.bfloat16)
    back_time = jnp.einsum(
        "ps,pd->sd",
        onehot,
        back_h0,
        precision=lax.Precision.HIGHEST,
        preferred_element_type=jnp.float32,
    )
    grad_bouter = jnp.sum(back_time, axis=0)
    back_time_low = back_time.astype(jnp.bfloat16)
    grad_outer = jnp.einsum("su,sd->ud", act_low, back_time_low, preferred_element_type=jnp.float32)
    back_act = jnp.einsum("sd,ud->su", back_time_low, w_outer, preferred_element_type=jnp.float32)
    (back_inner,) = silu_pull(back_act)
    grad_binner = jnp.sum(back_inner, axis=0)
    grad_inner = jnp.einsum(
        "st,su->tu",
        feature_low,
        back_inner.astype(jnp.bfloat16),
        preferred_element_type=jnp.float32,
    )
    grad_head = jnp.concatenate([grad_bq[None], grad_bv[None], grad_bup], axis=0).reshape(
        6, 1, local_width
    )
    grad_layer = jnp.stack(
        [grad_bout, back_gain1, back_shift1, part_bdown, back_gain2, back_shift2, grad_bouter],
        axis=0,
    )
    red_qkv, red_out, red_up, red_down, red_inner, red_outer, red_binner, red_head, red_layer = (
        lax.psum_scatter(grad_qkv, "dp", scatter_dimension=0, tiled=True),
        lax.psum_scatter(grad_out, "dp", scatter_dimension=1, tiled=True),
        lax.psum_scatter(grad_up, "dp", scatter_dimension=0, tiled=True),
        lax.psum_scatter(grad_down, "dp", scatter_dimension=2, tiled=True),
        lax.psum_scatter(grad_inner, "dp", scatter_dimension=0, tiled=True),
        lax.psum_scatter(grad_outer, "dp", scatter_dimension=0, tiled=True),
        lax.psum_scatter(grad_binner, "dp", scatter_dimension=0, tiled=True),
        lax.psum_scatter(grad_head, "dp", scatter_dimension=2, tiled=True),
        lax.psum_scatter(grad_layer, "dp", scatter_dimension=1, tiled=True),
    )
    split_squares = sum(
        (jnp.sum(piece * piece) for piece in (red_qkv, red_out, red_up, red_down, red_head))
    )
    shared_squares = sum(
        (jnp.sum(piece * piece) for piece in (red_inner, red_outer, red_binner, red_layer))
    )
    local_squares = split_squares + shared_squares / lax.axis_size("tensor")
    norm = jnp.sqrt(lax.psum(local_squares, ("dp", "tensor")))
    factor = 1.0 / jnp.maximum(norm, 1.0)
    step_rate = 4.0 * math.sqrt(MPARAMS / D)
    qkv_master, qkv_velocity, qkv_smoothed = advance(
        qkv_weight, qkv_moment, qkv_average, red_qkv, factor, step_rate
    )
    out_master, out_velocity, out_smoothed = advance(
        out_weight, out_moment, out_average, red_out, factor, step_rate
    )
    up_master, up_velocity, up_smoothed = advance(
        up_weight, up_moment, up_average, red_up, factor, step_rate
    )
    down_master, down_velocity, down_smoothed = advance(
        down_weight, down_moment, down_average, red_down, factor, step_rate
    )
    inner_master, inner_velocity, inner_smoothed = advance(
        time_inner, inner_moment, inner_average, red_inner, factor, step_rate
    )
    outer_master, outer_velocity, outer_smoothed = advance(
        time_outer, outer_moment, outer_average, red_outer, factor, step_rate
    )
    bias_master, bias_velocity, bias_smoothed = advance(
        time_bias, bias_moment, bias_average, red_binner, factor, step_rate
    )
    head_master, head_velocity, head_smoothed = advance(
        head_vectors, head_moment, head_average, red_head, factor, step_rate
    )
    layer_master, layer_velocity, layer_smoothed = advance(
        layer_vectors, layer_moment, layer_average, red_layer, factor, step_rate
    )
    return (
        output_here,
        input_grad,
        norm,
        qkv_master,
        out_master,
        up_master,
        down_master,
        inner_master,
        outer_master,
        bias_master,
        head_master,
        layer_master,
        qkv_velocity,
        out_velocity,
        up_velocity,
        down_velocity,
        inner_velocity,
        outer_velocity,
        bias_velocity,
        head_velocity,
        layer_velocity,
        qkv_smoothed,
        out_smoothed,
        up_smoothed,
        down_smoothed,
        inner_smoothed,
        outer_smoothed,
        bias_smoothed,
        head_smoothed,
        layer_smoothed,
    )


F32=jnp.float32; BF=jnp.bfloat16
MESH=pl.DeviceIdType.MESH
NZ,NX,NC,NT=4,2,2,2
ROWS=48; PIECE=384

def place():
    dp=lax.axis_index("dp"); t=lax.axis_index("tensor")
    z=lax.div(dp,4); x=lax.rem(lax.div(dp,2),2); c=lax.rem(dp,2)
    return z,x,c,t
def dev(z,x,c,t):
    return ((z*NX+x)*NC+c,t)

def peers():
    z,x,c,t=place()
    zp=[dev(lax.rem(z+d,NZ),x,c,t) for d in range(1,NZ)]
    return zp,dev(z,1-x,c,t),dev(z,x,c,1-t),dev(z,x,1-c,t)

def greet():
    zp,xp,yp,sp=peers()
    bar=pltpu.get_barrier_semaphore()
    for d in zp+[xp,yp,sp]:
        pl.semaphore_signal(bar,inc=1,device_id=d,device_id_type=MESH)
    pl.semaphore_wait(bar,6)

def rcopy(src,dst,ssem,rsem,d):
    return pltpu.make_async_remote_copy(src_ref=src,dst_ref=dst,send_sem=ssem,recv_sem=rsem,device_id=d,device_id_type=MESH)

L=1024
def dot(a,b,ca,cb):
    return lax.dot_general(a,b,(((ca,),(cb,)),((),())),preferred_element_type=F32)
def ln_stats(v):
    mean=jnp.mean(v,axis=-1,keepdims=True)
    cen=v-mean
    inv=lax.rsqrt(jnp.mean(cen*cen,axis=-1,keepdims=True)+EPSILON)
    return cen*inv,inv

def ln_back(gain,dy,xhat,inv):
    gd=gain*dy
    return (gd-jnp.mean(gd,axis=-1,keepdims=True)-xhat*jnp.mean(gd*xhat,axis=-1,keepdims=True))*inv

def phi_cdf(u):
    return 0.5*(1.0+lax.erf(u*(1.0/math.sqrt(2.0))))

WIDE=13*PIECE
RB=256
def spread(blocks,w,tiles):
    lane=lax.broadcasted_iota(jnp.int32,(16,128),1)
    acc=[jnp.zeros((16,128),F32) for _ in range(tiles+1)]
    for n,b in enumerate(blocks):
        tile,s=divmod(n*w,128)
        wide=jnp.concatenate([jnp.where(lane<w,b,0.0),jnp.zeros((16,128),F32)],axis=1)
        if s: wide=pltpu.roll(wide,s,1)
        acc[tile]=acc[tile]+wide[:,:128]
        acc[tile+1]=acc[tile+1]+wide[:,128:]
    return jnp.concatenate(acc[:tiles],axis=1)

def attend_pair(q_ref,k_ref,v_ref,o_ref,lse_ref,bias_ref,i,bq=512):
    lane=lax.broadcasted_iota(jnp.int32,(1,128),1)
    cs=pl.ds(pl.multiple_of(i*128,128),128)
    kp=k_ref[:,cs]; vT=v_ref[:,cs].T
    bias=bias_ref[...]
    khs=[]
    for h in range(2):
        khs.append(jnp.where((lane//64)==h,kp,jnp.where(lane==(64*(1-h)),bias,jnp.zeros_like(kp))))
    for qi in range(L//bq):
        qp=q_ref[pl.ds(qi*bq,bq),cs]*0.125
        oT=[]
        for h in range(2):
            qh=jnp.where((lane//64)==h,qp,jnp.where(lane==(64*(1-h)),jnp.ones_like(qp),jnp.zeros_like(qp)))
            sT=dot(khs[h],qh,1,1)
            m=jnp.max(sT,axis=0,keepdims=True)
            e=jnp.exp(sT-m)
            l=jnp.sum(e,axis=0,keepdims=True)
            p=(e*(1.0/l)).astype(BF)
            oT.append(dot(vT[h*64:(h+1)*64],p,1,0))
            lse_ref[i,h:h+1,qi*bq:(qi+1)*bq]=m+jnp.log(l)
        o_ref[pl.ds(qi*bq,bq),cs]=jnp.concatenate(oT,axis=0).T.astype(BF)

GCH=[(n*PIECE,PIECE,128*(1+n%2)) for n in range(13)]

def slots(n):
    out={}
    for i in range(n):
        for stage,lag in enumerate((0,1,2,3) if i<4 else (0,2,4,5)): out.setdefault(i+lag,[]).append((stage,i))
    return {k:sorted(v) for k,v in out.items()}
SLOTS=slots(len(GCH)-1)

def gather_steps(g,zs,zr,fs,fr,ss,sr):
    z,x,c,t=place(); zp,xp,yp,sp=peers(); n=len(GCH)-1
    def cols(i): return pl.ds(GCH[i][0],GCH[i][1])
    def ca(i): return pl.ds(GCH[i][0],GCH[i][2])
    def cb(i): return pl.ds(GCH[i][0]+GCH[i][2],GCH[i][1]-GCH[i][2])
    same=lambda r,s,q,d:rcopy(r,r,s,q,d)
    def Z(i):
        src=g.at[:,z,:,c,:,cols(i)] if i==n else g.at[t,z,x,c,:,cols(i)]
        return [same(src,zs.at[i,d],zr.at[i,d],zp[d]) for d in range(3)]
    def A(i):
        if i==n: return [same(g.at[t,z,x,c,:,ca(i)],fs.at[i,0],fr.at[i,0],xp),same(g.at[t,z,x,c,:,cb(i)],fs.at[i,1],fr.at[i,1],yp)]
        return [same(g.at[t,:,x,c,:,ca(i)],fs.at[i,0],fr.at[i,0],xp),same(g.at[t,:,x,c,:,cb(i)],fs.at[i,1],fr.at[i,1],yp)]
    def B(i):
        if i==n: return [same(g.at[t,z,:,c,:,ca(i)],fs.at[i,2],fr.at[i,2],yp),same(g.at[:,z,x,c,:,cb(i)],fs.at[i,3],fr.at[i,3],xp)]
        return [same(g.at[t,:,:,c,:,ca(i)],fs.at[i,2],fr.at[i,2],yp),same(g.at[:,:,x,c,:,cb(i)],fs.at[i,3],fr.at[i,3],xp)]
    S=lambda i:[same(g.at[:,:,:,c,:,cols(i)],ss.at[i],sr.at[i],sp)]
    def go(cs):
        for q in cs: q.start()
    def got(cs):
        for q in cs: q.wait_recv()
    def step(k):
        for stage,i in SLOTS.get(k,()):
            if stage==0:
                got(Z(i)); go(A(i))
                if i+4<n: go(Z(i+4))
            if stage==1: got(A(i)); go(B(i))
            if stage==2: got(B(i)); go(S(i))
            if stage==3: got(S(i))
    def late(k):
        if k==0: go(A(n))
        if k==1: got(A(n)); go(B(n))
        if k==2: got(B(n)); go(Z(n))
        if k==3: got(Z(n)); go(S(n))
        if k==4: got(S(n))
    def first(k): go(Z(k))
    def finish():
        for i in range(n+1):
            for q in Z(i)+A(i)+B(i)+S(i): q.wait_send()
    return step,late,first,finish

def front_kernel(ts_ref,qkv_m,out_m,up_m,down_m,w1_m,w2_m,b1_m,hv_m,lv_m,tok_hbm,cot_hbm,seg_ref,
        q_o,k_o,v_o,o_o,lse_o,out_o,outp_o,dmbT_o,abT_o,drbT_o,hid_o,dub_o,dr1_o,dob_o,hbT_o,wqkv_o,aux_o,sums_o,bup_o,time_o,feat_o,
        g,tok,cot,q,k,v,o,lse,own,bias,vecs,temb,hbT,gp,hid,inv,dmbT,abT,drbT,dr1,a32,
        zs,zr,fs,fr,ss,sr,lsem,osem,hsem,bsem,ysem):
    z,x,c,t=place()
    step,late,first,finish=gather_steps(g,zs,zr,fs,fr,ss,sr)
    win=pl.ds(pl.multiple_of(t*512,512),L)
    ltok=pltpu.make_async_copy(tok_hbm.at[win,:],tok,lsem.at[0]); ltok.start()
    lcot=pltpu.make_async_copy(cot_hbm.at[win,:],cot,lsem.at[1]); lcot.start()
    greet_out()
    a32[...]=jnp.zeros((ROWS,PIECE),F32)
    a32[0:32,:]=w2_m[:,pl.ds(pl.multiple_of(t*PIECE,128),PIECE)]
    a32[32:40,0:256]=w1_m[:,pl.ds(pl.multiple_of(t*256,128),256)]
    a32[32:39,256:304]=lv_m[...]
    a32[39:45,256:280]=hv_m[:,0,:]
    a32[45:46,256:288]=b1_m[...]
    def put(p,val): g[t,z,x,c,:,p*PIECE:(p+1)*PIECE]=val.astype(BF)
    put(0,a32[...])
    greet_in()
    first(0)
    for j in range(3): put(1+j,qkv_m[j])
    put(4,out_m[...])
    first(1); first(2); first(3)
    for j in range(4): put(5+j,up_m[:,j,:])
    for j in range(4): put(9+j,down_m[j])
    late(0)
    ln=lax.broadcasted_iota(jnp.int32,(16,256),1)
    fi=lax.div(ln,16)*8+lax.rem(ln,16)
    theta=jnp.exp(lax.rem(fi,64).astype(F32)*(-math.log(10000.0)/64.0))
    ang=theta*ts_ref[0,t].astype(F32)
    feat=jnp.where(lax.rem(ln,16)<8,jnp.where(fi<64,jnp.cos(ang),jnp.sin(ang)),0.0).astype(BF)
    feat_o[...]=feat
    seg=seg_ref[:,pl.ds(pl.multiple_of(t*512,128),L)]
    own_row=jnp.where(seg==t,1.0,0.0)
    ownT=jnp.broadcast_to(own_row,(128,L)).T
    own[...]=ownT
    bias[...]=jnp.where(ownT>0.5,0.0,-1e30).astype(BF)
    for n in range(4): step(n)
    def vecblk(tt,n): return g[tt,n//4,(n//2)%2,n%2,32:48,256:384].astype(F32)
    b0=[vecblk(0,n) for n in range(16)]; b1=[vecblk(1,n) for n in range(16)]
    lv=spread(b0,48,6)
    hv=jnp.concatenate([spread(b0,24,3),spread(b1,24,3)],axis=1)
    vecs[0:16,:]=lv
    vecs[16:32,:]=hv
    bin_=spread(b0,32,4)[13:14,:]
    w1=jnp.concatenate([g[0,:,:,:,32:48,0:256].reshape(256,256),g[1,:,:,:,32:48,0:256].reshape(256,256)],axis=1)
    inner=dot(feat,w1,1,0)[0:1]+bin_
    sig=1.0/(1.0+jnp.exp(-inner))
    act=inner*sig
    w2=jnp.concatenate([g[0,:,:,:,0:32,0:384].reshape(512,384),g[1,:,:,:,0:32,0:384].reshape(512,384)],axis=1)
    actb=jnp.broadcast_to(act,(16,512)).astype(BF)
    te=dot(actb,w2,1,0)[0:1]+lv[6:7]
    temb[...]=jnp.broadcast_to(te,(8,D))
    time_o[...]=jnp.concatenate([inner,sig,jnp.zeros((6,512),F32)],axis=0)
    ltok.wait()
    outs=[]
    def emit(src,dst):
        cp=pltpu.make_async_copy(src,dst,osem.at[len(outs)]); cp.start(); outs.append(cp)
    def hid_rows(r,_):
        rows=pl.ds(pl.multiple_of(r*RB,RB),RB)
        hb=(tok[rows,:].astype(F32)+temb[0:1,:]).astype(BF)
        hbT[:,rows]=hb.T
        return 0
    lax.fori_loop(0,L//RB,hid_rows,0)
    def project(which,ref,brow):
        def rows_body(r,_):
            rows=pl.ds(pl.multiple_of(r*RB,RB),RB)
            hb=(tok[rows,:].astype(F32)+temb[0:1,:]).astype(BF)
            for tt in range(2):
                val=dot(hb,g[tt,:,:,:,:,(1+which)*PIECE:(2+which)*PIECE].reshape(D,PIECE),1,0)
                if brow is not None: val=val+vecs[brow:brow+1,tt*PIECE:(tt+1)*PIECE]
                ref[rows,tt*PIECE:(tt+1)*PIECE]=val.astype(BF)
            return 0
        lax.fori_loop(0,L//RB,rows_body,0)
    emit(hbT,hbT_o)
    step(4)
    project(0,q,16+7)
    emit(q,q_o)
    step(5); late(1)
    project(1,k,None)
    emit(k,k_o)
    step(6)
    project(2,v,16+8)
    emit(v,v_o)
    emit(g.at[:,:,:,:,:,0:PIECE],aux_o); emit(g.at[:,:,:,:,:,PIECE:4*PIECE],wqkv_o)
    def pair(i,_):
        attend_pair(q,k,v,o,lse,bias,i)
        for s in range(6):
            @pl.when(i==s)
            def _():
                if s==3: late(2)
                step(7+s)
        return 0
    lax.fori_loop(0,6,pair,0)
    emit(o,o_o); emit(lse,lse_o)
    lcot.wait()
    for cp in outs: cp.wait()
    out,dob=q,k
    yp=peers()[2]
    def emits(r):
        rows=pl.ds(pl.multiple_of(r*RB,RB),RB)
        byrow=[(out,out_o),(dr1,dr1_o),(dob,dob_o)]; bycol=[(dmbT,dmbT_o),(abT,abT_o),(drbT,drbT_o)]
        cs=[pltpu.make_async_copy(a.at[rows,:],b.at[rows,:],bsem.at[n,r]) for n,(a,b) in enumerate(byrow)]
        cs+=[pltpu.make_async_copy(a.at[:,rows],b.at[:,rows],bsem.at[3+n,r]) for n,(a,b) in enumerate(bycol)]
        return cs,rcopy(out.at[rows,:],outp_o.at[rows,:],ysem.at[0,r],ysem.at[1,r],yp)
    mid_body(g,tok,cot,o,own,vecs,temb,gp,hid,inv,out,dmbT,abT,drbT,dr1,dob,sums_o,bup_o,hid_o,dub_o,hsem,step,late,emits)
    for r in range(L//RB):
        cs,far=emits(r)
        for cp in cs: cp.wait()
        if r<2: far.wait()
    finish()

def mid_body(g,tok,cot,o,own,vecs,temb,gp,hid,inv,out,dmbT,abT,drbT,dr1,dob,sums_o,bup_o,hid_o,dub_o,hsem,step,late,emits):
    def W(tt,piece,n=1): return g[tt,:,:,:,:,piece*PIECE:(piece+n)*PIECE].reshape(D,n*PIECE)
    row=lambda r:vecs[r:r+1,:]
    sums_o[...]=jnp.zeros((8,D),F32); bup_o[...]=jnp.zeros((8,4*D),F32)
    csum=lambda a:jnp.sum(a,axis=0,keepdims=True)
    def emit_rows(buf,dst,r,which):
        rows=pl.ds(pl.multiple_of(r*RB,RB),RB)
        return pltpu.make_async_copy(buf.at[rows,:],dst.at[rows,:],hsem.at[which,r])
    def up_block(r,_):
        rows=pl.ds(pl.multiple_of(r*RB,RB),RB)
        for n in range(4):
            @pl.when(r==n)
            def _():
                if n==1: late(3)
                step(13+n)
        attn=dot(o[rows,0:PIECE],W(0,4),1,1)+dot(o[rows,PIECE:D],W(1,4),1,1)
        r1=(tok[rows,:].astype(F32)+temb[0:1,:])+(attn+row(0))
        x1,inv1=ln_stats(r1)
        dr1[rows,:]=x1
        inv[rows,:]=jnp.broadcast_to(inv1,(RB,128))
        ab=(x1*row(1)+row(2)).astype(BF)
        abT[:,rows]=ab.T
        for tt in range(2):
            for j in range(4):
                cc=pl.ds((tt*4+j)*PIECE,PIECE)
                u=dot(ab,W(tt,5+j),1,0)+vecs[16+9+j:16+10+j,tt*PIECE:(tt+1)*PIECE]
                cdf=phi_cdf(u)
                gp[rows,cc]=(cdf+u*jnp.exp(-0.5*u*u)*(1.0/math.sqrt(2*math.pi))).astype(BF)
                hid[rows,cc]=(u*cdf).astype(BF)
        emit_rows(hid,hid_o,r,0).start()
        return 0
    lax.fori_loop(0,L//RB,up_block,0)
    late(4)
    def block(r,_):
        rows=pl.ds(pl.multiple_of(r*RB,RB),RB)
        x1=dr1[rows,:]; inv1=inv[rows,0:1]
        a=x1*row(1)+row(2)
        mlp=row(3)
        for tt in range(2):
            mlp=mlp+dot(hid[rows,tt*4*PIECE:(tt+1)*4*PIECE],W(tt,9,4),1,1)
        x2,inv2=ln_stats(a+mlp)
        out[rows,:]=(x2*row(4)+row(5)).astype(BF)
        @pl.when(r<2)
        def _(): emits(r)[1].start()
        dy=jnp.where(own[rows,0:1]>0.5,cot[rows,:].astype(F32),0.0)
        sums_o[4:5,:]+=csum(dy*x2); sums_o[5:6,:]+=csum(dy)
        dr2=ln_back(row(4),dy,x2,inv2)
        sums_o[3:4,:]+=csum(dr2)
        dmb=dr2.astype(BF)
        dmbT[:,rows]=dmb.T
        da=dr2
        for tt in range(2):
            for j in range(4):
                cc=pl.ds((tt*4+j)*PIECE,PIECE)
                du=dot(dmb,W(tt,9+j),1,0)*gp[rows,cc].astype(F32)
                bup_o[0:1,cc]+=csum(du)
                gp[rows,cc]=du.astype(BF)
            da=da+dot(gp[rows,tt*4*PIECE:(tt+1)*4*PIECE],W(tt,5,4),1,1)
        emit_rows(gp,dub_o,r,1).start()
        sums_o[1:2,:]+=csum(da*x1); sums_o[2:3,:]+=csum(da)
        d1=ln_back(row(1),da,x1,inv1)
        sums_o[0:1,:]+=csum(d1)
        dr1[rows,:]=d1
        drb=d1.astype(BF)
        drbT[:,rows]=drb.T
        for tt in range(2):
            dob[rows,tt*PIECE:(tt+1)*PIECE]=dot(drb,W(tt,4),1,0).astype(BF)
        for cp in emits(r)[0]: cp.start()
        return 0
    lax.fori_loop(0,L//RB,block,0)
    for r in range(L//RB):
        emit_rows(hid,hid_o,r,0).wait(); emit_rows(gp,dub_o,r,1).wait()

def front(ts,masters,tokens,cotangent,seg,cid=0):
    DMA=pltpu.SemaphoreType.DMA; n=len(GCH)
    V=lambda s,d=BF:pltpu.VMEM(s,d)
    A=pl.BlockSpec(memory_space=pl.ANY); M=pl.BlockSpec(memory_space=pltpu.VMEM)
    big=lambda s,d=BF:jax.ShapeDtypeStruct(s,d)
    row=(L,D); tr=(D,L)
    G6=lambda w_:(NT,NZ,NX,NC,ROWS,w_)
    return pl.pallas_call(front_kernel,
        in_specs=[pl.BlockSpec(memory_space=pltpu.SMEM)]+[M]*9+[A,A,M],
        out_specs=[A]*17+[M]*4,
        out_shape=[big(row),big(row),big(row),big(row),big((6,2,L),F32),big(row),big((512,D)),big(tr),big(tr),big(tr),big((L,4*D)),big((L,4*D)),
            big(row,F32),big(row),big(tr),big(G6(3*PIECE)),big(G6(PIECE)),big((8,D),F32),big((8,4*D),F32),big((8,512),F32),big((16,256))],
        scratch_shapes=[V(G6(WIDE)),V(row),V(row),V(row),V(row),V(row),V(row),V((6,2,L),F32),V((L,128),F32),V((L,128)),V((32,D),F32),V((8,D),F32),
            V(tr),V((L,4*D)),V((L,4*D)),V((L,128),F32),V(tr),V(tr),V(tr),V(row,F32),V((ROWS,PIECE),F32),
            DMA((n,3)),DMA((n,3)),DMA((n,4)),DMA((n,4)),DMA((n,)),DMA((n,)),DMA((2,)),DMA((8,)),DMA((2,L//RB)),DMA((6,L//RB)),DMA((2,L//RB))],
        compiler_params=pltpu.CompilerParams(collective_id=cid,has_side_effects=True,vmem_limit_bytes=63*2**20),name="front")(ts,*masters,tokens,cotangent,seg)

def group(g,r,w,a): return dict(g=g,r=r,w=w,a=a)
RGR=[group(0,0,768,-1),group(768,768,768,0),group(1536,1536,768,-1),group(2304,2304,768,0),group(3072,3072,384,-1),
     group(3456,3456,384,0),group(3840,3840,384,0),group(0,4224,384,256)]
RW=12*PIECE
GBW=11*PIECE
_a=_b=_p=_q=0
for _g in RGR:
    if _g["a"]>=0:
        _g["ao"]=_a; _g["bo"]=_b; _g["po"]=_p; _a+=_g["a"]; _b+=_g["w"]-_g["a"]; _p+=_g["w"]
    else:
        _g["qo"]=_q; _q+=_g["w"]
RWA,RWB,RWP,RWQ=max(_a,128),_b,_p,_q

def scatter_steps(gb,rs,ra,rc,rb,rz,rx,rq,ry,red,ss,sr,as_,ar,bs,br,zs,zr):
    z,x,c,t=place(); zp,xp,yp,sp=peers()
    def go(cs):
        for q in cs: q.start()
    def got(cs):
        for q in cs: q.wait_recv()
    def sums(a,b): return a+b
    def sl(i):
        q=RGR[i]; g,r,w,a=q["g"],q["r"],q["w"],q["a"]
        k=dict(g=pl.ds(g,w),r=pl.ds(r,w))
        if a>=0: k.update(ga=pl.ds(g,a),gb=pl.ds(g+a,w-a),a=pl.ds(q["ao"],a),b=pl.ds(q["bo"],w-a),p=pl.ds(q["po"],w),pa=pl.ds(q["po"],a),pb=pl.ds(q["po"]+a,w-a))
        else: k.update(q=pl.ds(q["qo"],w))
        return k
    def S(i):
        k=sl(i); return [rcopy(gb.at[:,:,:,1-c,:,k["g"]],rs.at[:,:,:,:,k["r"]],ss.at[i],sr.at[i],sp)]
    def A(i):
        k=sl(i)
        if "q" in k: return [rcopy(gb.at[:,:,1-x,c,:,k["g"]],rx.at[:,:,:,k["q"]],as_.at[i,0],ar.at[i,0],xp)]
        one=[rcopy(gb.at[:,:,1-x,c,:,k["ga"]],ra.at[:,:,:,k["a"]],as_.at[i,0],ar.at[i,0],xp)] if RGR[i]["a"] else []
        return one+[rcopy(gb.at[1-t,:,:,c,:,k["gb"]],rc.at[:,:,:,k["b"]],as_.at[i,1],ar.at[i,1],yp)]
    def zdst(d): return lax.rem(z+d+1,NZ)
    def B(i):
        k=sl(i)
        if "q" in k: return [rcopy(gb.at[:,zdst(d),x,c,:,k["g"]],rq.at[d,:,:,k["q"]],bs.at[i,d],br.at[i,d],zp[d]) for d in range(3)]
        one=[rcopy(gb.at[1-t,:,x,c,:,k["ga"]],rb.at[:,:,k["pa"]],bs.at[i,0],br.at[i,0],yp)] if RGR[i]["a"] else []
        return one+[rcopy(gb.at[t,:,1-x,c,:,k["gb"]],rb.at[:,:,k["pb"]],bs.at[i,1],br.at[i,1],xp)]
    def Z(i):
        k=sl(i)
        if "q" in k: return [rcopy(gb.at[1-t,z,x,c,:,k["g"]],ry.at[:,k["q"]],zs.at[i,0],zr.at[i,0],yp)]
        return [rcopy(gb.at[t,zdst(d),x,c,:,k["g"]],rz.at[d,:,k["p"]],zs.at[i,d],zr.at[i,d],zp[d]) for d in range(3)]
    def s_to_a(i):
        got(S(i)); k=sl(i)
        def body(n,_):
            tt=lax.div(n,8); zz=lax.rem(lax.div(n,2),4); xx=lax.rem(n,2)
            gb[tt,zz,xx,c,:,k["g"]]=sums(gb[tt,zz,xx,c,:,k["g"]],rs[tt,zz,xx,:,k["r"]])
            return 0
        lax.fori_loop(0,16,body,0)
        go(A(i))
    def a_to_b(i):
        got(A(i)); k=sl(i)
        def body(n,_):
            a=lax.div(n,4); b=lax.rem(n,4)
            if "q" in k:
                gb[a,b,x,c,:,k["g"]]=sums(gb[a,b,x,c,:,k["g"]],rx[a,b,:,k["q"]])
            else:
                if RGR[i]["a"]: gb[a,b,x,c,:,k["ga"]]=sums(gb[a,b,x,c,:,k["ga"]],ra[a,b,:,k["a"]])
                zz=lax.div(n,2); xx=lax.rem(n,2)
                gb[t,zz,xx,c,:,k["gb"]]=sums(gb[t,zz,xx,c,:,k["gb"]],rc[zz,xx,:,k["b"]])
            return 0
        lax.fori_loop(0,8,body,0)
        go(B(i))
    def b_to_z(i):
        got(B(i)); k=sl(i)
        if "q" in k:
            for a in range(2):
                acc=gb[a,z,x,c,:,k["g"]].astype(F32)
                for d in range(3): acc=acc+rq[d,a,:,k["q"]].astype(F32)
                gb[a,z,x,c,:,k["g"]]=acc.astype(BF)
        else:
            def body(n,_):
                gb[t,n,x,c,:,k["g"]]=sums(gb[t,n,x,c,:,k["g"]],rb[n,:,k["p"]])
                return 0
            lax.fori_loop(0,4,body,0)
        go(Z(i))
    def z_end(i):
        got(Z(i)); k=sl(i)
        acc=gb[t,z,x,c,:,k["g"]].astype(F32)
        if "q" in k: acc=acc+ry[:,k["q"]].astype(F32)
        else:
            for d in range(3): acc=acc+rz[d,:,k["p"]].astype(F32)
        red[:,k["r"]]=acc
    def drain(i):
        for q in S(i)+A(i)+B(i)+Z(i): q.wait_send()
    return S,go,s_to_a,a_to_b,b_to_z,z_end,drain

def attend_back(q_ref,k_ref,v_ref,do_ref,lse_ref,bias_ref,hvs,i,bq=512):
    lane=lax.broadcasted_iota(jnp.int32,(1,128),1)
    cs=pl.ds(pl.multiple_of(i*128,128),128)
    kp=k_ref[:,cs]; vp=v_ref[:,cs]; bias=bias_ref[...]
    khs=[];vhs=[]
    for h in range(2):
        sel=(lane//64)==h; one=lane==(64*(1-h))
        khs.append(jnp.where(sel,kp,jnp.where(one,bias,jnp.zeros_like(kp))))
        vhs.append(jnp.where(sel,vp,jnp.zeros_like(vp)))
    kT=kp.T
    dk=[None,None];dv=[None,None]; sq=None
    for qi in range(L//bq):
        rows=pl.ds(qi*bq,bq)
        qp=q_ref[rows,cs]*0.125; dop=do_ref[rows,cs]
        dqT=[]
        for h in range(2):
            sel=(lane//64)==h; one=lane==(64*(1-h))
            zero=jnp.zeros_like(qp)
            qh=jnp.where(sel,qp,jnp.where(one,jnp.ones_like(qp),zero))
            doh=jnp.where(sel,dop,zero)
            qz=jnp.where(sel,qp,zero)
            sT=dot(khs[h],qh,1,1)
            p=jnp.exp(sT-lse_ref[i,h:h+1,qi*bq:(qi+1)*bq])
            dp=dot(vhs[h],doh,1,1)
            d=jnp.sum(p*dp,axis=0,keepdims=True)
            ds=(p*(dp-d)).astype(BF)
            pb=p.astype(BF)
            a=dot(pb,doh,1,0); dv[h]=a if dv[h] is None else dv[h]+a
            a=dot(ds,qz,1,0); dk[h]=a if dk[h] is None else dk[h]+a
            dqT.append(dot(kT[h*64:(h+1)*64],ds,1,0))
        dq=jnp.concatenate(dqT,axis=0).T*0.125
        s=jnp.sum(dq,axis=0,keepdims=True); sq=s if sq is None else sq+s
        q_ref[rows,cs]=dq.astype(BF)
    k_ref[:,cs]=(dk[0]+dk[1]).astype(BF)
    dvv=dv[0]+dv[1]
    v_ref[:,cs]=dvv.astype(BF)
    hvs[0:1,cs]=sq
    hvs[1:2,cs]=jnp.sum(dvv,axis=0,keepdims=True)

def unspread(src,w,n):
    lane=lax.broadcasted_iota(jnp.int32,(16,128),1)
    tile,s=divmod(n*w,128)
    wide=src[:,tile*128:(tile+2)*128]
    if s: wide=pltpu.roll(wide,256-s,1)
    return jnp.where(lane<w,wide[:,:128],0.0)

def back_kernel(q_h,k_h,v_h,do_h,o_h,lse_h,dmbT_h,abT_h,drbT_h,hbT_h,hid_h,dub_h,dr1_h,wqkv_h,aux_h,out_h,seg_ref,feat_ref,sums_ref,bup_ref,time_ref,
        in_o,inp_o,outp_o,red,w2g,w1g,vecg,tot,
        q,k,v,do,lse,bias,st,ta,tb,wq,dr1,aux,ow,hvs,lvs,hsrc,dtm,nv,nr,nz,vg,vs,vx,vz,vy,sg,mat,aT,fT,dT,
        gb,rs,ra,rc,rb,rz,rx,rq,ry,ss,sr,as_,ar,bs,br,zs,zr,ls,ts,xs,ns,nrs,os,vsm,vrm,gsm,grm):
    z,x,c,t=place(); zp,xp,yp,sp=peers()
    inw=do
    S,go,s_to_a,a_to_b,b_to_z,z_end,drain=scatter_steps(gb,rs,ra,rc,rb,rz,rx,rq,ry,red,ss,sr,as_,ar,bs,br,zs,zr)
    def load(src,dst,n):
        return pltpu.make_async_copy(src,dst,ls.at[n])
    LQ=[load(q_h,q,0),load(k_h,k,1),load(v_h,v,2),load(do_h,do,3),load(lse_h,lse,4)]
    LW=[load(wqkv_h,wq,5),load(dr1_h,dr1,6),load(aux_h,aux,7)]
    def tcopy(src,buf,n): return pltpu.make_async_copy(src,buf,ts.at[n])
    def stage(src,cols,n):
        return [pltpu.make_async_copy(src.at[:,pl.ds(cs,PIECE)],st.at[s],ts.at[n+s]) for s,cs in enumerate(cols)]
    pc=lambda j:[tt*4*PIECE+jj*PIECE for jj in (j,j+1) for tt in range(2)]
    ST=[stage(hid_h,pc(0),4),stage(hid_h,pc(2),8),stage(dub_h,pc(0),4),stage(dub_h,pc(2),8),stage(o_h,[0,PIECE],4)]
    for q_ in [tcopy(dmbT_h,ta,0),*ST[0],tcopy(abT_h,tb,1)]+LQ+LW: q_.start()
    greet_out()
    lo=load(out_h.at[pl.ds(512,512),:],ow,9); lo.start()
    cout=[rcopy(ow.at[pl.ds(n*256,256),:],outp_o.at[pl.ds(n*256,256),:],os.at[0,n],os.at[1,n],yp) for n in range(2)]
    seg=seg_ref[:,pl.ds(pl.multiple_of(t*512,128),L)]
    bias[...]=jnp.broadcast_to(jnp.where(seg==t,0.0,-1e30),(128,L)).T.astype(BF)
    def compute(i,lhs,n):
        base=RGR[i]["g"]
        for q_ in ST[i]: q_.wait()
        def body(s,_):
            tt=lax.rem(s,2); cs=pl.ds(pl.multiple_of(base+lax.div(s,2)*PIECE,128),PIECE)
            gb[tt,:,:,:,:,cs]=dot(lhs[...],st[s],1,0).astype(BF).reshape(NZ,NX,NC,ROWS,PIECE)
            return 0
        lax.fori_loop(0,n,body,0)
        if i+1<len(ST):
            for q_ in ST[i+1]: q_.start()
        if i==0:
            greet_in()
            lo.wait()
            for q_ in cout: q_.start()
        go(S(i))
    tcopy(dmbT_h,ta,0).wait()
    compute(0,ta,4)
    compute(1,ta,4)
    tcopy(drbT_h,ta,2).start()
    tcopy(abT_h,tb,1).wait()
    s_to_a(0)
    compute(2,tb,4)
    s_to_a(1)
    compute(3,tb,4)
    tcopy(hbT_h,tb,3).start()
    s_to_a(2)
    tcopy(drbT_h,ta,2).wait()
    compute(4,ta,2)
    s_to_a(3); a_to_b(0)
    for q_ in LQ: q_.wait()
    tcopy(hbT_h,tb,3).wait()
    def quad(i,n):
        base=RGR[i]["g"]
        for tt in range(2):
            o_=tt*PIECE+n*128
            rhs=jnp.concatenate([q[:,o_:o_+128],k[:,o_:o_+128],v[:,o_:o_+128]],axis=1)
            gb[tt,:,:,:,:,base:base+PIECE]=dot(tb[...],rhs,1,0).astype(BF).reshape(NZ,NX,NC,ROWS,PIECE)
        go(S(i))
    def pair(i,_):
        @pl.when(i==1)
        def _():
            s_to_a(4); a_to_b(1)
        @pl.when(i==2)
        def _():
            a_to_b(2); b_to_z(0); quad(5,0)
        @pl.when(i==3)
        def _():
            s_to_a(5); a_to_b(3); b_to_z(1)
        @pl.when(i==4)
        def _():
            a_to_b(4); z_end(0); b_to_z(2); quad(6,1)
        @pl.when(i==5)
        def _():
            s_to_a(6); a_to_b(5); b_to_z(3); z_end(1)
        attend_back(q,k,v,do,lse,bias,hvs,lax.div(i,2)+3*lax.rem(i,2))
        return 0
    lax.fori_loop(0,6,pair,0)
    z_end(2); b_to_z(4)
    lvs[...]=jnp.zeros((16,D+128),F32)
    lvs[0:6,0:D]=sums_ref[0:6,:]
    hsrc[...]=jnp.zeros((16,2*(PIECE+128)),F32)
    for tt in range(2):
        o0=tt*(PIECE+128); cc=slice(tt*PIECE,(tt+1)*PIECE)
        hsrc[7:9,o0:o0+PIECE]=hvs[0:2,cc]
        for j in range(4): hsrc[9+j:10+j,o0:o0+PIECE]=bup_ref[0:1,(tt*4+j)*PIECE:(tt*4+j+1)*PIECE]
    for n in range(16):
        both=unspread(lvs[...],48,n)
        for tt in range(2):
            vg[tt,n//4,(n//2)%2,n%2]=(both+unspread(hsrc[:,tt*(PIECE+128):(tt+1)*(PIECE+128)],24,n)).astype(BF)
    def pass_on(k):
        src=[sg.at[t,z,x,c],sg.at[:,z,x,c],sg.at[:,z,:,c],sg.at[:,z]][k]
        if k==3: return [rcopy(src,src,gsm.at[3+d],grm.at[3+d],zp[d]) for d in range(3)]
        return [rcopy(src,src,gsm.at[k],grm.at[k],(yp,xp,sp)[k])]
    def vec_send(k):
        if k==0: return [rcopy(vg.at[1-t],vy,vsm.at[0],vrm.at[0],yp)]
        if k==1: return [rcopy(vg.at[t,:,1-x],vx,vsm.at[1],vrm.at[1],xp)]
        if k==2: return [rcopy(vg.at[t,:,x,1-c],vs,vsm.at[2],vrm.at[2],sp)]
        return [rcopy(vg.at[t,lax.rem(z+d+1,NZ),x,c],vz.at[d],vsm.at[3+d],vrm.at[3+d],zp[d]) for d in range(3)]
    def vec(k):
        if k>0:
            for q_ in vec_send(k-1): q_.wait_recv()
        if k==1: vg[t]=vg[t]+vy[...]
        if k==2: vg[t,:,x]=vg[t,:,x]+vx[...]
        if k==3: vg[t,:,x,c]=vg[t,:,x,c]+vs[...]
        if k<4:
            for q_ in vec_send(k): q_.start()
        else:
            acc=vg[t,z,x,c].astype(F32)
            for d in range(3): acc=acc+vz[d].astype(F32)
            vecg[...]=acc
    def rows_on(k):
        if k>0:
            for q_ in pass_on(k-1): q_.wait_recv()
        if k<4:
            for q_ in pass_on(k): q_.start()
    vec(0)
    drain(0)
    quad(7,2)
    a_to_b(6); z_end(3); b_to_z(5)
    vec(1)
    for q_ in LW: q_.wait()
    dtm[...]=jnp.zeros((8,D),F32)
    def far(r):
        rows=pl.ds(pl.multiple_of(r*RB,RB),RB)
        return rcopy(inw.at[rows,:],inp_o.at[rows,:],xs.at[0,r],xs.at[1,r],yp)
    def rows_body(r,_):
        rows=pl.ds(pl.multiple_of(r*RB,RB),RB)
        acc=dr1[rows,:]
        for n,ref in enumerate((q,k,v)):
            for tt in range(2):
                acc=acc+dot(ref[rows,tt*PIECE:(tt+1)*PIECE],wq[tt,:,:,:,:,n*PIECE:(n+1)*PIECE].reshape(D,PIECE),1,1)
        inw[rows,:]=acc.astype(BF)
        dtm[0:1,:]+=jnp.sum(acc,axis=0,keepdims=True)
        return 0
    s_to_a(7)
    lax.fori_loop(0,2,rows_body,0)
    a_to_b(7)
    far(0).start()
    vec(2)
    lax.fori_loop(2,L//RB,rows_body,0)
    cinl=pltpu.make_async_copy(inw,in_o,ls.at[8]); cinl.start()
    dtb=dtm[0:1,:].astype(BF)
    inner=time_ref[0:1,:]; sig=time_ref[1:2,:]
    w2=jnp.concatenate([aux[0,:,:,:,0:32,:].reshape(512,PIECE),aux[1,:,:,:,0:32,:].reshape(512,PIECE)],axis=1)
    dinner=dot(jnp.broadcast_to(dtb,(16,D)),w2,1,1)[0:1]*(sig*(1.0+inner*(1.0-sig)))
    act=(inner*sig).astype(BF).astype(F32)
    sg[t,z,x,c,0:1,:]=jnp.concatenate([act,dtm[0:1,:],dinner,feat_ref[0:1,:].astype(F32)],axis=1)
    rows_on(0)
    far(1).start(); far(2).start(); far(3).start()
    vec(3)
    b_to_z(6); z_end(4); z_end(5)
    rows_on(1)
    b_to_z(7)
    vec(4)
    rows_on(2)
    z_end(6)
    rows_on(3)
    z_end(7)
    vv=vecg[...]
    big=red[...]
    part=jnp.sum(big*big)+jnp.sum(jnp.where(lax.broadcasted_iota(jnp.int32,(16,128),0)<7,0.5,1.0)*vv*vv)
    nv[0]=jnp.full((8,128),part,F32)
    def swap(s,peer): return rcopy(nv.at[s],nr.at[s],ns.at[s],nrs.at[s],peer)
    swap(0,xp).start()
    rows_on(4)
    for n in range(32): mat[n:n+1,:]=sg[n//16,(n//4)%4,(n//2)%2,n%2]
    aT[...]=mat[:,0:512].T
    fT[...]=mat[:,1792:2048].T
    dp=lax.axis_index("dp")
    g2=dot(aT[pl.ds(pl.multiple_of(dp*32,32),32),:].astype(BF),mat[:,512:1280].astype(BF),1,0)
    g1=dot(fT[pl.ds(pl.multiple_of(dp*16,16),16),:].astype(BF),mat[:,1280:1792].astype(BF),1,0)
    w2g[...]=g2; w1g[...]=g1
    def own_sum(m,w):
        dT[0:m.shape[1],:]=m.T
        col=jnp.sum(dT[pl.ds(pl.multiple_of(dp*w,16),w),:],axis=1,keepdims=True)
        return jnp.broadcast_to(col,(w,128)).T[0:1,:]
    vecg[6:7,0:48]=own_sum(mat[:,512:1280],48)
    vecg[13:14,0:32]=own_sum(mat[:,1280:1792],32)
    sq=lambda a:jnp.sum(a*a)
    rest=(sq(dot(aT[...].astype(BF),mat[:,512:1280].astype(BF),1,0))+sq(dot(fT[...].astype(BF),mat[:,1280:1792].astype(BF),1,0))
        +sq(jnp.sum(mat[:,512:1280],axis=0,keepdims=True))+sq(jnp.sum(mat[:,1280:1792],axis=0,keepdims=True)))
    swap(0,xp).wait()
    nv[1]=nv[0]+nr[0]
    swap(1,sp).start(); swap(1,sp).wait()
    nv[2]=nv[1]+nr[1]
    cz=[rcopy(nv.at[2],nz.at[z],ns.at[3+d],nrs.at[3+d],zp[d]) for d in range(3)]
    for q_ in cz: q_.start()
    nz[z]=nv[2]
    for q_ in cz: q_.wait()
    nv[3]=((nz[0]+nz[1])+nz[2])+nz[3]
    cy=rcopy(nv.at[3],nr.at[2],ns.at[2],nrs.at[2],yp); cy.start(); cy.wait()
    tot[...]=(nv[3]+nr[2])+rest
    cinl.wait()
    for q_ in cout: q_.wait()
    for k_ in range(4):
        for q_ in pass_on(k_)+vec_send(k_): q_.wait_send()
    for r in range(4): far(r).wait()
    for i in range(1,8): drain(i)

def back(q,k,v,dob,o,lse,dmbT,abT,drbT,hbT,hid,dub,dr1,wqkv,aux,out_win,seg,featp,sums,bups,tstate,cid=1):
    DMA=pltpu.SemaphoreType.DMA; n=len(RGR)
    V=lambda s,d=BF:pltpu.VMEM(s,d)
    A=pl.BlockSpec(memory_space=pl.ANY); M=pl.BlockSpec(memory_space=pltpu.VMEM)
    sd=jax.ShapeDtypeStruct; row=(L,D); tr=(D,L)
    return pl.pallas_call(back_kernel,
        in_specs=[A]*16+[M]*5,out_specs=[A]*3+[M]*5,
        out_shape=[sd(row,BF),sd(row,BF),sd((512,D),BF),sd((ROWS,RW),F32),sd((32,D),F32),sd((16,512),F32),sd((16,128),F32),sd((8,128),F32)],
        scratch_shapes=[V(row),V(row),V(row),V(row),V((6,2,L),F32),V((L,128)),V((4,L,PIECE)),V(tr),V(tr),V((NT,NZ,NX,NC,ROWS,3*PIECE)),V(row,F32),
            V((NT,NZ,NX,NC,ROWS,PIECE)),V((512,D)),V((8,D),F32),V((16,D+128),F32),V((16,2*(PIECE+128)),F32),V((8,D),F32),
            V((4,8,128),F32),V((3,8,128),F32),V((4,8,128),F32),
            V((NT,NZ,NX,NC,16,128)),V((NZ,16,128)),V((NZ,NC,16,128)),V((3,16,128)),V((NZ,NX,NC,16,128)),V((NT,NZ,NX,NC,1,2048),F32),V((32,2048),F32),V((512,32),F32),V((256,32),F32),V((D,32),F32),
            V((NT,NZ,NX,NC,ROWS,GBW)),V((NT,NZ,NX,ROWS,RW)),V((NT,NZ,ROWS,RWA)),V((NZ,NX,ROWS,RWB)),V((NZ,ROWS,RWP)),V((3,ROWS,RWP)),
            V((NT,NZ,ROWS,RWQ)),V((3,NT,ROWS,RWQ)),V((ROWS,RWQ)),
            DMA((n,)),DMA((n,)),DMA((n,2)),DMA((n,2)),DMA((n,3)),DMA((n,3)),DMA((n,3)),DMA((n,3)),DMA((10,)),DMA((12,)),DMA((2,4)),DMA((6,)),DMA((6,)),DMA((2,2)),DMA((6,)),DMA((6,)),DMA((6,)),DMA((6,))],
        compiler_params=pltpu.CompilerParams(collective_id=cid,has_side_effects=True,vmem_limit_bytes=63*2**20),name="back")(
            q,k,v,dob,o,lse,dmbT,abT,drbT,hbT,hid,dub,dr1,wqkv,aux,out_win,seg,featp,sums,bups,tstate)

def greet_out():
    zp,xp,yp,sp=peers()
    bar=pltpu.get_barrier_semaphore()
    for d in zp+[xp,yp,sp]:
        pl.semaphore_signal(bar,inc=1,device_id=d,device_id_type=MESH)
def greet_in():
    pl.semaphore_wait(pltpu.get_barrier_semaphore(),6)

def update_kernel(*refs):
    red,w2g,w1g,vecg,tot,seg_ref,ow,op,op2,iw,ip=refs[:11]
    hbm=refs[11:38]
    out_o,in_o,norm_o=refs[38:41]
    far=refs[41:68]
    ps,ns=refs[68:95],refs[95:122]
    ms,vs,avs=ps[:9],ps[9:18],ps[18:]
    nm,nv,na=ns[:9],ns[9:18],ns[18:]
    mine,theirs,mid,sem,psem,nsem=refs[122:]
    pin=[pltpu.make_async_copy(a,b,psem.at[n]) for n,(a,b) in enumerate(zip(hbm,ps))]
    for q in pin: q.start()
    t=lax.axis_index("tensor")
    half=lambda k:pl.ds(pl.multiple_of(k*512,512),512)
    ins=[]
    for n,(w,ps_) in enumerate(((ow,(op,op2)),(iw,(ip,)))):
        ins.append(pltpu.make_async_copy(w,mine.at[n],sem.at[n,0]))
        step=L//len(ps_)
        ins+=[pltpu.make_async_copy(p,theirs.at[n,pl.ds(m*step,step),:],sem.at[n,5+m]) for m,p in enumerate(ps_)]
    for q in ins: q.start()
    norm=jnp.sqrt(tot[...])
    norm_o[0,0]=norm[0,0]
    factor=(1.0/jnp.maximum(norm,1.0))[0:1,0:1]
    rate=4.0*math.sqrt(MPARAMS/D)
    def upd(i,idx,g):
        sc=g*factor
        vel=MOMENTUM*vs[i][idx]+sc
        fm=ms[i][idx]-rate*(sc+MOMENTUM*vel)
        nv[i][idx]=vel; nm[i][idx]=fm
        na[i][idx]=AVERAGE_DECAY*avs[i][idx]+(1.0-AVERAGE_DECAY)*fm
    al=slice(None)
    for q in pin: q.wait()
    nout=[pltpu.make_async_copy(a,b,nsem.at[n]) for n,(a,b) in enumerate(zip(ns,far))]
    def flush(i):
        for n in (i,i+9,i+18): nout[n].start()
    for n in range(3):
        for c in range(3):
            b=9*PIECE+n*PIECE+c*128
            upd(0,(c,al,slice(n*128,(n+1)*128)),red[:,b:b+128])
    flush(0)
    upd(1,(al,al),red[:,8*PIECE:9*PIECE])
    flush(1)
    for j in range(4):
        upd(2,(al,j,al),red[:,(4+j)*PIECE:(5+j)*PIECE])
        upd(3,(j,),red[:,j*PIECE:(j+1)*PIECE])
    flush(2); flush(3)
    upd(4,(al,al),w1g[0:8,:])
    upd(5,(al,al),w2g[...])
    upd(6,(al,al),vecg[13:14,0:32])
    upd(7,(al,0,al),vecg[7:13,0:24])
    upd(8,(al,al),vecg[0:7,0:48])
    for i in range(4,9): flush(i)
    own=jnp.broadcast_to(jnp.where(seg_ref[:,512:1024]==t,1.0,0.0),(128,512)).T[:,0:1]>0.5
    for q in ins: q.wait()
    last=[]
    for n,o in enumerate((out_o,in_o)):
        last+=[pltpu.make_async_copy(mine.at[n,half(t),:],o.at[half(2*t),:],sem.at[n,2]),pltpu.make_async_copy(theirs.at[n,half(1-t),:],o.at[half(2*(1-t)),:],sem.at[n,3])]
        mid[n]=jnp.where(own,mine[n,half(1-t),:].astype(F32),theirs[n,half(t),:].astype(F32)).astype(BF)
        last.append(pltpu.make_async_copy(mid.at[n],o.at[pl.ds(512,512),:],sem.at[n,4]))
        for q in last[-3:]: q.start()
    for q in last+nout: q.wait()

def update(red,w2g,w1g,vecg,tot,seg,ow,op,op2,iw,ip,masters,moments,averages):
    A=pl.BlockSpec(memory_space=pl.ANY); M=pl.BlockSpec(memory_space=pltpu.VMEM)
    sd=jax.ShapeDtypeStruct
    ps=[sd(m.shape,F32) for m in masters]
    whole=sd((PACK,D),BF)
    return pl.pallas_call(update_kernel,in_specs=[M]*6+[A]*5+[A]*27,out_specs=[A,A,pl.BlockSpec(memory_space=pltpu.SMEM)]+[A]*27,
        out_shape=[whole,whole,sd((1,1),F32)]+ps*3,
        scratch_shapes=[pltpu.VMEM(p.shape,F32) for p in ps*6]+[pltpu.VMEM((2,L,D),BF),pltpu.VMEM((2,L,D),BF),pltpu.VMEM((2,512,D),BF),pltpu.SemaphoreType.DMA((2,7)),pltpu.SemaphoreType.DMA((27,)),pltpu.SemaphoreType.DMA((27,))],
        compiler_params=pltpu.CompilerParams(vmem_limit_bytes=63*2**20),name="upd")(red,w2g,w1g,vecg,tot,seg,ow,op,op2,iw,ip,*masters,*moments,*averages)

def shards_fast(tokens,cotangent,segment_ids,timesteps,*params):
    def turn(n,p): return {0:lambda:p.transpose(1,0,2),1:lambda:p.T,3:lambda:p.transpose(0,2,1),6:lambda:p.reshape(1,-1)}.get(n,lambda:p)()
    def back_turn(n,p): return {0:lambda:p.transpose(1,0,2),1:lambda:p.T,3:lambda:p.transpose(0,2,1),6:lambda:p.reshape(-1)}.get(n,lambda:p)()
    line=lambda ps:[turn(n,p) for n,p in enumerate(ps)]
    masters,moments,averages=line(params[:9]),line(params[9:18]),line(params[18:])
    q,k,v,o,lse,out_win,out_peer,dmbT,abT,drbT,hid,dub,dr1,dob,hbT,wq6,aux6,sums,bups,tstate,featp=front(timesteps,masters,tokens,cotangent,segment_ids)
    in_win,in_peer,out_peer2,red,w2g,w1g,vecg,total=back(q,k,v,dob,o,lse,dmbT,abT,drbT,hbT,hid,dub,dr1,wq6,aux6,out_win,segment_ids,featp,sums,bups,tstate)
    res=update(red,w2g,w1g,vecg,total,segment_ids,out_win,out_peer,out_peer2,in_win,in_peer,masters,moments,averages)
    return (res[0],res[1],res[2].reshape(()))+tuple(back_turn(n%9,r) for n,r in enumerate(res[3:]))


def solution(mesh):
    fast=dict(mesh.shape)=={'dp':16,'tensor':2}
    return jax.shard_map(
        shards_fast if fast else shards_any,
        mesh=mesh,
        in_specs=(
            P("dp", None),
            P("dp", None),
            P("dp", None),
            P("dp", None),
            P("dp", None, "tensor"),
            P("tensor", "dp"),
            P("dp", None, "tensor"),
            P(None, "tensor", "dp"),
            P("dp", None),
            P("dp", None),
            P("dp"),
            P(None, "tensor", "dp"),
            P(None, "dp"),
            P("dp", None, "tensor"),
            P("tensor", "dp"),
            P("dp", None, "tensor"),
            P(None, "tensor", "dp"),
            P("dp", None),
            P("dp", None),
            P("dp"),
            P(None, "tensor", "dp"),
            P(None, "dp"),
            P("dp", None, "tensor"),
            P("tensor", "dp"),
            P("dp", None, "tensor"),
            P(None, "tensor", "dp"),
            P("dp", None),
            P("dp", None),
            P("dp"),
            P(None, "tensor", "dp"),
            P(None, "dp"),
        ),
        out_specs=(
            P("dp", None),
            P("dp", None),
            P(),
            P("dp", None, "tensor"),
            P("tensor", "dp"),
            P("dp", None, "tensor"),
            P(None, "tensor", "dp"),
            P("dp", None),
            P("dp", None),
            P("dp"),
            P(None, "tensor", "dp"),
            P(None, "dp"),
            P("dp", None, "tensor"),
            P("tensor", "dp"),
            P("dp", None, "tensor"),
            P(None, "tensor", "dp"),
            P("dp", None),
            P("dp", None),
            P("dp"),
            P(None, "tensor", "dp"),
            P(None, "dp"),
            P("dp", None, "tensor"),
            P("tensor", "dp"),
            P("dp", None, "tensor"),
            P(None, "tensor", "dp"),
            P("dp", None),
            P("dp", None),
            P("dp"),
            P(None, "tensor", "dp"),
            P(None, "dp"),
        ),
        check_vma=False,
    )
```

```python
import functools
import math

import jax
import jax.numpy as jnp
from jax import lax
from jax.experimental import pallas as pl
from jax.experimental.pallas import tpu as pltpu
from jax.sharding import PartitionSpec as P

D = 768
HD = 64
TD = 128
SEGS = 2
PACK = 1536
MPARAMS = 7536640


EPSILON = 1e-05
MOMENTUM = 0.5
AVERAGE_DECAY = 0.5


def layer_norm(values, gain_vec, shift_vec):
    centre = jnp.mean(values, axis=-1, keepdims=True)
    centred = values - centre
    spread = jnp.mean(centred * centred, axis=-1, keepdims=True)
    return centred * lax.rsqrt(spread + EPSILON) * gain_vec + shift_vec


def time_features(step_ids, feat_width):
    midpoint = feat_width // 2
    frequency = jnp.exp(-math.log(10000.0) * jnp.arange(midpoint, dtype=jnp.float32) / midpoint)
    angles = step_ids.astype(jnp.float32)[..., None] * frequency
    return jnp.concatenate([jnp.cos(angles), jnp.sin(angles)], axis=-1)


def gelu_exact(values):
    return jax.nn.gelu(values, approximate=False)


def head_slice(matrix, head_index):
    return lax.dynamic_slice_in_dim(matrix, head_index * HD, HD, 1)


def merge_heads(stacked):
    return stacked.transpose(1, 0, 2).reshape(stacked.shape[1], stacked.shape[0] * stacked.shape[2])


def advance(master, moment, average, grad, factor, step_rate):
    scaled = grad * factor
    velocity = MOMENTUM * moment + scaled
    fresh_master = master - step_rate * (scaled + MOMENTUM * velocity)
    smoothed = AVERAGE_DECAY * average + (1.0 - AVERAGE_DECAY) * fresh_master
    return (fresh_master, velocity, smoothed)


def shards_any(
    tokens,
    cotangent,
    segment_ids,
    timesteps,
    qkv_weight,
    out_weight,
    up_weight,
    down_weight,
    time_inner,
    time_outer,
    time_bias,
    head_vectors,
    layer_vectors,
    qkv_moment,
    out_moment,
    up_moment,
    down_moment,
    inner_moment,
    outer_moment,
    bias_moment,
    head_moment,
    layer_moment,
    qkv_average,
    out_average,
    up_average,
    down_average,
    inner_average,
    outer_average,
    bias_average,
    head_average,
    layer_average,
):
    w_qkv, w_out, w_up, w_down, w_inner, w_outer, b_inner, head_vec, layer_vec = (
        lax.all_gather(qkv_weight.astype(jnp.bfloat16), "dp", axis=0, tiled=True),
        lax.all_gather(out_weight.astype(jnp.bfloat16), "dp", axis=1, tiled=True),
        lax.all_gather(up_weight.astype(jnp.bfloat16), "dp", axis=0, tiled=True),
        lax.all_gather(down_weight.astype(jnp.bfloat16), "dp", axis=2, tiled=True),
        lax.all_gather(time_inner.astype(jnp.bfloat16), "dp", axis=0, tiled=True),
        lax.all_gather(time_outer.astype(jnp.bfloat16), "dp", axis=0, tiled=True),
        lax.all_gather(time_bias.astype(jnp.bfloat16), "dp", axis=0, tiled=True),
        lax.all_gather(head_vectors.astype(jnp.bfloat16), "dp", axis=2, tiled=True),
        lax.all_gather(layer_vectors.astype(jnp.bfloat16), "dp", axis=1, tiled=True),
    )
    local_width = w_out.shape[0]
    head_count = local_width // HD
    packed = tokens.shape[0]
    head_rows = head_vec.astype(jnp.float32).reshape(6, local_width)
    layer_rows = layer_vec.astype(jnp.float32)
    score_scale = 1.0 / math.sqrt(HD)
    block_rows = min(PACK, 512)
    block_count = packed // block_rows
    seg_row = segment_ids[0]
    features = time_features(timesteps[0], TD)
    feature_low = features.astype(jnp.bfloat16)
    inner_pre = jnp.dot(feature_low, w_inner, preferred_element_type=jnp.float32) + b_inner.astype(
        jnp.float32
    )
    silu_out, silu_pull = jax.vjp(jax.nn.silu, inner_pre)
    act_low = silu_out.astype(jnp.bfloat16)
    time_embed = jnp.dot(act_low, w_outer, preferred_element_type=jnp.float32) + layer_rows[6]
    onehot = (seg_row[:, None] == jnp.arange(SEGS, dtype=jnp.int32)[None, :]).astype(jnp.float32)
    hidden0 = tokens.astype(jnp.float32) + jnp.dot(
        onehot, time_embed, precision=lax.Precision.HIGHEST, preferred_element_type=jnp.float32
    )
    hidden_low = hidden0.astype(jnp.bfloat16)
    projected = jnp.einsum("pd,dce->pce", hidden_low, w_qkv, preferred_element_type=jnp.float32)
    queries = (projected[:, 0] + head_rows[0]).astype(jnp.bfloat16)
    keys_low = projected[:, 1].astype(jnp.bfloat16)
    values_low = (projected[:, 2] + head_rows[1]).astype(jnp.bfloat16)

    def block_scores(query_blk, key_all, seg_query):
        raw_scores = (
            jnp.einsum("qd,kd->qk", query_blk, key_all, preferred_element_type=jnp.float32)
            * score_scale
        )
        same_doc = seg_query[:, None] == seg_row[None, :]
        return (raw_scores, same_doc)

    def attend_head(head_index):
        query_h = head_slice(queries, head_index)
        key_h = head_slice(keys_low, head_index)
        value_h = head_slice(values_low, head_index)
        out_blocks = []
        sum_blocks = []
        for block_index in range(block_count):
            first_row = block_index * block_rows
            raw_scores, same_doc = block_scores(
                query_h[first_row : first_row + block_rows],
                key_h,
                seg_row[first_row : first_row + block_rows],
            )
            masked = jnp.where(same_doc, raw_scores, -1e30)
            row_peak = jnp.max(masked, axis=1, keepdims=True)
            exponent = jnp.exp(masked - row_peak)
            row_total = jnp.sum(exponent, axis=1, keepdims=True)
            soft_weights = exponent / row_total
            out_blocks.append(
                jnp.dot(
                    soft_weights.astype(jnp.bfloat16), value_h, preferred_element_type=jnp.float32
                )
            )
            sum_blocks.append((row_peak + jnp.log(row_total))[:, 0])
        return (jnp.concatenate(out_blocks, axis=0), jnp.concatenate(sum_blocks, axis=0))

    head_out, log_sums = lax.map(attend_head, jnp.arange(head_count, dtype=jnp.int32))
    att_low = merge_heads(head_out).astype(jnp.bfloat16)
    attn_partial = jnp.dot(att_low, w_out, preferred_element_type=jnp.float32)
    attn_branch = (
        lax.psum(attn_partial.astype(jnp.bfloat16), "tensor").astype(jnp.float32) + layer_rows[0]
    )
    residual1 = hidden0 + attn_branch
    cot_here = cotangent.astype(jnp.float32)
    normed1, norm1_pull = jax.vjp(layer_norm, residual1, layer_rows[1], layer_rows[2])
    norm_here = normed1.astype(jnp.bfloat16)
    up_pre = (
        jnp.einsum("pd,dje->pje", norm_here, w_up, preferred_element_type=jnp.float32)
        + head_rows[2:]
    )
    gelu_out, gelu_pull = jax.vjp(gelu_exact, up_pre)
    hid_low = gelu_out.astype(jnp.bfloat16)
    down_partial = jnp.einsum("pje,jef->pf", hid_low, w_down, preferred_element_type=jnp.float32)
    mlp_branch = (
        lax.psum(down_partial.astype(jnp.bfloat16), "tensor").astype(jnp.float32) + layer_rows[3]
    )
    result, norm2_pull = jax.vjp(layer_norm, normed1 + mlp_branch, layer_rows[4], layer_rows[5])
    output_here = result.astype(jnp.bfloat16)
    back_r2, back_gain2, back_shift2 = norm2_pull(cot_here)
    part_bdown = jnp.sum(back_r2, axis=0)
    back_r2_here = back_r2.astype(jnp.bfloat16)
    grad_down = jnp.einsum("pje,pf->jef", hid_low, back_r2_here, preferred_element_type=jnp.float32)
    back_hid = jnp.einsum("pf,jef->pje", back_r2_here, w_down, preferred_element_type=jnp.float32)
    (back_up,) = gelu_pull(back_hid)
    grad_bup = jnp.sum(back_up, axis=0)
    back_up_low = back_up.astype(jnp.bfloat16)
    grad_up = jnp.einsum("pd,pje->dje", norm_here, back_up_low, preferred_element_type=jnp.float32)
    back_a_part = jnp.einsum("pje,dje->pd", back_up_low, w_up, preferred_element_type=jnp.float32)
    back_a = lax.psum(back_a_part.astype(jnp.bfloat16), "tensor").astype(jnp.float32) + back_r2
    back_r1, back_gain1, back_shift1 = norm1_pull(back_a)
    grad_bout = jnp.sum(back_r1, axis=0)
    back_r1_low = back_r1.astype(jnp.bfloat16)
    grad_out = jnp.einsum("pe,pf->ef", att_low, back_r1_low, preferred_element_type=jnp.float32)
    back_att = jnp.einsum(
        "pf,ef->pe", back_r1_low, w_out, preferred_element_type=jnp.float32
    ).astype(jnp.bfloat16)

    def head_back(head_index):
        query_h = head_slice(queries, head_index)
        key_h = head_slice(keys_low, head_index)
        value_h = head_slice(values_low, head_index)
        grad_h = head_slice(back_att, head_index)
        lse_h = log_sums[head_index]
        key_grad = jnp.zeros((packed, HD), jnp.float32)
        value_grad = jnp.zeros((packed, HD), jnp.float32)
        query_blocks = []
        for block_index in range(block_count):
            first_row = block_index * block_rows
            query_blk = query_h[first_row : first_row + block_rows]
            raw_scores, same_doc = block_scores(
                query_blk, key_h, seg_row[first_row : first_row + block_rows]
            )
            lse_blk = lse_h[first_row : first_row + block_rows]
            soft_weights = jnp.where(same_doc, jnp.exp(raw_scores - lse_blk[:, None]), 0.0)
            grad_blk = grad_h[first_row : first_row + block_rows]
            value_grad = value_grad + jnp.einsum(
                "qk,qd->kd",
                soft_weights.astype(jnp.bfloat16),
                grad_blk,
                preferred_element_type=jnp.float32,
            )
            weight_grad = jnp.einsum(
                "qd,kd->qk", grad_blk, value_h, preferred_element_type=jnp.float32
            )
            row_inner = jnp.sum(soft_weights * weight_grad, axis=1, keepdims=True)
            score_low = (soft_weights * (weight_grad - row_inner)).astype(jnp.bfloat16)
            query_blocks.append(
                jnp.dot(score_low, key_h, preferred_element_type=jnp.float32) * score_scale
            )
            key_grad = (
                key_grad
                + jnp.einsum("qk,qd->kd", score_low, query_blk, preferred_element_type=jnp.float32)
                * score_scale
            )
        return (jnp.concatenate(query_blocks, axis=0), key_grad, value_grad)

    query_grads, key_grads, value_grads = lax.map(
        head_back, jnp.arange(head_count, dtype=jnp.int32)
    )
    query_grad_all = merge_heads(query_grads)
    key_grad_all = merge_heads(key_grads)
    value_grad_all = merge_heads(value_grads)
    grad_bq = jnp.sum(query_grad_all, axis=0)
    grad_bv = jnp.sum(value_grad_all, axis=0)
    proj_grad_low = jnp.stack([query_grad_all, key_grad_all, value_grad_all], axis=1).astype(
        jnp.bfloat16
    )
    grad_qkv = jnp.einsum(
        "pd,pce->dce", hidden_low, proj_grad_low, preferred_element_type=jnp.float32
    )
    back_h_part = jnp.einsum(
        "pce,dce->pd", proj_grad_low, w_qkv, preferred_element_type=jnp.float32
    )
    back_h0 = lax.psum(back_h_part.astype(jnp.bfloat16), "tensor").astype(jnp.float32) + back_r1
    input_grad = back_h0.astype(jnp.bfloat16)
    back_time = jnp.einsum(
        "ps,pd->sd",
        onehot,
        back_h0,
        precision=lax.Precision.HIGHEST,
        preferred_element_type=jnp.float32,
    )
    grad_bouter = jnp.sum(back_time, axis=0)
    back_time_low = back_time.astype(jnp.bfloat16)
    grad_outer = jnp.einsum("su,sd->ud", act_low, back_time_low, preferred_element_type=jnp.float32)
    back_act = jnp.einsum("sd,ud->su", back_time_low, w_outer, preferred_element_type=jnp.float32)
    (back_inner,) = silu_pull(back_act)
    grad_binner = jnp.sum(back_inner, axis=0)
    grad_inner = jnp.einsum(
        "st,su->tu",
        feature_low,
        back_inner.astype(jnp.bfloat16),
        preferred_element_type=jnp.float32,
    )
    grad_head = jnp.concatenate([grad_bq[None], grad_bv[None], grad_bup], axis=0).reshape(
        6, 1, local_width
    )
    grad_layer = jnp.stack(
        [grad_bout, back_gain1, back_shift1, part_bdown, back_gain2, back_shift2, grad_bouter],
        axis=0,
    )
    red_qkv, red_out, red_up, red_down, red_inner, red_outer, red_binner, red_head, red_layer = (
        lax.psum_scatter(grad_qkv, "dp", scatter_dimension=0, tiled=True),
        lax.psum_scatter(grad_out, "dp", scatter_dimension=1, tiled=True),
        lax.psum_scatter(grad_up, "dp", scatter_dimension=0, tiled=True),
        lax.psum_scatter(grad_down, "dp", scatter_dimension=2, tiled=True),
        lax.psum_scatter(grad_inner, "dp", scatter_dimension=0, tiled=True),
        lax.psum_scatter(grad_outer, "dp", scatter_dimension=0, tiled=True),
        lax.psum_scatter(grad_binner, "dp", scatter_dimension=0, tiled=True),
        lax.psum_scatter(grad_head, "dp", scatter_dimension=2, tiled=True),
        lax.psum_scatter(grad_layer, "dp", scatter_dimension=1, tiled=True),
    )
    split_squares = sum(
        (jnp.sum(piece * piece) for piece in (red_qkv, red_out, red_up, red_down, red_head))
    )
    shared_squares = sum(
        (jnp.sum(piece * piece) for piece in (red_inner, red_outer, red_binner, red_layer))
    )
    local_squares = split_squares + shared_squares / lax.axis_size("tensor")
    norm = jnp.sqrt(lax.psum(local_squares, ("dp", "tensor")))
    factor = 1.0 / jnp.maximum(norm, 1.0)
    step_rate = 4.0 * math.sqrt(MPARAMS / D)
    qkv_master, qkv_velocity, qkv_smoothed = advance(
        qkv_weight, qkv_moment, qkv_average, red_qkv, factor, step_rate
    )
    out_master, out_velocity, out_smoothed = advance(
        out_weight, out_moment, out_average, red_out, factor, step_rate
    )
    up_master, up_velocity, up_smoothed = advance(
        up_weight, up_moment, up_average, red_up, factor, step_rate
    )
    down_master, down_velocity, down_smoothed = advance(
        down_weight, down_moment, down_average, red_down, factor, step_rate
    )
    inner_master, inner_velocity, inner_smoothed = advance(
        time_inner, inner_moment, inner_average, red_inner, factor, step_rate
    )
    outer_master, outer_velocity, outer_smoothed = advance(
        time_outer, outer_moment, outer_average, red_outer, factor, step_rate
    )
    bias_master, bias_velocity, bias_smoothed = advance(
        time_bias, bias_moment, bias_average, red_binner, factor, step_rate
    )
    head_master, head_velocity, head_smoothed = advance(
        head_vectors, head_moment, head_average, red_head, factor, step_rate
    )
    layer_master, layer_velocity, layer_smoothed = advance(
        layer_vectors, layer_moment, layer_average, red_layer, factor, step_rate
    )
    return (
        output_here,
        input_grad,
        norm,
        qkv_master,
        out_master,
        up_master,
        down_master,
        inner_master,
        outer_master,
        bias_master,
        head_master,
        layer_master,
        qkv_velocity,
        out_velocity,
        up_velocity,
        down_velocity,
        inner_velocity,
        outer_velocity,
        bias_velocity,
        head_velocity,
        layer_velocity,
        qkv_smoothed,
        out_smoothed,
        up_smoothed,
        down_smoothed,
        inner_smoothed,
        outer_smoothed,
        bias_smoothed,
        head_smoothed,
        layer_smoothed,
    )


F32=jnp.float32; BF=jnp.bfloat16
MESH=pl.DeviceIdType.MESH
NZ,NX,NC,NT=4,2,2,2
ROWS=48; PIECE=384

def place():
    dp=lax.axis_index("dp"); t=lax.axis_index("tensor")
    z=lax.div(dp,4); x=lax.rem(lax.div(dp,2),2); c=lax.rem(dp,2)
    return z,x,c,t
def dev(z,x,c,t):
    return ((z*NX+x)*NC+c,t)

def peers():
    z,x,c,t=place()
    zp=[dev(lax.rem(z+d,NZ),x,c,t) for d in range(1,NZ)]
    return zp,dev(z,1-x,c,t),dev(z,x,c,1-t),dev(z,x,1-c,t)

def greet():
    zp,xp,yp,sp=peers()
    bar=pltpu.get_barrier_semaphore()
    for d in zp+[xp,yp,sp]:
        pl.semaphore_signal(bar,inc=1,device_id=d,device_id_type=MESH)
    pl.semaphore_wait(bar,6)

def rcopy(src,dst,ssem,rsem,d):
    return pltpu.make_async_remote_copy(src_ref=src,dst_ref=dst,send_sem=ssem,recv_sem=rsem,device_id=d,device_id_type=MESH)

L=1024
def dot(a,b,ca,cb):
    return lax.dot_general(a,b,(((ca,),(cb,)),((),())),preferred_element_type=F32)
def ln_stats(v):
    mean=jnp.mean(v,axis=-1,keepdims=True)
    cen=v-mean
    inv=lax.rsqrt(jnp.mean(cen*cen,axis=-1,keepdims=True)+EPSILON)
    return cen*inv,inv

def ln_back(gain,dy,xhat,inv):
    gd=gain*dy
    return (gd-jnp.mean(gd,axis=-1,keepdims=True)-xhat*jnp.mean(gd*xhat,axis=-1,keepdims=True))*inv

def phi_cdf(u):
    return 0.5*(1.0+lax.erf(u*(1.0/math.sqrt(2.0))))

WIDE=13*PIECE
RB=256
def spread(blocks,w,tiles):
    lane=lax.broadcasted_iota(jnp.int32,(16,128),1)
    acc=[jnp.zeros((16,128),F32) for _ in range(tiles+1)]
    for n,b in enumerate(blocks):
        tile,s=divmod(n*w,128)
        wide=jnp.concatenate([jnp.where(lane<w,b,0.0),jnp.zeros((16,128),F32)],axis=1)
        if s: wide=pltpu.roll(wide,s,1)
        acc[tile]=acc[tile]+wide[:,:128]
        acc[tile+1]=acc[tile+1]+wide[:,128:]
    return jnp.concatenate(acc[:tiles],axis=1)

def attend_pair(q_ref,k_ref,v_ref,o_ref,lse_ref,bias_ref,i,bq=512):
    lane=lax.broadcasted_iota(jnp.int32,(1,128),1)
    cs=pl.ds(pl.multiple_of(i*128,128),128)
    kp=k_ref[:,cs]; vT=v_ref[:,cs].T
    bias=bias_ref[...]
    khs=[]
    for h in range(2):
        khs.append(jnp.where((lane//64)==h,kp,jnp.where(lane==(64*(1-h)),bias,jnp.zeros_like(kp))))
    for qi in range(L//bq):
        qp=q_ref[pl.ds(qi*bq,bq),cs]*0.125
        oT=[]
        for h in range(2):
            qh=jnp.where((lane//64)==h,qp,jnp.where(lane==(64*(1-h)),jnp.ones_like(qp),jnp.zeros_like(qp)))
            sT=dot(khs[h],qh,1,1)
            m=jnp.max(sT,axis=0,keepdims=True)
            e=jnp.exp(sT-m)
            l=jnp.sum(e,axis=0,keepdims=True)
            p=(e*(1.0/l)).astype(BF)
            oT.append(dot(vT[h*64:(h+1)*64],p,1,0))
            lse_ref[i,h:h+1,qi*bq:(qi+1)*bq]=m+jnp.log(l)
        o_ref[pl.ds(qi*bq,bq),cs]=jnp.concatenate(oT,axis=0).T.astype(BF)

GCH=[(n*PIECE,PIECE,128*(1+n%2)) for n in range(13)]

def slots(n):
    out={}
    for i in range(n):
        for stage,lag in enumerate((0,1,2,3) if i<4 else (0,2,4,5)): out.setdefault(i+lag,[]).append((stage,i))
    return {k:sorted(v) for k,v in out.items()}
SLOTS=slots(len(GCH)-1)

def gather_steps(g,zs,zr,fs,fr,ss,sr):
    z,x,c,t=place(); zp,xp,yp,sp=peers(); n=len(GCH)-1
    def cols(i): return pl.ds(GCH[i][0],GCH[i][1])
    def ca(i): return pl.ds(GCH[i][0],GCH[i][2])
    def cb(i): return pl.ds(GCH[i][0]+GCH[i][2],GCH[i][1]-GCH[i][2])
    same=lambda r,s,q,d:rcopy(r,r,s,q,d)
    def Z(i):
        src=g.at[:,z,:,c,:,cols(i)] if i==n else g.at[t,z,x,c,:,cols(i)]
        return [same(src,zs.at[i,d],zr.at[i,d],zp[d]) for d in range(3)]
    def A(i):
        if i==n: return [same(g.at[t,z,x,c,:,ca(i)],fs.at[i,0],fr.at[i,0],xp),same(g.at[t,z,x,c,:,cb(i)],fs.at[i,1],fr.at[i,1],yp)]
        return [same(g.at[t,:,x,c,:,ca(i)],fs.at[i,0],fr.at[i,0],xp),same(g.at[t,:,x,c,:,cb(i)],fs.at[i,1],fr.at[i,1],yp)]
    def B(i):
        if i==n: return [same(g.at[t,z,:,c,:,ca(i)],fs.at[i,2],fr.at[i,2],yp),same(g.at[:,z,x,c,:,cb(i)],fs.at[i,3],fr.at[i,3],xp)]
        return [same(g.at[t,:,:,c,:,ca(i)],fs.at[i,2],fr.at[i,2],yp),same(g.at[:,:,x,c,:,cb(i)],fs.at[i,3],fr.at[i,3],xp)]
    S=lambda i:[same(g.at[:,:,:,c,:,cols(i)],ss.at[i],sr.at[i],sp)]
    def go(cs):
        for q in cs: q.start()
    def got(cs):
        for q in cs: q.wait_recv()
    def step(k):
        for stage,i in SLOTS.get(k,()):
            if stage==0:
                got(Z(i)); go(A(i))
                if i+4<n: go(Z(i+4))
            if stage==1: got(A(i)); go(B(i))
            if stage==2: got(B(i)); go(S(i))
            if stage==3: got(S(i))
    def late(k):
        if k==0: go(A(n))
        if k==1: got(A(n)); go(B(n))
        if k==2: got(B(n)); go(Z(n))
        if k==3: got(Z(n)); go(S(n))
        if k==4: got(S(n))
    def first(k): go(Z(k))
    def finish():
        for i in range(n+1):
            for q in Z(i)+A(i)+B(i)+S(i): q.wait_send()
    return step,late,first,finish

def front_kernel(ts_ref,qkv_m,out_m,up_m,down_m,w1_m,w2_m,b1_m,hv_m,lv_m,tok_hbm,cot_hbm,seg_ref,
        q_o,k_o,v_o,o_o,lse_o,out_o,outp_o,dmbT_o,abT_o,drbT_o,hid_o,dub_o,dr1_o,dob_o,hbT_o,wqkv_o,aux_o,sums_o,bup_o,time_o,feat_o,
        g,tok,cot,q,k,v,o,lse,own,bias,vecs,temb,hbT,gp,hid,inv,dmbT,abT,drbT,dr1,a32,
        zs,zr,fs,fr,ss,sr,lsem,osem,hsem,bsem,ysem):
    z,x,c,t=place()
    step,late,first,finish=gather_steps(g,zs,zr,fs,fr,ss,sr)
    win=pl.ds(pl.multiple_of(t*512,512),L)
    ltok=pltpu.make_async_copy(tok_hbm.at[win,:],tok,lsem.at[0]); ltok.start()
    lcot=pltpu.make_async_copy(cot_hbm.at[win,:],cot,lsem.at[1]); lcot.start()
    greet_out()
    a32[...]=jnp.zeros((ROWS,PIECE),F32)
    a32[0:32,:]=w2_m[:,pl.ds(pl.multiple_of(t*PIECE,128),PIECE)]
    a32[32:40,0:256]=w1_m[:,pl.ds(pl.multiple_of(t*256,128),256)]
    a32[32:39,256:304]=lv_m[...]
    a32[39:45,256:280]=hv_m[:,0,:]
    a32[45:46,256:288]=b1_m[...]
    def put(p,val): g[t,z,x,c,:,p*PIECE:(p+1)*PIECE]=val.astype(BF)
    put(0,a32[...])
    greet_in()
    first(0)
    for j in range(3): put(1+j,qkv_m[j])
    put(4,out_m[...])
    first(1); first(2); first(3)
    for j in range(4): put(5+j,up_m[:,j,:])
    for j in range(4): put(9+j,down_m[j])
    late(0)
    ln=lax.broadcasted_iota(jnp.int32,(16,256),1)
    fi=lax.div(ln,16)*8+lax.rem(ln,16)
    theta=jnp.exp(lax.rem(fi,64).astype(F32)*(-math.log(10000.0)/64.0))
    ang=theta*ts_ref[0,t].astype(F32)
    feat=jnp.where(lax.rem(ln,16)<8,jnp.where(fi<64,jnp.cos(ang),jnp.sin(ang)),0.0).astype(BF)
    feat_o[...]=feat
    seg=seg_ref[:,pl.ds(pl.multiple_of(t*512,128),L)]
    own_row=jnp.where(seg==t,1.0,0.0)
    ownT=jnp.broadcast_to(own_row,(128,L)).T
    own[...]=ownT
    bias[...]=jnp.where(ownT>0.5,0.0,-1e30).astype(BF)
    for n in range(4): step(n)
    def vecblk(tt,n): return g[tt,n//4,(n//2)%2,n%2,32:48,256:384].astype(F32)
    b0=[vecblk(0,n) for n in range(16)]; b1=[vecblk(1,n) for n in range(16)]
    lv=spread(b0,48,6)
    hv=jnp.concatenate([spread(b0,24,3),spread(b1,24,3)],axis=1)
    vecs[0:16,:]=lv
    vecs[16:32,:]=hv
    bin_=spread(b0,32,4)[13:14,:]
    w1=jnp.concatenate([g[0,:,:,:,32:48,0:256].reshape(256,256),g[1,:,:,:,32:48,0:256].reshape(256,256)],axis=1)
    inner=dot(feat,w1,1,0)[0:1]+bin_
    sig=1.0/(1.0+jnp.exp(-inner))
    act=inner*sig
    w2=jnp.concatenate([g[0,:,:,:,0:32,0:384].reshape(512,384),g[1,:,:,:,0:32,0:384].reshape(512,384)],axis=1)
    actb=jnp.broadcast_to(act,(16,512)).astype(BF)
    te=dot(actb,w2,1,0)[0:1]+lv[6:7]
    temb[...]=jnp.broadcast_to(te,(8,D))
    time_o[...]=jnp.concatenate([inner,sig,jnp.zeros((6,512),F32)],axis=0)
    ltok.wait()
    outs=[]
    def emit(src,dst):
        cp=pltpu.make_async_copy(src,dst,osem.at[len(outs)]); cp.start(); outs.append(cp)
    def hid_rows(r,_):
        rows=pl.ds(pl.multiple_of(r*RB,RB),RB)
        hb=(tok[rows,:].astype(F32)+temb[0:1,:]).astype(BF)
        hbT[:,rows]=hb.T
        return 0
    lax.fori_loop(0,L//RB,hid_rows,0)
    def project(which,ref,brow):
        def rows_body(r,_):
            rows=pl.ds(pl.multiple_of(r*RB,RB),RB)
            hb=(tok[rows,:].astype(F32)+temb[0:1,:]).astype(BF)
            for tt in range(2):
                val=dot(hb,g[tt,:,:,:,:,(1+which)*PIECE:(2+which)*PIECE].reshape(D,PIECE),1,0)
                if brow is not None: val=val+vecs[brow:brow+1,tt*PIECE:(tt+1)*PIECE]
                ref[rows,tt*PIECE:(tt+1)*PIECE]=val.astype(BF)
            return 0
        lax.fori_loop(0,L//RB,rows_body,0)
    emit(hbT,hbT_o)
    step(4)
    project(0,q,16+7)
    emit(q,q_o)
    step(5); late(1)
    project(1,k,None)
    emit(k,k_o)
    step(6)
    project(2,v,16+8)
    emit(v,v_o)
    emit(g.at[:,:,:,:,:,0:PIECE],aux_o); emit(g.at[:,:,:,:,:,PIECE:4*PIECE],wqkv_o)
    def pair(i,_):
        attend_pair(q,k,v,o,lse,bias,i)
        for s in range(6):
            @pl.when(i==s)
            def _():
                if s==3: late(2)
                step(7+s)
        return 0
    lax.fori_loop(0,6,pair,0)
    emit(o,o_o); emit(lse,lse_o)
    lcot.wait()
    for cp in outs: cp.wait()
    out,dob=q,k
    yp=peers()[2]
    def emits(r):
        rows=pl.ds(pl.multiple_of(r*RB,RB),RB)
        byrow=[(out,out_o),(dr1,dr1_o),(dob,dob_o)]; bycol=[(dmbT,dmbT_o),(abT,abT_o),(drbT,drbT_o)]
        cs=[pltpu.make_async_copy(a.at[rows,:],b.at[rows,:],bsem.at[n,r]) for n,(a,b) in enumerate(byrow)]
        cs+=[pltpu.make_async_copy(a.at[:,rows],b.at[:,rows],bsem.at[3+n,r]) for n,(a,b) in enumerate(bycol)]
        return cs,rcopy(out.at[rows,:],outp_o.at[rows,:],ysem.at[0,r],ysem.at[1,r],yp)
    mid_body(g,tok,cot,o,own,vecs,temb,gp,hid,inv,out,dmbT,abT,drbT,dr1,dob,sums_o,bup_o,hid_o,dub_o,hsem,step,late,emits)
    for r in range(L//RB):
        cs,far=emits(r)
        for cp in cs: cp.wait()
        if r<2: far.wait()
    finish()

def mid_body(g,tok,cot,o,own,vecs,temb,gp,hid,inv,out,dmbT,abT,drbT,dr1,dob,sums_o,bup_o,hid_o,dub_o,hsem,step,late,emits):
    def W(tt,piece,n=1): return g[tt,:,:,:,:,piece*PIECE:(piece+n)*PIECE].reshape(D,n*PIECE)
    row=lambda r:vecs[r:r+1,:]
    sums_o[...]=jnp.zeros((8,D),F32); bup_o[...]=jnp.zeros((8,4*D),F32)
    csum=lambda a:jnp.sum(a,axis=0,keepdims=True)
    def emit_rows(buf,dst,r,which):
        rows=pl.ds(pl.multiple_of(r*RB,RB),RB)
        return pltpu.make_async_copy(buf.at[rows,:],dst.at[rows,:],hsem.at[which,r])
    def up_block(r,_):
        rows=pl.ds(pl.multiple_of(r*RB,RB),RB)
        for n in range(4):
            @pl.when(r==n)
            def _():
                if n==1: late(3)
                step(13+n)
        attn=dot(o[rows,0:PIECE],W(0,4),1,1)+dot(o[rows,PIECE:D],W(1,4),1,1)
        r1=(tok[rows,:].astype(F32)+temb[0:1,:])+(attn+row(0))
        x1,inv1=ln_stats(r1)
        dr1[rows,:]=x1
        inv[rows,:]=jnp.broadcast_to(inv1,(RB,128))
        ab=(x1*row(1)+row(2)).astype(BF)
        abT[:,rows]=ab.T
        for tt in range(2):
            for j in range(4):
                cc=pl.ds((tt*4+j)*PIECE,PIECE)
                u=dot(ab,W(tt,5+j),1,0)+vecs[16+9+j:16+10+j,tt*PIECE:(tt+1)*PIECE]
                cdf=phi_cdf(u)
                gp[rows,cc]=(cdf+u*jnp.exp(-0.5*u*u)*(1.0/math.sqrt(2*math.pi))).astype(BF)
                hid[rows,cc]=(u*cdf).astype(BF)
        emit_rows(hid,hid_o,r,0).start()
        return 0
    lax.fori_loop(0,L//RB,up_block,0)
    late(4)
    def block(r,_):
        rows=pl.ds(pl.multiple_of(r*RB,RB),RB)
        x1=dr1[rows,:]; inv1=inv[rows,0:1]
        a=x1*row(1)+row(2)
        mlp=row(3)
        for tt in range(2):
            mlp=mlp+dot(hid[rows,tt*4*PIECE:(tt+1)*4*PIECE],W(tt,9,4),1,1)
        x2,inv2=ln_stats(a+mlp)
        out[rows,:]=(x2*row(4)+row(5)).astype(BF)
        @pl.when(r<2)
        def _(): emits(r)[1].start()
        dy=jnp.where(own[rows,0:1]>0.5,cot[rows,:].astype(F32),0.0)
        sums_o[4:5,:]+=csum(dy*x2); sums_o[5:6,:]+=csum(dy)
        dr2=ln_back(row(4),dy,x2,inv2)
        sums_o[3:4,:]+=csum(dr2)
        dmb=dr2.astype(BF)
        dmbT[:,rows]=dmb.T
        da=dr2
        for tt in range(2):
            for j in range(4):
                cc=pl.ds((tt*4+j)*PIECE,PIECE)
                du=dot(dmb,W(tt,9+j),1,0)*gp[rows,cc].astype(F32)
                bup_o[0:1,cc]+=csum(du)
                gp[rows,cc]=du.astype(BF)
            da=da+dot(gp[rows,tt*4*PIECE:(tt+1)*4*PIECE],W(tt,5,4),1,1)
        emit_rows(gp,dub_o,r,1).start()
        sums_o[1:2,:]+=csum(da*x1); sums_o[2:3,:]+=csum(da)
        d1=ln_back(row(1),da,x1,inv1)
        sums_o[0:1,:]+=csum(d1)
        dr1[rows,:]=d1
        drb=d1.astype(BF)
        drbT[:,rows]=drb.T
        for tt in range(2):
            dob[rows,tt*PIECE:(tt+1)*PIECE]=dot(drb,W(tt,4),1,0).astype(BF)
        for cp in emits(r)[0]: cp.start()
        return 0
    lax.fori_loop(0,L//RB,block,0)
    for r in range(L//RB):
        emit_rows(hid,hid_o,r,0).wait(); emit_rows(gp,dub_o,r,1).wait()

def front(ts,masters,tokens,cotangent,seg,cid=0):
    DMA=pltpu.SemaphoreType.DMA; n=len(GCH)
    V=lambda s,d=BF:pltpu.VMEM(s,d)
    A=pl.BlockSpec(memory_space=pl.ANY); M=pl.BlockSpec(memory_space=pltpu.VMEM)
    big=lambda s,d=BF:jax.ShapeDtypeStruct(s,d)
    row=(L,D); tr=(D,L)
    G6=lambda w_:(NT,NZ,NX,NC,ROWS,w_)
    return pl.pallas_call(front_kernel,
        in_specs=[pl.BlockSpec(memory_space=pltpu.SMEM)]+[M]*9+[A,A,M],
        out_specs=[A]*17+[M]*4,
        out_shape=[big(row),big(row),big(row),big(row),big((6,2,L),F32),big(row),big((512,D)),big(tr),big(tr),big(tr),big((L,4*D)),big((L,4*D)),
            big(row,F32),big(row),big(tr),big(G6(3*PIECE)),big(G6(PIECE)),big((8,D),F32),big((8,4*D),F32),big((8,512),F32),big((16,256))],
        scratch_shapes=[V(G6(WIDE)),V(row),V(row),V(row),V(row),V(row),V(row),V((6,2,L),F32),V((L,128),F32),V((L,128)),V((32,D),F32),V((8,D),F32),
            V(tr),V((L,4*D)),V((L,4*D)),V((L,128),F32),V(tr),V(tr),V(tr),V(row,F32),V((ROWS,PIECE),F32),
            DMA((n,3)),DMA((n,3)),DMA((n,4)),DMA((n,4)),DMA((n,)),DMA((n,)),DMA((2,)),DMA((8,)),DMA((2,L//RB)),DMA((6,L//RB)),DMA((2,L//RB))],
        compiler_params=pltpu.CompilerParams(collective_id=cid,has_side_effects=True,vmem_limit_bytes=63*2**20),name="front")(ts,*masters,tokens,cotangent,seg)

def group(g,r,w,a): return dict(g=g,r=r,w=w,a=a)
RGR=[group(0,0,768,-1),group(768,768,768,0),group(1536,1536,768,-1),group(2304,2304,768,0),group(3072,3072,384,-1),
     group(3456,3456,384,0),group(3840,3840,384,256),group(0,4224,384,256)]
RW=12*PIECE
GBW=11*PIECE
_a=_b=_p=_q=0
for _g in RGR:
    if _g["a"]>=0:
        _g["ao"]=_a; _g["bo"]=_b; _g["po"]=_p; _a+=_g["a"]; _b+=_g["w"]-_g["a"]; _p+=_g["w"]
    else:
        _g["qo"]=_q; _q+=_g["w"]
RWA,RWB,RWP,RWQ=max(_a,128),_b,_p,_q

def scatter_steps(gb,rs,ra,rc,rb,rz,rx,rq,ry,red,ss,sr,as_,ar,bs,br,zs,zr):
    z,x,c,t=place(); zp,xp,yp,sp=peers()
    def go(cs):
        for q in cs: q.start()
    def got(cs):
        for q in cs: q.wait_recv()
    def sums(a,b): return a+b
    def sl(i):
        q=RGR[i]; g,r,w,a=q["g"],q["r"],q["w"],q["a"]
        k=dict(g=pl.ds(g,w),r=pl.ds(r,w))
        if a>=0: k.update(ga=pl.ds(g,a),gb=pl.ds(g+a,w-a),a=pl.ds(q["ao"],a),b=pl.ds(q["bo"],w-a),p=pl.ds(q["po"],w),pa=pl.ds(q["po"],a),pb=pl.ds(q["po"]+a,w-a))
        else: k.update(q=pl.ds(q["qo"],w))
        return k
    def S(i):
        k=sl(i); return [rcopy(gb.at[:,:,:,1-c,:,k["g"]],rs.at[:,:,:,:,k["r"]],ss.at[i],sr.at[i],sp)]
    def A(i):
        k=sl(i)
        if "q" in k: return [rcopy(gb.at[:,:,1-x,c,:,k["g"]],rx.at[:,:,:,k["q"]],as_.at[i,0],ar.at[i,0],xp)]
        one=[rcopy(gb.at[:,:,1-x,c,:,k["ga"]],ra.at[:,:,:,k["a"]],as_.at[i,0],ar.at[i,0],xp)] if RGR[i]["a"] else []
        return one+[rcopy(gb.at[1-t,:,:,c,:,k["gb"]],rc.at[:,:,:,k["b"]],as_.at[i,1],ar.at[i,1],yp)]
    def zdst(d): return lax.rem(z+d+1,NZ)
    def B(i):
        k=sl(i)
        if "q" in k: return [rcopy(gb.at[:,zdst(d),x,c,:,k["g"]],rq.at[d,:,:,k["q"]],bs.at[i,d],br.at[i,d],zp[d]) for d in range(3)]
        one=[rcopy(gb.at[1-t,:,x,c,:,k["ga"]],rb.at[:,:,k["pa"]],bs.at[i,0],br.at[i,0],yp)] if RGR[i]["a"] else []
        return one+[rcopy(gb.at[t,:,1-x,c,:,k["gb"]],rb.at[:,:,k["pb"]],bs.at[i,1],br.at[i,1],xp)]
    def Z(i):
        k=sl(i)
        if "q" in k: return [rcopy(gb.at[1-t,z,x,c,:,k["g"]],ry.at[:,k["q"]],zs.at[i,0],zr.at[i,0],yp)]
        return [rcopy(gb.at[t,zdst(d),x,c,:,k["g"]],rz.at[d,:,k["p"]],zs.at[i,d],zr.at[i,d],zp[d]) for d in range(3)]
    def s_to_a(i):
        got(S(i)); k=sl(i)
        def body(n,_):
            tt=lax.div(n,8); zz=lax.rem(lax.div(n,2),4); xx=lax.rem(n,2)
            gb[tt,zz,xx,c,:,k["g"]]=sums(gb[tt,zz,xx,c,:,k["g"]],rs[tt,zz,xx,:,k["r"]])
            return 0
        lax.fori_loop(0,16,body,0)
        go(A(i))
    def a_to_b(i):
        got(A(i)); k=sl(i)
        def body(n,_):
            a=lax.div(n,4); b=lax.rem(n,4)
            if "q" in k:
                gb[a,b,x,c,:,k["g"]]=sums(gb[a,b,x,c,:,k["g"]],rx[a,b,:,k["q"]])
            else:
                if RGR[i]["a"]: gb[a,b,x,c,:,k["ga"]]=sums(gb[a,b,x,c,:,k["ga"]],ra[a,b,:,k["a"]])
                zz=lax.div(n,2); xx=lax.rem(n,2)
                gb[t,zz,xx,c,:,k["gb"]]=sums(gb[t,zz,xx,c,:,k["gb"]],rc[zz,xx,:,k["b"]])
            return 0
        lax.fori_loop(0,8,body,0)
        go(B(i))
    def b_to_z(i):
        got(B(i)); k=sl(i)
        if "q" in k:
            for a in range(2):
                acc=gb[a,z,x,c,:,k["g"]].astype(F32)
                for d in range(3): acc=acc+rq[d,a,:,k["q"]].astype(F32)
                gb[a,z,x,c,:,k["g"]]=acc.astype(BF)
        else:
            def body(n,_):
                gb[t,n,x,c,:,k["g"]]=sums(gb[t,n,x,c,:,k["g"]],rb[n,:,k["p"]])
                return 0
            lax.fori_loop(0,4,body,0)
        go(Z(i))
    def z_end(i):
        got(Z(i)); k=sl(i)
        acc=gb[t,z,x,c,:,k["g"]].astype(F32)
        if "q" in k: acc=acc+ry[:,k["q"]].astype(F32)
        else:
            for d in range(3): acc=acc+rz[d,:,k["p"]].astype(F32)
        red[:,k["r"]]=acc
    def drain(i):
        for q in S(i)+A(i)+B(i)+Z(i): q.wait_send()
    return S,go,s_to_a,a_to_b,b_to_z,z_end,drain

def attend_back(q_ref,k_ref,v_ref,do_ref,lse_ref,bias_ref,hvs,i,bq=512):
    lane=lax.broadcasted_iota(jnp.int32,(1,128),1)
    cs=pl.ds(pl.multiple_of(i*128,128),128)
    kp=k_ref[:,cs]; vp=v_ref[:,cs]; bias=bias_ref[...]
    khs=[];vhs=[]
    for h in range(2):
        sel=(lane//64)==h; one=lane==(64*(1-h))
        khs.append(jnp.where(sel,kp,jnp.where(one,bias,jnp.zeros_like(kp))))
        vhs.append(jnp.where(sel,vp,jnp.zeros_like(vp)))
    kT=kp.T
    dk=[None,None];dv=[None,None]; sq=None
    for qi in range(L//bq):
        rows=pl.ds(qi*bq,bq)
        qp=q_ref[rows,cs]*0.125; dop=do_ref[rows,cs]
        dqT=[]
        for h in range(2):
            sel=(lane//64)==h; one=lane==(64*(1-h))
            zero=jnp.zeros_like(qp)
            qh=jnp.where(sel,qp,jnp.where(one,jnp.ones_like(qp),zero))
            doh=jnp.where(sel,dop,zero)
            qz=jnp.where(sel,qp,zero)
            sT=dot(khs[h],qh,1,1)
            p=jnp.exp(sT-lse_ref[i,h:h+1,qi*bq:(qi+1)*bq])
            dp=dot(vhs[h],doh,1,1)
            d=jnp.sum(p*dp,axis=0,keepdims=True)
            ds=(p*(dp-d)).astype(BF)
            pb=p.astype(BF)
            a=dot(pb,doh,1,0); dv[h]=a if dv[h] is None else dv[h]+a
            a=dot(ds,qz,1,0); dk[h]=a if dk[h] is None else dk[h]+a
            dqT.append(dot(kT[h*64:(h+1)*64],ds,1,0))
        dq=jnp.concatenate(dqT,axis=0).T*0.125
        s=jnp.sum(dq,axis=0,keepdims=True); sq=s if sq is None else sq+s
        q_ref[rows,cs]=dq.astype(BF)
    k_ref[:,cs]=(dk[0]+dk[1]).astype(BF)
    dvv=dv[0]+dv[1]
    v_ref[:,cs]=dvv.astype(BF)
    hvs[0:1,cs]=sq
    hvs[1:2,cs]=jnp.sum(dvv,axis=0,keepdims=True)

def unspread(src,w,n):
    lane=lax.broadcasted_iota(jnp.int32,(16,128),1)
    tile,s=divmod(n*w,128)
    wide=src[:,tile*128:(tile+2)*128]
    if s: wide=pltpu.roll(wide,256-s,1)
    return jnp.where(lane<w,wide[:,:128],0.0)

def back_kernel(q_h,k_h,v_h,do_h,o_h,lse_h,dmbT_h,abT_h,drbT_h,hbT_h,hid_h,dub_h,dr1_h,wqkv_h,aux_h,out_h,seg_ref,feat_ref,sums_ref,bup_ref,time_ref,
        in_o,inp_o,outp_o,red,w2g,w1g,vecg,tot,
        q,k,v,do,lse,bias,st,ta,tb,wq,dr1,aux,ow,hvs,lvs,hsrc,dtm,nv,nr,nz,vg,vs,vx,vz,vy,sg,mat,aT,fT,dT,
        gb,rs,ra,rc,rb,rz,rx,rq,ry,ss,sr,as_,ar,bs,br,zs,zr,ls,ts,xs,ns,nrs,os,vsm,vrm,gsm,grm):
    z,x,c,t=place(); zp,xp,yp,sp=peers()
    inw=do
    S,go,s_to_a,a_to_b,b_to_z,z_end,drain=scatter_steps(gb,rs,ra,rc,rb,rz,rx,rq,ry,red,ss,sr,as_,ar,bs,br,zs,zr)
    def load(src,dst,n):
        return pltpu.make_async_copy(src,dst,ls.at[n])
    LQ=[load(q_h,q,0),load(k_h,k,1),load(v_h,v,2),load(do_h,do,3),load(lse_h,lse,4)]
    LW=[load(wqkv_h,wq,5),load(dr1_h,dr1,6),load(aux_h,aux,7)]
    def tcopy(src,buf,n): return pltpu.make_async_copy(src,buf,ts.at[n])
    def stage(src,cols,n):
        return [pltpu.make_async_copy(src.at[:,pl.ds(cs,PIECE)],st.at[s],ts.at[n+s]) for s,cs in enumerate(cols)]
    pc=lambda j:[tt*4*PIECE+jj*PIECE for jj in (j,j+1) for tt in range(2)]
    ST=[stage(hid_h,pc(0),4),stage(hid_h,pc(2),8),stage(dub_h,pc(0),4),stage(dub_h,pc(2),8),stage(o_h,[0,PIECE],4)]
    for q_ in [tcopy(dmbT_h,ta,0),*ST[0],tcopy(abT_h,tb,1)]+LQ+LW: q_.start()
    greet()
    lo=load(out_h.at[pl.ds(512,512),:],ow,9); lo.start(); lo.wait()
    cout=[rcopy(ow.at[pl.ds(n*256,256),:],outp_o.at[pl.ds(n*256,256),:],os.at[0,n],os.at[1,n],yp) for n in range(2)]
    for q_ in cout: q_.start()
    seg=seg_ref[:,pl.ds(pl.multiple_of(t*512,128),L)]
    bias[...]=jnp.broadcast_to(jnp.where(seg==t,0.0,-1e30),(128,L)).T.astype(BF)
    def compute(i,lhs,n):
        base=RGR[i]["g"]
        for q_ in ST[i]: q_.wait()
        def body(s,_):
            tt=lax.rem(s,2); cs=pl.ds(pl.multiple_of(base+lax.div(s,2)*PIECE,128),PIECE)
            gb[tt,:,:,:,:,cs]=dot(lhs[...],st[s],1,0).astype(BF).reshape(NZ,NX,NC,ROWS,PIECE)
            return 0
        lax.fori_loop(0,n,body,0)
        if i+1<len(ST):
            for q_ in ST[i+1]: q_.start()
        go(S(i))
    tcopy(dmbT_h,ta,0).wait()
    compute(0,ta,4)
    compute(1,ta,4)
    tcopy(drbT_h,ta,2).start()
    tcopy(abT_h,tb,1).wait()
    s_to_a(0)
    compute(2,tb,4)
    s_to_a(1)
    compute(3,tb,4)
    tcopy(hbT_h,tb,3).start()
    s_to_a(2)
    tcopy(drbT_h,ta,2).wait()
    compute(4,ta,2)
    s_to_a(3); a_to_b(0)
    for q_ in LQ: q_.wait()
    tcopy(hbT_h,tb,3).wait()
    def quad(i,n):
        base=RGR[i]["g"]
        for tt in range(2):
            o_=tt*PIECE+n*128
            rhs=jnp.concatenate([q[:,o_:o_+128],k[:,o_:o_+128],v[:,o_:o_+128]],axis=1)
            gb[tt,:,:,:,:,base:base+PIECE]=dot(tb[...],rhs,1,0).astype(BF).reshape(NZ,NX,NC,ROWS,PIECE)
        go(S(i))
    def pair(i,_):
        @pl.when(i==1)
        def _():
            s_to_a(4); a_to_b(1)
        @pl.when(i==2)
        def _():
            a_to_b(2); b_to_z(0); quad(5,0)
        @pl.when(i==3)
        def _():
            s_to_a(5); a_to_b(3); b_to_z(1)
        @pl.when(i==4)
        def _():
            a_to_b(4); z_end(0); b_to_z(2); quad(6,1)
        @pl.when(i==5)
        def _():
            s_to_a(6); a_to_b(5); b_to_z(3); z_end(1)
        attend_back(q,k,v,do,lse,bias,hvs,lax.div(i,2)+3*lax.rem(i,2))
        return 0
    lax.fori_loop(0,6,pair,0)
    z_end(2); b_to_z(4)
    lvs[...]=jnp.zeros((16,D+128),F32)
    lvs[0:6,0:D]=sums_ref[0:6,:]
    hsrc[...]=jnp.zeros((16,2*(PIECE+128)),F32)
    for tt in range(2):
        o0=tt*(PIECE+128); cc=slice(tt*PIECE,(tt+1)*PIECE)
        hsrc[7:9,o0:o0+PIECE]=hvs[0:2,cc]
        for j in range(4): hsrc[9+j:10+j,o0:o0+PIECE]=bup_ref[0:1,(tt*4+j)*PIECE:(tt*4+j+1)*PIECE]
    for n in range(16):
        both=unspread(lvs[...],48,n)
        for tt in range(2):
            vg[tt,n//4,(n//2)%2,n%2]=(both+unspread(hsrc[:,tt*(PIECE+128):(tt+1)*(PIECE+128)],24,n)).astype(BF)
    def pass_on(k):
        src=[sg.at[t,z,x,c],sg.at[:,z,x,c],sg.at[:,z,:,c],sg.at[:,z]][k]
        if k==3: return [rcopy(src,src,gsm.at[3+d],grm.at[3+d],zp[d]) for d in range(3)]
        return [rcopy(src,src,gsm.at[k],grm.at[k],(yp,xp,sp)[k])]
    def vec_send(k):
        if k==0: return [rcopy(vg.at[1-t],vy,vsm.at[0],vrm.at[0],yp)]
        if k==1: return [rcopy(vg.at[t,:,1-x],vx,vsm.at[1],vrm.at[1],xp)]
        if k==2: return [rcopy(vg.at[t,:,x,1-c],vs,vsm.at[2],vrm.at[2],sp)]
        return [rcopy(vg.at[t,lax.rem(z+d+1,NZ),x,c],vz.at[d],vsm.at[3+d],vrm.at[3+d],zp[d]) for d in range(3)]
    def vec(k):
        if k>0:
            for q_ in vec_send(k-1): q_.wait_recv()
        if k==1: vg[t]=vg[t]+vy[...]
        if k==2: vg[t,:,x]=vg[t,:,x]+vx[...]
        if k==3: vg[t,:,x,c]=vg[t,:,x,c]+vs[...]
        if k<4:
            for q_ in vec_send(k): q_.start()
        else:
            acc=vg[t,z,x,c].astype(F32)
            for d in range(3): acc=acc+vz[d].astype(F32)
            vecg[...]=acc
    def rows_on(k):
        if k>0:
            for q_ in pass_on(k-1): q_.wait_recv()
        if k<4:
            for q_ in pass_on(k): q_.start()
    vec(0)
    drain(0)
    quad(7,2)
    a_to_b(6); z_end(3); b_to_z(5)
    vec(1)
    for q_ in LW: q_.wait()
    dtm[...]=jnp.zeros((8,D),F32)
    def far(r):
        rows=pl.ds(pl.multiple_of(r*RB,RB),RB)
        return rcopy(inw.at[rows,:],inp_o.at[rows,:],xs.at[0,r],xs.at[1,r],yp)
    def rows_body(r,_):
        rows=pl.ds(pl.multiple_of(r*RB,RB),RB)
        acc=dr1[rows,:]
        for n,ref in enumerate((q,k,v)):
            for tt in range(2):
                acc=acc+dot(ref[rows,tt*PIECE:(tt+1)*PIECE],wq[tt,:,:,:,:,n*PIECE:(n+1)*PIECE].reshape(D,PIECE),1,1)
        inw[rows,:]=acc.astype(BF)
        dtm[0:1,:]+=jnp.sum(acc,axis=0,keepdims=True)
        return 0
    s_to_a(7)
    lax.fori_loop(0,2,rows_body,0)
    a_to_b(7)
    far(0).start()
    vec(2)
    lax.fori_loop(2,L//RB,rows_body,0)
    cinl=pltpu.make_async_copy(inw,in_o,ls.at[8]); cinl.start()
    dtb=dtm[0:1,:].astype(BF)
    inner=time_ref[0:1,:]; sig=time_ref[1:2,:]
    w2=jnp.concatenate([aux[0,:,:,:,0:32,:].reshape(512,PIECE),aux[1,:,:,:,0:32,:].reshape(512,PIECE)],axis=1)
    dinner=dot(jnp.broadcast_to(dtb,(16,D)),w2,1,1)[0:1]*(sig*(1.0+inner*(1.0-sig)))
    act=(inner*sig).astype(BF).astype(F32)
    sg[t,z,x,c,0:1,:]=jnp.concatenate([act,dtm[0:1,:],dinner,feat_ref[0:1,:].astype(F32)],axis=1)
    rows_on(0)
    far(1).start(); far(2).start(); far(3).start()
    vec(3)
    b_to_z(6); z_end(4); z_end(5)
    rows_on(1)
    b_to_z(7)
    vec(4)
    rows_on(2)
    z_end(6)
    rows_on(3)
    z_end(7)
    vv=vecg[...]
    big=red[...]
    part=jnp.sum(big*big)+jnp.sum(jnp.where(lax.broadcasted_iota(jnp.int32,(16,128),0)<7,0.5,1.0)*vv*vv)
    nv[0]=jnp.full((8,128),part,F32)
    def swap(s,peer): return rcopy(nv.at[s],nr.at[s],ns.at[s],nrs.at[s],peer)
    swap(0,xp).start()
    rows_on(4)
    for n in range(32): mat[n:n+1,:]=sg[n//16,(n//4)%4,(n//2)%2,n%2]
    aT[...]=mat[:,0:512].T
    fT[...]=mat[:,1792:2048].T
    dp=lax.axis_index("dp")
    g2=dot(aT[pl.ds(pl.multiple_of(dp*32,32),32),:].astype(BF),mat[:,512:1280].astype(BF),1,0)
    g1=dot(fT[pl.ds(pl.multiple_of(dp*16,16),16),:].astype(BF),mat[:,1280:1792].astype(BF),1,0)
    w2g[...]=g2; w1g[...]=g1
    def own_sum(m,w):
        dT[0:m.shape[1],:]=m.T
        col=jnp.sum(dT[pl.ds(pl.multiple_of(dp*w,16),w),:],axis=1,keepdims=True)
        return jnp.broadcast_to(col,(w,128)).T[0:1,:]
    vecg[6:7,0:48]=own_sum(mat[:,512:1280],48)
    vecg[13:14,0:32]=own_sum(mat[:,1280:1792],32)
    sq=lambda a:jnp.sum(a*a)
    rest=(sq(dot(aT[...].astype(BF),mat[:,512:1280].astype(BF),1,0))+sq(dot(fT[...].astype(BF),mat[:,1280:1792].astype(BF),1,0))
        +sq(jnp.sum(mat[:,512:1280],axis=0,keepdims=True))+sq(jnp.sum(mat[:,1280:1792],axis=0,keepdims=True)))
    swap(0,xp).wait()
    nv[1]=nv[0]+nr[0]
    swap(1,sp).start(); swap(1,sp).wait()
    nv[2]=nv[1]+nr[1]
    cz=[rcopy(nv.at[2],nz.at[z],ns.at[3+d],nrs.at[3+d],zp[d]) for d in range(3)]
    for q_ in cz: q_.start()
    nz[z]=nv[2]
    for q_ in cz: q_.wait()
    nv[3]=((nz[0]+nz[1])+nz[2])+nz[3]
    cy=rcopy(nv.at[3],nr.at[2],ns.at[2],nrs.at[2],yp); cy.start(); cy.wait()
    tot[...]=(nv[3]+nr[2])+rest
    cinl.wait()
    for q_ in cout: q_.wait()
    for k_ in range(4):
        for q_ in pass_on(k_)+vec_send(k_): q_.wait_send()
    for r in range(4): far(r).wait()
    for i in range(1,8): drain(i)

def back(q,k,v,dob,o,lse,dmbT,abT,drbT,hbT,hid,dub,dr1,wqkv,aux,out_win,seg,featp,sums,bups,tstate,cid=1):
    DMA=pltpu.SemaphoreType.DMA; n=len(RGR)
    V=lambda s,d=BF:pltpu.VMEM(s,d)
    A=pl.BlockSpec(memory_space=pl.ANY); M=pl.BlockSpec(memory_space=pltpu.VMEM)
    sd=jax.ShapeDtypeStruct; row=(L,D); tr=(D,L)
    return pl.pallas_call(back_kernel,
        in_specs=[A]*16+[M]*5,out_specs=[A]*3+[M]*5,
        out_shape=[sd(row,BF),sd(row,BF),sd((512,D),BF),sd((ROWS,RW),F32),sd((32,D),F32),sd((16,512),F32),sd((16,128),F32),sd((8,128),F32)],
        scratch_shapes=[V(row),V(row),V(row),V(row),V((6,2,L),F32),V((L,128)),V((4,L,PIECE)),V(tr),V(tr),V((NT,NZ,NX,NC,ROWS,3*PIECE)),V(row,F32),
            V((NT,NZ,NX,NC,ROWS,PIECE)),V((512,D)),V((8,D),F32),V((16,D+128),F32),V((16,2*(PIECE+128)),F32),V((8,D),F32),
            V((4,8,128),F32),V((3,8,128),F32),V((4,8,128),F32),
            V((NT,NZ,NX,NC,16,128)),V((NZ,16,128)),V((NZ,NC,16,128)),V((3,16,128)),V((NZ,NX,NC,16,128)),V((NT,NZ,NX,NC,1,2048),F32),V((32,2048),F32),V((512,32),F32),V((256,32),F32),V((D,32),F32),
            V((NT,NZ,NX,NC,ROWS,GBW)),V((NT,NZ,NX,ROWS,RW)),V((NT,NZ,ROWS,RWA)),V((NZ,NX,ROWS,RWB)),V((NZ,ROWS,RWP)),V((3,ROWS,RWP)),
            V((NT,NZ,ROWS,RWQ)),V((3,NT,ROWS,RWQ)),V((ROWS,RWQ)),
            DMA((n,)),DMA((n,)),DMA((n,2)),DMA((n,2)),DMA((n,3)),DMA((n,3)),DMA((n,3)),DMA((n,3)),DMA((10,)),DMA((12,)),DMA((2,4)),DMA((6,)),DMA((6,)),DMA((2,2)),DMA((6,)),DMA((6,)),DMA((6,)),DMA((6,))],
        compiler_params=pltpu.CompilerParams(collective_id=cid,has_side_effects=True,vmem_limit_bytes=63*2**20),name="back")(
            q,k,v,dob,o,lse,dmbT,abT,drbT,hbT,hid,dub,dr1,wqkv,aux,out_win,seg,featp,sums,bups,tstate)

def greet_out():
    zp,xp,yp,sp=peers()
    bar=pltpu.get_barrier_semaphore()
    for d in zp+[xp,yp,sp]:
        pl.semaphore_signal(bar,inc=1,device_id=d,device_id_type=MESH)
def greet_in():
    pl.semaphore_wait(pltpu.get_barrier_semaphore(),6)

def update_kernel(*refs):
    red,w2g,w1g,vecg,tot,seg_ref,ow,op,op2,iw,ip=refs[:11]
    hbm=refs[11:38]
    out_o,in_o,norm_o=refs[38:41]
    far=refs[41:68]
    ps,ns=refs[68:95],refs[95:122]
    ms,vs,avs=ps[:9],ps[9:18],ps[18:]
    nm,nv,na=ns[:9],ns[9:18],ns[18:]
    mine,theirs,mid,sem,psem,nsem=refs[122:]
    pin=[pltpu.make_async_copy(a,b,psem.at[n]) for n,(a,b) in enumerate(zip(hbm,ps))]
    for q in pin: q.start()
    t=lax.axis_index("tensor")
    half=lambda k:pl.ds(pl.multiple_of(k*512,512),512)
    ins=[]
    for n,(w,ps_) in enumerate(((ow,(op,op2)),(iw,(ip,)))):
        ins.append(pltpu.make_async_copy(w,mine.at[n],sem.at[n,0]))
        step=L//len(ps_)
        ins+=[pltpu.make_async_copy(p,theirs.at[n,pl.ds(m*step,step),:],sem.at[n,5+m]) for m,p in enumerate(ps_)]
    for q in ins: q.start()
    norm=jnp.sqrt(tot[...])
    norm_o[0,0]=norm[0,0]
    factor=(1.0/jnp.maximum(norm,1.0))[0:1,0:1]
    rate=4.0*math.sqrt(MPARAMS/D)
    def upd(i,idx,g):
        sc=g*factor
        vel=MOMENTUM*vs[i][idx]+sc
        fm=ms[i][idx]-rate*(sc+MOMENTUM*vel)
        nv[i][idx]=vel; nm[i][idx]=fm
        na[i][idx]=AVERAGE_DECAY*avs[i][idx]+(1.0-AVERAGE_DECAY)*fm
    al=slice(None)
    for q in pin: q.wait()
    nout=[pltpu.make_async_copy(a,b,nsem.at[n]) for n,(a,b) in enumerate(zip(ns,far))]
    def flush(i):
        for n in (i,i+9,i+18): nout[n].start()
    for n in range(3):
        for c in range(3):
            b=9*PIECE+n*PIECE+c*128
            upd(0,(c,al,slice(n*128,(n+1)*128)),red[:,b:b+128])
    flush(0)
    upd(1,(al,al),red[:,8*PIECE:9*PIECE])
    flush(1)
    for j in range(4):
        upd(2,(al,j,al),red[:,(4+j)*PIECE:(5+j)*PIECE])
        upd(3,(j,),red[:,j*PIECE:(j+1)*PIECE])
    flush(2); flush(3)
    upd(4,(al,al),w1g[0:8,:])
    upd(5,(al,al),w2g[...])
    upd(6,(al,al),vecg[13:14,0:32])
    upd(7,(al,0,al),vecg[7:13,0:24])
    upd(8,(al,al),vecg[0:7,0:48])
    for i in range(4,9): flush(i)
    own=jnp.broadcast_to(jnp.where(seg_ref[:,512:1024]==t,1.0,0.0),(128,512)).T[:,0:1]>0.5
    for q in ins: q.wait()
    last=[]
    for n,o in enumerate((out_o,in_o)):
        last+=[pltpu.make_async_copy(mine.at[n,half(t),:],o.at[half(2*t),:],sem.at[n,2]),pltpu.make_async_copy(theirs.at[n,half(1-t),:],o.at[half(2*(1-t)),:],sem.at[n,3])]
        mid[n]=jnp.where(own,mine[n,half(1-t),:].astype(F32),theirs[n,half(t),:].astype(F32)).astype(BF)
        last.append(pltpu.make_async_copy(mid.at[n],o.at[pl.ds(512,512),:],sem.at[n,4]))
        for q in last[-3:]: q.start()
    for q in last+nout: q.wait()

def update(red,w2g,w1g,vecg,tot,seg,ow,op,op2,iw,ip,masters,moments,averages):
    A=pl.BlockSpec(memory_space=pl.ANY); M=pl.BlockSpec(memory_space=pltpu.VMEM)
    sd=jax.ShapeDtypeStruct
    ps=[sd(m.shape,F32) for m in masters]
    whole=sd((PACK,D),BF)
    return pl.pallas_call(update_kernel,in_specs=[M]*6+[A]*5+[A]*27,out_specs=[A,A,pl.BlockSpec(memory_space=pltpu.SMEM)]+[A]*27,
        out_shape=[whole,whole,sd((1,1),F32)]+ps*3,
        scratch_shapes=[pltpu.VMEM(p.shape,F32) for p in ps*6]+[pltpu.VMEM((2,L,D),BF),pltpu.VMEM((2,L,D),BF),pltpu.VMEM((2,512,D),BF),pltpu.SemaphoreType.DMA((2,7)),pltpu.SemaphoreType.DMA((27,)),pltpu.SemaphoreType.DMA((27,))],
        compiler_params=pltpu.CompilerParams(vmem_limit_bytes=63*2**20),name="upd")(red,w2g,w1g,vecg,tot,seg,ow,op,op2,iw,ip,*masters,*moments,*averages)

def shards_fast(tokens,cotangent,segment_ids,timesteps,*params):
    def turn(n,p): return {0:lambda:p.transpose(1,0,2),1:lambda:p.T,3:lambda:p.transpose(0,2,1),6:lambda:p.reshape(1,-1)}.get(n,lambda:p)()
    def back_turn(n,p): return {0:lambda:p.transpose(1,0,2),1:lambda:p.T,3:lambda:p.transpose(0,2,1),6:lambda:p.reshape(-1)}.get(n,lambda:p)()
    line=lambda ps:[turn(n,p) for n,p in enumerate(ps)]
    masters,moments,averages=line(params[:9]),line(params[9:18]),line(params[18:])
    q,k,v,o,lse,out_win,out_peer,dmbT,abT,drbT,hid,dub,dr1,dob,hbT,wq6,aux6,sums,bups,tstate,featp=front(timesteps,masters,tokens,cotangent,segment_ids)
    in_win,in_peer,out_peer2,red,w2g,w1g,vecg,total=back(q,k,v,dob,o,lse,dmbT,abT,drbT,hbT,hid,dub,dr1,wq6,aux6,out_win,segment_ids,featp,sums,bups,tstate)
    res=update(red,w2g,w1g,vecg,total,segment_ids,out_win,out_peer,out_peer2,in_win,in_peer,masters,moments,averages)
    return (res[0],res[1],res[2].reshape(()))+tuple(back_turn(n%9,r) for n,r in enumerate(res[3:]))


def solution(mesh):
    fast=dict(mesh.shape)=={'dp':16,'tensor':2}
    return jax.shard_map(
        shards_fast if fast else shards_any,
        mesh=mesh,
        in_specs=(
            P("dp", None),
            P("dp", None),
            P("dp", None),
            P("dp", None),
            P("dp", None, "tensor"),
            P("tensor", "dp"),
            P("dp", None, "tensor"),
            P(None, "tensor", "dp"),
            P("dp", None),
            P("dp", None),
            P("dp"),
            P(None, "tensor", "dp"),
            P(None, "dp"),
            P("dp", None, "tensor"),
            P("tensor", "dp"),
            P("dp", None, "tensor"),
            P(None, "tensor", "dp"),
            P("dp", None),
            P("dp", None),
            P("dp"),
            P(None, "tensor", "dp"),
            P(None, "dp"),
            P("dp", None, "tensor"),
            P("tensor", "dp"),
            P("dp", None, "tensor"),
            P(None, "tensor", "dp"),
            P("dp", None),
            P("dp", None),
            P("dp"),
            P(None, "tensor", "dp"),
            P(None, "dp"),
        ),
        out_specs=(
            P("dp", None),
            P("dp", None),
            P(),
            P("dp", None, "tensor"),
            P("tensor", "dp"),
            P("dp", None, "tensor"),
            P(None, "tensor", "dp"),
            P("dp", None),
            P("dp", None),
            P("dp"),
            P(None, "tensor", "dp"),
            P(None, "dp"),
            P("dp", None, "tensor"),
            P("tensor", "dp"),
            P("dp", None, "tensor"),
            P(None, "tensor", "dp"),
            P("dp", None),
            P("dp", None),
            P("dp"),
            P(None, "tensor", "dp"),
            P(None, "dp"),
            P("dp", None, "tensor"),
            P("tensor", "dp"),
            P("dp", None, "tensor"),
            P(None, "tensor", "dp"),
            P("dp", None),
            P("dp", None),
            P("dp"),
            P(None, "tensor", "dp"),
            P(None, "dp"),
        ),
        check_vma=False,
    )
```
